32 devices in a mesh: frames: 16 (over z, y, core), mp: 2 (over x).
Axes of the slice: x: 2, y: 2, z: 4, core: 2. Of those that a mesh axis runs over, the one named last changes fastest.
Arguments:
- latents: float32 [256, 1024], P('frames'), may hold values from -6 to 6
- noise: float32 [256, 1024], P('frames'), may hold values from -6 to 6
- levels: float32 [256], P('frames'), may hold values from 0.05 to 0.95
- clip_ids: int32 [256], replicated, may hold values from 0 to 7, never falling along the last dimension, each value on 1 to 64 neighbouring positions
- clean_flags: int32 [256], replicated, may hold values 0 or 1
- attn_weights: float32 [4, 1024, 1024], P(None, 'frames', 'mp')
- mlp_weights: float32 [2, 1024, 4096], P(None, 'frames', 'mp'), may hold values from -0.1875 to 0.1875
- mod_weight: float32 [1024, 6144], P('frames', 'mp'), may hold values from -0.1875 to 0.1875
- small_weights: float32 [1312, 1024], P(None, ('frames', 'mp'))
- attn_moment: float32 [4, 1024, 1024], P(None, 'frames', 'mp'), may hold values from -0.01171875 to 0.01171875
- mlp_moment: float32 [2, 1024, 4096], P(None, 'frames', 'mp'), may hold values from -0.01171875 to 0.01171875
- mod_moment: float32 [1024, 6144], P('frames', 'mp'), may hold values from -0.01171875 to 0.01171875
- small_moment: float32 [1312, 1024], P(None, ('frames', 'mp')), may hold values from -0.01171875 to 0.01171875
- attn_average: float32 [4, 1024, 1024], P(None, 'frames', 'mp'), may hold values from -0.1875 to 0.1875
- mlp_average: float32 [2, 1024, 4096], P(None, 'frames', 'mp'), may hold values from -0.1875 to 0.1875
- mod_average: float32 [1024, 6144], P('frames', 'mp'), may hold values from -0.1875 to 0.1875
- small_average: float32 [1312, 1024], P(None, ('frames', 'mp')), may hold values from -0.1875 to 0.1875
Outputs:
- loss_sum: float32 [], replicated
- noised_count: float32 [], replicated
- attn_new: float32 [4, 1024, 1024], P(None, 'frames', 'mp')
- attn_moment_new: float32 [4, 1024, 1024], P(None, 'frames', 'mp')
- attn_average_new: float32 [4, 1024, 1024], P(None, 'frames', 'mp')
- attn_copy: bfloat16 [4, 1024, 1024], P(None, 'frames', 'mp')
- mlp_new: float32 [2, 1024, 4096], P(None, 'frames', 'mp')
- mlp_moment_new: float32 [2, 1024, 4096], P(None, 'frames', 'mp')
- mlp_average_new: float32 [2, 1024, 4096], P(None, 'frames', 'mp')
- mlp_copy: bfloat16 [2, 1024, 4096], P(None, 'frames', 'mp')
- mod_new: float32 [1024, 6144], P('frames', 'mp')
- mod_moment_new: float32 [1024, 6144], P('frames', 'mp')
- mod_average_new: float32 [1024, 6144], P('frames', 'mp')
- mod_copy: bfloat16 [1024, 6144], P('frames', 'mp')
- small_new: float32 [1312, 1024], P(None, ('frames', 'mp'))
- small_moment_new: float32 [1312, 1024], P(None, ('frames', 'mp'))
- small_average_new: float32 [1312, 1024], P(None, ('frames', 'mp'))
- small_copy: bfloat16 [1312, 1024], P(None, ('frames', 'mp'))
The draws below stay inside these ranges and needn't reach their ends.
Inputs may be any that keep to these rules, and one draw needn't show every extreme that they name: clip_ids never fall along the frames; each clip holds 1 to 64 frames, and some clip holds exactly 64.
All inputs are finite; a program needn't handle non-finite values.
Results may differ from the reference program's by a relative error of at most 0.0085.
Values may be sent and summed in bfloat16 or wider, within the bound.
A program may use at most 320 MiB of HBM per device.

```python
import math
import jax
import jax.numpy as jnp
import numpy as np
from jax import lax

D = 1024
HEADS = 16
HD = 64
FF = 4096
CH = 4
FREQ = 256
GRID = 16
CLIP_MOST = 64
FRAMES_DEV = 16
P_SIZE = 16
TPF = 64
PD = 1024
REACH = 4
FRAMES = 256
TOKENS = 16384


def draw_attn_weights(key, part):
    key = jax.random.fold_in(key, 11)
    sample = jnp.clip(jax.random.normal(key, (4, D, D), jnp.float32), -4.0, 4.0)
    block_scale = jnp.array([1.0, 1.0, 1.0, 16.0], jnp.float32) * D ** (-0.5)
    return sample * block_scale[:, None, None]


def draw_small_weights(key, part):
    key = jax.random.fold_in(key, 12)
    row_count = FREQ + D + 2 * P_SIZE
    sample = jnp.clip(jax.random.normal(key, (row_count, D), jnp.float32), -4.0, 4.0)
    row_index = jnp.arange(row_count)
    row_scale = jnp.where(row_index < FREQ, FREQ ** (-0.5), jnp.where(row_index < FREQ + D, D ** (-0.5), jnp.where(row_index < FREQ + D + P_SIZE, P_SIZE ** (-0.5), D ** (-0.5))))
    return sample * row_scale[:, None]


def place_ends(values, stream_key, low, largest):
    extent = values.shape
    place = [jax.random.randint(jax.random.fold_in(stream_key, axis), (), 0, extent[axis]) for axis in range(len(extent))]
    values = values.at[tuple(place)].set(low)
    longest = extent.index(max(extent))
    place[longest] = (place[longest] + 1) % extent[longest]
    return values.at[tuple(place)].set(largest)


def level_of(stream_key, shape, split, least, high):
    gain = 1.0
    for dim, parts in split:
        steps = jax.random.uniform(jax.random.fold_in(jax.random.fold_in(stream_key, 6), dim), (parts,), jnp.float32, least / len(split), high / len(split))
        gain = gain * jnp.repeat(jnp.exp(steps), shape[dim] // parts).reshape((-1,) + (1,) * (len(shape) - 1 - dim))
    return gain


def profile(number_of, total, reach, slope):
    loads = [(1 << 20) // math.isqrt(standing ** slope) + 1 for standing in range(2, number_of + 1)]
    rest, holding = total - reach - (number_of - 1), [1] * (number_of - 1)
    while rest > 0:
        candidates = [i for i in range(number_of - 1) if holding[i] < reach]
        pool, remaining = sum([loads[i] for i in candidates]), rest
        for i in candidates:
            more = min(reach - holding[i], max(1, remaining * loads[i] // pool), rest)
            holding[i] = holding[i] + more
            rest = rest - more
    return np.array([reach] + holding)


def ragged(stream_key, number_of, total, reach, lean):
    if number_of == 2:
        one = jax.random.randint(stream_key, (), max(1, total - reach), min(reach, total - 1) + 1)
        return jnp.stack([one, total - one])
    lengths = jnp.asarray(profile(number_of, total, reach, lean), jnp.int32)
    pairs = (number_of - 1) // 2
    donor, sink = lengths[1:1 + 2 * pairs:2], lengths[2:2 + 2 * pairs:2]
    room = jnp.minimum(donor - 1, reach - sink)
    moved = jax.random.randint(jax.random.fold_in(stream_key, 1), (pairs,), 0, 1 << 20) % (room + 1)
    lengths = lengths.at[1:1 + 2 * pairs:2].set(donor - moved).at[2:2 + 2 * pairs:2].set(sink + moved)
    return lengths[jax.random.permutation(jax.random.fold_in(stream_key, 2), number_of)]


def gaussian(stream_key, dims, spread, reach, cuts=(), kind=jnp.bfloat16):
    result = jax.random.normal(stream_key, dims, jnp.float32) * spread
    if len(cuts) > 0:
        result = level_of(stream_key, dims, cuts, -0.22, 0.18) * result
    return jnp.clip(result, min=-reach, max=reach).astype(kind)


def setup_inputs(seed: int = 0) -> dict:
    streams_of = jax.random.split(jax.random.key(seed), 18)
    return {
        "latents": gaussian(streams_of[0], (FRAMES, PD), 1.0, 6.0, ((0, 16),), jnp.float32),
        "noise": gaussian(streams_of[1], (FRAMES, PD), 1.0, 6.0, ((0, 16),), jnp.float32),
        "levels": jnp.clip(0.05 + 0.9 * jax.random.uniform(streams_of[2], (FRAMES,), jnp.float32) ** level_of(streams_of[2], (FRAMES,), ((0, 16),), -0.2, 0.2), 0.05, 0.95),
        "clip_ids": jnp.searchsorted(jnp.cumsum(ragged(streams_of[3], FRAMES // (CLIP_MOST // 2), FRAMES, CLIP_MOST, 1)), jnp.arange(FRAMES), side="right").astype(jnp.int32),
        "clean_flags": place_ends((jax.random.randint(streams_of[4], (FRAMES,), 0, 4) < 1).astype(jnp.int32), jax.random.fold_in(streams_of[4], 1), 0, 1),
        "attn_weights": draw_attn_weights(jax.random.fold_in(streams_of[17], 71), 0),
        "mlp_weights": gaussian(streams_of[6], (2, D, FF), D ** -0.5, 0.1875, ((1, 16), (2, 2)), jnp.float32),
        "mod_weight": gaussian(streams_of[7], (D, 6 * D), D ** -0.5, 0.1875, ((0, 16), (1, 2)), jnp.float32),
        "small_weights": draw_small_weights(jax.random.fold_in(streams_of[17], 71), 0),
        "attn_moment": gaussian(streams_of[9], (4, D, D), (TOKENS * P_SIZE) ** -0.5, 0.01171875, ((1, 16), (2, 2)), jnp.float32),
        "mlp_moment": gaussian(streams_of[10], (2, D, FF), (TOKENS * P_SIZE) ** -0.5, 0.01171875, ((1, 16), (2, 2)), jnp.float32),
        "mod_moment": gaussian(streams_of[11], (D, 6 * D), (TOKENS * P_SIZE) ** -0.5, 0.01171875, ((0, 16), (1, 2)), jnp.float32),
        "small_moment": gaussian(streams_of[12], (FREQ + D + 2 * P_SIZE, D), (TOKENS * P_SIZE) ** -0.5, 0.01171875, ((1, 32),), jnp.float32),
        "attn_average": gaussian(streams_of[13], (4, D, D), D ** -0.5, 0.1875, ((1, 16), (2, 2)), jnp.float32),
        "mlp_average": gaussian(streams_of[14], (2, D, FF), D ** -0.5, 0.1875, ((1, 16), (2, 2)), jnp.float32),
        "mod_average": gaussian(streams_of[15], (D, 6 * D), D ** -0.5, 0.1875, ((0, 16), (1, 2)), jnp.float32),
        "small_average": gaussian(streams_of[16], (FREQ + D + 2 * P_SIZE, D), D ** -0.5, 0.1875, ((1, 32),), jnp.float32),
    }


@jax.custom_vjp
def low(v):
    return lax.optimization_barrier(v.astype(jnp.bfloat16)).astype(jnp.float32)

@jax.custom_vjp
def low_back(v):
    return v

def low_keep(v):
    return (low(v), None)

def low_pass(kept, grad):
    return (grad,)

def back_keep(v):
    return (v, None)

def back_low(kept, grad):
    return (low(grad),)
low.defvjp(low_keep, low_pass)
low_back.defvjp(back_keep, back_low)
HIGH = lax.Precision.HIGHEST
EPSILON = 1e-06
MOMENTUM = 0.5
EMA_DECAY = 0.5

def rotation_matrix(head_width):
    groups = [head_width // 4, 3 * head_width // 8, 3 * head_width // 8]
    rotation = np.zeros((head_width, head_width), np.float32)
    offset = 0
    for group_size in groups:
        half_size = group_size // 2
        for pair_index in range(half_size):
            rotation[offset + half_size + pair_index, offset + pair_index] = -1.0
            rotation[offset + pair_index, offset + half_size + pair_index] = 1.0
        offset += group_size
    return rotation

def rotary_angles(frame_pos, row_pos, col_pos, head_width):
    pieces = []
    for position, group_size in ((frame_pos, head_width // 4), (row_pos, 3 * head_width // 8), (col_pos, 3 * head_width // 8)):
        half_size = group_size // 2
        frequency = 10000.0 ** (-jnp.arange(half_size, dtype=jnp.float32) / half_size)
        phases = position[:, None] * frequency[None, :]
        pieces += [phases, phases]
    return jnp.concatenate(pieces, axis=1)

def clip_positions(clip_ids):
    frame_index = jnp.arange(clip_ids.shape[0], dtype=jnp.int32)
    starts_here = jnp.concatenate([jnp.ones((1,), bool), clip_ids[1:] != clip_ids[:-1]])
    clip_start = lax.cummax(jnp.where(starts_here, frame_index, 0), axis=0)
    return frame_index - clip_start

def patchify(frame_data):
    frame_total = frame_data.shape[0]
    patch_side = GRID // 2
    shaped = frame_data.reshape(frame_total, CH, patch_side, 2, patch_side, 2)
    return shaped.transpose(0, 2, 4, 1, 3, 5).reshape(frame_total * patch_side * patch_side, CH * 4)

def layer_norm(vector):
    row_mean = lax.optimization_barrier(jnp.mean(vector, axis=-1, keepdims=True))
    centred = vector - row_mean
    variance = lax.optimization_barrier(jnp.mean(centred * centred, axis=-1, keepdims=True))
    return centred * lax.rsqrt(variance + EPSILON)

def time_features(level_eff):
    half_size = FREQ // 2
    frequency = jnp.exp(-math.log(10000.0) * jnp.arange(half_size, dtype=jnp.float32) / half_size)
    phases = (level_eff * 1000.0)[:, None] * frequency[None, :]
    return jnp.concatenate([jnp.cos(phases), jnp.sin(phases)], axis=1)

def conditioning_of(features, time_rows):
    first_layer = jax.nn.silu(jnp.dot(features, time_rows[:FREQ], precision=HIGH))
    return jax.nn.silu(jnp.dot(first_layer, time_rows[FREQ:FREQ + D], precision=HIGH))

def rotate(vector, cosine_table, sine_table, rotation):
    turned = jnp.einsum('thd,de->the', vector, rotation, precision=HIGH)
    return vector * cosine_table[:, None, :] + turned * sine_table[:, None, :]

def attend(queries, key_rows, value_rows, clip_tok, frame_tok):
    block_rows = FRAMES_DEV * TPF
    key_span = (REACH + 1) * block_rows
    margin = REACH * block_rows
    pad_keys = jnp.concatenate([jnp.zeros((margin, HEADS, HD), key_rows.dtype), key_rows])
    pad_values = jnp.concatenate([jnp.zeros((margin, HEADS, HD), value_rows.dtype), value_rows])
    pad_clip = jnp.concatenate([jnp.full((margin,), -1, jnp.int32), clip_tok])
    pad_frame = jnp.concatenate([jnp.full((margin,), -1, jnp.int32), frame_tok])

    def one_block(start):
        query_block = lax.dynamic_slice_in_dim(queries, start, block_rows)
        key_block = lax.dynamic_slice_in_dim(pad_keys, start, key_span)
        value_block = lax.dynamic_slice_in_dim(pad_values, start, key_span)
        clip_query = lax.dynamic_slice_in_dim(clip_tok, start, block_rows)
        frame_query = lax.dynamic_slice_in_dim(frame_tok, start, block_rows)
        clip_key = lax.dynamic_slice_in_dim(pad_clip, start, key_span)
        frame_key = lax.dynamic_slice_in_dim(pad_frame, start, key_span)
        scores = jnp.einsum('qhd,khd->hqk', query_block, key_block, precision=HIGH) * HD ** (-0.5)
        scores = low_back(scores)
        allowed = (clip_query[:, None] == clip_key[None, :]) & (frame_key[None, :] <= frame_query[:, None])
        scores = jnp.where(allowed[None], scores, -1e+30)
        attn_probs = low(jax.nn.softmax(scores, axis=-1))
        return jnp.einsum('hqk,khd->qhd', attn_probs, value_block, precision=HIGH)
    starts = jnp.arange(TOKENS // block_rows, dtype=jnp.int32) * block_rows
    return lax.map(jax.checkpoint(one_block), starts).reshape(TOKENS, HEADS, HD)

def reference(latents, noise, levels, clip_ids, clean_flags, attn_weights, mlp_weights, mod_weight, small_weights, attn_moment, mlp_moment, mod_moment, small_moment, attn_average, mlp_average, mod_average, small_average):
    patch_side = GRID // 2
    noised = (1 - clean_flags).astype(jnp.float32)
    level_eff = levels * noised
    signal_scale = jnp.repeat(jnp.cos(0.5 * math.pi * level_eff), TPF)
    noise_scale = jnp.repeat(jnp.sin(0.5 * math.pi * level_eff), TPF)
    clean_patches = patchify(latents)
    noise_patches = patchify(noise)
    inputs = signal_scale[:, None] * clean_patches + noise_scale[:, None] * noise_patches
    frame_tok = jnp.repeat(jnp.arange(FRAMES, dtype=jnp.int32), TPF)
    clip_tok = jnp.repeat(clip_ids, TPF)
    in_clip = jnp.repeat(clip_positions(clip_ids), TPF).astype(jnp.float32)
    within = jnp.arange(TOKENS, dtype=jnp.int32) % TPF
    angles = rotary_angles(in_clip, (within // patch_side).astype(jnp.float32), (within % patch_side).astype(jnp.float32), HD)
    cosine_table = jnp.cos(angles)
    sine_table = jnp.sin(angles)
    rotation = jnp.asarray(rotation_matrix(HD))
    token_weight = jnp.repeat(noised, TPF) / (TPF * P_SIZE)
    noised_count = jnp.sum(noised)
    features = time_features(level_eff)

    def loss_of(attn_param, mlp_param, mod_param, small_param):
        attn_param = low(attn_param)
        mlp_param = low(mlp_param)
        mod_param = low(mod_param)
        small_param = low(small_param)
        conditioning = conditioning_of(features, small_param[:FREQ + D])
        modulation = jnp.dot(conditioning, mod_param, precision=HIGH)
        pieces = [modulation[:, None, piece_index * D:(piece_index + 1) * D] for piece_index in range(6)]
        shift_one, scale_one, gate_one, shift_two, scale_two, gate_two = pieces
        hidden = low_back(jnp.dot(low(inputs), small_param[FREQ + D:FREQ + D + P_SIZE], precision=HIGH))
        shaped = hidden.reshape(FRAMES, TPF, D)
        normed = low((layer_norm(shaped) * (1.0 + scale_one) + shift_one).reshape(TOKENS, D))
        queries = low(rotate(low_back(jnp.dot(normed, attn_param[0], precision=HIGH)).reshape(TOKENS, HEADS, HD), cosine_table, sine_table, rotation))
        key_rows = low(rotate(low_back(jnp.dot(normed, attn_param[1], precision=HIGH)).reshape(TOKENS, HEADS, HD), cosine_table, sine_table, rotation))
        value_rows = low_back(low(jnp.dot(normed, attn_param[2], precision=HIGH))).reshape(TOKENS, HEADS, HD)
        mixed_heads = attend(queries, key_rows, value_rows, clip_tok, frame_tok)
        mixed_heads = low_back(low(mixed_heads.reshape(TOKENS, D)))
        attended = low_back(jnp.dot(mixed_heads, attn_param[3].T, precision=HIGH))
        shaped = shaped + gate_one * attended.reshape(FRAMES, TPF, D)
        normed = low((layer_norm(shaped) * (1.0 + scale_two) + shift_two).reshape(TOKENS, D))
        up_proj = low_back(jnp.dot(normed, mlp_param[0], precision=HIGH))
        activated = low(jax.nn.gelu(up_proj))
        output = low_back(jnp.dot(activated, mlp_param[1].T, precision=HIGH))
        shaped = shaped + gate_two * output.reshape(FRAMES, TPF, D)
        final_norm = low(layer_norm(shaped).reshape(TOKENS, D))
        predicted = low_back(jnp.dot(final_norm, small_param[FREQ + D + P_SIZE:].T, precision=HIGH))
        misfit = predicted - noise_patches
        return jnp.sum(token_weight[:, None] * misfit * misfit)
    loss_sum, pull_back = jax.vjp(loss_of, attn_weights, mlp_weights, mod_weight, small_weights)
    grad_attn, grad_mlp, grad_mod, grad_small = pull_back(1.0 / jnp.maximum(noised_count, 1.0))
    learning_rate = 0.5 * math.sqrt(TOKENS * P_SIZE / D)

    def update(weight, gradient, moment, average):
        moment_new = MOMENTUM * moment + gradient
        weight_new = weight - learning_rate * (gradient + MOMENTUM * moment_new)
        average_new = EMA_DECAY * average + (1.0 - EMA_DECAY) * weight_new
        return (weight_new, moment_new, average_new, weight_new.astype(jnp.bfloat16))
    attn_new, attn_moment_new, attn_average_new, attn_copy = update(attn_weights, grad_attn, attn_moment, attn_average)
    mlp_new, mlp_moment_new, mlp_average_new, mlp_copy = update(mlp_weights, grad_mlp, mlp_moment, mlp_average)
    mod_new, mod_moment_new, mod_average_new, mod_copy = update(mod_weight, grad_mod, mod_moment, mod_average)
    small_new, small_moment_new, small_average_new, small_copy = update(small_weights, grad_small, small_moment, small_average)
    return (loss_sum, noised_count, attn_new, attn_moment_new, attn_average_new, attn_copy, mlp_new, mlp_moment_new, mlp_average_new, mlp_copy, mod_new, mod_moment_new, mod_average_new, mod_copy, small_new, small_moment_new, small_average_new, small_copy)
```

```python
import functools
import math

import jax
import jax.numpy as jnp
import numpy as np
from jax import lax
from jax.experimental import pallas as pl
from jax.experimental.pallas import tpu as pltpu
from jax.sharding import PartitionSpec as P

D = 1024
HD = 64
CH = 4
FREQ = 256
GRID = 16
P_SIZE = 16
TPF = 64
REACH = 4


HIGH = lax.Precision.HIGHEST
EPSILON = 1e-06
MOMENTUM = 0.5
EMA_DECAY = 0.5


def shifted(shard, axis, by):
    peers = lax.axis_size(axis)
    pairs = [(i, i + by) for i in range(peers) if 0 <= i + by < peers]
    return lax.ppermute(shard, axis, pairs)


def rotation_matrix(head_width):
    groups = [head_width // 4, 3 * head_width // 8, 3 * head_width // 8]
    rotation = np.zeros((head_width, head_width), np.float32)
    offset = 0
    for group_size in groups:
        half_size = group_size // 2
        for pair_index in range(half_size):
            rotation[offset + half_size + pair_index, offset + pair_index] = -1.0
            rotation[offset + pair_index, offset + half_size + pair_index] = 1.0
        offset += group_size
    return rotation


def rotary_angles(frame_pos, row_pos, col_pos, head_width):
    pieces = []
    for position, group_size in (
        (frame_pos, head_width // 4),
        (row_pos, 3 * head_width // 8),
        (col_pos, 3 * head_width // 8),
    ):
        half_size = group_size // 2
        frequency = 10000.0 ** (-jnp.arange(half_size, dtype=jnp.float32) / half_size)
        phases = position[:, None] * frequency[None, :]
        pieces += [phases, phases]
    return jnp.concatenate(pieces, axis=1)


def clip_positions(clip_ids):
    frame_index = jnp.arange(clip_ids.shape[0], dtype=jnp.int32)
    starts_here = jnp.concatenate([jnp.ones((1,), bool), clip_ids[1:] != clip_ids[:-1]])
    clip_start = lax.cummax(jnp.where(starts_here, frame_index, 0), axis=0)
    return frame_index - clip_start


def patchify(frame_data):
    frame_total = frame_data.shape[0]
    patch_side = GRID // 2
    shaped = frame_data.reshape(frame_total, CH, patch_side, 2, patch_side, 2)
    return shaped.transpose(0, 2, 4, 1, 3, 5).reshape(frame_total * patch_side * patch_side, CH * 4)


def layer_norm(vector):
    row_mean = jnp.mean(vector, axis=-1, keepdims=True)
    centred = vector - row_mean
    variance = jnp.mean(centred * centred, axis=-1, keepdims=True)
    return centred * lax.rsqrt(variance + EPSILON)


def modulate_local(shaped, shift_rows, scale_rows):
    return layer_norm(shaped) * (1.0 + scale_rows) + shift_rows


def time_features(level_eff):
    half_size = FREQ // 2
    frequency = jnp.exp(-math.log(10000.0) * jnp.arange(half_size, dtype=jnp.float32) / half_size)
    phases = (level_eff * 1000.0)[:, None] * frequency[None, :]
    return jnp.concatenate([jnp.cos(phases), jnp.sin(phases)], axis=1)


def rotate_back(gradient, cosine_table, sine_table, rotation):
    scaled = gradient * sine_table
    high = scaled.astype(jnp.bfloat16)
    left = scaled - high.astype(jnp.float32)
    middle = left.astype(jnp.bfloat16)
    low = (left - middle.astype(jnp.float32)).astype(jnp.bfloat16)
    turned = sum(
        jnp.einsum("te,de->td", part, rotation, preferred_element_type=jnp.float32)
        for part in (high, middle, low)
    )
    return (gradient * cosine_table + turned).astype(jnp.bfloat16)


NT=(((1,),(1,)),((),()))
NN=(((1,),(0,)),((),()))

def dotf(a,b,dims=NN):
    return lax.dot_general(a,b,dims,preferred_element_type=jnp.float32)

def split_pair(xT):
    r=lax.broadcasted_iota(jnp.int32,xT.shape,0)
    z=jnp.zeros_like(xT)
    return jnp.where(r<HD,xT,z), jnp.where(r<HD,z,xT)

def keep_of(t,TK,TQ,cs,qf):
    kf=lax.broadcasted_iota(jnp.int32,(TK,TQ),0)//TPF+t*(TK//TPF)
    return (kf>=cs)&(kf<=qf)

def fwd_kernel(lo_ref,mid_ref,hi_ref,q_ref,k_ref,v_ref,cs_ref,o_ref,lse_ref,vT,*,TQ,TK,W0,NQ):
    KS=k_ref.shape[0]
    def tr(i,_):
        s=pl.multiple_of(i*TK,TK)
        vT[:,pl.ds(s,TK)]=v_ref[pl.ds(s,TK),:].T
        return 0
    lax.fori_loop(lo_ref[0],KS//TK,tr,0)
    def qtile(j,_):
        qs=pl.multiple_of(j*TQ,TQ)
        qT=(q_ref[pl.ds(qs,TQ),:].T)*jnp.bfloat16(0.125)
        qA,qB=split_pair(qT)
        cs=cs_ref[0:1,pl.ds(qs,TQ)]
        qf=lax.broadcasted_iota(jnp.int32,(1,TQ),1)//TPF+(W0+j*(TQ//TPF))
        def step(t,carry,masked):
            ks=pl.multiple_of(t*TK,TK)
            kt=k_ref[pl.ds(ks,TK),:]
            out=[]
            if masked: keep=keep_of(t,TK,TQ,cs,qf)
            for h,(qh,(m,l,o)) in enumerate(zip((qA,qB),carry)):
                s=dotf(kt,qh)
                if masked: s=jnp.where(keep,s,-1e30)
                mn=jnp.maximum(m,jnp.max(s,axis=0,keepdims=True))
                a=jnp.exp(m-mn)
                p=jnp.exp(s-mn)
                l=l*a+jnp.sum(p,axis=0,keepdims=True)
                o=o*a+dotf(vT[h*HD:(h+1)*HD,pl.ds(ks,TK)],p.astype(jnp.bfloat16))
                out.append((mn,l,o))
            return tuple(out)
        init=tuple((jnp.full((1,TQ),-1e29,jnp.float32),jnp.zeros((1,TQ),jnp.float32),jnp.zeros((HD,TQ),jnp.float32)) for _ in range(2))
        c=lax.fori_loop(lo_ref[j],mid_ref[j],lambda t,c:step(t,c,True),init)
        c=lax.fori_loop(mid_ref[j],hi_ref[j],lambda t,c:step(t,c,False),c)
        c=lax.fori_loop(hi_ref[j],(W0*TPF+(j+1)*TQ+TK-1)//TK,lambda t,c:step(t,c,True),c)
        oT=jnp.concatenate([c[0][2]/c[0][1],c[1][2]/c[1][1]],axis=0)
        o_ref[pl.ds(qs,TQ),:]=oT.T.astype(o_ref.dtype)
        lse_ref[0,0:1,pl.ds(qs,TQ)]=c[0][0]+jnp.log(c[0][1])
        lse_ref[0,1:2,pl.ds(qs,TQ)]=c[1][0]+jnp.log(c[1][1])
        return 0
    lax.fori_loop(0,NQ,qtile,0)

def tile_bounds(cs_rel,TQ,TK,W0,NQ):
    fq=TQ//TPF; fk=TK//TPF
    j=jnp.arange(NQ)
    first=cs_rel[::fq]; last=cs_rel[fq-1::fq]
    lo=first//fk
    dg=(W0+j*fq+1)//fk
    mid=jnp.minimum((last+fk-1)//fk,dg)
    mid=jnp.maximum(mid,lo)
    hi=jnp.maximum(dg,mid)
    return lo.astype(jnp.int32),mid.astype(jnp.int32),hi.astype(jnp.int32)

def attn_fwd(q,k,v,cs_rel,TQ=512,TK=512):
    T,Wd=q.shape; KS=k.shape[0]; P=Wd//128
    W0=(KS-T)//TPF; NQ=T//TQ
    lo,mid,hi=tile_bounds(cs_rel,TQ,TK,W0,NQ)
    cs_tok=jnp.broadcast_to(jnp.repeat(cs_rel,TPF)[None,:],(8,T)).astype(jnp.int32)
    return pl.pallas_call(
        functools.partial(fwd_kernel,TQ=TQ,TK=TK,W0=W0,NQ=NQ),
        grid_spec=pltpu.PrefetchScalarGridSpec(num_scalar_prefetch=3,grid=(P,),
            in_specs=[pl.BlockSpec((T,128),lambda p,*_:(0,p)),pl.BlockSpec((KS,128),lambda p,*_:(0,p)),pl.BlockSpec((KS,128),lambda p,*_:(0,p)),pl.BlockSpec((8,T),lambda p,*_:(0,0))],
            out_specs=[pl.BlockSpec((T,128),lambda p,*_:(0,p)),pl.BlockSpec((1,8,T),lambda p,*_:(p,0,0))],
            scratch_shapes=[pltpu.VMEM((128,KS),jnp.bfloat16)]),
        out_shape=[jax.ShapeDtypeStruct((T,Wd),jnp.float32),jax.ShapeDtypeStruct((P,8,T),jnp.float32)],
        compiler_params=pltpu.CompilerParams(vmem_limit_bytes=48<<20),
        cost_estimate=pl.CostEstimate(flops=10**11,bytes_accessed=2*10**7,transcendentals=3*10**7),
        name="attn_forward",
    )(lo,mid,hi,q,k,v,cs_tok)

def bwd_kernel(lo_ref,mid_ref,hi_ref,q_ref,k_ref,v_ref,do_ref,o_ref,lse_ref,cs_ref,dq_ref,dk_ref,dv_ref,kT,dkT,dvT,*,TQ,TK,W0,NQ):
    KS=k_ref.shape[0]
    def tr(i,_):
        s=pl.multiple_of(i*TK,TK)
        kT[:,pl.ds(s,TK)]=k_ref[pl.ds(s,TK),:].T
        return 0
    lax.fori_loop(lo_ref[0],KS//TK,tr,0)
    dkT[...]=jnp.zeros_like(dkT); dvT[...]=jnp.zeros_like(dvT)
    def qtile(j,_):
        qs=pl.multiple_of(j*TQ,TQ)
        qT=(q_ref[pl.ds(qs,TQ),:].T)*jnp.bfloat16(0.125)
        qh=split_pair(qT)
        doT=do_ref[pl.ds(qs,TQ),:].T
        doh=split_pair(doT)
        oT=o_ref[pl.ds(qs,TQ),:].T
        prod=oT*doT.astype(jnp.float32)
        delta=(jnp.sum(prod[:HD],axis=0,keepdims=True),jnp.sum(prod[HD:],axis=0,keepdims=True))
        lse=(lse_ref[0,0:1,pl.ds(qs,TQ)],lse_ref[0,1:2,pl.ds(qs,TQ)])
        cs=cs_ref[0:1,pl.ds(qs,TQ)]
        qf=lax.broadcasted_iota(jnp.int32,(1,TQ),1)//TPF+(W0+j*(TQ//TPF))
        def step(t,carry,masked):
            ks=pl.multiple_of(t*TK,TK)
            kt=k_ref[pl.ds(ks,TK),:]; vt=v_ref[pl.ds(ks,TK),:]
            out=[]
            if masked: keep=keep_of(t,TK,TQ,cs,qf)
            for h in range(2):
                r=slice(h*HD,(h+1)*HD)
                s=dotf(kt,qh[h])
                p=jnp.exp(s-lse[h])
                if masked: p=jnp.where(keep,p,0.0)
                dp=dotf(vt,doh[h])
                ds=(p*(dp-delta[h])).astype(jnp.bfloat16)
                pb=p.astype(jnp.bfloat16)
                dvT[r,pl.ds(ks,TK)]+=dotf(doT[r],pb,NT)
                dkT[r,pl.ds(ks,TK)]+=dotf(qT[r],ds,NT)
                out.append(carry[h]+dotf(kT[r,pl.ds(ks,TK)],ds))
            return tuple(out)
        init=(jnp.zeros((HD,TQ),jnp.float32),)*2
        c=lax.fori_loop(lo_ref[j],mid_ref[j],lambda t,c:step(t,c,True),init)
        c=lax.fori_loop(mid_ref[j],hi_ref[j],lambda t,c:step(t,c,False),c)
        c=lax.fori_loop(hi_ref[j],(W0*TPF+(j+1)*TQ+TK-1)//TK,lambda t,c:step(t,c,True),c)
        dq_ref[pl.ds(qs,TQ),:]=(jnp.concatenate(c,axis=0)*0.125).T
        return 0
    lax.fori_loop(0,NQ,qtile,0)
    def back(i,_):
        s=pl.multiple_of(i*TK,TK)
        dk_ref[pl.ds(s,TK),:]=dkT[:,pl.ds(s,TK)].T.astype(dk_ref.dtype)
        dv_ref[pl.ds(s,TK),:]=dvT[:,pl.ds(s,TK)].T.astype(dv_ref.dtype)
        return 0
    lax.fori_loop(0,KS//TK,back,0)

def attn_bwd(q,k,v,do,o,lse,cs_rel,TQ=512,TK=512,out_dt=jnp.bfloat16):
    T,Wd=q.shape; KS=k.shape[0]; P=Wd//128
    W0=(KS-T)//TPF; NQ=T//TQ
    lo,mid,hi=tile_bounds(cs_rel,TQ,TK,W0,NQ)
    cs_tok=jnp.broadcast_to(jnp.repeat(cs_rel,TPF)[None,:],(8,T)).astype(jnp.int32)
    tb=pl.BlockSpec((T,128),lambda p,*_:(0,p)); kb=pl.BlockSpec((KS,128),lambda p,*_:(0,p))
    return pl.pallas_call(
        functools.partial(bwd_kernel,TQ=TQ,TK=TK,W0=W0,NQ=NQ),
        grid_spec=pltpu.PrefetchScalarGridSpec(num_scalar_prefetch=3,grid=(P,),
            in_specs=[tb,kb,kb,tb,tb,pl.BlockSpec((1,8,T),lambda p,*_:(p,0,0)),pl.BlockSpec((8,T),lambda p,*_:(0,0))],
            out_specs=[tb,kb,kb],
            scratch_shapes=[pltpu.VMEM((128,KS),jnp.bfloat16),pltpu.VMEM((128,KS),jnp.float32),pltpu.VMEM((128,KS),jnp.float32)]),
        out_shape=[jax.ShapeDtypeStruct((T,Wd),jnp.float32),jax.ShapeDtypeStruct((KS,Wd),out_dt),jax.ShapeDtypeStruct((KS,Wd),out_dt)],
        compiler_params=pltpu.CompilerParams(vmem_limit_bytes=56<<20),
        cost_estimate=pl.CostEstimate(flops=2*10**11,bytes_accessed=5*10**7,transcendentals=3*10**7),
        name="attn_backward",
    )(lo,mid,hi,q,k,v,do,o,lse,cs_tok)


def unit_sum(partial_rows):
    return lax.psum(partial_rows.astype(jnp.bfloat16), "mp").astype(jnp.float32)


def update(weight, gradient, moment, average, learning_rate):
    moment_new = MOMENTUM * moment + gradient
    weight_new = weight - learning_rate * (gradient + MOMENTUM * moment_new)
    average_new = EMA_DECAY * average + (1.0 - EMA_DECAY) * weight_new
    return (weight_new, moment_new, average_new, weight_new.astype(jnp.bfloat16))


def per_device(
    latents,
    noise,
    levels,
    clip_ids,
    clean_flags,
    attn_weights,
    mlp_weights,
    mod_weight,
    small_weights,
    attn_moment,
    mlp_moment,
    mod_moment,
    small_moment,
    attn_average,
    mlp_average,
    mod_average,
    small_average,
):
    frame_count = latents.shape[0]
    tok_count = frame_count * TPF
    patch_side = GRID // 2
    frames_total = clip_ids.shape[0]
    tokens_total = frames_total * TPF
    width_local = attn_weights.shape[2]
    heads_local = width_local // HD
    key_span = (REACH + 1) * tok_count
    device = lax.axis_index("frames")
    mp_index = lax.axis_index("mp")
    first_frame = device * frame_count
    scale_qk = HD ** (-0.5)
    w_attn = lax.all_gather(attn_weights.astype(jnp.bfloat16), "frames", axis=1, tiled=True)
    w_mlp = lax.all_gather(mlp_weights.astype(jnp.bfloat16), "frames", axis=1, tiled=True)
    low_mod = mod_weight.astype(jnp.bfloat16)
    w_mod = lax.all_gather(low_mod, "frames", axis=0, tiled=True)
    small_low = lax.all_gather(
        small_weights.astype(jnp.bfloat16), ("frames", "mp"), axis=1, tiled=True
    )
    levels_all = lax.all_gather(levels, "frames", axis=0, tiled=True)
    small_full = small_low.astype(jnp.float32)
    noised_all = (1 - clean_flags).astype(jnp.float32)
    noised_count = jnp.sum(noised_all)
    noised = lax.dynamic_slice_in_dim(noised_all, first_frame, frame_count)
    level_eff = levels * noised
    signal_scale = jnp.repeat(jnp.cos(0.5 * math.pi * level_eff), TPF)
    noise_scale = jnp.repeat(jnp.sin(0.5 * math.pi * level_eff), TPF)
    noise_patches = patchify(noise)
    inputs = signal_scale[:, None] * patchify(latents) + noise_scale[:, None] * noise_patches
    in_clip_all = clip_positions(clip_ids)
    in_clip = jnp.repeat(
        lax.dynamic_slice_in_dim(in_clip_all, first_frame, frame_count), TPF
    ).astype(jnp.float32)
    within = jnp.arange(tok_count, dtype=jnp.int32) % TPF
    angles = rotary_angles(
        in_clip,
        (within // patch_side).astype(jnp.float32),
        (within % patch_side).astype(jnp.float32),
        HD,
    )
    cosine_table = jnp.tile(jnp.cos(angles), (1, heads_local))
    sine_table = jnp.tile(jnp.sin(angles), (1, heads_local))
    rotation = jnp.asarray(
        np.kron(np.eye(heads_local, dtype=np.float32), rotation_matrix(HD)), jnp.bfloat16
    )
    clip_start = (
        lax.dynamic_slice_in_dim(
            jnp.arange(frames_total, dtype=jnp.int32) - in_clip_all, first_frame, frame_count
        )
        - first_frame
        + REACH * frame_count
    )
    features_all = time_features(levels_all * noised_all)
    pre_one = jnp.dot(features_all, small_full[:FREQ], precision=HIGH)
    first_all = jax.nn.silu(pre_one)
    pre_two = jnp.dot(first_all, small_full[FREQ : FREQ + D], precision=HIGH)
    conditioning_all = jax.nn.silu(pre_two)
    conditioning = lax.dynamic_slice_in_dim(conditioning_all, first_frame, frame_count)
    mod_full = w_mod.astype(jnp.float32)
    modulation = lax.all_gather(
        jnp.dot(conditioning, mod_full, precision=HIGH), "mp", axis=1, tiled=True
    )
    pieces = [
        modulation[:, None, piece_index * D : (piece_index + 1) * D] for piece_index in range(6)
    ]
    shift_one, scale_one, gate_one, shift_two, scale_two, gate_two = pieces
    w_in = small_low[FREQ + D : FREQ + D + P_SIZE]
    w_head = small_low[FREQ + D + P_SIZE :]
    inputs_low = inputs.astype(jnp.bfloat16)
    shaped_zero = jnp.dot(inputs_low, w_in, preferred_element_type=jnp.float32).reshape(
        frame_count, TPF, D
    )
    normed_one = (
        modulate_local(shaped_zero, shift_one, scale_one).reshape(tok_count, D).astype(jnp.bfloat16)
    )
    turned_weights = jnp.einsum(
        "kde,ef->kdf", w_attn[:2], rotation, preferred_element_type=jnp.bfloat16
    )
    projected = jnp.einsum(
        "td,kde->kte", normed_one, w_attn[:3], preferred_element_type=jnp.float32
    )
    turned = jnp.einsum(
        "td,kde->kte", normed_one, turned_weights, preferred_element_type=jnp.float32
    )
    queries = (projected[0] * cosine_table + turned[0] * sine_table).astype(jnp.bfloat16)
    keys_own = (projected[1] * cosine_table + turned[1] * sine_table).astype(jnp.bfloat16)
    values_own = projected[2].astype(jnp.bfloat16)
    key_parts = [keys_own]
    value_parts = [values_own]
    for reach_step in range(1, REACH + 1):
        far_keys, far_values = shifted((keys_own, values_own), "frames", reach_step)
        key_parts.insert(0, far_keys)
        value_parts.insert(0, far_values)
    keys_wide = jnp.concatenate(key_parts, axis=0)
    values_wide = jnp.concatenate(value_parts, axis=0)

    heads_wide, log_totals = attn_fwd(queries, keys_wide, values_wide, clip_start)
    mixed_heads = heads_wide.astype(jnp.bfloat16)
    attended = unit_sum(
        jnp.einsum("te,de->td", mixed_heads, w_attn[3], preferred_element_type=jnp.float32)
    )
    attended_shaped = attended.reshape(frame_count, TPF, D)
    shaped_one = shaped_zero + gate_one * attended_shaped
    normed_two = (
        modulate_local(shaped_one, shift_two, scale_two).reshape(tok_count, D).astype(jnp.bfloat16)
    )
    up_proj = jnp.dot(normed_two, w_mlp[0], preferred_element_type=jnp.float32)
    activated = jax.nn.gelu(up_proj).astype(jnp.bfloat16)
    output = unit_sum(
        jnp.einsum("tf,df->td", activated, w_mlp[1], preferred_element_type=jnp.float32)
    )
    output_shaped = output.reshape(frame_count, TPF, D)
    shaped_two = shaped_one + gate_two * output_shaped
    final_norm = layer_norm(shaped_two).reshape(tok_count, D).astype(jnp.bfloat16)
    predicted = jnp.einsum("td,pd->tp", final_norm, w_head, preferred_element_type=jnp.float32)
    misfit = predicted - noise_patches
    token_weight = jnp.repeat(noised, TPF) / (TPF * P_SIZE)
    loss_own = jnp.sum(token_weight[:, None] * misfit * misfit)
    grad_scale = 1.0 / jnp.maximum(noised_count, 1.0)
    d_pred = (2.0 * grad_scale * token_weight[:, None] * misfit).astype(jnp.bfloat16)
    grad_head = jnp.einsum("tp,td->pd", d_pred, final_norm, preferred_element_type=jnp.float32)
    d_final = jnp.einsum("tp,pd->td", d_pred, w_head, preferred_element_type=jnp.float32).reshape(
        frame_count, TPF, D
    )
    norm_pull = jax.vjp(layer_norm, shaped_two)[1]
    d_shaped_two = norm_pull(d_final)[0]
    d_gate_two = jnp.sum(d_shaped_two * output_shaped, axis=1)
    d_output = (gate_two * d_shaped_two).reshape(tok_count, D).astype(jnp.bfloat16)
    grad_down = jnp.einsum("td,tf->df", d_output, activated, preferred_element_type=jnp.float32)
    d_activated = jnp.einsum("td,df->tf", d_output, w_mlp[1], preferred_element_type=jnp.float32)
    gelu_pull = jax.vjp(jax.nn.gelu, up_proj)[1]
    d_up = gelu_pull(d_activated)[0].astype(jnp.bfloat16)
    grad_up = jnp.einsum("td,tf->df", normed_two, d_up, preferred_element_type=jnp.float32)
    grad_mlp = jnp.stack([grad_up.astype(jnp.bfloat16), grad_down.astype(jnp.bfloat16)])
    sum_mlp = lax.psum_scatter(grad_mlp, "frames", scatter_dimension=1, tiled=True).astype(
        jnp.float32
    )
    d_norm_two = unit_sum(
        jnp.einsum("tf,df->td", d_up, w_mlp[0], preferred_element_type=jnp.float32)
    ).reshape(frame_count, TPF, D)
    mod_pull_two = jax.vjp(modulate_local, shaped_one, shift_two, scale_two)[1]
    d_from_two, d_shift_two, d_scale_two = mod_pull_two(d_norm_two)
    d_shaped_one = d_shaped_two + d_from_two
    d_gate_one = jnp.sum(d_shaped_one * attended_shaped, axis=1)
    d_attended = (gate_one * d_shaped_one).reshape(tok_count, D).astype(jnp.bfloat16)
    grad_out = jnp.einsum("td,te->de", d_attended, mixed_heads, preferred_element_type=jnp.float32)
    d_mixed = jnp.einsum(
        "td,de->te", d_attended, w_attn[3], preferred_element_type=jnp.float32
    ).astype(jnp.bfloat16)

    d_queries, keys_grad_wide, values_grad_wide = attn_bwd(
        queries, keys_wide, values_wide, d_mixed, heads_wide, log_totals, clip_start
    )
    own_key_grad = keys_grad_wide[REACH * tok_count :].astype(jnp.float32)
    own_value_grad = values_grad_wide[REACH * tok_count :].astype(jnp.float32)
    for reach_step in range(1, REACH + 1):
        offset = (REACH - reach_step) * tok_count
        back_keys, back_values = (
            shifted(
                keys_grad_wide[offset : offset + tok_count].astype(jnp.bfloat16),
                "frames",
                -reach_step,
            ).astype(jnp.float32),
            shifted(
                values_grad_wide[offset : offset + tok_count].astype(jnp.bfloat16),
                "frames",
                -reach_step,
            ).astype(jnp.float32),
        )
        own_key_grad = own_key_grad + back_keys
        own_value_grad = own_value_grad + back_values
    d_query_pre = rotate_back(d_queries, cosine_table, sine_table, rotation)
    d_key_pre = rotate_back(own_key_grad, cosine_table, sine_table, rotation)
    d_projected = jnp.stack([d_query_pre, d_key_pre, own_value_grad.astype(jnp.bfloat16)])
    grad_qkv = jnp.einsum(
        "td,kte->kde", normed_one, d_projected, preferred_element_type=jnp.float32
    )
    d_norm_one = unit_sum(
        jnp.einsum("kte,kde->td", d_projected, w_attn[:3], preferred_element_type=jnp.float32)
    ).reshape(frame_count, TPF, D)
    mod_pull_one = jax.vjp(modulate_local, shaped_zero, shift_one, scale_one)[1]
    d_from_one, d_shift_one, d_scale_one = mod_pull_one(d_norm_one)
    d_hidden = (d_shaped_one + d_from_one).reshape(tok_count, D).astype(jnp.bfloat16)
    grad_in = jnp.einsum("tp,td->pd", inputs_low, d_hidden, preferred_element_type=jnp.float32)
    d_modulation = jnp.concatenate(
        [
            d_shift_one[:, 0],
            d_scale_one[:, 0],
            d_gate_one,
            d_shift_two[:, 0],
            d_scale_two[:, 0],
            d_gate_two,
        ],
        axis=1,
    )
    mod_cols = mod_weight.shape[1]
    mod_rows = mod_weight.shape[0]
    small_cols = small_weights.shape[1]
    d_mod_own = lax.dynamic_slice_in_dim(d_modulation, mp_index * mod_cols, mod_cols, 1)
    d_mod_all = lax.all_gather(d_mod_own, "frames", axis=0, tiled=True)
    cond_rows = lax.dynamic_slice_in_dim(conditioning_all, device * mod_rows, mod_rows, 1)
    sum_mod = jnp.einsum("fr,fc->rc", cond_rows, d_mod_all, precision=HIGH)
    d_cond_part = jnp.einsum("fc,rc->fr", d_mod_all, low_mod.astype(jnp.float32), precision=HIGH)
    loss_rows = jnp.broadcast_to(loss_own, (8, mod_rows))
    d_cond_rows = jnp.concatenate([lax.psum(d_cond_part, "mp"), loss_rows], axis=0)
    d_cond_all = lax.all_gather(d_cond_rows, "frames", axis=1, tiled=True)
    loss_sum = jnp.sum(d_cond_all[frames_total]) / mod_rows
    d_pre_two = jax.vjp(jax.nn.silu, pre_two)[1](d_cond_all[:frames_total])[0]
    first_col = (device * lax.axis_size("mp") + mp_index) * small_cols

    def own(array):
        return lax.dynamic_slice_in_dim(array, first_col, small_cols, 1)

    grad_second = jnp.einsum("fi,fj->ij", first_all, own(d_pre_two), precision=HIGH)
    second_rows = lax.dynamic_slice_in_dim(small_full, FREQ + first_col, small_cols, 0)
    d_first = jnp.einsum("fk,jk->fj", d_pre_two, second_rows, precision=HIGH)
    d_pre_one = jax.vjp(jax.nn.silu, own(pre_one))[1](d_first)[0]
    grad_first = jnp.einsum("fi,fj->ij", features_all, d_pre_one, precision=HIGH)
    joined = jnp.concatenate(
        [grad_qkv[0], grad_qkv[1], grad_qkv[2], grad_out, grad_in.T, grad_head.T], axis=1
    ).astype(jnp.bfloat16)
    joined_sum = lax.psum_scatter(joined, "frames", scatter_dimension=0, tiled=True).astype(
        jnp.float32
    )
    sum_attn = jnp.stack(
        [joined_sum[:, k * width_local : (k + 1) * width_local] for k in range(4)]
    )
    sum_ends = lax.dynamic_slice_in_dim(
        joined_sum[:, 4 * width_local :].T, mp_index * small_cols, small_cols, 1
    )
    sum_small = jnp.concatenate([grad_first, grad_second, sum_ends], axis=0)
    learning_rate = 0.5 * math.sqrt(tokens_total * P_SIZE / D)
    attn_new, attn_moment_new, attn_average_new, attn_copy = update(
        attn_weights, sum_attn, attn_moment, attn_average, learning_rate
    )
    mlp_new, mlp_moment_new, mlp_average_new, mlp_copy = update(
        mlp_weights, sum_mlp, mlp_moment, mlp_average, learning_rate
    )
    mod_new, mod_moment_new, mod_average_new, mod_copy = update(
        mod_weight, sum_mod, mod_moment, mod_average, learning_rate
    )
    small_new, small_moment_new, small_average_new, small_copy = update(
        small_weights, sum_small, small_moment, small_average, learning_rate
    )
    return (
        loss_sum,
        noised_count,
        attn_new,
        attn_moment_new,
        attn_average_new,
        attn_copy,
        mlp_new,
        mlp_moment_new,
        mlp_average_new,
        mlp_copy,
        mod_new,
        mod_moment_new,
        mod_average_new,
        mod_copy,
        small_new,
        small_moment_new,
        small_average_new,
        small_copy,
    )


def solution(mesh):
    return jax.shard_map(
        per_device,
        mesh=mesh,
        in_specs=(
            P("frames", None),
            P("frames", None),
            P("frames"),
            P(),
            P(),
            P(None, "frames", "mp"),
            P(None, "frames", "mp"),
            P("frames", "mp"),
            P(None, ("frames", "mp")),
            P(None, "frames", "mp"),
            P(None, "frames", "mp"),
            P("frames", "mp"),
            P(None, ("frames", "mp")),
            P(None, "frames", "mp"),
            P(None, "frames", "mp"),
            P("frames", "mp"),
            P(None, ("frames", "mp")),
        ),
        out_specs=(
            P(),
            P(),
            P(None, "frames", "mp"),
            P(None, "frames", "mp"),
            P(None, "frames", "mp"),
            P(None, "frames", "mp"),
            P(None, "frames", "mp"),
            P(None, "frames", "mp"),
            P(None, "frames", "mp"),
            P(None, "frames", "mp"),
            P("frames", "mp"),
            P("frames", "mp"),
            P("frames", "mp"),
            P("frames", "mp"),
            P(None, ("frames", "mp")),
            P(None, ("frames", "mp")),
            P(None, ("frames", "mp")),
            P(None, ("frames", "mp")),
        ),
        check_vma=False,
    )
```

```python
import functools
import math

import jax
import jax.numpy as jnp
import numpy as np
from jax import lax
from jax.experimental import pallas as pl
from jax.experimental.pallas import tpu as pltpu
from jax.sharding import PartitionSpec as P

D = 1024
HD = 64
CH = 4
FREQ = 256
GRID = 16
P_SIZE = 16
TPF = 64
REACH = 4


HIGH = lax.Precision.HIGHEST
EPSILON = 1e-06
MOMENTUM = 0.5
EMA_DECAY = 0.5
TP_AXIS = "mp"


def shifted(shard, axis, by):
    peers = lax.axis_size(axis)
    pairs = [(i, i + by) for i in range(peers) if 0 <= i + by < peers]
    return lax.ppermute(shard, axis, pairs)


def rotation_matrix(head_width):
    groups = [head_width // 4, 3 * head_width // 8, 3 * head_width // 8]
    rotation = np.zeros((head_width, head_width), np.float32)
    offset = 0
    for group_size in groups:
        half_size = group_size // 2
        for pair_index in range(half_size):
            rotation[offset + half_size + pair_index, offset + pair_index] = -1.0
            rotation[offset + pair_index, offset + half_size + pair_index] = 1.0
        offset += group_size
    return rotation


def rotary_angles(frame_pos, row_pos, col_pos, head_width):
    pieces = []
    for position, group_size in (
        (frame_pos, head_width // 4),
        (row_pos, 3 * head_width // 8),
        (col_pos, 3 * head_width // 8),
    ):
        half_size = group_size // 2
        frequency = 10000.0 ** (-jnp.arange(half_size, dtype=jnp.float32) / half_size)
        phases = position[:, None] * frequency[None, :]
        pieces += [phases, phases]
    return jnp.concatenate(pieces, axis=1)


def clip_positions(clip_ids):
    frame_index = jnp.arange(clip_ids.shape[0], dtype=jnp.int32)
    starts_here = jnp.concatenate([jnp.ones((1,), bool), clip_ids[1:] != clip_ids[:-1]])
    clip_start = lax.cummax(jnp.where(starts_here, frame_index, 0), axis=0)
    return frame_index - clip_start


def patchify(frame_data):
    frame_total = frame_data.shape[0]
    patch_side = GRID // 2
    shaped = frame_data.reshape(frame_total, CH, patch_side, 2, patch_side, 2)
    return shaped.transpose(0, 2, 4, 1, 3, 5).reshape(frame_total * patch_side * patch_side, CH * 4)


def layer_norm(vector):
    row_mean = jnp.mean(vector, axis=-1, keepdims=True)
    centred = vector - row_mean
    variance = jnp.mean(centred * centred, axis=-1, keepdims=True)
    return centred * lax.rsqrt(variance + EPSILON)


def modulate_local(shaped, shift_rows, scale_rows):
    return layer_norm(shaped) * (1.0 + scale_rows) + shift_rows


def time_features(level_eff):
    half_size = FREQ // 2
    frequency = jnp.exp(-math.log(10000.0) * jnp.arange(half_size, dtype=jnp.float32) / half_size)
    phases = (level_eff * 1000.0)[:, None] * frequency[None, :]
    return jnp.concatenate([jnp.cos(phases), jnp.sin(phases)], axis=1)


def rotate_back(gradient, cosine_table, sine_table, rotation):
    scaled = gradient * sine_table
    high = scaled.astype(jnp.bfloat16)
    left = scaled - high.astype(jnp.float32)
    middle = left.astype(jnp.bfloat16)
    low = (left - middle.astype(jnp.float32)).astype(jnp.bfloat16)
    turned = sum(
        jnp.einsum("te,de->td", part, rotation, preferred_element_type=jnp.float32)
        for part in (high, middle, low)
    )
    return (gradient * cosine_table + turned).astype(jnp.bfloat16)


NT=(((1,),(1,)),((),()))
NN=(((1,),(0,)),((),()))

def dotf(a,b,dims=NN):
    return lax.dot_general(a,b,dims,preferred_element_type=jnp.float32)

def split_pair(xT):
    r=lax.broadcasted_iota(jnp.int32,xT.shape,0)
    z=jnp.zeros_like(xT)
    return jnp.where(r<HD,xT,z), jnp.where(r<HD,z,xT)

def keep_of(t,TK,TQ,cs,qf):
    kf=lax.broadcasted_iota(jnp.int32,(TK,TQ),0)//TPF+t*(TK//TPF)
    return (kf>=cs)&(kf<=qf)

def fwd_kernel(lo_ref,mid_ref,hi_ref,q_ref,k_ref,v_ref,cs_ref,o_ref,lse_ref,vT,*,TQ,TK,W0,NQ):
    KS=k_ref.shape[0]
    def tr(i,_):
        s=pl.multiple_of(i*TK,TK)
        vT[:,pl.ds(s,TK)]=v_ref[pl.ds(s,TK),:].T
        return 0
    lax.fori_loop(lo_ref[0],KS//TK,tr,0)
    def qtile(j,_):
        qs=pl.multiple_of(j*TQ,TQ)
        qT=(q_ref[pl.ds(qs,TQ),:].T)*jnp.bfloat16(0.125)
        qA,qB=split_pair(qT)
        cs=cs_ref[0:1,pl.ds(qs,TQ)]
        qf=lax.broadcasted_iota(jnp.int32,(1,TQ),1)//TPF+(W0+j*(TQ//TPF))
        def step(t,carry,masked):
            ks=pl.multiple_of(t*TK,TK)
            kt=k_ref[pl.ds(ks,TK),:]
            out=[]
            if masked: keep=keep_of(t,TK,TQ,cs,qf)
            for h,(qh,(m,l,o)) in enumerate(zip((qA,qB),carry)):
                s=dotf(kt,qh)
                if masked: s=jnp.where(keep,s,-1e30)
                mn=jnp.maximum(m,jnp.max(s,axis=0,keepdims=True))
                a=jnp.exp(m-mn)
                p=jnp.exp(s-mn)
                l=l*a+jnp.sum(p,axis=0,keepdims=True)
                o=o*a+dotf(vT[h*HD:(h+1)*HD,pl.ds(ks,TK)],p.astype(jnp.bfloat16))
                out.append((mn,l,o))
            return tuple(out)
        init=tuple((jnp.full((1,TQ),-1e29,jnp.float32),jnp.zeros((1,TQ),jnp.float32),jnp.zeros((HD,TQ),jnp.float32)) for _ in range(2))
        c=lax.fori_loop(lo_ref[j],mid_ref[j],lambda t,c:step(t,c,True),init)
        c=lax.fori_loop(mid_ref[j],hi_ref[j],lambda t,c:step(t,c,False),c)
        c=lax.fori_loop(hi_ref[j],(W0*TPF+(j+1)*TQ+TK-1)//TK,lambda t,c:step(t,c,True),c)
        oT=jnp.concatenate([c[0][2]/c[0][1],c[1][2]/c[1][1]],axis=0)
        o_ref[pl.ds(qs,TQ),:]=oT.T.astype(o_ref.dtype)
        lse_ref[0,0:1,pl.ds(qs,TQ)]=c[0][0]+jnp.log(c[0][1])
        lse_ref[0,1:2,pl.ds(qs,TQ)]=c[1][0]+jnp.log(c[1][1])
        return 0
    lax.fori_loop(0,NQ,qtile,0)

def tile_bounds(cs_rel,TQ,TK,W0,NQ):
    fq=TQ//TPF; fk=TK//TPF
    j=jnp.arange(NQ)
    first=cs_rel[::fq]; last=cs_rel[fq-1::fq]
    lo=first//fk
    dg=(W0+j*fq+1)//fk
    mid=jnp.minimum((last+fk-1)//fk,dg)
    mid=jnp.maximum(mid,lo)
    hi=jnp.maximum(dg,mid)
    return lo.astype(jnp.int32),mid.astype(jnp.int32),hi.astype(jnp.int32)

def attn_fwd(q,k,v,cs_rel,TQ=512,TK=512):
    T,Wd=q.shape; KS=k.shape[0]; P=Wd//128
    W0=(KS-T)//TPF; NQ=T//TQ
    lo,mid,hi=tile_bounds(cs_rel,TQ,TK,W0,NQ)
    cs_tok=jnp.broadcast_to(jnp.repeat(cs_rel,TPF)[None,:],(8,T)).astype(jnp.int32)
    return pl.pallas_call(
        functools.partial(fwd_kernel,TQ=TQ,TK=TK,W0=W0,NQ=NQ),
        grid_spec=pltpu.PrefetchScalarGridSpec(num_scalar_prefetch=3,grid=(P,),
            in_specs=[pl.BlockSpec((T,128),lambda p,*_:(0,p)),pl.BlockSpec((KS,128),lambda p,*_:(0,p)),pl.BlockSpec((KS,128),lambda p,*_:(0,p)),pl.BlockSpec((8,T),lambda p,*_:(0,0))],
            out_specs=[pl.BlockSpec((T,128),lambda p,*_:(0,p)),pl.BlockSpec((1,8,T),lambda p,*_:(p,0,0))],
            scratch_shapes=[pltpu.VMEM((128,KS),jnp.bfloat16)]),
        out_shape=[jax.ShapeDtypeStruct((T,Wd),jnp.float32),jax.ShapeDtypeStruct((P,8,T),jnp.float32)],
        compiler_params=pltpu.CompilerParams(vmem_limit_bytes=48<<20),
        cost_estimate=pl.CostEstimate(flops=10**11,bytes_accessed=2*10**7,transcendentals=3*10**7),
        name="attn_forward",
    )(lo,mid,hi,q,k,v,cs_tok)

def bwd_kernel(lo_ref,mid_ref,hi_ref,q_ref,k_ref,v_ref,do_ref,o_ref,lse_ref,cs_ref,dq_ref,dk_ref,dv_ref,kT,dkT,dvT,*,TQ,TK,W0,NQ):
    KS=k_ref.shape[0]
    def tr(i,_):
        s=pl.multiple_of(i*TK,TK)
        kT[:,pl.ds(s,TK)]=k_ref[pl.ds(s,TK),:].T
        return 0
    lax.fori_loop(lo_ref[0],KS//TK,tr,0)
    dkT[...]=jnp.zeros_like(dkT); dvT[...]=jnp.zeros_like(dvT)
    def qtile(j,_):
        qs=pl.multiple_of(j*TQ,TQ)
        qT=(q_ref[pl.ds(qs,TQ),:].T)*jnp.bfloat16(0.125)
        qh=split_pair(qT)
        doT=do_ref[pl.ds(qs,TQ),:].T
        doh=split_pair(doT)
        oT=o_ref[pl.ds(qs,TQ),:].T
        prod=oT*doT.astype(jnp.float32)
        delta=(jnp.sum(prod[:HD],axis=0,keepdims=True),jnp.sum(prod[HD:],axis=0,keepdims=True))
        lse=(lse_ref[0,0:1,pl.ds(qs,TQ)],lse_ref[0,1:2,pl.ds(qs,TQ)])
        cs=cs_ref[0:1,pl.ds(qs,TQ)]
        qf=lax.broadcasted_iota(jnp.int32,(1,TQ),1)//TPF+(W0+j*(TQ//TPF))
        def step(t,carry,masked):
            ks=pl.multiple_of(t*TK,TK)
            kt=k_ref[pl.ds(ks,TK),:]; vt=v_ref[pl.ds(ks,TK),:]
            out=[]
            if masked: keep=keep_of(t,TK,TQ,cs,qf)
            for h in range(2):
                r=slice(h*HD,(h+1)*HD)
                s=dotf(kt,qh[h])
                p=jnp.exp(s-lse[h])
                if masked: p=jnp.where(keep,p,0.0)
                dp=dotf(vt,doh[h])
                ds=(p*(dp-delta[h])).astype(jnp.bfloat16)
                pb=p.astype(jnp.bfloat16)
                dvT[r,pl.ds(ks,TK)]+=dotf(doT[r],pb,NT)
                dkT[r,pl.ds(ks,TK)]+=dotf(qT[r],ds,NT)
                out.append(carry[h]+dotf(kT[r,pl.ds(ks,TK)],ds))
            return tuple(out)
        init=(jnp.zeros((HD,TQ),jnp.float32),)*2
        c=lax.fori_loop(lo_ref[j],mid_ref[j],lambda t,c:step(t,c,True),init)
        c=lax.fori_loop(mid_ref[j],hi_ref[j],lambda t,c:step(t,c,False),c)
        c=lax.fori_loop(hi_ref[j],(W0*TPF+(j+1)*TQ+TK-1)//TK,lambda t,c:step(t,c,True),c)
        dq_ref[pl.ds(qs,TQ),:]=(jnp.concatenate(c,axis=0)*0.125).T
        return 0
    lax.fori_loop(0,NQ,qtile,0)
    def back(i,_):
        s=pl.multiple_of(i*TK,TK)
        dk_ref[pl.ds(s,TK),:]=dkT[:,pl.ds(s,TK)].T.astype(dk_ref.dtype)
        dv_ref[pl.ds(s,TK),:]=dvT[:,pl.ds(s,TK)].T.astype(dv_ref.dtype)
        return 0
    lax.fori_loop(0,KS//TK,back,0)

def attn_bwd(q,k,v,do,o,lse,cs_rel,TQ=512,TK=512,out_dt=jnp.bfloat16):
    T,Wd=q.shape; KS=k.shape[0]; P=Wd//128
    W0=(KS-T)//TPF; NQ=T//TQ
    lo,mid,hi=tile_bounds(cs_rel,TQ,TK,W0,NQ)
    cs_tok=jnp.broadcast_to(jnp.repeat(cs_rel,TPF)[None,:],(8,T)).astype(jnp.int32)
    tb=pl.BlockSpec((T,128),lambda p,*_:(0,p)); kb=pl.BlockSpec((KS,128),lambda p,*_:(0,p))
    return pl.pallas_call(
        functools.partial(bwd_kernel,TQ=TQ,TK=TK,W0=W0,NQ=NQ),
        grid_spec=pltpu.PrefetchScalarGridSpec(num_scalar_prefetch=3,grid=(P,),
            in_specs=[tb,kb,kb,tb,tb,pl.BlockSpec((1,8,T),lambda p,*_:(p,0,0)),pl.BlockSpec((8,T),lambda p,*_:(0,0))],
            out_specs=[tb,kb,kb],
            scratch_shapes=[pltpu.VMEM((128,KS),jnp.bfloat16),pltpu.VMEM((128,KS),jnp.float32),pltpu.VMEM((128,KS),jnp.float32)]),
        out_shape=[jax.ShapeDtypeStruct((T,Wd),jnp.float32),jax.ShapeDtypeStruct((KS,Wd),out_dt),jax.ShapeDtypeStruct((KS,Wd),out_dt)],
        compiler_params=pltpu.CompilerParams(vmem_limit_bytes=56<<20),
        cost_estimate=pl.CostEstimate(flops=2*10**11,bytes_accessed=5*10**7,transcendentals=3*10**7),
        name="attn_backward",
    )(lo,mid,hi,q,k,v,do,o,lse,cs_tok)


def update(weight, gradient, moment, average, learning_rate):
    moment_new = MOMENTUM * moment + gradient
    weight_new = weight - learning_rate * (gradient + MOMENTUM * moment_new)
    average_new = EMA_DECAY * average + (1.0 - EMA_DECAY) * weight_new
    return (weight_new, moment_new, average_new, weight_new.astype(jnp.bfloat16))


TN = (((0,), (0,)), ((), ()))


def norm_rows(v):
    centred = v - jnp.mean(v, axis=-1, keepdims=True)
    inverse = lax.rsqrt(jnp.mean(centred * centred, axis=-1, keepdims=True) + EPSILON)
    return centred * inverse, inverse


def norm_rows_back(grad, normed, inverse):
    return inverse * (
        grad
        - jnp.mean(grad, axis=-1, keepdims=True)
        - normed * jnp.mean(grad * normed, axis=-1, keepdims=True)
    )


def gelu_pair(x):
    c = math.sqrt(2.0 / math.pi)
    sq = x * x
    t = jnp.tanh(c * (x + 0.044715 * (x * sq)))
    half = 0.5 * (1.0 + t)
    return x * half, half + (0.5 * c) * x * (1.0 - t * t) * (1.0 + 0.134145 * sq)


def mid_kernel(
    o_ref, wo_ref, hid_ref, mod_ref, noise_ref, tw_ref, head_ref, gs_ref, wu_hbm, wd_hbm,
    dmix_ref, dx1_ref, dmod_ref, ghead_ref, loss_ref, go_ref, gmlp_hbm,
    wu_ref, wd_ref, att, x1, out, dx2, n2, n2t, act, dgl, dout, doutt, datt, datt_t,
    send_a, recv_a, send_c, recv_c, send_e, recv_e, stage,
    wsem, gsem, ssem, rsem, *, tp,
):
    f = lax.axis_index("frames")
    h = lax.axis_index("mp")
    bf16 = jnp.bfloat16
    x_peer = {"mp": 1 - h}
    tp_peer = {"frames": f + 1 - 2 * lax.rem(f, 2)} if tp == "core" else x_peer
    half = hid_ref.shape[0]
    rows = 128
    chunks = half // rows
    width = hid_ref.shape[1]
    ff = wu_hbm.shape[1]
    ft = 512
    dt = 256

    weights = [
        pltpu.make_async_copy(wu_hbm, wu_ref, wsem.at[0]),
        pltpu.make_async_copy(wd_hbm, wd_ref, wsem.at[1]),
    ]
    for w in weights:
        w.start()

    barrier = pltpu.get_barrier_semaphore()
    pl.semaphore_signal(barrier, inc=1, device_id=x_peer, device_id_type=pl.DeviceIdType.MESH)
    if tp == "core":
        pl.semaphore_signal(barrier, inc=1, device_id=tp_peer, device_id_type=pl.DeviceIdType.MESH)
    pl.semaphore_wait(barrier, 2 if tp == "core" else 1)

    def at(start, size):
        return pl.ds(pl.multiple_of(start, size), size)

    def copy(src, dst, phase, c, peer):
        return pltpu.make_async_remote_copy(
            src_ref=src, dst_ref=dst, send_sem=ssem.at[phase, c], recv_sem=rsem.at[phase, c],
            device_id=peer, device_id_type=pl.DeviceIdType.MESH,
        )

    def copy_a(c):
        return copy(send_a.at[at(c * rows, rows)], recv_a.at[at(c * rows, rows)], 0, c, x_peer)

    def copy_b(c):
        return copy(
            n2.at[at(c * 2 * rows, rows)], n2.at[at(c * 2 * rows + rows, rows)], 1, c, tp_peer
        )

    def copy_c(c):
        return copy(send_c.at[at(c * rows, rows)], recv_c.at[at(c * rows, rows)], 2, c, tp_peer)

    def copy_d(c):
        return copy(
            dout.at[at(c * 2 * rows, rows)], dout.at[at(c * 2 * rows + rows, rows)], 3, c, tp_peer
        )

    def copy_e(c):
        return copy(send_e.at[at(c * rows, rows)], recv_e.at[at(c * rows, rows)], 4, c, tp_peer)

    def copy_f(c):
        mine = datt.at[at(h * half + c * rows, rows)]
        return copy(mine, mine, 5, c, x_peer)

    def phase_a(c, _):
        part = o_ref[at((1 - h) * half + c * rows, rows), :].astype(bf16)
        send_a[at(c * rows, rows), :] = dotf(part, wo_ref[...], NT).astype(bf16)
        copy_a(c).start()
        return 0

    lax.fori_loop(0, chunks, phase_a, 0)

    def phase_b(c, _):
        part = o_ref[at(h * half + c * rows, rows), :].astype(bf16)
        att[at(c * rows, rows), :] = dotf(part, wo_ref[...], NT)
        copy_a(c).wait_recv()
        for k in range(rows // TPF):
            r = at(c * rows + k * TPF, TPF)
            frame = pl.ds(c * (rows // TPF) + k, 1)
            a = att[r, :] + recv_a[r, :].astype(jnp.float32)
            att[r, :] = a
            v = hid_ref[r, :] + mod_ref[0, frame, :] * a
            x1[r, :] = v
            y, _inv = norm_rows(v)
            n2[at(c * 2 * rows + k * TPF, TPF), :] = (
                y * (1.0 + mod_ref[2, frame, :]) + mod_ref[1, frame, :]
            ).astype(bf16)
        copy_b(c).start()
        return 0

    lax.fori_loop(0, chunks, phase_b, 0)
    for w in weights:
        w.wait()

    def phase_c(c, _):
        copy_b(c).wait_recv()
        tok = at(c * 2 * rows, 2 * rows)
        n2t[:, tok] = n2[tok, :].T

        def up(i, _):
            cols = at(i * ft, ft)
            a, g = gelu_pair(dotf(n2[tok, :], wu_ref[:, cols]))
            act[tok, cols] = a.astype(bf16)
            dgl[tok, cols] = g.astype(bf16)
            return 0

        lax.fori_loop(0, ff // ft, up, 0)

        def down(i, _):
            cols = at(i * dt, dt)
            res = dotf(act[tok, :], wd_ref[cols, :], NT)
            out[at(c * rows, rows), cols] = res[:rows]
            send_c[at(c * rows, rows), cols] = res[rows:].astype(bf16)
            return 0

        lax.fori_loop(0, width // dt, down, 0)
        copy_c(c).start()
        return 0

    lax.fori_loop(0, chunks, phase_c, 0)

    ghead_ref[...] = jnp.zeros_like(ghead_ref)
    loss_ref[...] = jnp.zeros_like(loss_ref)

    def phase_d(c, _):
        copy_c(c).wait_recv()
        for k in range(rows // TPF):
            r = at(c * rows + k * TPF, TPF)
            frame = pl.ds(c * (rows // TPF) + k, 1)
            o = out[r, :] + recv_c[r, :].astype(jnp.float32)
            gate = mod_ref[3, frame, :]
            y, inv = norm_rows(x1[r, :] + gate * o)
            fn = y.astype(bf16)
            misfit = dotf(fn, head_ref[...], NT) - noise_ref[r, :]
            weighted = tw_ref[r, :] * misfit
            loss_ref[...] += weighted * misfit
            d_pred = (2.0 * gs_ref[0] * weighted).astype(bf16)
            ghead_ref[...] += dotf(d_pred, fn, TN)
            d_x2 = norm_rows_back(dotf(d_pred, head_ref[...]), y, inv)
            dx2[r, :] = d_x2
            dmod_ref[3, frame, :] = jnp.sum(d_x2 * o, axis=0, keepdims=True)
            dout[at(c * 2 * rows + k * TPF, TPF), :] = (gate * d_x2).astype(bf16)
        copy_d(c).start()
        return 0

    lax.fori_loop(0, chunks, phase_d, 0)

    def phase_e(c, _):
        copy_d(c).wait_recv()
        tok = at(c * 2 * rows, 2 * rows)
        doutt[:, tok] = dout[tok, :].T

        def down(i, _):
            cols = at(i * ft, ft)
            g = dotf(dout[tok, :], wd_ref[:, cols]) * dgl[tok, cols].astype(jnp.float32)
            dgl[tok, cols] = g.astype(bf16)
            return 0

        lax.fori_loop(0, ff // ft, down, 0)

        def up(i, _):
            cols = at(i * dt, dt)
            res = dotf(dgl[tok, :], wu_ref[cols, :], NT)
            out[at(c * rows, rows), cols] = res[:rows]
            send_e[at(c * rows, rows), cols] = res[rows:].astype(bf16)
            return 0

        lax.fori_loop(0, width // dt, up, 0)
        copy_e(c).start()
        return 0

    lax.fori_loop(0, chunks, phase_e, 0)

    def phase_f(c, _):
        copy_e(c).wait_recv()
        for k in range(rows // TPF):
            r = at(c * rows + k * TPF, TPF)
            frame = pl.ds(c * (rows // TPF) + k, 1)
            g = out[r, :] + recv_e[r, :].astype(jnp.float32)
            y, inv = norm_rows(x1[r, :])
            dmod_ref[1, frame, :] = jnp.sum(g, axis=0, keepdims=True)
            dmod_ref[2, frame, :] = jnp.sum(g * y, axis=0, keepdims=True)
            d_x1 = dx2[r, :] + norm_rows_back(g * (1.0 + mod_ref[2, frame, :]), y, inv)
            dx1_ref[r, :] = d_x1
            dmod_ref[0, frame, :] = jnp.sum(d_x1 * att[r, :], axis=0, keepdims=True)
            datt[at(h * half + c * rows + k * TPF, TPF), :] = (mod_ref[0, frame, :] * d_x1).astype(
                bf16
            )
        copy_f(c).start()
        return 0

    lax.fori_loop(0, chunks, phase_f, 0)

    def put(slot, i):
        k = lax.div(i, width // dt)
        return pltpu.make_async_copy(
            stage.at[slot], gmlp_hbm.at[k, at(lax.rem(i, width // dt) * dt, dt), :], gsem.at[slot]
        )

    def weight_grads(left, right, k):
        def tile(i, _):
            step = k * (width // dt) + i
            slot = lax.rem(step, 2)

            @pl.when(step >= 2)
            def _():
                put(slot, step - 2).wait()

            def cols_of(j, _):
                cols = at(j * ft, ft)
                stage[slot, :, cols] = dotf(left[at(i * dt, dt), :], right[:, cols]).astype(bf16)
                return 0

            lax.fori_loop(0, ff // ft, cols_of, 0)
            put(slot, step).start()
            return 0

        lax.fori_loop(0, width // dt, tile, 0)

    weight_grads(n2t, dgl, 0)
    weight_grads(doutt, act, 1)

    def own_mix(c, _):
        tok = at(h * half + c * rows, rows)
        datt_t[:, tok] = datt[tok, :].T
        dmix_ref[tok, :] = dotf(datt[tok, :], wo_ref[...]).astype(bf16)
        return 0

    lax.fori_loop(0, chunks, own_mix, 0)

    def phase_g(c, _):
        tok = at((1 - h) * half + c * rows, rows)
        theirs = datt.at[tok]
        copy(theirs, theirs, 5, c, x_peer).wait_recv()
        datt_t[:, tok] = datt[tok, :].T
        dmix_ref[tok, :] = dotf(datt[tok, :], wo_ref[...]).astype(bf16)
        return 0

    lax.fori_loop(0, chunks, phase_g, 0)

    def grad_out(i, _):
        d = at(i * dt, dt)
        go_ref[d, :] = dotf(datt_t[d, :], o_ref[...].astype(bf16)).astype(bf16)
        return 0

    lax.fori_loop(0, width // dt, grad_out, 0)
    last = 2 * (width // dt)
    put((last - 2) % 2, last - 2).wait()
    put((last - 1) % 2, last - 1).wait()

    def sent(c, _):
        for one in (copy_a, copy_b, copy_c, copy_d, copy_e, copy_f):
            one(c).wait_send()
        return 0

    lax.fori_loop(0, chunks, sent, 0)


def mid_block(o, wo, hid, mod, noise, tw, head, gs, wu, wd, tp, cid):
    tok, e = o.shape
    half, width = hid.shape
    ff = wu.shape[1]
    own_frames = half // TPF
    f32, bf16 = jnp.float32, jnp.bfloat16
    vm = pl.BlockSpec(memory_space=pltpu.VMEM)
    anym = pl.BlockSpec(memory_space=pl.ANY)
    V = pltpu.VMEM
    return pl.pallas_call(
        functools.partial(mid_kernel, tp=tp),
        in_specs=[vm] * 7 + [pl.BlockSpec(memory_space=pltpu.SMEM), anym, anym],
        out_specs=[vm] * 6 + [anym],
        out_shape=[
            jax.ShapeDtypeStruct((tok, e), bf16),
            jax.ShapeDtypeStruct((half, width), f32),
            jax.ShapeDtypeStruct((4, own_frames, width), f32),
            jax.ShapeDtypeStruct((128, width), f32),
            jax.ShapeDtypeStruct((TPF, 128), f32),
            jax.ShapeDtypeStruct((width, e), bf16),
            jax.ShapeDtypeStruct((2, width, ff), bf16),
        ],
        scratch_shapes=[
            V((width, ff), bf16), V((width, ff), bf16),
            V((half, width), f32), V((half, width), f32), V((half, width), f32),
            V((half, width), f32),
            V((2 * half, width), bf16), V((width, 2 * half), bf16),
            V((2 * half, ff), bf16), V((2 * half, ff), bf16),
            V((2 * half, width), bf16), V((width, 2 * half), bf16),
            V((tok, width), bf16), V((width, tok), bf16),
            V((half, width), bf16), V((half, width), bf16),
            V((half, width), bf16), V((half, width), bf16),
            V((half, width), bf16), V((half, width), bf16),
            V((2, 256, ff), bf16),
            pltpu.SemaphoreType.DMA((2,)), pltpu.SemaphoreType.DMA((2,)),
            pltpu.SemaphoreType.DMA((6, half // 128)), pltpu.SemaphoreType.DMA((6, half // 128)),
        ],
        compiler_params=pltpu.CompilerParams(
            vmem_limit_bytes=62 << 20, collective_id=cid, has_side_effects=True
        ),
        cost_estimate=pl.CostEstimate(
            flops=4 * 10**10, bytes_accessed=3 * 10**7, transcendentals=2 * 10**6
        ),
        name="feed_forward",
    )(o, wo, hid, mod, noise, tw, head, gs, wu, wd)


def per_device(
    latents,
    noise,
    levels,
    clip_ids,
    clean_flags,
    attn_weights,
    mlp_weights,
    mod_weight,
    small_weights,
    attn_moment,
    mlp_moment,
    mod_moment,
    small_moment,
    attn_average,
    mlp_average,
    mod_average,
    small_average,
):
    frame_count = latents.shape[0]
    tok_count = frame_count * TPF
    patch_side = GRID // 2
    frames_total = clip_ids.shape[0]
    tokens_total = frames_total * TPF
    width_local = attn_weights.shape[2]
    heads_local = width_local // HD
    key_span = (REACH + 1) * tok_count
    device = lax.axis_index("frames")
    mp_index = lax.axis_index("mp")
    first_frame = device * frame_count
    scale_qk = HD ** (-0.5)
    w_attn = lax.all_gather(attn_weights.astype(jnp.bfloat16), "frames", axis=1, tiled=True)
    w_mlp = lax.all_gather(mlp_weights.astype(jnp.bfloat16), "frames", axis=1, tiled=True)
    low_mod = mod_weight.astype(jnp.bfloat16)
    w_mod = lax.all_gather(low_mod, "frames", axis=0, tiled=True)
    small_low = lax.all_gather(
        small_weights.astype(jnp.bfloat16), ("frames", "mp"), axis=1, tiled=True
    )
    levels_all = lax.all_gather(levels, "frames", axis=0, tiled=True)
    small_full = small_low.astype(jnp.float32)
    noised_all = (1 - clean_flags).astype(jnp.float32)
    noised_count = jnp.sum(noised_all)
    noised = lax.dynamic_slice_in_dim(noised_all, first_frame, frame_count)
    level_eff = levels * noised
    signal_scale = jnp.repeat(jnp.cos(0.5 * math.pi * level_eff), TPF)
    noise_scale = jnp.repeat(jnp.sin(0.5 * math.pi * level_eff), TPF)
    noise_patches = patchify(noise)
    inputs = signal_scale[:, None] * patchify(latents) + noise_scale[:, None] * noise_patches
    in_clip_all = clip_positions(clip_ids)
    in_clip = jnp.repeat(
        lax.dynamic_slice_in_dim(in_clip_all, first_frame, frame_count), TPF
    ).astype(jnp.float32)
    within = jnp.arange(tok_count, dtype=jnp.int32) % TPF
    angles = rotary_angles(
        in_clip,
        (within // patch_side).astype(jnp.float32),
        (within % patch_side).astype(jnp.float32),
        HD,
    )
    cosine_table = jnp.tile(jnp.cos(angles), (1, heads_local))
    sine_table = jnp.tile(jnp.sin(angles), (1, heads_local))
    rotation = jnp.asarray(
        np.kron(np.eye(heads_local, dtype=np.float32), rotation_matrix(HD)), jnp.bfloat16
    )
    clip_start = (
        lax.dynamic_slice_in_dim(
            jnp.arange(frames_total, dtype=jnp.int32) - in_clip_all, first_frame, frame_count
        )
        - first_frame
        + REACH * frame_count
    )
    features_all = time_features(levels_all * noised_all)
    pre_one = jnp.dot(features_all, small_full[:FREQ], precision=HIGH)
    first_all = jax.nn.silu(pre_one)
    pre_two = jnp.dot(first_all, small_full[FREQ : FREQ + D], precision=HIGH)
    conditioning_all = jax.nn.silu(pre_two)
    conditioning = lax.dynamic_slice_in_dim(conditioning_all, first_frame, frame_count)
    mod_full = w_mod.astype(jnp.float32)
    modulation = lax.all_gather(
        jnp.dot(conditioning, mod_full, precision=HIGH), "mp", axis=1, tiled=True
    )
    pieces = [
        modulation[:, None, piece_index * D : (piece_index + 1) * D] for piece_index in range(6)
    ]
    shift_one, scale_one, gate_one, shift_two, scale_two, gate_two = pieces
    w_in = small_low[FREQ + D : FREQ + D + P_SIZE]
    w_head = small_low[FREQ + D + P_SIZE :]
    inputs_low = inputs.astype(jnp.bfloat16)
    shaped_zero = jnp.dot(inputs_low, w_in, preferred_element_type=jnp.float32).reshape(
        frame_count, TPF, D
    )
    normed_one = (
        modulate_local(shaped_zero, shift_one, scale_one).reshape(tok_count, D).astype(jnp.bfloat16)
    )
    turned_weights = jnp.einsum(
        "kde,ef->kdf", w_attn[:2], rotation, preferred_element_type=jnp.bfloat16
    )
    projected = jnp.einsum(
        "td,kde->kte", normed_one, w_attn[:3], preferred_element_type=jnp.float32
    )
    turned = jnp.einsum(
        "td,kde->kte", normed_one, turned_weights, preferred_element_type=jnp.float32
    )
    queries = (projected[0] * cosine_table + turned[0] * sine_table).astype(jnp.bfloat16)
    keys_own = (projected[1] * cosine_table + turned[1] * sine_table).astype(jnp.bfloat16)
    values_own = projected[2].astype(jnp.bfloat16)
    key_parts = [keys_own]
    value_parts = [values_own]
    for reach_step in range(1, REACH + 1):
        far_keys, far_values = shifted((keys_own, values_own), "frames", reach_step)
        key_parts.insert(0, far_keys)
        value_parts.insert(0, far_values)
    keys_wide = jnp.concatenate(key_parts, axis=0)
    values_wide = jnp.concatenate(value_parts, axis=0)

    heads_wide, log_totals = attn_fwd(queries, keys_wide, values_wide, clip_start)
    half = tok_count // 2
    own_frames = frame_count // 2

    def half_of(array, dim=0):
        size = array.shape[dim] // 2
        return lax.dynamic_slice_in_dim(array, mp_index * size, size, dim)

    token_weight = jnp.repeat(noised, TPF) / (TPF * P_SIZE)
    grad_scale = 1.0 / jnp.maximum(noised_count, 1.0)
    padding = ((0, 0), (0, 128 - P_SIZE))
    mod_mid = jnp.stack(
        [half_of(piece[:, 0]) for piece in (gate_one, shift_two, scale_two, gate_two)]
    )
    d_mixed, d_shaped_one, d_mod_mid, grad_head, loss_parts, grad_out, grad_mlp = mid_block(
        heads_wide,
        w_attn[3],
        half_of(shaped_zero.reshape(tok_count, D)),
        mod_mid,
        jnp.pad(half_of(noise_patches), padding),
        jnp.broadcast_to(half_of(token_weight)[:, None], (half, 128)),
        jnp.pad(w_head, ((0, 128 - P_SIZE), (0, 0))),
        grad_scale.reshape(1),
        w_mlp[0],
        w_mlp[1],
        TP_AXIS,
        0,
    )
    loss_own = jnp.sum(loss_parts)
    grad_head = grad_head[:P_SIZE]
    sum_mlp = lax.psum_scatter(grad_mlp, "frames", scatter_dimension=1, tiled=True)
    d_queries, keys_grad_wide, values_grad_wide = attn_bwd(
        queries, keys_wide, values_wide, d_mixed, heads_wide, log_totals, clip_start
    )
    own_key_grad = keys_grad_wide[REACH * tok_count :].astype(jnp.float32)
    own_value_grad = values_grad_wide[REACH * tok_count :].astype(jnp.float32)
    for reach_step in range(1, REACH + 1):
        offset = (REACH - reach_step) * tok_count
        back_keys, back_values = (
            shifted(
                keys_grad_wide[offset : offset + tok_count].astype(jnp.bfloat16),
                "frames",
                -reach_step,
            ).astype(jnp.float32),
            shifted(
                values_grad_wide[offset : offset + tok_count].astype(jnp.bfloat16),
                "frames",
                -reach_step,
            ).astype(jnp.float32),
        )
        own_key_grad = own_key_grad + back_keys
        own_value_grad = own_value_grad + back_values
    d_query_pre = rotate_back(d_queries, cosine_table, sine_table, rotation)
    d_key_pre = rotate_back(own_key_grad, cosine_table, sine_table, rotation)
    d_projected = jnp.stack([d_query_pre, d_key_pre, own_value_grad.astype(jnp.bfloat16)])
    grad_qkv = jnp.einsum(
        "td,kte->kde", normed_one, d_projected, preferred_element_type=jnp.float32
    )
    d_norm_part = jnp.einsum(
        "kte,kde->td", d_projected, w_attn[:3], preferred_element_type=jnp.float32
    )
    flip = [(0, 1), (1, 0)]
    theirs = lax.dynamic_slice_in_dim(d_norm_part, (1 - mp_index) * half, half, 0)
    d_norm_one = (
        half_of(d_norm_part)
        + lax.ppermute(theirs.astype(jnp.bfloat16), "mp", flip).astype(jnp.float32)
    ).reshape(own_frames, TPF, D)
    mod_pull_one = jax.vjp(
        modulate_local, half_of(shaped_zero), half_of(shift_one), half_of(scale_one)
    )[1]
    d_from_one, d_shift_one, d_scale_one = mod_pull_one(d_norm_one)
    d_hidden = (d_shaped_one + d_from_one.reshape(half, D)).astype(jnp.bfloat16)
    grad_in = jnp.einsum(
        "tp,td->pd", half_of(inputs_low), d_hidden, preferred_element_type=jnp.float32
    )
    first_cols = jnp.concatenate([d_shift_one[:, 0], d_scale_one[:, 0], d_mod_mid[0]], axis=1)
    later_cols = jnp.concatenate([d_mod_mid[1], d_mod_mid[2], d_mod_mid[3]], axis=1)
    kept_cols = jnp.where(mp_index == 0, first_cols, later_cols)
    their_cols = lax.ppermute(jnp.where(mp_index == 0, later_cols, first_cols), "mp", flip)
    d_mod_own = jnp.concatenate(
        [
            jnp.where(mp_index == 0, kept_cols, their_cols),
            jnp.where(mp_index == 0, their_cols, kept_cols),
        ],
        axis=0,
    )
    mod_rows = mod_weight.shape[0]
    small_cols = small_weights.shape[1]
    d_mod_all = lax.all_gather(d_mod_own, "frames", axis=0, tiled=True)
    cond_rows = lax.dynamic_slice_in_dim(conditioning_all, device * mod_rows, mod_rows, 1)
    sum_mod = jnp.einsum("fr,fc->rc", cond_rows, d_mod_all, precision=HIGH)
    d_cond_part = jnp.einsum("fc,rc->fr", d_mod_all, low_mod.astype(jnp.float32), precision=HIGH)
    loss_both = loss_own + lax.ppermute(loss_own, "mp", flip)
    loss_rows = jnp.broadcast_to(loss_both, (8, mod_rows))
    d_cond_rows = jnp.concatenate([d_cond_part + lax.ppermute(d_cond_part, "mp", flip), loss_rows], axis=0)
    d_cond_all = lax.all_gather(d_cond_rows, "frames", axis=1, tiled=True)
    loss_sum = jnp.sum(d_cond_all[frames_total]) / mod_rows
    d_pre_two = jax.vjp(jax.nn.silu, pre_two)[1](d_cond_all[:frames_total])[0]
    first_col = (device * lax.axis_size("mp") + mp_index) * small_cols

    def own(array):
        return lax.dynamic_slice_in_dim(array, first_col, small_cols, 1)

    grad_second = jnp.einsum("fi,fj->ij", first_all, own(d_pre_two), precision=HIGH)
    second_rows = lax.dynamic_slice_in_dim(small_full, FREQ + first_col, small_cols, 0)
    d_first = jnp.einsum("fk,jk->fj", d_pre_two, second_rows, precision=HIGH)
    d_pre_one = jax.vjp(jax.nn.silu, own(pre_one))[1](d_first)[0]
    grad_first = jnp.einsum("fi,fj->ij", features_all, d_pre_one, precision=HIGH)
    joined = jnp.concatenate(
        [
            part.astype(jnp.bfloat16)
            for part in (grad_qkv[0], grad_qkv[1], grad_qkv[2], grad_out, grad_in.T, grad_head.T)
        ],
        axis=1,
    )
    joined_sum = lax.psum_scatter(joined, "frames", scatter_dimension=0, tiled=True).astype(
        jnp.float32
    )
    sum_attn = jnp.stack(
        [joined_sum[:, k * width_local : (k + 1) * width_local] for k in range(4)]
    )
    ends = joined_sum[:, 4 * width_local :].T
    sum_ends = half_of(ends, 1) + lax.ppermute(
        lax.dynamic_slice_in_dim(ends, (1 - mp_index) * small_cols, small_cols, 1), "mp", flip
    )
    sum_small = jnp.concatenate([grad_first, grad_second, sum_ends], axis=0)
    learning_rate = 0.5 * math.sqrt(tokens_total * P_SIZE / D)
    attn_new, attn_moment_new, attn_average_new, attn_copy = update(
        attn_weights, sum_attn, attn_moment, attn_average, learning_rate
    )
    mlp_new, mlp_moment_new, mlp_average_new, mlp_copy = update(
        mlp_weights, sum_mlp.astype(jnp.float32), mlp_moment, mlp_average, learning_rate
    )
    mod_new, mod_moment_new, mod_average_new, mod_copy = update(
        mod_weight, sum_mod, mod_moment, mod_average, learning_rate
    )
    small_new, small_moment_new, small_average_new, small_copy = update(
        small_weights, sum_small, small_moment, small_average, learning_rate
    )
    return (
        loss_sum,
        noised_count,
        attn_new,
        attn_moment_new,
        attn_average_new,
        attn_copy,
        mlp_new,
        mlp_moment_new,
        mlp_average_new,
        mlp_copy,
        mod_new,
        mod_moment_new,
        mod_average_new,
        mod_copy,
        small_new,
        small_moment_new,
        small_average_new,
        small_copy,
    )


def solution(mesh):
    return jax.shard_map(
        per_device,
        mesh=mesh,
        in_specs=(
            P("frames", None),
            P("frames", None),
            P("frames"),
            P(),
            P(),
            P(None, "frames", "mp"),
            P(None, "frames", "mp"),
            P("frames", "mp"),
            P(None, ("frames", "mp")),
            P(None, "frames", "mp"),
            P(None, "frames", "mp"),
            P("frames", "mp"),
            P(None, ("frames", "mp")),
            P(None, "frames", "mp"),
            P(None, "frames", "mp"),
            P("frames", "mp"),
            P(None, ("frames", "mp")),
        ),
        out_specs=(
            P(),
            P(),
            P(None, "frames", "mp"),
            P(None, "frames", "mp"),
            P(None, "frames", "mp"),
            P(None, "frames", "mp"),
            P(None, "frames", "mp"),
            P(None, "frames", "mp"),
            P(None, "frames", "mp"),
            P(None, "frames", "mp"),
            P("frames", "mp"),
            P("frames", "mp"),
            P("frames", "mp"),
            P("frames", "mp"),
            P(None, ("frames", "mp")),
            P(None, ("frames", "mp")),
            P(None, ("frames", "mp")),
            P(None, ("frames", "mp")),
        ),
        check_vma=False,
    )
```

```python
import functools
import math

import jax
import jax.numpy as jnp
import numpy as np
from jax import lax
from jax.experimental import pallas as pl
from jax.experimental.pallas import tpu as pltpu
from jax.sharding import PartitionSpec as P

D = 1024
HD = 64
CH = 4
FREQ = 256
GRID = 16
P_SIZE = 16
TPF = 64
REACH = 4


HIGH = lax.Precision.HIGHEST
EPSILON = 1e-06
MOMENTUM = 0.5
EMA_DECAY = 0.5
TP_AXIS = "mp"


def shifted(shard, axis, by):
    peers = lax.axis_size(axis)
    pairs = [(i, i + by) for i in range(peers) if 0 <= i + by < peers]
    return lax.ppermute(shard, axis, pairs)


def rotation_matrix(head_width):
    groups = [head_width // 4, 3 * head_width // 8, 3 * head_width // 8]
    rotation = np.zeros((head_width, head_width), np.float32)
    offset = 0
    for group_size in groups:
        half_size = group_size // 2
        for pair_index in range(half_size):
            rotation[offset + half_size + pair_index, offset + pair_index] = -1.0
            rotation[offset + pair_index, offset + half_size + pair_index] = 1.0
        offset += group_size
    return rotation


def rotary_angles(frame_pos, row_pos, col_pos, head_width):
    pieces = []
    for position, group_size in (
        (frame_pos, head_width // 4),
        (row_pos, 3 * head_width // 8),
        (col_pos, 3 * head_width // 8),
    ):
        half_size = group_size // 2
        frequency = 10000.0 ** (-jnp.arange(half_size, dtype=jnp.float32) / half_size)
        phases = position[:, None] * frequency[None, :]
        pieces += [phases, phases]
    return jnp.concatenate(pieces, axis=1)


def clip_positions(clip_ids):
    frame_index = jnp.arange(clip_ids.shape[0], dtype=jnp.int32)
    starts_here = jnp.concatenate([jnp.ones((1,), bool), clip_ids[1:] != clip_ids[:-1]])
    clip_start = lax.cummax(jnp.where(starts_here, frame_index, 0), axis=0)
    return frame_index - clip_start


def patchify(frame_data):
    frame_total = frame_data.shape[0]
    patch_side = GRID // 2
    shaped = frame_data.reshape(frame_total, CH, patch_side, 2, patch_side, 2)
    return shaped.transpose(0, 2, 4, 1, 3, 5).reshape(frame_total * patch_side * patch_side, CH * 4)


def layer_norm(vector):
    row_mean = jnp.mean(vector, axis=-1, keepdims=True)
    centred = vector - row_mean
    variance = jnp.mean(centred * centred, axis=-1, keepdims=True)
    return centred * lax.rsqrt(variance + EPSILON)


def modulate_local(shaped, shift_rows, scale_rows):
    return layer_norm(shaped) * (1.0 + scale_rows) + shift_rows


def time_features(level_eff):
    half_size = FREQ // 2
    frequency = jnp.exp(-math.log(10000.0) * jnp.arange(half_size, dtype=jnp.float32) / half_size)
    phases = (level_eff * 1000.0)[:, None] * frequency[None, :]
    return jnp.concatenate([jnp.cos(phases), jnp.sin(phases)], axis=1)


NT=(((1,),(1,)),((),()))
NN=(((1,),(0,)),((),()))

def dotf(a,b,dims=NN):
    return lax.dot_general(a,b,dims,preferred_element_type=jnp.float32)

def split_pair(xT):
    r=lax.broadcasted_iota(jnp.int32,xT.shape,0)
    z=jnp.zeros_like(xT)
    return jnp.where(r<HD,xT,z), jnp.where(r<HD,z,xT)

def keep_of(t,TK,TQ,cs,qf):
    kf=lax.broadcasted_iota(jnp.int32,(TK,TQ),0)//TPF+t*(TK//TPF)
    return (kf>=cs)&(kf<=qf)

def fwd_kernel(lo_ref,mid_ref,hi_ref,q_ref,k_ref,v_ref,cs_ref,o_ref,lse_ref,vT,*,TQ,TK,W0,NQ):
    KS=k_ref.shape[0]
    def tr(i,_):
        s=pl.multiple_of(i*TK,TK)
        vT[:,pl.ds(s,TK)]=v_ref[pl.ds(s,TK),:].T
        return 0
    lax.fori_loop(lo_ref[0],KS//TK,tr,0)
    def qtile(j,_):
        qs=pl.multiple_of(j*TQ,TQ)
        qT=(q_ref[pl.ds(qs,TQ),:].T)*jnp.bfloat16(0.125)
        qA,qB=split_pair(qT)
        cs=cs_ref[0:1,pl.ds(qs,TQ)]
        qf=lax.broadcasted_iota(jnp.int32,(1,TQ),1)//TPF+(W0+j*(TQ//TPF))
        def step(t,carry,masked):
            ks=pl.multiple_of(t*TK,TK)
            kt=k_ref[pl.ds(ks,TK),:]
            out=[]
            if masked: keep=keep_of(t,TK,TQ,cs,qf)
            for h,(qh,(m,l,o)) in enumerate(zip((qA,qB),carry)):
                s=dotf(kt,qh)
                if masked: s=jnp.where(keep,s,-1e30)
                mn=jnp.maximum(m,jnp.max(s,axis=0,keepdims=True))
                a=jnp.exp(m-mn)
                p=jnp.exp(s-mn)
                l=l*a+jnp.sum(p,axis=0,keepdims=True)
                o=o*a+dotf(vT[h*HD:(h+1)*HD,pl.ds(ks,TK)],p.astype(jnp.bfloat16))
                out.append((mn,l,o))
            return tuple(out)
        init=tuple((jnp.full((1,TQ),-1e29,jnp.float32),jnp.zeros((1,TQ),jnp.float32),jnp.zeros((HD,TQ),jnp.float32)) for _ in range(2))
        c=lax.fori_loop(lo_ref[j],mid_ref[j],lambda t,c:step(t,c,True),init)
        c=lax.fori_loop(mid_ref[j],hi_ref[j],lambda t,c:step(t,c,False),c)
        c=lax.fori_loop(hi_ref[j],(W0*TPF+(j+1)*TQ+TK-1)//TK,lambda t,c:step(t,c,True),c)
        oT=jnp.concatenate([c[0][2]/c[0][1],c[1][2]/c[1][1]],axis=0)
        o_ref[pl.ds(qs,TQ),:]=oT.T.astype(o_ref.dtype)
        lse_ref[0,0:1,pl.ds(qs,TQ)]=c[0][0]+jnp.log(c[0][1])
        lse_ref[0,1:2,pl.ds(qs,TQ)]=c[1][0]+jnp.log(c[1][1])
        return 0
    lax.fori_loop(0,NQ,qtile,0)

def tile_bounds(cs_rel,TQ,TK,W0,NQ):
    fq=TQ//TPF; fk=TK//TPF
    j=jnp.arange(NQ)
    first=cs_rel[::fq]; last=cs_rel[fq-1::fq]
    lo=first//fk
    dg=(W0+j*fq+1)//fk
    mid=jnp.minimum((last+fk-1)//fk,dg)
    mid=jnp.maximum(mid,lo)
    hi=jnp.maximum(dg,mid)
    return lo.astype(jnp.int32),mid.astype(jnp.int32),hi.astype(jnp.int32)

def attn_fwd(q,k,v,cs_rel,TQ=512,TK=512):
    T,Wd=q.shape; KS=k.shape[0]; P=Wd//128
    W0=(KS-T)//TPF; NQ=T//TQ
    lo,mid,hi=tile_bounds(cs_rel,TQ,TK,W0,NQ)
    cs_tok=jnp.broadcast_to(jnp.repeat(cs_rel,TPF)[None,:],(8,T)).astype(jnp.int32)
    return pl.pallas_call(
        functools.partial(fwd_kernel,TQ=TQ,TK=TK,W0=W0,NQ=NQ),
        grid_spec=pltpu.PrefetchScalarGridSpec(num_scalar_prefetch=3,grid=(P,),
            in_specs=[pl.BlockSpec((T,128),lambda p,*_:(0,p)),pl.BlockSpec((KS,128),lambda p,*_:(0,p)),pl.BlockSpec((KS,128),lambda p,*_:(0,p)),pl.BlockSpec((8,T),lambda p,*_:(0,0))],
            out_specs=[pl.BlockSpec((T,128),lambda p,*_:(0,p)),pl.BlockSpec((1,8,T),lambda p,*_:(p,0,0))],
            scratch_shapes=[pltpu.VMEM((128,KS),jnp.bfloat16)]),
        out_shape=[jax.ShapeDtypeStruct((T,Wd),jnp.float32),jax.ShapeDtypeStruct((P,8,T),jnp.float32)],
        compiler_params=pltpu.CompilerParams(vmem_limit_bytes=48<<20),
        cost_estimate=pl.CostEstimate(flops=10**11,bytes_accessed=2*10**7,transcendentals=3*10**7),
        name="attn_forward",
    )(lo,mid,hi,q,k,v,cs_tok)

def bwd_kernel(lo_ref,mid_ref,hi_ref,q_ref,k_ref,v_ref,do_ref,o_ref,lse_ref,cs_ref,dq_ref,dk_ref,dv_ref,kT,dkT,dvT,*,TQ,TK,W0,NQ):
    KS=k_ref.shape[0]
    def tr(i,_):
        s=pl.multiple_of(i*TK,TK)
        kT[:,pl.ds(s,TK)]=k_ref[pl.ds(s,TK),:].T
        return 0
    lax.fori_loop(lo_ref[0],KS//TK,tr,0)
    dkT[...]=jnp.zeros_like(dkT); dvT[...]=jnp.zeros_like(dvT)
    def qtile(j,_):
        qs=pl.multiple_of(j*TQ,TQ)
        qT=(q_ref[pl.ds(qs,TQ),:].T)*jnp.bfloat16(0.125)
        qh=split_pair(qT)
        doT=do_ref[pl.ds(qs,TQ),:].T
        doh=split_pair(doT)
        oT=o_ref[pl.ds(qs,TQ),:].T
        prod=oT*doT.astype(jnp.float32)
        delta=(jnp.sum(prod[:HD],axis=0,keepdims=True),jnp.sum(prod[HD:],axis=0,keepdims=True))
        lse=(lse_ref[0,0:1,pl.ds(qs,TQ)],lse_ref[0,1:2,pl.ds(qs,TQ)])
        cs=cs_ref[0:1,pl.ds(qs,TQ)]
        qf=lax.broadcasted_iota(jnp.int32,(1,TQ),1)//TPF+(W0+j*(TQ//TPF))
        def step(t,carry,masked):
            ks=pl.multiple_of(t*TK,TK)
            kt=k_ref[pl.ds(ks,TK),:]; vt=v_ref[pl.ds(ks,TK),:]
            out=[]
            if masked: keep=keep_of(t,TK,TQ,cs,qf)
            for h in range(2):
                r=slice(h*HD,(h+1)*HD)
                s=dotf(kt,qh[h])
                p=jnp.exp(s-lse[h])
                if masked: p=jnp.where(keep,p,0.0)
                dp=dotf(vt,doh[h])
                ds=(p*(dp-delta[h])).astype(jnp.bfloat16)
                pb=p.astype(jnp.bfloat16)
                dvT[r,pl.ds(ks,TK)]+=dotf(doT[r],pb,NT)
                dkT[r,pl.ds(ks,TK)]+=dotf(qT[r],ds,NT)
                out.append(carry[h]+dotf(kT[r,pl.ds(ks,TK)],ds))
            return tuple(out)
        init=(jnp.zeros((HD,TQ),jnp.float32),)*2
        c=lax.fori_loop(lo_ref[j],mid_ref[j],lambda t,c:step(t,c,True),init)
        c=lax.fori_loop(mid_ref[j],hi_ref[j],lambda t,c:step(t,c,False),c)
        c=lax.fori_loop(hi_ref[j],(W0*TPF+(j+1)*TQ+TK-1)//TK,lambda t,c:step(t,c,True),c)
        dq_ref[pl.ds(qs,TQ),:]=(jnp.concatenate(c,axis=0)*0.125).T
        return 0
    lax.fori_loop(0,NQ,qtile,0)
    def back(i,_):
        s=pl.multiple_of(i*TK,TK)
        dk_ref[pl.ds(s,TK),:]=dkT[:,pl.ds(s,TK)].T.astype(dk_ref.dtype)
        dv_ref[pl.ds(s,TK),:]=dvT[:,pl.ds(s,TK)].T.astype(dv_ref.dtype)
        return 0
    lax.fori_loop(0,KS//TK,back,0)

def attn_bwd(q,k,v,do,o,lse,cs_rel,TQ=512,TK=512,out_dt=jnp.bfloat16):
    T,Wd=q.shape; KS=k.shape[0]; P=Wd//128
    W0=(KS-T)//TPF; NQ=T//TQ
    lo,mid,hi=tile_bounds(cs_rel,TQ,TK,W0,NQ)
    cs_tok=jnp.broadcast_to(jnp.repeat(cs_rel,TPF)[None,:],(8,T)).astype(jnp.int32)
    tb=pl.BlockSpec((T,128),lambda p,*_:(0,p)); kb=pl.BlockSpec((KS,128),lambda p,*_:(0,p))
    return pl.pallas_call(
        functools.partial(bwd_kernel,TQ=TQ,TK=TK,W0=W0,NQ=NQ),
        grid_spec=pltpu.PrefetchScalarGridSpec(num_scalar_prefetch=3,grid=(P,),
            in_specs=[tb,kb,kb,tb,tb,pl.BlockSpec((1,8,T),lambda p,*_:(p,0,0)),pl.BlockSpec((8,T),lambda p,*_:(0,0))],
            out_specs=[tb,kb,kb],
            scratch_shapes=[pltpu.VMEM((128,KS),jnp.bfloat16),pltpu.VMEM((128,KS),jnp.float32),pltpu.VMEM((128,KS),jnp.float32)]),
        out_shape=[jax.ShapeDtypeStruct((T,Wd),jnp.float32),jax.ShapeDtypeStruct((KS,Wd),out_dt),jax.ShapeDtypeStruct((KS,Wd),out_dt)],
        compiler_params=pltpu.CompilerParams(vmem_limit_bytes=56<<20),
        cost_estimate=pl.CostEstimate(flops=2*10**11,bytes_accessed=5*10**7,transcendentals=3*10**7),
        name="attn_backward",
    )(lo,mid,hi,q,k,v,do,o,lse,cs_tok)


def update(weight, gradient, moment, average, learning_rate):
    moment_new = MOMENTUM * moment + gradient
    weight_new = weight - learning_rate * (gradient + MOMENTUM * moment_new)
    average_new = EMA_DECAY * average + (1.0 - EMA_DECAY) * weight_new
    return (weight_new, moment_new, average_new, weight_new.astype(jnp.bfloat16))


TN = (((0,), (0,)), ((), ()))


def norm_rows(v):
    centred = v - jnp.mean(v, axis=-1, keepdims=True)
    inverse = lax.rsqrt(jnp.mean(centred * centred, axis=-1, keepdims=True) + EPSILON)
    return centred * inverse, inverse


def norm_rows_back(grad, normed, inverse):
    return inverse * (
        grad
        - jnp.mean(grad, axis=-1, keepdims=True)
        - normed * jnp.mean(grad * normed, axis=-1, keepdims=True)
    )


def gelu_pair(x):
    c = math.sqrt(2.0 / math.pi)
    sq = x * x
    t = jnp.tanh(c * (x + 0.044715 * (x * sq)))
    half = 0.5 * (1.0 + t)
    return x * half, half + (0.5 * c) * x * (1.0 - t * t) * (1.0 + 0.134145 * sq)


def mid_kernel(
    o_ref, wo_ref, hid_ref, mod_ref, noise_ref, tw_ref, head_ref, gs_ref, wu_hbm, wd_hbm,
    dmix_ref, dx1_ref, dmod_ref, loss_ref, joint_hbm,
    wu_ref, wd_ref, att, x1, out, dx2, n2, n2t, act, dgl, dout, doutt, datt, datt_t,
    send_a, recv_a, send_c, recv_c, send_e, recv_e, stage, ghead_ref, go_ref, gh_t,
    wsem, gsem, ssem, rsem, *, tp,
):
    f = lax.axis_index("frames")
    h = lax.axis_index("mp")
    bf16 = jnp.bfloat16
    x_peer = {"mp": 1 - h}
    tp_peer = {"frames": f + 1 - 2 * lax.rem(f, 2)} if tp == "core" else x_peer
    half = hid_ref.shape[0]
    rows = 128
    chunks = half // rows
    width = hid_ref.shape[1]
    ff = wu_hbm.shape[1]
    e = o_ref.shape[1]
    ft = 512
    dt = 256

    weights = [
        pltpu.make_async_copy(wu_hbm, wu_ref, wsem.at[0]),
        pltpu.make_async_copy(wd_hbm, wd_ref, wsem.at[1]),
    ]
    for w in weights:
        w.start()

    barrier = pltpu.get_barrier_semaphore()
    pl.semaphore_signal(barrier, inc=1, device_id=x_peer, device_id_type=pl.DeviceIdType.MESH)
    if tp == "core":
        pl.semaphore_signal(barrier, inc=1, device_id=tp_peer, device_id_type=pl.DeviceIdType.MESH)
    pl.semaphore_wait(barrier, 2 if tp == "core" else 1)

    def at(start, size):
        return pl.ds(pl.multiple_of(start, size), size)

    def copy(src, dst, phase, c, peer):
        return pltpu.make_async_remote_copy(
            src_ref=src, dst_ref=dst, send_sem=ssem.at[phase, c], recv_sem=rsem.at[phase, c],
            device_id=peer, device_id_type=pl.DeviceIdType.MESH,
        )

    def copy_a(c):
        return copy(send_a.at[at(c * rows, rows)], recv_a.at[at(c * rows, rows)], 0, c, x_peer)

    def copy_b(c):
        return copy(
            n2.at[at(c * 2 * rows, rows)], n2.at[at(c * 2 * rows + rows, rows)], 1, c, tp_peer
        )

    def copy_c(c):
        return copy(send_c.at[at(c * rows, rows)], recv_c.at[at(c * rows, rows)], 2, c, tp_peer)

    def copy_d(c):
        return copy(
            dout.at[at(c * 2 * rows, rows)], dout.at[at(c * 2 * rows + rows, rows)], 3, c, tp_peer
        )

    def copy_e(c):
        return copy(send_e.at[at(c * rows, rows)], recv_e.at[at(c * rows, rows)], 4, c, tp_peer)

    def copy_f(c):
        mine = datt.at[at(h * half + c * rows, rows)]
        return copy(mine, mine, 5, c, x_peer)

    def phase_a(c, _):
        part = o_ref[at((1 - h) * half + c * rows, rows), :].astype(bf16)
        send_a[at(c * rows, rows), :] = dotf(part, wo_ref[...], NT).astype(bf16)
        copy_a(c).start()
        return 0

    lax.fori_loop(0, chunks, phase_a, 0)

    def phase_b(c, _):
        part = o_ref[at(h * half + c * rows, rows), :].astype(bf16)
        att[at(c * rows, rows), :] = dotf(part, wo_ref[...], NT)
        copy_a(c).wait_recv()
        for k in range(rows // TPF):
            r = at(c * rows + k * TPF, TPF)
            frame = pl.ds(c * (rows // TPF) + k, 1)
            a = att[r, :] + recv_a[r, :].astype(jnp.float32)
            att[r, :] = a
            v = hid_ref[r, :] + mod_ref[0, frame, :] * a
            x1[r, :] = v
            y, _inv = norm_rows(v)
            n2[at(c * 2 * rows + k * TPF, TPF), :] = (
                y * (1.0 + mod_ref[2, frame, :]) + mod_ref[1, frame, :]
            ).astype(bf16)
        copy_b(c).start()
        return 0

    lax.fori_loop(0, chunks, phase_b, 0)
    for w in weights:
        w.wait()

    def phase_c(c, _):
        copy_b(c).wait_recv()
        tok = at(c * 2 * rows, 2 * rows)
        n2t[:, tok] = n2[tok, :].T

        def up(i, _):
            cols = at(i * ft, ft)
            a, g = gelu_pair(dotf(n2[tok, :], wu_ref[:, cols]))
            act[tok, cols] = a.astype(bf16)
            dgl[tok, cols] = g.astype(bf16)
            return 0

        lax.fori_loop(0, ff // ft, up, 0)

        def down(i, _):
            cols = at(i * dt, dt)
            res = dotf(act[tok, :], wd_ref[cols, :], NT)
            out[at(c * rows, rows), cols] = res[:rows]
            send_c[at(c * rows, rows), cols] = res[rows:].astype(bf16)
            return 0

        lax.fori_loop(0, width // dt, down, 0)
        copy_c(c).start()
        return 0

    lax.fori_loop(0, chunks, phase_c, 0)

    ghead_ref[...] = jnp.zeros_like(ghead_ref)
    loss_ref[...] = jnp.zeros_like(loss_ref)

    def phase_d(c, _):
        copy_c(c).wait_recv()
        for k in range(rows // TPF):
            r = at(c * rows + k * TPF, TPF)
            frame = pl.ds(c * (rows // TPF) + k, 1)
            o = out[r, :] + recv_c[r, :].astype(jnp.float32)
            gate = mod_ref[3, frame, :]
            y, inv = norm_rows(x1[r, :] + gate * o)
            fn = y.astype(bf16)
            misfit = dotf(fn, head_ref[...], NT) - noise_ref[r, :]
            weighted = tw_ref[r, :] * misfit
            loss_ref[...] += weighted * misfit
            d_pred = (2.0 * gs_ref[0] * weighted).astype(bf16)
            ghead_ref[...] += dotf(d_pred, fn, TN)
            d_x2 = norm_rows_back(dotf(d_pred, head_ref[...]), y, inv)
            dx2[r, :] = d_x2
            dmod_ref[3, frame, :] = jnp.sum(d_x2 * o, axis=0, keepdims=True)
            dout[at(c * 2 * rows + k * TPF, TPF), :] = (gate * d_x2).astype(bf16)
        copy_d(c).start()
        return 0

    lax.fori_loop(0, chunks, phase_d, 0)

    def phase_e(c, _):
        copy_d(c).wait_recv()
        tok = at(c * 2 * rows, 2 * rows)
        doutt[:, tok] = dout[tok, :].T

        def down(i, _):
            cols = at(i * ft, ft)
            g = dotf(dout[tok, :], wd_ref[:, cols]) * dgl[tok, cols].astype(jnp.float32)
            dgl[tok, cols] = g.astype(bf16)
            return 0

        lax.fori_loop(0, ff // ft, down, 0)

        def up(i, _):
            cols = at(i * dt, dt)
            res = dotf(dgl[tok, :], wu_ref[cols, :], NT)
            out[at(c * rows, rows), cols] = res[:rows]
            send_e[at(c * rows, rows), cols] = res[rows:].astype(bf16)
            return 0

        lax.fori_loop(0, width // dt, up, 0)
        copy_e(c).start()
        return 0

    lax.fori_loop(0, chunks, phase_e, 0)

    def phase_f(c, _):
        copy_e(c).wait_recv()
        for k in range(rows // TPF):
            r = at(c * rows + k * TPF, TPF)
            frame = pl.ds(c * (rows // TPF) + k, 1)
            g = out[r, :] + recv_e[r, :].astype(jnp.float32)
            y, inv = norm_rows(x1[r, :])
            dmod_ref[1, frame, :] = jnp.sum(g, axis=0, keepdims=True)
            dmod_ref[2, frame, :] = jnp.sum(g * y, axis=0, keepdims=True)
            d_x1 = dx2[r, :] + norm_rows_back(g * (1.0 + mod_ref[2, frame, :]), y, inv)
            dx1_ref[r, :] = d_x1
            dmod_ref[0, frame, :] = jnp.sum(d_x1 * att[r, :], axis=0, keepdims=True)
            datt[at(h * half + c * rows + k * TPF, TPF), :] = (mod_ref[0, frame, :] * d_x1).astype(
                bf16
            )
        copy_f(c).start()
        return 0

    lax.fori_loop(0, chunks, phase_f, 0)

    def put(slot, i):
        k = lax.div(i, width // dt)
        return pltpu.make_async_copy(
            stage.at[slot],
            joint_hbm.at[at(lax.rem(i, width // dt) * dt, dt), at(k * ff, ff)],
            gsem.at[slot],
        )

    def weight_grads(left, right, k):
        def tile(i, _):
            step = k * (width // dt) + i
            slot = lax.rem(step, 2)

            @pl.when(step >= 2)
            def _():
                put(slot, step - 2).wait()

            def cols_of(j, _):
                cols = at(j * ft, ft)
                stage[slot, :, cols] = dotf(left[at(i * dt, dt), :], right[:, cols]).astype(bf16)
                return 0

            lax.fori_loop(0, ff // ft, cols_of, 0)
            put(slot, step).start()
            return 0

        lax.fori_loop(0, width // dt, tile, 0)

    weight_grads(n2t, dgl, 0)
    weight_grads(doutt, act, 1)

    def own_mix(c, _):
        tok = at(h * half + c * rows, rows)
        datt_t[:, tok] = datt[tok, :].T
        dmix_ref[tok, :] = dotf(datt[tok, :], wo_ref[...]).astype(bf16)
        return 0

    lax.fori_loop(0, chunks, own_mix, 0)

    def phase_g(c, _):
        tok = at((1 - h) * half + c * rows, rows)
        theirs = datt.at[tok]
        copy(theirs, theirs, 5, c, x_peer).wait_recv()
        datt_t[:, tok] = datt[tok, :].T
        dmix_ref[tok, :] = dotf(datt[tok, :], wo_ref[...]).astype(bf16)
        return 0

    lax.fori_loop(0, chunks, phase_g, 0)

    def grad_out(i, _):
        d = at(i * dt, dt)
        go_ref[d, :] = dotf(datt_t[d, :], o_ref[...].astype(bf16)).astype(bf16)
        return 0

    lax.fori_loop(0, width // dt, grad_out, 0)
    gh_t[...] = ghead_ref[...].T.astype(bf16)
    ends = [
        pltpu.make_async_copy(go_ref, joint_hbm.at[:, pl.ds(2 * ff, e)], gsem.at[2]),
        pltpu.make_async_copy(gh_t, joint_hbm.at[:, pl.ds(2 * ff + e, 128)], gsem.at[3]),
    ]
    for one in ends:
        one.start()
    for one in ends:
        one.wait()
    last = 2 * (width // dt)
    put((last - 2) % 2, last - 2).wait()
    put((last - 1) % 2, last - 1).wait()

    def sent(c, _):
        for one in (copy_a, copy_b, copy_c, copy_d, copy_e, copy_f):
            one(c).wait_send()
        return 0

    lax.fori_loop(0, chunks, sent, 0)


def mid_block(o, wo, hid, mod, noise, tw, head, gs, wu, wd, tp, cid):
    tok, e = o.shape
    half, width = hid.shape
    ff = wu.shape[1]
    own_frames = half // TPF
    f32, bf16 = jnp.float32, jnp.bfloat16
    vm = pl.BlockSpec(memory_space=pltpu.VMEM)
    anym = pl.BlockSpec(memory_space=pl.ANY)
    V = pltpu.VMEM
    return pl.pallas_call(
        functools.partial(mid_kernel, tp=tp),
        in_specs=[vm] * 7 + [pl.BlockSpec(memory_space=pltpu.SMEM), anym, anym],
        out_specs=[vm] * 4 + [anym],
        out_shape=[
            jax.ShapeDtypeStruct((tok, e), bf16),
            jax.ShapeDtypeStruct((half, width), f32),
            jax.ShapeDtypeStruct((4, own_frames, width), f32),
            jax.ShapeDtypeStruct((TPF, 128), f32),
            jax.ShapeDtypeStruct((width, 2 * ff + e + 128), bf16),
        ],
        scratch_shapes=[
            V((width, ff), bf16), V((width, ff), bf16),
            V((half, width), f32), V((half, width), f32), V((half, width), f32),
            V((half, width), f32),
            V((2 * half, width), bf16), V((width, 2 * half), bf16),
            V((2 * half, ff), bf16), V((2 * half, ff), bf16),
            V((2 * half, width), bf16), V((width, 2 * half), bf16),
            V((tok, width), bf16), V((width, tok), bf16),
            V((half, width), bf16), V((half, width), bf16),
            V((half, width), bf16), V((half, width), bf16),
            V((half, width), bf16), V((half, width), bf16),
            V((2, 256, ff), bf16), V((128, width), f32), V((width, e), bf16),
            V((width, 128), bf16),
            pltpu.SemaphoreType.DMA((2,)), pltpu.SemaphoreType.DMA((4,)),
            pltpu.SemaphoreType.DMA((6, half // 128)), pltpu.SemaphoreType.DMA((6, half // 128)),
        ],
        compiler_params=pltpu.CompilerParams(
            vmem_limit_bytes=62 << 20, collective_id=cid, has_side_effects=True
        ),
        cost_estimate=pl.CostEstimate(
            flops=4 * 10**10, bytes_accessed=3 * 10**7, transcendentals=2 * 10**6
        ),
        name="feed_forward",
    )(o, wo, hid, mod, noise, tw, head, gs, wu, wd)


def split_three(v):
    high = v.astype(jnp.bfloat16)
    left = v - high.astype(jnp.float32)
    middle = left.astype(jnp.bfloat16)
    return high, middle, (left - middle.astype(jnp.float32)).astype(jnp.bfloat16)


def turn_back(g, cosine, sine, rot):
    parts = split_three(g * sine)
    return (g * cosine + sum(dotf(p, rot, NT) for p in parts)).astype(jnp.bfloat16)


def tail_kernel(
    dq_ref, n1_ref, w_ref, cos_ref, sin_ref, rot_ref, hid_ref, scale_ref, dx1_ref, inp_ref,
    dk_hbm, dv_hbm,
    gq_ref, gin_ref, dss_ref,
    own, near, yrecv, zrecv, n1t, dproj, send_x, recv_x, part,
    lsem, s_near, r_near, s_y, r_y, s_z, r_z, s_x, r_x,
):
    f = lax.axis_index("frames")
    h = lax.axis_index("mp")
    n = lax.axis_size("frames")
    core = lax.rem(f, 2)
    odd = lax.rem(lax.div(f, 2), 2)
    core_peer = {"frames": f + 1 - 2 * core}
    y_peer = {"frames": f + 2 - 4 * odd}
    before = {"frames": lax.rem(f - 4 + n, n)}
    after = {"frames": lax.rem(f + 4, n)}
    x_peer = {"mp": 1 - h}
    tok, e = dq_ref.shape
    width = n1_ref.shape[1]
    half = tok // 2
    rows = 256
    chunks = tok // rows
    f32, bf16 = jnp.float32, jnp.bfloat16
    MESH = pl.DeviceIdType.MESH
    sides = (dk_hbm, dv_hbm)

    def at(start, size):
        return pl.ds(pl.multiple_of(start, size), size)

    loads = [
        pltpu.make_async_copy(
            sides[s].at[pl.ds(b * tok, tok)], own.at[s, j], lsem.at[s, j]
        )
        for s in range(2)
        for j, b in enumerate((4, 2, 0))
    ]
    for one in loads:
        one.start()

    barrier = pltpu.get_barrier_semaphore()
    for peer in (core_peer, y_peer, x_peer):
        pl.semaphore_signal(barrier, inc=1, device_id=peer, device_id_type=MESH)

    @pl.when(f >= 4)
    def _():
        pl.semaphore_signal(barrier, inc=1, device_id=before, device_id_type=MESH)

    @pl.when(f + 4 < n)
    def _():
        pl.semaphore_signal(barrier, inc=1, device_id=after, device_id_type=MESH)

    pl.semaphore_wait(barrier, 3 + jnp.where(f >= 4, 1, 0) + jnp.where(f + 4 < n, 1, 0))

    def rows_of(i):
        return lax.rem(i + (chunks // 2) * (1 - h), chunks) * rows

    def remote(src, dst, send, recv, peer):
        return pltpu.make_async_remote_copy(
            src_ref=src, dst_ref=dst, send_sem=send, recv_sem=recv, device_id=peer,
            device_id_type=MESH,
        )

    def near_copy(i, s, j):
        b = (3, 1)[j]
        return remote(
            sides[s].at[at(b * tok + rows_of(i), rows)],
            near.at[s, j, at(rows_of(i), rows)],
            s_near.at[s, j, i], r_near.at[s, j, i], core_peer,
        )

    def y_copy(i, s):
        r = at(rows_of(i), rows)
        return remote(own.at[s, 1, r], yrecv.at[s, r], s_y.at[s, i], r_y.at[s, i], y_peer)

    def z_copy(i, s):
        r = at(rows_of(i), rows)
        return remote(own.at[s, 2, r], zrecv.at[s, r], s_z.at[s, i], r_z.at[s, i], before)

    def x_copy(i):
        r = at(i * rows, rows)
        return remote(send_x.at[r], recv_x.at[r], s_x.at[i], r_x.at[i], x_peer)

    def start_near(i, _):
        for s in range(2):
            for j in range(2):
                near_copy(i, s, j).start()
        return 0

    lax.fori_loop(0, chunks, start_near, 0)

    @pl.when(f + 4 >= n)
    def _():
        zrecv[...] = jnp.zeros_like(zrecv)

    for one in loads:
        one.wait()
    low_core = core == 0

    def combine(i, _):
        r = at(rows_of(i), rows)
        for s in range(2):
            for j in range(2):
                near_copy(i, s, j).wait_recv()
            n3 = near[s, 0, r, :].astype(f32)
            n1_ = near[s, 1, r, :].astype(f32)
            own[s, 1, r, :] = (
                own[s, 1, r, :].astype(f32) + jnp.where(low_core, n1_, n3)
            ).astype(bf16)
            y_copy(i, s).start()
            own[s, 2, r, :] = (
                own[s, 2, r, :].astype(f32) + jnp.where(low_core, 0.0, n1_)
            ).astype(bf16)

            @pl.when((odd == 0) & (f >= 4))
            def _():
                z_copy(i, s).start()

        return 0

    lax.fori_loop(0, chunks, combine, 0)

    def turned(g, r, k):
        for b in range(e // 256):
            cols = slice(b * 256, (b + 1) * 256)
            dproj[k, r, cols] = turn_back(
                g[:, cols], cos_ref[r, :], sin_ref[r, :], rot_ref[...]
            )

    def relay(i, _):
        r = at(rows_of(i), rows)
        turned(dq_ref[r, :], r, 0)
        n1t[:, r] = n1_ref[r, :].T

        @pl.when(odd == 1)
        def _():
            for s in range(2):
                y_copy(i, s).wait_recv()

                @pl.when(f >= 4)
                def _():
                    own[s, 2, r, :] = (
                        own[s, 2, r, :].astype(f32) + yrecv[s, r, :].astype(f32)
                    ).astype(bf16)
                    z_copy(i, s).start()

        return 0

    lax.fori_loop(0, chunks, relay, 0)

    def grads(k):
        def tile(i, _):
            d = at(i * 256, 256)
            gq_ref[k, d, :] = dotf(n1t[d, :], dproj[k]).astype(bf16)
            return 0

        lax.fori_loop(0, width // 256, tile, 0)

    grads(0)

    def finish(i, _):
        r = at(rows_of(i), rows)
        for s in range(2):

            @pl.when(odd == 0)
            def _():
                y_copy(i, s).wait_recv()

            @pl.when(f + 4 < n)
            def _():
                z_copy(i, s).wait_recv()

            total = (
                own[s, 0, r, :].astype(f32)
                + jnp.where(low_core, near[s, 0, r, :].astype(f32), 0.0)
                + jnp.where(odd == 0, yrecv[s, r, :].astype(f32), 0.0)
                + zrecv[s, r, :].astype(f32)
            )
            if s == 0:
                turned(total, r, 1)
            else:
                dproj[2, r, :] = total.astype(bf16)

        def cols_of(j, _):
            cols = at(j * 256, 256)
            res = sum(dotf(dproj[k, r, :], w_ref[k, cols, :], NT) for k in range(3))

            @pl.when(i < chunks // 2)
            def _():
                send_x[at(i * rows, rows), cols] = res.astype(bf16)

            @pl.when(i >= chunks // 2)
            def _():
                part[at((i - chunks // 2) * rows, rows), cols] = res

            return 0

        lax.fori_loop(0, width // 256, cols_of, 0)

        @pl.when(i < chunks // 2)
        def _():
            x_copy(i).start()

        return 0

    lax.fori_loop(0, chunks, finish, 0)
    grads(1)
    grads(2)
    gin_ref[...] = jnp.zeros_like(gin_ref)

    def norm_back(i, _):
        x_copy(i).wait_recv()
        for k in range(rows // TPF):
            r = at(i * rows + k * TPF, TPF)
            frame = pl.ds(i * (rows // TPF) + k, 1)
            g = part[r, :] + recv_x[r, :].astype(f32)
            y, inv = norm_rows(hid_ref[r, :])
            dss_ref[0, frame, :] = jnp.sum(g, axis=0, keepdims=True)
            dss_ref[1, frame, :] = jnp.sum(g * y, axis=0, keepdims=True)
            d_hid = dx1_ref[r, :] + norm_rows_back(g * (1.0 + scale_ref[frame, :]), y, inv)
            gin_ref[...] += dotf(inp_ref[r, :], d_hid.astype(bf16), TN)
        return 0

    lax.fori_loop(0, half // rows, norm_back, 0)

    def sent(i, _):
        for s in range(2):
            for j in range(2):
                near_copy(i, s, j).wait_send()
            y_copy(i, s).wait_send()

            @pl.when(f >= 4)
            def _():
                z_copy(i, s).wait_send()

        @pl.when(i < chunks // 2)
        def _():
            x_copy(i).wait_send()

        return 0

    lax.fori_loop(0, chunks, sent, 0)


def tail_block(dq, n1, w, cosine, sine, rot, hid, scale, dx1, inp, dk, dv, cid):
    tok, e = dq.shape
    width = n1.shape[1]
    half = tok // 2
    f32, bf16 = jnp.float32, jnp.bfloat16
    vm = pl.BlockSpec(memory_space=pltpu.VMEM)
    anym = pl.BlockSpec(memory_space=pl.ANY)
    V = pltpu.VMEM
    D_ = pltpu.SemaphoreType.DMA
    chunks = tok // 256
    return pl.pallas_call(
        tail_kernel,
        in_specs=[vm] * 10 + [anym] * 2,
        out_specs=[vm] * 3,
        out_shape=[
            jax.ShapeDtypeStruct((3, width, e), bf16),
            jax.ShapeDtypeStruct((128, width), f32),
            jax.ShapeDtypeStruct((2, half // TPF, width), f32),
        ],
        scratch_shapes=[
            V((2, 3, tok, e), bf16), V((2, 2, tok, e), bf16), V((2, tok, e), bf16),
            V((2, tok, e), bf16), V((width, tok), bf16), V((3, tok, e), bf16),
            V((half, width), bf16), V((half, width), bf16), V((half, width), f32),
            D_((2, 3)), D_((2, 2, chunks)), D_((2, 2, chunks)), D_((2, chunks)), D_((2, chunks)),
            D_((2, chunks)), D_((2, chunks)), D_((chunks // 2,)), D_((chunks // 2,)),
        ],
        compiler_params=pltpu.CompilerParams(
            vmem_limit_bytes=56 << 20, collective_id=cid, has_side_effects=True
        ),
        cost_estimate=pl.CostEstimate(
            flops=2 * 10**10, bytes_accessed=3 * 10**7, transcendentals=0
        ),
        name="projection_backward",
    )(dq, n1, w, cosine, sine, rot, hid, scale, dx1, inp, dk, dv)


def per_device(
    latents,
    noise,
    levels,
    clip_ids,
    clean_flags,
    attn_weights,
    mlp_weights,
    mod_weight,
    small_weights,
    attn_moment,
    mlp_moment,
    mod_moment,
    small_moment,
    attn_average,
    mlp_average,
    mod_average,
    small_average,
):
    frame_count = latents.shape[0]
    tok_count = frame_count * TPF
    patch_side = GRID // 2
    frames_total = clip_ids.shape[0]
    tokens_total = frames_total * TPF
    width_local = attn_weights.shape[2]
    heads_local = width_local // HD
    key_span = (REACH + 1) * tok_count
    device = lax.axis_index("frames")
    mp_index = lax.axis_index("mp")
    first_frame = device * frame_count
    scale_qk = HD ** (-0.5)
    w_attn = lax.all_gather(attn_weights.astype(jnp.bfloat16), "frames", axis=1, tiled=True)
    w_mlp = lax.all_gather(mlp_weights.astype(jnp.bfloat16), "frames", axis=1, tiled=True)
    low_mod = mod_weight.astype(jnp.bfloat16)
    w_mod = lax.all_gather(low_mod, "frames", axis=0, tiled=True)
    small_low = lax.all_gather(
        small_weights.astype(jnp.bfloat16), ("frames", "mp"), axis=1, tiled=True
    )
    levels_all = lax.all_gather(levels, "frames", axis=0, tiled=True)
    small_full = small_low.astype(jnp.float32)
    noised_all = (1 - clean_flags).astype(jnp.float32)
    noised_count = jnp.sum(noised_all)
    noised = lax.dynamic_slice_in_dim(noised_all, first_frame, frame_count)
    level_eff = levels * noised
    signal_scale = jnp.repeat(jnp.cos(0.5 * math.pi * level_eff), TPF)
    noise_scale = jnp.repeat(jnp.sin(0.5 * math.pi * level_eff), TPF)
    noise_patches = patchify(noise)
    inputs = signal_scale[:, None] * patchify(latents) + noise_scale[:, None] * noise_patches
    in_clip_all = clip_positions(clip_ids)
    in_clip = jnp.repeat(
        lax.dynamic_slice_in_dim(in_clip_all, first_frame, frame_count), TPF
    ).astype(jnp.float32)
    within = jnp.arange(tok_count, dtype=jnp.int32) % TPF
    angles = rotary_angles(
        in_clip,
        (within // patch_side).astype(jnp.float32),
        (within % patch_side).astype(jnp.float32),
        HD,
    )
    cosine_table = jnp.tile(jnp.cos(angles), (1, heads_local))
    sine_table = jnp.tile(jnp.sin(angles), (1, heads_local))
    rotation = jnp.asarray(
        np.kron(np.eye(heads_local, dtype=np.float32), rotation_matrix(HD)), jnp.bfloat16
    )
    turn_four = jnp.asarray(np.kron(np.eye(4, dtype=np.float32), rotation_matrix(HD)), jnp.bfloat16)
    clip_start = (
        lax.dynamic_slice_in_dim(
            jnp.arange(frames_total, dtype=jnp.int32) - in_clip_all, first_frame, frame_count
        )
        - first_frame
        + REACH * frame_count
    )
    features_all = time_features(levels_all * noised_all)
    pre_one = jnp.dot(features_all, small_full[:FREQ], precision=HIGH)
    first_all = jax.nn.silu(pre_one)
    pre_two = jnp.dot(first_all, small_full[FREQ : FREQ + D], precision=HIGH)
    conditioning_all = jax.nn.silu(pre_two)
    conditioning = lax.dynamic_slice_in_dim(conditioning_all, first_frame, frame_count)
    mod_full = w_mod.astype(jnp.float32)
    modulation = lax.all_gather(
        jnp.dot(conditioning, mod_full, precision=HIGH), "mp", axis=1, tiled=True
    )
    pieces = [
        modulation[:, None, piece_index * D : (piece_index + 1) * D] for piece_index in range(6)
    ]
    shift_one, scale_one, gate_one, shift_two, scale_two, gate_two = pieces
    w_in = small_low[FREQ + D : FREQ + D + P_SIZE]
    w_head = small_low[FREQ + D + P_SIZE :]
    inputs_low = inputs.astype(jnp.bfloat16)
    shaped_zero = jnp.dot(inputs_low, w_in, preferred_element_type=jnp.float32).reshape(
        frame_count, TPF, D
    )
    normed_one = (
        modulate_local(shaped_zero, shift_one, scale_one).reshape(tok_count, D).astype(jnp.bfloat16)
    )
    turned_weights = jnp.einsum(
        "kde,ef->kdf", w_attn[:2], rotation, preferred_element_type=jnp.bfloat16
    )
    projected = jnp.einsum(
        "td,kde->kte", normed_one, w_attn[:3], preferred_element_type=jnp.float32
    )
    turned = jnp.einsum(
        "td,kde->kte", normed_one, turned_weights, preferred_element_type=jnp.float32
    )
    queries = (projected[0] * cosine_table + turned[0] * sine_table).astype(jnp.bfloat16)
    keys_own = (projected[1] * cosine_table + turned[1] * sine_table).astype(jnp.bfloat16)
    values_own = projected[2].astype(jnp.bfloat16)
    key_parts = [keys_own]
    value_parts = [values_own]
    for reach_step in range(1, REACH + 1):
        far_keys, far_values = shifted((keys_own, values_own), "frames", reach_step)
        key_parts.insert(0, far_keys)
        value_parts.insert(0, far_values)
    keys_wide = jnp.concatenate(key_parts, axis=0)
    values_wide = jnp.concatenate(value_parts, axis=0)

    heads_wide, log_totals = attn_fwd(queries, keys_wide, values_wide, clip_start)
    half = tok_count // 2
    own_frames = frame_count // 2

    def half_of(array, dim=0):
        size = array.shape[dim] // 2
        return lax.dynamic_slice_in_dim(array, mp_index * size, size, dim)

    token_weight = jnp.repeat(noised, TPF) / (TPF * P_SIZE)
    grad_scale = 1.0 / jnp.maximum(noised_count, 1.0)
    padding = ((0, 0), (0, 128 - P_SIZE))
    mod_mid = jnp.stack(
        [half_of(piece[:, 0]) for piece in (gate_one, shift_two, scale_two, gate_two)]
    )
    d_mixed, d_shaped_one, d_mod_mid, loss_parts, grad_joint = mid_block(
        heads_wide,
        w_attn[3],
        half_of(shaped_zero.reshape(tok_count, D)),
        mod_mid,
        jnp.pad(half_of(noise_patches), padding),
        jnp.broadcast_to(half_of(token_weight)[:, None], (half, 128)),
        jnp.pad(w_head, ((0, 128 - P_SIZE), (0, 0))),
        grad_scale.reshape(1),
        w_mlp[0],
        w_mlp[1],
        TP_AXIS,
        0,
    )
    loss_own = jnp.sum(loss_parts)
    sum_joint = lax.psum_scatter(grad_joint, "frames", scatter_dimension=0, tiled=True)
    d_queries, keys_grad_wide, values_grad_wide = attn_bwd(
        queries, keys_wide, values_wide, d_mixed, heads_wide, log_totals, clip_start
    )
    d_queries, sum_joint = lax.optimization_barrier((d_queries, sum_joint))
    grad_qkv, grad_in, d_first_mods = tail_block(
        d_queries,
        normed_one,
        w_attn[:3],
        cosine_table[:, : 4 * HD],
        sine_table[:, : 4 * HD],
        turn_four,
        half_of(shaped_zero.reshape(tok_count, D)),
        half_of(scale_one[:, 0]),
        d_shaped_one,
        jnp.pad(half_of(inputs_low), padding),
        keys_grad_wide,
        values_grad_wide,
        1,
    )
    grad_in = grad_in[:P_SIZE]
    flip = [(0, 1), (1, 0)]
    first_cols = jnp.concatenate([d_first_mods[0], d_first_mods[1], d_mod_mid[0]], axis=1)
    later_cols = jnp.concatenate([d_mod_mid[1], d_mod_mid[2], d_mod_mid[3]], axis=1)
    kept_cols = jnp.where(mp_index == 0, first_cols, later_cols)
    their_cols = lax.ppermute(jnp.where(mp_index == 0, later_cols, first_cols), "mp", flip)
    d_mod_own = jnp.concatenate(
        [
            jnp.where(mp_index == 0, kept_cols, their_cols),
            jnp.where(mp_index == 0, their_cols, kept_cols),
        ],
        axis=0,
    )
    mod_rows = mod_weight.shape[0]
    small_cols = small_weights.shape[1]
    d_mod_all = lax.all_gather(d_mod_own, "frames", axis=0, tiled=True)
    cond_rows = lax.dynamic_slice_in_dim(conditioning_all, device * mod_rows, mod_rows, 1)
    sum_mod = jnp.einsum("fr,fc->rc", cond_rows, d_mod_all, precision=HIGH)
    d_cond_part = jnp.einsum("fc,rc->fr", d_mod_all, low_mod.astype(jnp.float32), precision=HIGH)
    loss_both = loss_own + lax.ppermute(loss_own, "mp", flip)
    loss_rows = jnp.broadcast_to(loss_both, (8, mod_rows))
    d_cond_rows = jnp.concatenate([d_cond_part + lax.ppermute(d_cond_part, "mp", flip), loss_rows], axis=0)
    d_cond_all = lax.all_gather(d_cond_rows, "frames", axis=1, tiled=True)
    loss_sum = jnp.sum(d_cond_all[frames_total]) / mod_rows
    d_pre_two = jax.vjp(jax.nn.silu, pre_two)[1](d_cond_all[:frames_total])[0]
    first_col = (device * lax.axis_size("mp") + mp_index) * small_cols

    def own(array):
        return lax.dynamic_slice_in_dim(array, first_col, small_cols, 1)

    grad_second = jnp.einsum("fi,fj->ij", first_all, own(d_pre_two), precision=HIGH)
    second_rows = lax.dynamic_slice_in_dim(small_full, FREQ + first_col, small_cols, 0)
    d_first = jnp.einsum("fk,jk->fj", d_pre_two, second_rows, precision=HIGH)
    d_pre_one = jax.vjp(jax.nn.silu, own(pre_one))[1](d_first)[0]
    grad_first = jnp.einsum("fi,fj->ij", features_all, d_pre_one, precision=HIGH)
    joined = jnp.concatenate(
        [
            part.astype(jnp.bfloat16)
            for part in (grad_qkv[0], grad_qkv[1], grad_qkv[2], grad_in.T)
        ],
        axis=1,
    )
    joined_sum = lax.psum_scatter(joined, "frames", scatter_dimension=0, tiled=True).astype(
        jnp.float32
    )
    ff_cols = mlp_weights.shape[2]
    sum_joint = sum_joint.astype(jnp.float32)
    sum_mlp = jnp.stack([sum_joint[:, :ff_cols], sum_joint[:, ff_cols : 2 * ff_cols]])
    sum_attn = jnp.stack(
        [joined_sum[:, k * width_local : (k + 1) * width_local] for k in range(3)]
        + [sum_joint[:, 2 * ff_cols : 2 * ff_cols + width_local]]
    )
    head_first = 2 * ff_cols + width_local
    ends = jnp.concatenate(
        [joined_sum[:, 3 * width_local :], sum_joint[:, head_first : head_first + P_SIZE]], axis=1
    ).T
    sum_ends = half_of(ends, 1) + lax.ppermute(
        lax.dynamic_slice_in_dim(ends, (1 - mp_index) * small_cols, small_cols, 1), "mp", flip
    )
    sum_small = jnp.concatenate([grad_first, grad_second, sum_ends], axis=0)
    learning_rate = 0.5 * math.sqrt(tokens_total * P_SIZE / D)
    attn_new, attn_moment_new, attn_average_new, attn_copy = update(
        attn_weights, sum_attn, attn_moment, attn_average, learning_rate
    )
    mlp_new, mlp_moment_new, mlp_average_new, mlp_copy = update(
        mlp_weights, sum_mlp, mlp_moment, mlp_average, learning_rate
    )
    mod_new, mod_moment_new, mod_average_new, mod_copy = update(
        mod_weight, sum_mod, mod_moment, mod_average, learning_rate
    )
    small_new, small_moment_new, small_average_new, small_copy = update(
        small_weights, sum_small, small_moment, small_average, learning_rate
    )
    return (
        loss_sum,
        noised_count,
        attn_new,
        attn_moment_new,
        attn_average_new,
        attn_copy,
        mlp_new,
        mlp_moment_new,
        mlp_average_new,
        mlp_copy,
        mod_new,
        mod_moment_new,
        mod_average_new,
        mod_copy,
        small_new,
        small_moment_new,
        small_average_new,
        small_copy,
    )


def solution(mesh):
    return jax.shard_map(
        per_device,
        mesh=mesh,
        in_specs=(
            P("frames", None),
            P("frames", None),
            P("frames"),
            P(),
            P(),
            P(None, "frames", "mp"),
            P(None, "frames", "mp"),
            P("frames", "mp"),
            P(None, ("frames", "mp")),
            P(None, "frames", "mp"),
            P(None, "frames", "mp"),
            P("frames", "mp"),
            P(None, ("frames", "mp")),
            P(None, "frames", "mp"),
            P(None, "frames", "mp"),
            P("frames", "mp"),
            P(None, ("frames", "mp")),
        ),
        out_specs=(
            P(),
            P(),
            P(None, "frames", "mp"),
            P(None, "frames", "mp"),
            P(None, "frames", "mp"),
            P(None, "frames", "mp"),
            P(None, "frames", "mp"),
            P(None, "frames", "mp"),
            P(None, "frames", "mp"),
            P(None, "frames", "mp"),
            P("frames", "mp"),
            P("frames", "mp"),
            P("frames", "mp"),
            P("frames", "mp"),
            P(None, ("frames", "mp")),
            P(None, ("frames", "mp")),
            P(None, ("frames", "mp")),
            P(None, ("frames", "mp")),
        ),
        check_vma=False,
    )
```

```python
import functools
import math

import jax
import jax.numpy as jnp
import numpy as np
from jax import lax
from jax.experimental import pallas as pl
from jax.experimental.pallas import tpu as pltpu
from jax.sharding import PartitionSpec as P

D = 1024
HD = 64
CH = 4
FREQ = 256
GRID = 16
P_SIZE = 16
TPF = 64
REACH = 4


HIGH = lax.Precision.HIGHEST
EPSILON = 1e-06
MOMENTUM = 0.5
EMA_DECAY = 0.5
TP_AXIS = "mp"


def rotation_matrix(head_width):
    groups = [head_width // 4, 3 * head_width // 8, 3 * head_width // 8]
    rotation = np.zeros((head_width, head_width), np.float32)
    offset = 0
    for group_size in groups:
        half_size = group_size // 2
        for pair_index in range(half_size):
            rotation[offset + half_size + pair_index, offset + pair_index] = -1.0
            rotation[offset + pair_index, offset + half_size + pair_index] = 1.0
        offset += group_size
    return rotation


def rotary_angles(frame_pos, row_pos, col_pos, head_width):
    pieces = []
    for position, group_size in (
        (frame_pos, head_width // 4),
        (row_pos, 3 * head_width // 8),
        (col_pos, 3 * head_width // 8),
    ):
        half_size = group_size // 2
        frequency = 10000.0 ** (-jnp.arange(half_size, dtype=jnp.float32) / half_size)
        phases = position[:, None] * frequency[None, :]
        pieces += [phases, phases]
    return jnp.concatenate(pieces, axis=1)


def clip_positions(clip_ids):
    frame_index = jnp.arange(clip_ids.shape[0], dtype=jnp.int32)
    starts_here = jnp.concatenate([jnp.ones((1,), bool), clip_ids[1:] != clip_ids[:-1]])
    clip_start = lax.cummax(jnp.where(starts_here, frame_index, 0), axis=0)
    return frame_index - clip_start


def patchify(frame_data):
    frame_total = frame_data.shape[0]
    patch_side = GRID // 2
    shaped = frame_data.reshape(frame_total, CH, patch_side, 2, patch_side, 2)
    return shaped.transpose(0, 2, 4, 1, 3, 5).reshape(frame_total * patch_side * patch_side, CH * 4)


def layer_norm(vector):
    row_mean = jnp.mean(vector, axis=-1, keepdims=True)
    centred = vector - row_mean
    variance = jnp.mean(centred * centred, axis=-1, keepdims=True)
    return centred * lax.rsqrt(variance + EPSILON)


def modulate_local(shaped, shift_rows, scale_rows):
    return layer_norm(shaped) * (1.0 + scale_rows) + shift_rows


def time_features(level_eff):
    half_size = FREQ // 2
    frequency = jnp.exp(-math.log(10000.0) * jnp.arange(half_size, dtype=jnp.float32) / half_size)
    phases = (level_eff * 1000.0)[:, None] * frequency[None, :]
    return jnp.concatenate([jnp.cos(phases), jnp.sin(phases)], axis=1)


NT=(((1,),(1,)),((),()))
NN=(((1,),(0,)),((),()))

def dotf(a,b,dims=NN):
    return lax.dot_general(a,b,dims,preferred_element_type=jnp.float32)

def split_pair(xT):
    r=lax.broadcasted_iota(jnp.int32,xT.shape,0)
    z=jnp.zeros_like(xT)
    return jnp.where(r<HD,xT,z), jnp.where(r<HD,z,xT)

def keep_of(t,TK,TQ,cs,qf):
    kf=lax.broadcasted_iota(jnp.int32,(TK,TQ),0)//TPF+t*(TK//TPF)
    return (kf>=cs)&(kf<=qf)

def fwd_kernel(lo_ref,mid_ref,hi_ref,q_ref,k_ref,v_ref,cs_ref,o_ref,lse_ref,vT,*,TQ,TK,W0,NQ):
    KS=k_ref.shape[0]
    def tr(i,_):
        s=pl.multiple_of(i*TK,TK)
        vT[:,pl.ds(s,TK)]=v_ref[pl.ds(s,TK),:].T
        return 0
    lax.fori_loop(lo_ref[0],KS//TK,tr,0)
    def qtile(j,_):
        qs=pl.multiple_of(j*TQ,TQ)
        qT=(q_ref[pl.ds(qs,TQ),:].T)*jnp.bfloat16(0.125)
        qA,qB=split_pair(qT)
        cs=cs_ref[0:1,pl.ds(qs,TQ)]
        qf=lax.broadcasted_iota(jnp.int32,(1,TQ),1)//TPF+(W0+j*(TQ//TPF))
        def step(t,carry,masked):
            ks=pl.multiple_of(t*TK,TK)
            kt=k_ref[pl.ds(ks,TK),:]
            out=[]
            if masked: keep=keep_of(t,TK,TQ,cs,qf)
            for h,(qh,(m,l,o)) in enumerate(zip((qA,qB),carry)):
                s=dotf(kt,qh)
                if masked: s=jnp.where(keep,s,-1e30)
                mn=jnp.maximum(m,jnp.max(s,axis=0,keepdims=True))
                a=jnp.exp(m-mn)
                p=jnp.exp(s-mn)
                l=l*a+jnp.sum(p,axis=0,keepdims=True)
                o=o*a+dotf(vT[h*HD:(h+1)*HD,pl.ds(ks,TK)],p.astype(jnp.bfloat16))
                out.append((mn,l,o))
            return tuple(out)
        init=tuple((jnp.full((1,TQ),-1e29,jnp.float32),jnp.zeros((1,TQ),jnp.float32),jnp.zeros((HD,TQ),jnp.float32)) for _ in range(2))
        c=lax.fori_loop(lo_ref[j],mid_ref[j],lambda t,c:step(t,c,True),init)
        c=lax.fori_loop(mid_ref[j],hi_ref[j],lambda t,c:step(t,c,False),c)
        c=lax.fori_loop(hi_ref[j],(W0*TPF+(j+1)*TQ+TK-1)//TK,lambda t,c:step(t,c,True),c)
        oT=jnp.concatenate([c[0][2]/c[0][1],c[1][2]/c[1][1]],axis=0)
        o_ref[pl.ds(qs,TQ),:]=oT.T.astype(o_ref.dtype)
        lse_ref[0,0:1,pl.ds(qs,TQ)]=c[0][0]+jnp.log(c[0][1])
        lse_ref[0,1:2,pl.ds(qs,TQ)]=c[1][0]+jnp.log(c[1][1])
        return 0
    lax.fori_loop(0,NQ,qtile,0)

def tile_bounds(cs_rel,TQ,TK,W0,NQ):
    fq=TQ//TPF; fk=TK//TPF
    j=jnp.arange(NQ)
    first=cs_rel[::fq]; last=cs_rel[fq-1::fq]
    lo=first//fk
    dg=(W0+j*fq+1)//fk
    mid=jnp.minimum((last+fk-1)//fk,dg)
    mid=jnp.maximum(mid,lo)
    hi=jnp.maximum(dg,mid)
    return lo.astype(jnp.int32),mid.astype(jnp.int32),hi.astype(jnp.int32)

def attn_fwd(q,k,v,cs_rel,TQ=512,TK=512):
    T,Wd=q.shape; KS=k.shape[0]; P=Wd//128
    W0=(KS-T)//TPF; NQ=T//TQ
    lo,mid,hi=tile_bounds(cs_rel,TQ,TK,W0,NQ)
    cs_tok=jnp.broadcast_to(jnp.repeat(cs_rel,TPF)[None,:],(8,T)).astype(jnp.int32)
    return pl.pallas_call(
        functools.partial(fwd_kernel,TQ=TQ,TK=TK,W0=W0,NQ=NQ),
        grid_spec=pltpu.PrefetchScalarGridSpec(num_scalar_prefetch=3,grid=(P,),
            in_specs=[pl.BlockSpec((T,128),lambda p,*_:(0,p)),pl.BlockSpec((KS,128),lambda p,*_:(0,p)),pl.BlockSpec((KS,128),lambda p,*_:(0,p)),pl.BlockSpec((8,T),lambda p,*_:(0,0))],
            out_specs=[pl.BlockSpec((T,128),lambda p,*_:(0,p)),pl.BlockSpec((1,8,T),lambda p,*_:(p,0,0))],
            scratch_shapes=[pltpu.VMEM((128,KS),jnp.bfloat16)]),
        out_shape=[jax.ShapeDtypeStruct((T,Wd),jnp.float32),jax.ShapeDtypeStruct((P,8,T),jnp.float32)],
        compiler_params=pltpu.CompilerParams(vmem_limit_bytes=48<<20),
        cost_estimate=pl.CostEstimate(flops=10**11,bytes_accessed=2*10**7,transcendentals=3*10**7),
        name="attn_forward",
    )(lo,mid,hi,q,k,v,cs_tok)

def bwd_kernel(lo_ref,mid_ref,hi_ref,q_ref,k_ref,v_ref,do_ref,o_ref,lse_ref,cs_ref,dq_ref,dk_ref,dv_ref,kT,dkT,dvT,*,TQ,TK,W0,NQ):
    KS=k_ref.shape[0]
    def tr(i,_):
        s=pl.multiple_of(i*TK,TK)
        kT[:,pl.ds(s,TK)]=k_ref[pl.ds(s,TK),:].T
        return 0
    lax.fori_loop(lo_ref[0],KS//TK,tr,0)
    dkT[...]=jnp.zeros_like(dkT); dvT[...]=jnp.zeros_like(dvT)
    def qtile(j,_):
        qs=pl.multiple_of(j*TQ,TQ)
        qT=(q_ref[pl.ds(qs,TQ),:].T)*jnp.bfloat16(0.125)
        qh=split_pair(qT)
        doT=do_ref[pl.ds(qs,TQ),:].T
        doh=split_pair(doT)
        oT=o_ref[pl.ds(qs,TQ),:].T
        prod=oT*doT.astype(jnp.float32)
        delta=(jnp.sum(prod[:HD],axis=0,keepdims=True),jnp.sum(prod[HD:],axis=0,keepdims=True))
        lse=(lse_ref[0,0:1,pl.ds(qs,TQ)],lse_ref[0,1:2,pl.ds(qs,TQ)])
        cs=cs_ref[0:1,pl.ds(qs,TQ)]
        qf=lax.broadcasted_iota(jnp.int32,(1,TQ),1)//TPF+(W0+j*(TQ//TPF))
        def step(t,carry,masked):
            ks=pl.multiple_of(t*TK,TK)
            kt=k_ref[pl.ds(ks,TK),:]; vt=v_ref[pl.ds(ks,TK),:]
            out=[]
            if masked: keep=keep_of(t,TK,TQ,cs,qf)
            for h in range(2):
                r=slice(h*HD,(h+1)*HD)
                s=dotf(kt,qh[h])
                p=jnp.exp(s-lse[h])
                if masked: p=jnp.where(keep,p,0.0)
                dp=dotf(vt,doh[h])
                ds=(p*(dp-delta[h])).astype(jnp.bfloat16)
                pb=p.astype(jnp.bfloat16)
                dvT[r,pl.ds(ks,TK)]+=dotf(doT[r],pb,NT)
                dkT[r,pl.ds(ks,TK)]+=dotf(qT[r],ds,NT)
                out.append(carry[h]+dotf(kT[r,pl.ds(ks,TK)],ds))
            return tuple(out)
        init=(jnp.zeros((HD,TQ),jnp.float32),)*2
        c=lax.fori_loop(lo_ref[j],mid_ref[j],lambda t,c:step(t,c,True),init)
        c=lax.fori_loop(mid_ref[j],hi_ref[j],lambda t,c:step(t,c,False),c)
        c=lax.fori_loop(hi_ref[j],(W0*TPF+(j+1)*TQ+TK-1)//TK,lambda t,c:step(t,c,True),c)
        dq_ref[pl.ds(qs,TQ),:]=(jnp.concatenate(c,axis=0)*0.125).T
        return 0
    lax.fori_loop(0,NQ,qtile,0)
    def back(i,_):
        s=pl.multiple_of(i*TK,TK)
        dk_ref[pl.ds(s,TK),:]=dkT[:,pl.ds(s,TK)].T.astype(dk_ref.dtype)
        dv_ref[pl.ds(s,TK),:]=dvT[:,pl.ds(s,TK)].T.astype(dv_ref.dtype)
        return 0
    lax.fori_loop(0,KS//TK,back,0)

def attn_bwd(q,k,v,do,o,lse,cs_rel,TQ=512,TK=512,out_dt=jnp.bfloat16):
    T,Wd=q.shape; KS=k.shape[0]; P=Wd//128
    W0=(KS-T)//TPF; NQ=T//TQ
    lo,mid,hi=tile_bounds(cs_rel,TQ,TK,W0,NQ)
    cs_tok=jnp.broadcast_to(jnp.repeat(cs_rel,TPF)[None,:],(8,T)).astype(jnp.int32)
    tb=pl.BlockSpec((T,128),lambda p,*_:(0,p)); kb=pl.BlockSpec((KS,128),lambda p,*_:(0,p))
    return pl.pallas_call(
        functools.partial(bwd_kernel,TQ=TQ,TK=TK,W0=W0,NQ=NQ),
        grid_spec=pltpu.PrefetchScalarGridSpec(num_scalar_prefetch=3,grid=(P,),
            in_specs=[tb,kb,kb,tb,tb,pl.BlockSpec((1,8,T),lambda p,*_:(p,0,0)),pl.BlockSpec((8,T),lambda p,*_:(0,0))],
            out_specs=[tb,kb,kb],
            scratch_shapes=[pltpu.VMEM((128,KS),jnp.bfloat16),pltpu.VMEM((128,KS),jnp.float32),pltpu.VMEM((128,KS),jnp.float32)]),
        out_shape=[jax.ShapeDtypeStruct((T,Wd),jnp.float32),jax.ShapeDtypeStruct((KS,Wd),out_dt),jax.ShapeDtypeStruct((KS,Wd),out_dt)],
        compiler_params=pltpu.CompilerParams(vmem_limit_bytes=56<<20),
        cost_estimate=pl.CostEstimate(flops=2*10**11,bytes_accessed=5*10**7,transcendentals=3*10**7),
        name="attn_backward",
    )(lo,mid,hi,q,k,v,do,o,lse,cs_tok)


def update(weight, gradient, moment, average, learning_rate):
    moment_new = MOMENTUM * moment + gradient
    weight_new = weight - learning_rate * (gradient + MOMENTUM * moment_new)
    average_new = EMA_DECAY * average + (1.0 - EMA_DECAY) * weight_new
    return (weight_new, moment_new, average_new, weight_new.astype(jnp.bfloat16))


TN = (((0,), (0,)), ((), ()))


def norm_rows(v):
    centred = v - jnp.mean(v, axis=-1, keepdims=True)
    inverse = lax.rsqrt(jnp.mean(centred * centred, axis=-1, keepdims=True) + EPSILON)
    return centred * inverse, inverse


def norm_rows_back(grad, normed, inverse):
    return inverse * (
        grad
        - jnp.mean(grad, axis=-1, keepdims=True)
        - normed * jnp.mean(grad * normed, axis=-1, keepdims=True)
    )


def gelu_pair(x):
    c = math.sqrt(2.0 / math.pi)
    sq = x * x
    t = jnp.tanh(c * (x + 0.044715 * (x * sq)))
    half = 0.5 * (1.0 + t)
    return x * half, half + (0.5 * c) * x * (1.0 - t * t) * (1.0 + 0.134145 * sq)


def mid_kernel(
    o_ref, wo_ref, hid_ref, mod_ref, noise_ref, tw_ref, head_ref, gs_ref, wu_hbm, wd_hbm,
    dmix_ref, dx1_ref, dmod_ref, loss_ref, up_hbm, rest_hbm,
    wu_ref, wd_ref, att, x1, out, dx2, n2, n2t, act, dgl, dout, doutt, datt, datt_t,
    send_a, recv_a, send_c, recv_c, send_e, recv_e, stage, ghead_ref, go_ref, gh_t,
    wsem, gsem, ssem, rsem, *, tp,
):
    f = lax.axis_index("frames")
    h = lax.axis_index("mp")
    bf16 = jnp.bfloat16
    x_peer = {"mp": 1 - h}
    tp_peer = {"frames": f + 1 - 2 * lax.rem(f, 2)} if tp == "core" else x_peer
    half = hid_ref.shape[0]
    rows = 128
    chunks = half // rows
    width = hid_ref.shape[1]
    ff = wu_hbm.shape[1]
    e = o_ref.shape[1]
    ft = 512
    dt = 256

    weights = [
        pltpu.make_async_copy(wu_hbm, wu_ref, wsem.at[0]),
        pltpu.make_async_copy(wd_hbm, wd_ref, wsem.at[1]),
    ]
    for w in weights:
        w.start()

    barrier = pltpu.get_barrier_semaphore()
    pl.semaphore_signal(barrier, inc=1, device_id=x_peer, device_id_type=pl.DeviceIdType.MESH)
    if tp == "core":
        pl.semaphore_signal(barrier, inc=1, device_id=tp_peer, device_id_type=pl.DeviceIdType.MESH)
    pl.semaphore_wait(barrier, 2 if tp == "core" else 1)

    def at(start, size):
        return pl.ds(pl.multiple_of(start, size), size)

    def copy(src, dst, phase, c, peer):
        return pltpu.make_async_remote_copy(
            src_ref=src, dst_ref=dst, send_sem=ssem.at[phase, c], recv_sem=rsem.at[phase, c],
            device_id=peer, device_id_type=pl.DeviceIdType.MESH,
        )

    def copy_a(c):
        return copy(send_a.at[at(c * rows, rows)], recv_a.at[at(c * rows, rows)], 0, c, x_peer)

    def copy_b(c):
        return copy(
            n2.at[at(c * 2 * rows, rows)], n2.at[at(c * 2 * rows + rows, rows)], 1, c, tp_peer
        )

    def copy_c(c):
        return copy(send_c.at[at(c * rows, rows)], recv_c.at[at(c * rows, rows)], 2, c, tp_peer)

    def copy_d(c):
        return copy(
            dout.at[at(c * 2 * rows, rows)], dout.at[at(c * 2 * rows + rows, rows)], 3, c, tp_peer
        )

    def copy_e(c):
        return copy(send_e.at[at(c * rows, rows)], recv_e.at[at(c * rows, rows)], 4, c, tp_peer)

    def copy_f(c):
        mine = datt.at[at(h * half + c * rows, rows)]
        return copy(mine, mine, 5, c, x_peer)

    def phase_a(c, _):
        part = o_ref[at((1 - h) * half + c * rows, rows), :].astype(bf16)
        send_a[at(c * rows, rows), :] = dotf(part, wo_ref[...], NT).astype(bf16)
        copy_a(c).start()
        return 0

    lax.fori_loop(0, chunks, phase_a, 0)

    def phase_b(c, _):
        part = o_ref[at(h * half + c * rows, rows), :].astype(bf16)
        att[at(c * rows, rows), :] = dotf(part, wo_ref[...], NT)
        copy_a(c).wait_recv()
        for k in range(rows // TPF):
            r = at(c * rows + k * TPF, TPF)
            frame = pl.ds(c * (rows // TPF) + k, 1)
            a = att[r, :] + recv_a[r, :].astype(jnp.float32)
            att[r, :] = a
            v = hid_ref[r, :] + mod_ref[0, frame, :] * a
            x1[r, :] = v
            y, _inv = norm_rows(v)
            n2[at(c * 2 * rows + k * TPF, TPF), :] = (
                y * (1.0 + mod_ref[2, frame, :]) + mod_ref[1, frame, :]
            ).astype(bf16)
        copy_b(c).start()
        return 0

    lax.fori_loop(0, chunks, phase_b, 0)
    for w in weights:
        w.wait()

    def phase_c(c, _):
        copy_b(c).wait_recv()
        tok = at(c * 2 * rows, 2 * rows)
        n2t[:, tok] = n2[tok, :].T

        def up(i, _):
            cols = at(i * ft, ft)
            a, g = gelu_pair(dotf(n2[tok, :], wu_ref[:, cols]))
            act[tok, cols] = a.astype(bf16)
            dgl[tok, cols] = g.astype(bf16)
            return 0

        lax.fori_loop(0, ff // ft, up, 0)

        def down(i, _):
            cols = at(i * dt, dt)
            res = dotf(act[tok, :], wd_ref[cols, :], NT)
            out[at(c * rows, rows), cols] = res[:rows]
            send_c[at(c * rows, rows), cols] = res[rows:].astype(bf16)
            return 0

        lax.fori_loop(0, width // dt, down, 0)
        copy_c(c).start()
        return 0

    lax.fori_loop(0, chunks, phase_c, 0)

    ghead_ref[...] = jnp.zeros_like(ghead_ref)
    loss_ref[...] = jnp.zeros_like(loss_ref)

    def phase_d(c, _):
        copy_c(c).wait_recv()
        for k in range(rows // TPF):
            r = at(c * rows + k * TPF, TPF)
            frame = pl.ds(c * (rows // TPF) + k, 1)
            o = out[r, :] + recv_c[r, :].astype(jnp.float32)
            gate = mod_ref[3, frame, :]
            y, inv = norm_rows(x1[r, :] + gate * o)
            fn = y.astype(bf16)
            misfit = dotf(fn, head_ref[...], NT) - noise_ref[r, :]
            weighted = tw_ref[r, :] * misfit
            loss_ref[...] += weighted * misfit
            d_pred = (2.0 * gs_ref[0] * weighted).astype(bf16)
            ghead_ref[...] += dotf(d_pred, fn, TN)
            d_x2 = norm_rows_back(dotf(d_pred, head_ref[...]), y, inv)
            dx2[r, :] = d_x2
            dmod_ref[3, frame, :] = jnp.sum(d_x2 * o, axis=0, keepdims=True)
            dout[at(c * 2 * rows + k * TPF, TPF), :] = (gate * d_x2).astype(bf16)
        copy_d(c).start()
        return 0

    lax.fori_loop(0, chunks, phase_d, 0)

    def phase_e(c, _):
        copy_d(c).wait_recv()
        tok = at(c * 2 * rows, 2 * rows)
        doutt[:, tok] = dout[tok, :].T

        def down(i, _):
            cols = at(i * ft, ft)
            g = dotf(dout[tok, :], wd_ref[:, cols]) * dgl[tok, cols].astype(jnp.float32)
            dgl[tok, cols] = g.astype(bf16)
            return 0

        lax.fori_loop(0, ff // ft, down, 0)

        def up(i, _):
            cols = at(i * dt, dt)
            res = dotf(dgl[tok, :], wu_ref[cols, :], NT)
            out[at(c * rows, rows), cols] = res[:rows]
            send_e[at(c * rows, rows), cols] = res[rows:].astype(bf16)
            return 0

        lax.fori_loop(0, width // dt, up, 0)
        copy_e(c).start()
        return 0

    lax.fori_loop(0, chunks, phase_e, 0)

    def phase_f(c, _):
        copy_e(c).wait_recv()
        for k in range(rows // TPF):
            r = at(c * rows + k * TPF, TPF)
            frame = pl.ds(c * (rows // TPF) + k, 1)
            g = out[r, :] + recv_e[r, :].astype(jnp.float32)
            y, inv = norm_rows(x1[r, :])
            dmod_ref[1, frame, :] = jnp.sum(g, axis=0, keepdims=True)
            dmod_ref[2, frame, :] = jnp.sum(g * y, axis=0, keepdims=True)
            d_x1 = dx2[r, :] + norm_rows_back(g * (1.0 + mod_ref[2, frame, :]), y, inv)
            dx1_ref[r, :] = d_x1
            dmod_ref[0, frame, :] = jnp.sum(d_x1 * att[r, :], axis=0, keepdims=True)
            datt[at(h * half + c * rows + k * TPF, TPF), :] = (mod_ref[0, frame, :] * d_x1).astype(
                bf16
            )
        copy_f(c).start()
        return 0

    lax.fori_loop(0, chunks, phase_f, 0)

    def weight_grads(left, right, target):
        def put(slot, i):
            return pltpu.make_async_copy(
                stage.at[slot], target.at[at(i * dt, dt), pl.ds(0, ff)], gsem.at[slot]
            )

        def tile(i, _):
            slot = lax.rem(i, 2)

            @pl.when(i >= 2)
            def _():
                put(slot, i - 2).wait()

            def cols_of(j, _):
                cols = at(j * ft, ft)
                stage[slot, :, cols] = dotf(left[at(i * dt, dt), :], right[:, cols]).astype(bf16)
                return 0

            lax.fori_loop(0, ff // ft, cols_of, 0)
            put(slot, i).start()
            return 0

        lax.fori_loop(0, width // dt, tile, 0)
        for i in (width // dt - 2, width // dt - 1):
            put(i % 2, i).wait()

    weight_grads(n2t, dgl, up_hbm)
    weight_grads(doutt, act, rest_hbm)

    def own_mix(c, _):
        tok = at(h * half + c * rows, rows)
        datt_t[:, tok] = datt[tok, :].T
        dmix_ref[tok, :] = dotf(datt[tok, :], wo_ref[...]).astype(bf16)
        return 0

    lax.fori_loop(0, chunks, own_mix, 0)

    def phase_g(c, _):
        tok = at((1 - h) * half + c * rows, rows)
        theirs = datt.at[tok]
        copy(theirs, theirs, 5, c, x_peer).wait_recv()
        datt_t[:, tok] = datt[tok, :].T
        dmix_ref[tok, :] = dotf(datt[tok, :], wo_ref[...]).astype(bf16)
        return 0

    lax.fori_loop(0, chunks, phase_g, 0)

    def grad_out(i, _):
        d = at(i * dt, dt)
        go_ref[d, :] = dotf(datt_t[d, :], o_ref[...].astype(bf16)).astype(bf16)
        return 0

    lax.fori_loop(0, width // dt, grad_out, 0)
    gh_t[...] = ghead_ref[...].T.astype(bf16)
    ends = [
        pltpu.make_async_copy(go_ref, rest_hbm.at[:, pl.ds(ff, e)], gsem.at[2]),
        pltpu.make_async_copy(gh_t, rest_hbm.at[:, pl.ds(ff + e, 128)], gsem.at[3]),
    ]
    for one in ends:
        one.start()
    for one in ends:
        one.wait()
    def sent(c, _):
        for one in (copy_a, copy_b, copy_c, copy_d, copy_e, copy_f):
            one(c).wait_send()
        return 0

    lax.fori_loop(0, chunks, sent, 0)


def mid_block(o, wo, hid, mod, noise, tw, head, gs, wu, wd, tp, cid):
    tok, e = o.shape
    half, width = hid.shape
    ff = wu.shape[1]
    own_frames = half // TPF
    f32, bf16 = jnp.float32, jnp.bfloat16
    vm = pl.BlockSpec(memory_space=pltpu.VMEM)
    anym = pl.BlockSpec(memory_space=pl.ANY)
    V = pltpu.VMEM
    return pl.pallas_call(
        functools.partial(mid_kernel, tp=tp),
        in_specs=[vm] * 7 + [pl.BlockSpec(memory_space=pltpu.SMEM), anym, anym],
        out_specs=[vm] * 4 + [anym] * 2,
        out_shape=[
            jax.ShapeDtypeStruct((tok, e), bf16),
            jax.ShapeDtypeStruct((half, width), f32),
            jax.ShapeDtypeStruct((4, own_frames, width), f32),
            jax.ShapeDtypeStruct((TPF, 128), f32),
            jax.ShapeDtypeStruct((width, ff), bf16),
            jax.ShapeDtypeStruct((width, ff + e + 128), bf16),
        ],
        scratch_shapes=[
            V((width, ff), bf16), V((width, ff), bf16),
            V((half, width), f32), V((half, width), f32), V((half, width), f32),
            V((half, width), f32),
            V((2 * half, width), bf16), V((width, 2 * half), bf16),
            V((2 * half, ff), bf16), V((2 * half, ff), bf16),
            V((2 * half, width), bf16), V((width, 2 * half), bf16),
            V((tok, width), bf16), V((width, tok), bf16),
            V((half, width), bf16), V((half, width), bf16),
            V((half, width), bf16), V((half, width), bf16),
            V((half, width), bf16), V((half, width), bf16),
            V((2, 256, ff), bf16), V((128, width), f32), V((width, e), bf16),
            V((width, 128), bf16),
            pltpu.SemaphoreType.DMA((2,)), pltpu.SemaphoreType.DMA((4,)),
            pltpu.SemaphoreType.DMA((6, half // 128)), pltpu.SemaphoreType.DMA((6, half // 128)),
        ],
        compiler_params=pltpu.CompilerParams(
            vmem_limit_bytes=62 << 20, collective_id=cid, has_side_effects=True
        ),
        cost_estimate=pl.CostEstimate(
            flops=4 * 10**10, bytes_accessed=3 * 10**7, transcendentals=2 * 10**6
        ),
        name="feed_forward",
    )(o, wo, hid, mod, noise, tw, head, gs, wu, wd)


def split_three(v):
    high = v.astype(jnp.bfloat16)
    left = v - high.astype(jnp.float32)
    middle = left.astype(jnp.bfloat16)
    return high, middle, (left - middle.astype(jnp.float32)).astype(jnp.bfloat16)


def turn_back(g, cosine, sine, rot):
    parts = split_three(g * sine)
    return (g * cosine + sum(dotf(p, rot, NT) for p in parts)).astype(jnp.bfloat16)


def tail_kernel(
    dq_ref, n1_ref, w_ref, cos_ref, sin_ref, rot_ref, hid_ref, scale_ref, dx1_ref, inp_ref,
    dk_hbm, dv_hbm,
    gq_ref, gin_ref, dss_ref,
    own, near, yrecv, zrecv, n1t, dproj, send_x, recv_x, part,
    lsem, s_near, r_near, s_y, r_y, s_z, r_z, s_x, r_x,
):
    f = lax.axis_index("frames")
    h = lax.axis_index("mp")
    n = lax.axis_size("frames")
    core = lax.rem(f, 2)
    odd = lax.rem(lax.div(f, 2), 2)
    core_peer = {"frames": f + 1 - 2 * core}
    y_peer = {"frames": f + 2 - 4 * odd}
    before = {"frames": lax.rem(f - 4 + n, n)}
    after = {"frames": lax.rem(f + 4, n)}
    x_peer = {"mp": 1 - h}
    tok, e = dq_ref.shape
    width = n1_ref.shape[1]
    half = tok // 2
    rows = 256
    chunks = tok // rows
    f32, bf16 = jnp.float32, jnp.bfloat16
    MESH = pl.DeviceIdType.MESH
    sides = (dk_hbm, dv_hbm)

    def at(start, size):
        return pl.ds(pl.multiple_of(start, size), size)

    loads = [
        pltpu.make_async_copy(
            sides[s].at[pl.ds(b * tok, tok)], own.at[s, j], lsem.at[s, j]
        )
        for s in range(2)
        for j, b in enumerate((4, 2, 0))
    ]
    for one in loads:
        one.start()

    barrier = pltpu.get_barrier_semaphore()
    for peer in (core_peer, y_peer, x_peer):
        pl.semaphore_signal(barrier, inc=1, device_id=peer, device_id_type=MESH)

    @pl.when(f >= 4)
    def _():
        pl.semaphore_signal(barrier, inc=1, device_id=before, device_id_type=MESH)

    @pl.when(f + 4 < n)
    def _():
        pl.semaphore_signal(barrier, inc=1, device_id=after, device_id_type=MESH)

    pl.semaphore_wait(barrier, 3 + jnp.where(f >= 4, 1, 0) + jnp.where(f + 4 < n, 1, 0))

    def rows_of(i):
        return lax.rem(i + (chunks // 2) * (1 - h), chunks) * rows

    def remote(src, dst, send, recv, peer):
        return pltpu.make_async_remote_copy(
            src_ref=src, dst_ref=dst, send_sem=send, recv_sem=recv, device_id=peer,
            device_id_type=MESH,
        )

    def near_copy(i, s, j):
        b = (3, 1)[j]
        return remote(
            sides[s].at[at(b * tok + rows_of(i), rows)],
            near.at[s, j, at(rows_of(i), rows)],
            s_near.at[s, j, i], r_near.at[s, j, i], core_peer,
        )

    def y_copy(i, s):
        r = at(rows_of(i), rows)
        return remote(own.at[s, 1, r], yrecv.at[s, r], s_y.at[s, i], r_y.at[s, i], y_peer)

    def z_copy(i, s):
        r = at(rows_of(i), rows)
        return remote(own.at[s, 2, r], zrecv.at[s, r], s_z.at[s, i], r_z.at[s, i], before)

    def x_copy(i):
        r = at(i * rows, rows)
        return remote(send_x.at[r], recv_x.at[r], s_x.at[i], r_x.at[i], x_peer)

    def start_near(i, _):
        for s in range(2):
            for j in range(2):
                near_copy(i, s, j).start()
        return 0

    lax.fori_loop(0, chunks, start_near, 0)

    @pl.when(f + 4 >= n)
    def _():
        zrecv[...] = jnp.zeros_like(zrecv)

    for one in loads:
        one.wait()
    low_core = core == 0

    def combine(i, _):
        r = at(rows_of(i), rows)
        for s in range(2):
            for j in range(2):
                near_copy(i, s, j).wait_recv()
            n3 = near[s, 0, r, :].astype(f32)
            n1_ = near[s, 1, r, :].astype(f32)
            own[s, 1, r, :] = (
                own[s, 1, r, :].astype(f32) + jnp.where(low_core, n1_, n3)
            ).astype(bf16)
            y_copy(i, s).start()
            own[s, 2, r, :] = (
                own[s, 2, r, :].astype(f32) + jnp.where(low_core, 0.0, n1_)
            ).astype(bf16)

            @pl.when((odd == 0) & (f >= 4))
            def _():
                z_copy(i, s).start()

        return 0

    lax.fori_loop(0, chunks, combine, 0)

    def turned(g, r, k):
        for b in range(e // 256):
            cols = slice(b * 256, (b + 1) * 256)
            dproj[k, r, cols] = turn_back(
                g[:, cols], cos_ref[r, :], sin_ref[r, :], rot_ref[...]
            )

    def relay(i, _):
        r = at(rows_of(i), rows)
        turned(dq_ref[r, :], r, 0)
        n1t[:, r] = n1_ref[r, :].T

        @pl.when(odd == 1)
        def _():
            for s in range(2):
                y_copy(i, s).wait_recv()

                @pl.when(f >= 4)
                def _():
                    own[s, 2, r, :] = (
                        own[s, 2, r, :].astype(f32) + yrecv[s, r, :].astype(f32)
                    ).astype(bf16)
                    z_copy(i, s).start()

        return 0

    lax.fori_loop(0, chunks, relay, 0)

    def grads(k):
        def tile(i, _):
            d = at(i * 256, 256)
            gq_ref[k, d, :] = dotf(n1t[d, :], dproj[k]).astype(bf16)
            return 0

        lax.fori_loop(0, width // 256, tile, 0)

    grads(0)

    def finish(i, _):
        r = at(rows_of(i), rows)
        for s in range(2):

            @pl.when(odd == 0)
            def _():
                y_copy(i, s).wait_recv()

            @pl.when(f + 4 < n)
            def _():
                z_copy(i, s).wait_recv()

            total = (
                own[s, 0, r, :].astype(f32)
                + jnp.where(low_core, near[s, 0, r, :].astype(f32), 0.0)
                + jnp.where(odd == 0, yrecv[s, r, :].astype(f32), 0.0)
                + zrecv[s, r, :].astype(f32)
            )
            if s == 0:
                turned(total, r, 1)
            else:
                dproj[2, r, :] = total.astype(bf16)

        def cols_of(j, _):
            cols = at(j * 256, 256)
            res = sum(dotf(dproj[k, r, :], w_ref[k, cols, :], NT) for k in range(3))

            @pl.when(i < chunks // 2)
            def _():
                send_x[at(i * rows, rows), cols] = res.astype(bf16)

            @pl.when(i >= chunks // 2)
            def _():
                part[at((i - chunks // 2) * rows, rows), cols] = res

            return 0

        lax.fori_loop(0, width // 256, cols_of, 0)

        @pl.when(i < chunks // 2)
        def _():
            x_copy(i).start()

        return 0

    lax.fori_loop(0, chunks, finish, 0)
    grads(1)
    grads(2)
    gin_ref[...] = jnp.zeros_like(gin_ref)

    def norm_back(i, _):
        x_copy(i).wait_recv()
        for k in range(rows // TPF):
            r = at(i * rows + k * TPF, TPF)
            frame = pl.ds(i * (rows // TPF) + k, 1)
            g = part[r, :] + recv_x[r, :].astype(f32)
            y, inv = norm_rows(hid_ref[r, :])
            dss_ref[0, frame, :] = jnp.sum(g, axis=0, keepdims=True)
            dss_ref[1, frame, :] = jnp.sum(g * y, axis=0, keepdims=True)
            d_hid = dx1_ref[r, :] + norm_rows_back(g * (1.0 + scale_ref[frame, :]), y, inv)
            gin_ref[...] += dotf(inp_ref[r, :], d_hid.astype(bf16), TN)
        return 0

    lax.fori_loop(0, half // rows, norm_back, 0)

    def sent(i, _):
        for s in range(2):
            for j in range(2):
                near_copy(i, s, j).wait_send()
            y_copy(i, s).wait_send()

            @pl.when(f >= 4)
            def _():
                z_copy(i, s).wait_send()

        @pl.when(i < chunks // 2)
        def _():
            x_copy(i).wait_send()

        return 0

    lax.fori_loop(0, chunks, sent, 0)


def tail_block(dq, n1, w, cosine, sine, rot, hid, scale, dx1, inp, dk, dv, cid):
    tok, e = dq.shape
    width = n1.shape[1]
    half = tok // 2
    f32, bf16 = jnp.float32, jnp.bfloat16
    vm = pl.BlockSpec(memory_space=pltpu.VMEM)
    anym = pl.BlockSpec(memory_space=pl.ANY)
    V = pltpu.VMEM
    D_ = pltpu.SemaphoreType.DMA
    chunks = tok // 256
    return pl.pallas_call(
        tail_kernel,
        in_specs=[vm] * 10 + [anym] * 2,
        out_specs=[vm] * 3,
        out_shape=[
            jax.ShapeDtypeStruct((3, width, e), bf16),
            jax.ShapeDtypeStruct((128, width), f32),
            jax.ShapeDtypeStruct((2, half // TPF, width), f32),
        ],
        scratch_shapes=[
            V((2, 3, tok, e), bf16), V((2, 2, tok, e), bf16), V((2, tok, e), bf16),
            V((2, tok, e), bf16), V((width, tok), bf16), V((3, tok, e), bf16),
            V((half, width), bf16), V((half, width), bf16), V((half, width), f32),
            D_((2, 3)), D_((2, 2, chunks)), D_((2, 2, chunks)), D_((2, chunks)), D_((2, chunks)),
            D_((2, chunks)), D_((2, chunks)), D_((chunks // 2,)), D_((chunks // 2,)),
        ],
        compiler_params=pltpu.CompilerParams(
            vmem_limit_bytes=56 << 20, collective_id=cid, has_side_effects=True
        ),
        cost_estimate=pl.CostEstimate(
            flops=2 * 10**10, bytes_accessed=3 * 10**7, transcendentals=0
        ),
        name="projection_backward",
    )(dq, n1, w, cosine, sine, rot, hid, scale, dx1, inp, dk, dv)


def proj_kernel(
    inp_ref, win_ref, mod_ref, w_ref, cos_ref, sin_ref, rot_ref,
    n1_ref, hid_ref, q_ref, k_hbm, v_hbm,
    kv, wr,
    lsem, s_core, r_core, s_y, r_y, s_z, r_z,
):
    f = lax.axis_index("frames")
    h = lax.axis_index("mp")
    n = lax.axis_size("frames")
    core = lax.rem(f, 2)
    odd = lax.rem(lax.div(f, 2), 2)
    core_peer = {"frames": f + 1 - 2 * core}
    y_peer = {"frames": f + 2 - 4 * odd}
    before = {"frames": lax.rem(f - 4 + n, n)}
    after = {"frames": lax.rem(f + 4, n)}
    tok, width = n1_ref.shape
    e = q_ref.shape[1]
    half = tok // 2
    rows = 256
    chunks = tok // rows
    bf16 = jnp.bfloat16
    MESH = pl.DeviceIdType.MESH
    sides = (k_hbm, v_hbm)
    has_z = f >= 4
    has_next = f + 4 < n
    has_y = has_z | (odd == 1)

    def at(start, size):
        return pl.ds(pl.multiple_of(start, size), size)

    barrier = pltpu.get_barrier_semaphore()
    for peer in (core_peer, y_peer):
        pl.semaphore_signal(barrier, inc=1, device_id=peer, device_id_type=MESH)

    @pl.when(has_z)
    def _():
        pl.semaphore_signal(barrier, inc=1, device_id=before, device_id_type=MESH)

    @pl.when(has_next)
    def _():
        pl.semaphore_signal(barrier, inc=1, device_id=after, device_id_type=MESH)

    def embed(i, _):
        for k in range(2):
            r = at(i * 2 * TPF + k * TPF, TPF)
            frame = pl.ds(i * 2 + k, 1)
            v = dotf(inp_ref[r, :], win_ref[...])
            y, _inv = norm_rows(v)
            n1_ref[r, :] = (y * (1.0 + mod_ref[1, frame, :]) + mod_ref[0, frame, :]).astype(bf16)

            @pl.when(lax.div(i * 2 * TPF, half) == h)
            def _():
                hid_ref[at(lax.rem(i * 2 * TPF, half) + k * TPF, TPF), :] = v

        return 0

    lax.fori_loop(0, tok // (2 * TPF), embed, 0)

    def turn_weights(i, _):
        d = at(i * 256, 256)
        for k in range(2):
            for b in range(e // 256):
                cols = slice(b * 256, (b + 1) * 256)
                wr[k, d, cols] = dotf(w_ref[k, d, cols], rot_ref[...]).astype(bf16)
        return 0

    lax.fori_loop(0, width // 256, turn_weights, 0)
    pl.semaphore_wait(barrier, 2 + jnp.where(has_z, 1, 0) + jnp.where(has_next, 1, 0))

    def remote(src, dst, send, recv, peer):
        return pltpu.make_async_remote_copy(
            src_ref=src, dst_ref=dst, send_sem=send, recv_sem=recv, device_id=peer,
            device_id_type=MESH,
        )

    def block(s, b, i):
        return sides[s].at[at(b * tok + i * rows, rows)]

    def mine(s, i):
        return kv.at[s, at(i * rows, rows)]

    def keep(s, i):
        return pltpu.make_async_copy(mine(s, i), block(s, 4, i), lsem.at[s, i])

    def z_copy(s, i):
        return remote(mine(s, i), block(s, 0, i), s_z.at[s, i], r_z.at[s, i], after)

    def y_copy(s, i, src):
        return remote(src, block(s, 2, i), s_y.at[s, i], r_y.at[s, i], y_peer)

    def core_copy(s, i, j, src):
        return remote(
            src, block(s, (3, 1)[j], i), s_core.at[j, s, i], r_core.at[j, s, i], core_peer
        )

    def rotated(r, k):
        cosine, sine = cos_ref[r, :], sin_ref[r, :]
        parts = []
        for b in range(e // 256):
            cols = slice(b * 256, (b + 1) * 256)
            plain = dotf(n1_ref[r, :], w_ref[k, :, cols])
            turned = dotf(n1_ref[r, :], wr[k, :, cols])
            parts.append((plain * cosine + turned * sine).astype(bf16))
        return parts

    def own_chunk(i, _):
        r = at(i * rows, rows)
        for b, part in enumerate(rotated(r, 1)):
            kv[0, r, b * 256 : (b + 1) * 256] = part
        kv[1, r, :] = dotf(n1_ref[r, :], w_ref[2]).astype(bf16)
        for s in range(2):
            keep(s, i).start()

            @pl.when(has_next)
            def _():
                z_copy(s, i).start()

            @pl.when(odd == 0)
            def _():
                y_copy(s, i, mine(s, i)).start()

            @pl.when(core == 0)
            def _():
                core_copy(s, i, 0, mine(s, i)).start()

        return 0

    lax.fori_loop(0, chunks, own_chunk, 0)

    def queries(i, _):
        r = at(i * rows, rows)
        for b, part in enumerate(rotated(r, 0)):
            q_ref[r, b * 256 : (b + 1) * 256] = part
        return 0

    lax.fori_loop(0, chunks, queries, 0)

    def from_z(i, _):
        @pl.when(has_z)
        def _():
            for s in range(2):
                z_copy(s, i).wait_recv()

                @pl.when(odd == 1)
                def _():
                    y_copy(s, i, block(s, 0, i)).start()

                @pl.when(core == 1)
                def _():
                    core_copy(s, i, 1, block(s, 0, i)).start()

        return 0

    lax.fori_loop(0, chunks, from_z, 0)

    def from_y(i, _):
        @pl.when(has_y)
        def _():
            for s in range(2):
                y_copy(s, i, mine(s, i)).wait_recv()

                @pl.when(core == 1)
                def _():
                    core_copy(s, i, 0, block(s, 2, i)).start()

                @pl.when(core == 0)
                def _():
                    core_copy(s, i, 1, block(s, 2, i)).start()

        return 0

    lax.fori_loop(0, chunks, from_y, 0)

    def ended(i, _):
        for s in range(2):
            keep(s, i).wait()

            @pl.when((core == 1) | has_y)
            def _():
                core_copy(s, i, 0, mine(s, i)).wait_recv()

            @pl.when(((core == 1) & has_y) | has_z)
            def _():
                core_copy(s, i, 1, mine(s, i)).wait_recv()

            @pl.when(has_next)
            def _():
                z_copy(s, i).wait_send()

            @pl.when((odd == 0) | has_z)
            def _():
                y_copy(s, i, mine(s, i)).wait_send()

            @pl.when((core == 0) | has_y)
            def _():
                core_copy(s, i, 0, mine(s, i)).wait_send()

            @pl.when(((core == 0) & has_y) | has_z)
            def _():
                core_copy(s, i, 1, mine(s, i)).wait_send()

        return 0

    lax.fori_loop(0, chunks, ended, 0)


def proj_block(inp, win, mod, w, cosine, sine, rot, reach, cid):
    tok = inp.shape[0]
    width, e = w.shape[1:]
    f32, bf16 = jnp.float32, jnp.bfloat16
    vm = pl.BlockSpec(memory_space=pltpu.VMEM)
    anym = pl.BlockSpec(memory_space=pl.ANY)
    V = pltpu.VMEM
    D_ = pltpu.SemaphoreType.DMA
    chunks = tok // 256
    return pl.pallas_call(
        proj_kernel,
        in_specs=[vm] * 7,
        out_specs=[vm] * 3 + [anym] * 2,
        out_shape=[
            jax.ShapeDtypeStruct((tok, width), bf16),
            jax.ShapeDtypeStruct((tok // 2, width), f32),
            jax.ShapeDtypeStruct((tok, e), bf16),
            jax.ShapeDtypeStruct(((reach + 1) * tok, e), bf16),
            jax.ShapeDtypeStruct(((reach + 1) * tok, e), bf16),
        ],
        scratch_shapes=[
            V((2, tok, e), bf16), V((2, width, e), bf16),
            D_((2, chunks)), D_((2, 2, chunks)), D_((2, 2, chunks)), D_((2, chunks)),
            D_((2, chunks)), D_((2, chunks)), D_((2, chunks)),
        ],
        compiler_params=pltpu.CompilerParams(
            vmem_limit_bytes=48 << 20, collective_id=cid, has_side_effects=True
        ),
        cost_estimate=pl.CostEstimate(
            flops=6 * 10**10, bytes_accessed=3 * 10**7, transcendentals=0
        ),
        name="projection_forward",
    )(inp, win, mod, w, cosine, sine, rot)


def per_device(
    latents,
    noise,
    levels,
    clip_ids,
    clean_flags,
    attn_weights,
    mlp_weights,
    mod_weight,
    small_weights,
    attn_moment,
    mlp_moment,
    mod_moment,
    small_moment,
    attn_average,
    mlp_average,
    mod_average,
    small_average,
):
    frame_count = latents.shape[0]
    tok_count = frame_count * TPF
    patch_side = GRID // 2
    frames_total = clip_ids.shape[0]
    tokens_total = frames_total * TPF
    width_local = attn_weights.shape[2]
    heads_local = width_local // HD
    key_span = (REACH + 1) * tok_count
    device = lax.axis_index("frames")
    mp_index = lax.axis_index("mp")
    first_frame = device * frame_count
    scale_qk = HD ** (-0.5)
    w_attn = lax.all_gather(attn_weights.astype(jnp.bfloat16), "frames", axis=1, tiled=True)
    w_mlp = lax.all_gather(mlp_weights.astype(jnp.bfloat16), "frames", axis=1, tiled=True)
    low_mod = mod_weight.astype(jnp.bfloat16)
    w_mod = lax.all_gather(low_mod, "frames", axis=0, tiled=True)
    small_low = lax.all_gather(
        small_weights.astype(jnp.bfloat16), ("frames", "mp"), axis=1, tiled=True
    )
    levels_all = lax.all_gather(levels, "frames", axis=0, tiled=True)
    small_full = small_low.astype(jnp.float32)
    noised_all = (1 - clean_flags).astype(jnp.float32)
    noised_count = jnp.sum(noised_all)
    noised = lax.dynamic_slice_in_dim(noised_all, first_frame, frame_count)
    level_eff = levels * noised
    signal_scale = jnp.repeat(jnp.cos(0.5 * math.pi * level_eff), TPF)
    noise_scale = jnp.repeat(jnp.sin(0.5 * math.pi * level_eff), TPF)
    noise_patches = patchify(noise)
    inputs = signal_scale[:, None] * patchify(latents) + noise_scale[:, None] * noise_patches
    in_clip_all = clip_positions(clip_ids)
    in_clip = jnp.repeat(
        lax.dynamic_slice_in_dim(in_clip_all, first_frame, frame_count), TPF
    ).astype(jnp.float32)
    within = jnp.arange(tok_count, dtype=jnp.int32) % TPF
    angles = rotary_angles(
        in_clip,
        (within // patch_side).astype(jnp.float32),
        (within % patch_side).astype(jnp.float32),
        HD,
    )
    cosine_table = jnp.tile(jnp.cos(angles), (1, 4))
    sine_table = jnp.tile(jnp.sin(angles), (1, 4))
    turn_four = jnp.asarray(np.kron(np.eye(4, dtype=np.float32), rotation_matrix(HD)), jnp.bfloat16)
    clip_start = (
        lax.dynamic_slice_in_dim(
            jnp.arange(frames_total, dtype=jnp.int32) - in_clip_all, first_frame, frame_count
        )
        - first_frame
        + REACH * frame_count
    )
    features_all = time_features(levels_all * noised_all)
    pre_one = jnp.dot(features_all, small_full[:FREQ], precision=HIGH)
    first_all = jax.nn.silu(pre_one)
    pre_two = jnp.dot(first_all, small_full[FREQ : FREQ + D], precision=HIGH)
    conditioning_all = jax.nn.silu(pre_two)
    conditioning = lax.dynamic_slice_in_dim(conditioning_all, first_frame, frame_count)
    mod_full = w_mod.astype(jnp.float32)
    modulation = lax.all_gather(
        jnp.dot(conditioning, mod_full, precision=HIGH), "mp", axis=1, tiled=True
    )
    pieces = [
        modulation[:, None, piece_index * D : (piece_index + 1) * D] for piece_index in range(6)
    ]
    shift_one, scale_one, gate_one, shift_two, scale_two, gate_two = pieces
    w_in = small_low[FREQ + D : FREQ + D + P_SIZE]
    w_head = small_low[FREQ + D + P_SIZE :]
    inputs_low = inputs.astype(jnp.bfloat16)
    padding = ((0, 0), (0, 128 - P_SIZE))
    inputs_low = jnp.pad(inputs_low, padding)
    normed_one, hidden_half, queries, keys_wide, values_wide = proj_block(
        inputs_low,
        jnp.pad(w_in, ((0, 128 - P_SIZE), (0, 0))),
        jnp.stack([shift_one[:, 0], scale_one[:, 0]]),
        w_attn[:3],
        cosine_table,
        sine_table,
        turn_four,
        REACH,
        2,
    )
    heads_wide, log_totals = attn_fwd(queries, keys_wide, values_wide, clip_start)
    half = tok_count // 2
    own_frames = frame_count // 2

    def half_of(array, dim=0):
        size = array.shape[dim] // 2
        return lax.dynamic_slice_in_dim(array, mp_index * size, size, dim)

    token_weight = jnp.repeat(noised, TPF) / (TPF * P_SIZE)
    grad_scale = 1.0 / jnp.maximum(noised_count, 1.0)
    mod_mid = jnp.stack(
        [half_of(piece[:, 0]) for piece in (gate_one, shift_two, scale_two, gate_two)]
    )
    d_mixed, d_shaped_one, d_mod_mid, loss_parts, grad_up, grad_rest = mid_block(
        heads_wide,
        w_attn[3],
        hidden_half,
        mod_mid,
        jnp.pad(half_of(noise_patches), padding),
        jnp.broadcast_to(half_of(token_weight)[:, None], (half, 128)),
        jnp.pad(w_head, ((0, 128 - P_SIZE), (0, 0))),
        grad_scale.reshape(1),
        w_mlp[0],
        w_mlp[1],
        TP_AXIS,
        0,
    )
    loss_own = jnp.sum(loss_parts)
    sum_up = lax.psum_scatter(grad_up, "frames", scatter_dimension=0, tiled=True)
    sum_rest = lax.psum_scatter(grad_rest, "frames", scatter_dimension=0, tiled=True)
    d_queries, keys_grad_wide, values_grad_wide = attn_bwd(
        queries, keys_wide, values_wide, d_mixed, heads_wide, log_totals, clip_start
    )
    d_queries, sum_up = lax.optimization_barrier((d_queries, sum_up))
    grad_qkv, grad_in, d_first_mods = tail_block(
        d_queries,
        normed_one,
        w_attn[:3],
        cosine_table,
        sine_table,
        turn_four,
        hidden_half,
        half_of(scale_one[:, 0]),
        d_shaped_one,
        half_of(inputs_low),
        keys_grad_wide,
        values_grad_wide,
        1,
    )
    d_first_mods, sum_rest = lax.optimization_barrier((d_first_mods, sum_rest))
    grad_in = grad_in[:P_SIZE]
    flip = [(0, 1), (1, 0)]
    first_cols = jnp.concatenate([d_first_mods[0], d_first_mods[1], d_mod_mid[0]], axis=1)
    later_cols = jnp.concatenate([d_mod_mid[1], d_mod_mid[2], d_mod_mid[3]], axis=1)
    kept_cols = jnp.where(mp_index == 0, first_cols, later_cols)
    their_cols = lax.ppermute(jnp.where(mp_index == 0, later_cols, first_cols), "mp", flip)
    d_mod_own = jnp.concatenate(
        [
            jnp.where(mp_index == 0, kept_cols, their_cols),
            jnp.where(mp_index == 0, their_cols, kept_cols),
        ],
        axis=0,
    )
    mod_rows = mod_weight.shape[0]
    small_cols = small_weights.shape[1]
    d_mod_all = lax.all_gather(d_mod_own, "frames", axis=0, tiled=True)
    cond_rows = lax.dynamic_slice_in_dim(conditioning_all, device * mod_rows, mod_rows, 1)
    sum_mod = jnp.einsum("fr,fc->rc", cond_rows, d_mod_all, precision=HIGH)
    d_cond_part = jnp.einsum("fc,rc->fr", d_mod_all, low_mod.astype(jnp.float32), precision=HIGH)
    loss_both = loss_own + lax.ppermute(loss_own, "mp", flip)
    loss_rows = jnp.broadcast_to(loss_both, (8, mod_rows))
    d_cond_rows = jnp.concatenate([d_cond_part + lax.ppermute(d_cond_part, "mp", flip), loss_rows], axis=0)
    d_cond_all = lax.all_gather(d_cond_rows, "frames", axis=1, tiled=True)
    loss_sum = jnp.sum(d_cond_all[frames_total]) / mod_rows
    d_pre_two = jax.vjp(jax.nn.silu, pre_two)[1](d_cond_all[:frames_total])[0]
    first_col = (device * lax.axis_size("mp") + mp_index) * small_cols

    def own(array):
        return lax.dynamic_slice_in_dim(array, first_col, small_cols, 1)

    grad_second = jnp.einsum("fi,fj->ij", first_all, own(d_pre_two), precision=HIGH)
    second_rows = lax.dynamic_slice_in_dim(small_full, FREQ + first_col, small_cols, 0)
    d_first = jnp.einsum("fk,jk->fj", d_pre_two, second_rows, precision=HIGH)
    d_pre_one = jax.vjp(jax.nn.silu, own(pre_one))[1](d_first)[0]
    grad_first = jnp.einsum("fi,fj->ij", features_all, d_pre_one, precision=HIGH)
    joined = jnp.concatenate(
        [
            part.astype(jnp.bfloat16)
            for part in (grad_qkv[0], grad_qkv[1], grad_qkv[2], grad_in.T)
        ],
        axis=1,
    )
    joined_sum = lax.psum_scatter(joined, "frames", scatter_dimension=0, tiled=True).astype(
        jnp.float32
    )
    ff_cols = mlp_weights.shape[2]
    sum_rest = sum_rest.astype(jnp.float32)
    sum_mlp = jnp.stack([sum_up.astype(jnp.float32), sum_rest[:, :ff_cols]])
    sum_attn = jnp.stack(
        [joined_sum[:, k * width_local : (k + 1) * width_local] for k in range(3)]
        + [sum_rest[:, ff_cols : ff_cols + width_local]]
    )
    head_first = ff_cols + width_local
    ends = jnp.concatenate(
        [joined_sum[:, 3 * width_local :], sum_rest[:, head_first : head_first + P_SIZE]], axis=1
    ).T
    sum_ends = half_of(ends, 1) + lax.ppermute(
        lax.dynamic_slice_in_dim(ends, (1 - mp_index) * small_cols, small_cols, 1), "mp", flip
    )
    sum_small = jnp.concatenate([grad_first, grad_second, sum_ends], axis=0)
    learning_rate = 0.5 * math.sqrt(tokens_total * P_SIZE / D)
    attn_new, attn_moment_new, attn_average_new, attn_copy = update(
        attn_weights, sum_attn, attn_moment, attn_average, learning_rate
    )
    mlp_new, mlp_moment_new, mlp_average_new, mlp_copy = update(
        mlp_weights, sum_mlp, mlp_moment, mlp_average, learning_rate
    )
    mod_new, mod_moment_new, mod_average_new, mod_copy = update(
        mod_weight, sum_mod, mod_moment, mod_average, learning_rate
    )
    small_new, small_moment_new, small_average_new, small_copy = update(
        small_weights, sum_small, small_moment, small_average, learning_rate
    )
    return (
        loss_sum,
        noised_count,
        attn_new,
        attn_moment_new,
        attn_average_new,
        attn_copy,
        mlp_new,
        mlp_moment_new,
        mlp_average_new,
        mlp_copy,
        mod_new,
        mod_moment_new,
        mod_average_new,
        mod_copy,
        small_new,
        small_moment_new,
        small_average_new,
        small_copy,
    )


def solution(mesh):
    return jax.shard_map(
        per_device,
        mesh=mesh,
        in_specs=(
            P("frames", None),
            P("frames", None),
            P("frames"),
            P(),
            P(),
            P(None, "frames", "mp"),
            P(None, "frames", "mp"),
            P("frames", "mp"),
            P(None, ("frames", "mp")),
            P(None, "frames", "mp"),
            P(None, "frames", "mp"),
            P("frames", "mp"),
            P(None, ("frames", "mp")),
            P(None, "frames", "mp"),
            P(None, "frames", "mp"),
            P("frames", "mp"),
            P(None, ("frames", "mp")),
        ),
        out_specs=(
            P(),
            P(),
            P(None, "frames", "mp"),
            P(None, "frames", "mp"),
            P(None, "frames", "mp"),
            P(None, "frames", "mp"),
            P(None, "frames", "mp"),
            P(None, "frames", "mp"),
            P(None, "frames", "mp"),
            P(None, "frames", "mp"),
            P("frames", "mp"),
            P("frames", "mp"),
            P("frames", "mp"),
            P("frames", "mp"),
            P(None, ("frames", "mp")),
            P(None, ("frames", "mp")),
            P(None, ("frames", "mp")),
            P(None, ("frames", "mp")),
        ),
        check_vma=False,
    )
```

```python
import functools
import math

import jax
import jax.numpy as jnp
import numpy as np
from jax import lax
from jax.experimental import pallas as pl
from jax.experimental.pallas import tpu as pltpu
from jax.sharding import PartitionSpec as P

D = 1024
HD = 64
CH = 4
FREQ = 256
GRID = 16
P_SIZE = 16
TPF = 64
REACH = 4


HIGH = lax.Precision.HIGHEST
EPSILON = 1e-06
MOMENTUM = 0.5
EMA_DECAY = 0.5
TP_AXIS = "mp"


def rotation_matrix(head_width):
    groups = [head_width // 4, 3 * head_width // 8, 3 * head_width // 8]
    rotation = np.zeros((head_width, head_width), np.float32)
    offset = 0
    for group_size in groups:
        half_size = group_size // 2
        for pair_index in range(half_size):
            rotation[offset + half_size + pair_index, offset + pair_index] = -1.0
            rotation[offset + pair_index, offset + half_size + pair_index] = 1.0
        offset += group_size
    return rotation


def rotary_angles(frame_pos, row_pos, col_pos, head_width):
    pieces = []
    for position, group_size in (
        (frame_pos, head_width // 4),
        (row_pos, 3 * head_width // 8),
        (col_pos, 3 * head_width // 8),
    ):
        half_size = group_size // 2
        frequency = 10000.0 ** (-jnp.arange(half_size, dtype=jnp.float32) / half_size)
        phases = position[:, None] * frequency[None, :]
        pieces += [phases, phases]
    return jnp.concatenate(pieces, axis=1)


def clip_positions(clip_ids):
    frame_index = jnp.arange(clip_ids.shape[0], dtype=jnp.int32)
    starts_here = jnp.concatenate([jnp.ones((1,), bool), clip_ids[1:] != clip_ids[:-1]])
    clip_start = lax.cummax(jnp.where(starts_here, frame_index, 0), axis=0)
    return frame_index - clip_start


def patchify(frame_data):
    frame_total = frame_data.shape[0]
    patch_side = GRID // 2
    shaped = frame_data.reshape(frame_total, CH, patch_side, 2, patch_side, 2)
    return shaped.transpose(0, 2, 4, 1, 3, 5).reshape(frame_total * patch_side * patch_side, CH * 4)


def layer_norm(vector):
    row_mean = jnp.mean(vector, axis=-1, keepdims=True)
    centred = vector - row_mean
    variance = jnp.mean(centred * centred, axis=-1, keepdims=True)
    return centred * lax.rsqrt(variance + EPSILON)


def modulate_local(shaped, shift_rows, scale_rows):
    return layer_norm(shaped) * (1.0 + scale_rows) + shift_rows


def time_features(level_eff):
    half_size = FREQ // 2
    frequency = jnp.exp(-math.log(10000.0) * jnp.arange(half_size, dtype=jnp.float32) / half_size)
    phases = (level_eff * 1000.0)[:, None] * frequency[None, :]
    return jnp.concatenate([jnp.cos(phases), jnp.sin(phases)], axis=1)


NT=(((1,),(1,)),((),()))
NN=(((1,),(0,)),((),()))

def dotf(a,b,dims=NN):
    return lax.dot_general(a,b,dims,preferred_element_type=jnp.float32)

def split_pair(xT):
    r=lax.broadcasted_iota(jnp.int32,xT.shape,0)
    z=jnp.zeros_like(xT)
    return jnp.where(r<HD,xT,z), jnp.where(r<HD,z,xT)

def keep_of(t,TK,TQ,cs,qf):
    kf=lax.broadcasted_iota(jnp.int32,(TK,TQ),0)//TPF+t*(TK//TPF)
    return (kf>=cs)&(kf<=qf)

def fwd_kernel(lo_ref,mid_ref,hi_ref,q_ref,k_ref,v_ref,cs_ref,o_ref,lse_ref,vT,*,TQ,TK,W0,NQ):
    KS=k_ref.shape[0]
    def tr(i,_):
        s=pl.multiple_of(i*TK,TK)
        vT[:,pl.ds(s,TK)]=v_ref[pl.ds(s,TK),:].T
        return 0
    lax.fori_loop(lo_ref[0],KS//TK,tr,0)
    def qtile(j,_):
        qs=pl.multiple_of(j*TQ,TQ)
        qT=(q_ref[pl.ds(qs,TQ),:].T)*jnp.bfloat16(0.125)
        qA,qB=split_pair(qT)
        cs=cs_ref[0:1,pl.ds(qs,TQ)]
        qf=lax.broadcasted_iota(jnp.int32,(1,TQ),1)//TPF+(W0+j*(TQ//TPF))
        def step(t,carry,masked):
            ks=pl.multiple_of(t*TK,TK)
            kt=k_ref[pl.ds(ks,TK),:]
            out=[]
            if masked: keep=keep_of(t,TK,TQ,cs,qf)
            for h,(qh,(m,l,o)) in enumerate(zip((qA,qB),carry)):
                s=dotf(kt,qh)
                if masked: s=jnp.where(keep,s,-1e30)
                mn=jnp.maximum(m,jnp.max(s,axis=0,keepdims=True))
                a=jnp.exp(m-mn)
                p=jnp.exp(s-mn)
                l=l*a+jnp.sum(p,axis=0,keepdims=True)
                o=o*a+dotf(vT[h*HD:(h+1)*HD,pl.ds(ks,TK)],p.astype(jnp.bfloat16))
                out.append((mn,l,o))
            return tuple(out)
        init=tuple((jnp.full((1,TQ),-1e29,jnp.float32),jnp.zeros((1,TQ),jnp.float32),jnp.zeros((HD,TQ),jnp.float32)) for _ in range(2))
        c=lax.fori_loop(lo_ref[j],mid_ref[j],lambda t,c:step(t,c,True),init)
        c=lax.fori_loop(mid_ref[j],hi_ref[j],lambda t,c:step(t,c,False),c)
        c=lax.fori_loop(hi_ref[j],(W0*TPF+(j+1)*TQ+TK-1)//TK,lambda t,c:step(t,c,True),c)
        oT=jnp.concatenate([c[0][2]/c[0][1],c[1][2]/c[1][1]],axis=0)
        o_ref[pl.ds(qs,TQ),:]=oT.T.astype(o_ref.dtype)
        lse_ref[0,0:1,pl.ds(qs,TQ)]=c[0][0]+jnp.log(c[0][1])
        lse_ref[0,1:2,pl.ds(qs,TQ)]=c[1][0]+jnp.log(c[1][1])
        return 0
    lax.fori_loop(0,NQ,qtile,0)

def tile_bounds(cs_rel,TQ,TK,W0,NQ):
    fq=TQ//TPF; fk=TK//TPF
    j=jnp.arange(NQ)
    first=cs_rel[::fq]; last=cs_rel[fq-1::fq]
    lo=first//fk
    dg=(W0+j*fq+1)//fk
    mid=jnp.minimum((last+fk-1)//fk,dg)
    mid=jnp.maximum(mid,lo)
    hi=jnp.maximum(dg,mid)
    return lo.astype(jnp.int32),mid.astype(jnp.int32),hi.astype(jnp.int32)

def attn_fwd(q,k,v,cs_rel,TQ=512,TK=512):
    T,Wd=q.shape; KS=k.shape[0]; P=Wd//128
    W0=(KS-T)//TPF; NQ=T//TQ
    lo,mid,hi=tile_bounds(cs_rel,TQ,TK,W0,NQ)
    cs_tok=jnp.broadcast_to(jnp.repeat(cs_rel,TPF)[None,:],(8,T)).astype(jnp.int32)
    return pl.pallas_call(
        functools.partial(fwd_kernel,TQ=TQ,TK=TK,W0=W0,NQ=NQ),
        grid_spec=pltpu.PrefetchScalarGridSpec(num_scalar_prefetch=3,grid=(P,),
            in_specs=[pl.BlockSpec((T,128),lambda p,*_:(0,p)),pl.BlockSpec((KS,128),lambda p,*_:(0,p)),pl.BlockSpec((KS,128),lambda p,*_:(0,p)),pl.BlockSpec((8,T),lambda p,*_:(0,0))],
            out_specs=[pl.BlockSpec((T,128),lambda p,*_:(0,p)),pl.BlockSpec((1,8,T),lambda p,*_:(p,0,0))],
            scratch_shapes=[pltpu.VMEM((128,KS),jnp.bfloat16)]),
        out_shape=[jax.ShapeDtypeStruct((T,Wd),jnp.float32),jax.ShapeDtypeStruct((P,8,T),jnp.float32)],
        compiler_params=pltpu.CompilerParams(vmem_limit_bytes=48<<20),
        cost_estimate=pl.CostEstimate(flops=10**11,bytes_accessed=2*10**7,transcendentals=3*10**7),
        name="attn_forward",
    )(lo,mid,hi,q,k,v,cs_tok)

def bwd_kernel(lo_ref,mid_ref,hi_ref,q_ref,k_ref,v_ref,do_ref,o_ref,lse_ref,cs_ref,dq_ref,dk_ref,dv_ref,kT,dkT,dvT,*,TQ,TK,W0,NQ):
    KS=k_ref.shape[0]
    def tr(i,_):
        s=pl.multiple_of(i*TK,TK)
        kT[:,pl.ds(s,TK)]=k_ref[pl.ds(s,TK),:].T
        return 0
    lax.fori_loop(lo_ref[0],KS//TK,tr,0)
    dkT[...]=jnp.zeros_like(dkT); dvT[...]=jnp.zeros_like(dvT)
    def qtile(j,_):
        qs=pl.multiple_of(j*TQ,TQ)
        qT=(q_ref[pl.ds(qs,TQ),:].T)*jnp.bfloat16(0.125)
        qh=split_pair(qT)
        doT=do_ref[pl.ds(qs,TQ),:].T
        doh=split_pair(doT)
        oT=o_ref[pl.ds(qs,TQ),:].T
        prod=oT*doT.astype(jnp.float32)
        delta=(jnp.sum(prod[:HD],axis=0,keepdims=True),jnp.sum(prod[HD:],axis=0,keepdims=True))
        lse=(lse_ref[0,0:1,pl.ds(qs,TQ)],lse_ref[0,1:2,pl.ds(qs,TQ)])
        cs=cs_ref[0:1,pl.ds(qs,TQ)]
        qf=lax.broadcasted_iota(jnp.int32,(1,TQ),1)//TPF+(W0+j*(TQ//TPF))
        def step(t,carry,masked):
            ks=pl.multiple_of(t*TK,TK)
            kt=k_ref[pl.ds(ks,TK),:]; vt=v_ref[pl.ds(ks,TK),:]
            out=[]
            if masked: keep=keep_of(t,TK,TQ,cs,qf)
            for h in range(2):
                r=slice(h*HD,(h+1)*HD)
                s=dotf(kt,qh[h])
                p=jnp.exp(s-lse[h])
                if masked: p=jnp.where(keep,p,0.0)
                dp=dotf(vt,doh[h])
                ds=(p*(dp-delta[h])).astype(jnp.bfloat16)
                pb=p.astype(jnp.bfloat16)
                dvT[r,pl.ds(ks,TK)]+=dotf(doT[r],pb,NT)
                dkT[r,pl.ds(ks,TK)]+=dotf(qT[r],ds,NT)
                out.append(carry[h]+dotf(kT[r,pl.ds(ks,TK)],ds))
            return tuple(out)
        init=(jnp.zeros((HD,TQ),jnp.float32),)*2
        c=lax.fori_loop(lo_ref[j],mid_ref[j],lambda t,c:step(t,c,True),init)
        c=lax.fori_loop(mid_ref[j],hi_ref[j],lambda t,c:step(t,c,False),c)
        c=lax.fori_loop(hi_ref[j],(W0*TPF+(j+1)*TQ+TK-1)//TK,lambda t,c:step(t,c,True),c)
        dq_ref[pl.ds(qs,TQ),:]=(jnp.concatenate(c,axis=0)*0.125).T
        return 0
    lax.fori_loop(0,NQ,qtile,0)
    def back(i,_):
        s=pl.multiple_of(i*TK,TK)
        dk_ref[pl.ds(s,TK),:]=dkT[:,pl.ds(s,TK)].T.astype(dk_ref.dtype)
        dv_ref[pl.ds(s,TK),:]=dvT[:,pl.ds(s,TK)].T.astype(dv_ref.dtype)
        return 0
    lax.fori_loop(0,KS//TK,back,0)

def attn_bwd(q,k,v,do,o,lse,cs_rel,TQ=512,TK=512,out_dt=jnp.bfloat16):
    T,Wd=q.shape; KS=k.shape[0]; P=Wd//128
    W0=(KS-T)//TPF; NQ=T//TQ
    lo,mid,hi=tile_bounds(cs_rel,TQ,TK,W0,NQ)
    cs_tok=jnp.broadcast_to(jnp.repeat(cs_rel,TPF)[None,:],(8,T)).astype(jnp.int32)
    tb=pl.BlockSpec((T,128),lambda p,*_:(0,p)); kb=pl.BlockSpec((KS,128),lambda p,*_:(0,p))
    return pl.pallas_call(
        functools.partial(bwd_kernel,TQ=TQ,TK=TK,W0=W0,NQ=NQ),
        grid_spec=pltpu.PrefetchScalarGridSpec(num_scalar_prefetch=3,grid=(P,),
            in_specs=[tb,kb,kb,tb,tb,pl.BlockSpec((1,8,T),lambda p,*_:(p,0,0)),pl.BlockSpec((8,T),lambda p,*_:(0,0))],
            out_specs=[tb,kb,kb],
            scratch_shapes=[pltpu.VMEM((128,KS),jnp.bfloat16),pltpu.VMEM((128,KS),jnp.float32),pltpu.VMEM((128,KS),jnp.float32)]),
        out_shape=[jax.ShapeDtypeStruct((T,Wd),jnp.float32),jax.ShapeDtypeStruct((KS,Wd),out_dt),jax.ShapeDtypeStruct((KS,Wd),out_dt)],
        compiler_params=pltpu.CompilerParams(vmem_limit_bytes=56<<20),
        cost_estimate=pl.CostEstimate(flops=2*10**11,bytes_accessed=5*10**7,transcendentals=3*10**7),
        name="attn_backward",
    )(lo,mid,hi,q,k,v,do,o,lse,cs_tok)


def update(weight, gradient, moment, average, learning_rate):
    moment_new = MOMENTUM * moment + gradient
    weight_new = weight - learning_rate * (gradient + MOMENTUM * moment_new)
    average_new = EMA_DECAY * average + (1.0 - EMA_DECAY) * weight_new
    return (weight_new, moment_new, average_new, weight_new.astype(jnp.bfloat16))


TN = (((0,), (0,)), ((), ()))


def norm_rows(v):
    centred = v - jnp.mean(v, axis=-1, keepdims=True)
    inverse = lax.rsqrt(jnp.mean(centred * centred, axis=-1, keepdims=True) + EPSILON)
    return centred * inverse, inverse


def norm_rows_back(grad, normed, inverse):
    return inverse * (
        grad
        - jnp.mean(grad, axis=-1, keepdims=True)
        - normed * jnp.mean(grad * normed, axis=-1, keepdims=True)
    )


def gelu_pair(x):
    c = math.sqrt(2.0 / math.pi)
    sq = x * x
    t = jnp.tanh(c * (x + 0.044715 * (x * sq)))
    half = 0.5 * (1.0 + t)
    return x * half, half + (0.5 * c) * x * (1.0 - t * t) * (1.0 + 0.134145 * sq)


def mid_kernel(
    o_ref, wo_ref, hid_ref, mod_ref, noise_ref, tw_ref, head_ref, gs_ref, wu_hbm, wd_hbm,
    dmix_ref, dx1_ref, dmod_ref, loss_ref, up_hbm, rest_hbm,
    wu_ref, wd_ref, att, x1, out, dx2, n2, n2t, act, dgl, dout, doutt, datt, datt_t,
    send_a, recv_a, send_c, recv_c, send_e, recv_e, stage, ghead_ref, go_ref, gh_t,
    wsem, gsem, ssem, rsem, *, tp,
):
    f = lax.axis_index("frames")
    h = lax.axis_index("mp")
    bf16 = jnp.bfloat16
    x_peer = {"mp": 1 - h}
    tp_peer = {"frames": f + 1 - 2 * lax.rem(f, 2)} if tp == "core" else x_peer
    half = hid_ref.shape[0]
    rows = 128
    chunks = half // rows
    width = hid_ref.shape[1]
    ff = wu_hbm.shape[1]
    e = o_ref.shape[1]
    ft = 512
    dt = 256

    weights = [
        pltpu.make_async_copy(wu_hbm, wu_ref, wsem.at[0]),
        pltpu.make_async_copy(wd_hbm, wd_ref, wsem.at[1]),
    ]
    for w in weights:
        w.start()

    barrier = pltpu.get_barrier_semaphore()
    pl.semaphore_signal(barrier, inc=1, device_id=x_peer, device_id_type=pl.DeviceIdType.MESH)
    if tp == "core":
        pl.semaphore_signal(barrier, inc=1, device_id=tp_peer, device_id_type=pl.DeviceIdType.MESH)
    pl.semaphore_wait(barrier, 2 if tp == "core" else 1)

    def at(start, size):
        return pl.ds(pl.multiple_of(start, size), size)

    def copy(src, dst, phase, c, peer):
        return pltpu.make_async_remote_copy(
            src_ref=src, dst_ref=dst, send_sem=ssem.at[phase, c], recv_sem=rsem.at[phase, c],
            device_id=peer, device_id_type=pl.DeviceIdType.MESH,
        )

    def copy_a(c):
        return copy(send_a.at[at(c * rows, rows)], recv_a.at[at(c * rows, rows)], 0, c, x_peer)

    def copy_b(c):
        return copy(
            n2.at[at(c * 2 * rows, rows)], n2.at[at(c * 2 * rows + rows, rows)], 1, c, tp_peer
        )

    def copy_c(c):
        return copy(send_c.at[at(c * rows, rows)], recv_c.at[at(c * rows, rows)], 2, c, tp_peer)

    def copy_d(c):
        return copy(
            dout.at[at(c * 2 * rows, rows)], dout.at[at(c * 2 * rows + rows, rows)], 3, c, tp_peer
        )

    def copy_e(c):
        return copy(send_e.at[at(c * rows, rows)], recv_e.at[at(c * rows, rows)], 4, c, tp_peer)

    def copy_f(c):
        mine = datt.at[at(h * half + c * rows, rows)]
        return copy(mine, mine, 5, c, x_peer)

    def phase_a(c, _):
        part = o_ref[at((1 - h) * half + c * rows, rows), :].astype(bf16)
        send_a[at(c * rows, rows), :] = dotf(part, wo_ref[...], NT).astype(bf16)
        copy_a(c).start()
        return 0

    lax.fori_loop(0, chunks, phase_a, 0)

    def phase_b(c, _):
        part = o_ref[at(h * half + c * rows, rows), :].astype(bf16)
        att[at(c * rows, rows), :] = dotf(part, wo_ref[...], NT)
        copy_a(c).wait_recv()
        for k in range(rows // TPF):
            r = at(c * rows + k * TPF, TPF)
            frame = pl.ds(c * (rows // TPF) + k, 1)
            a = att[r, :] + recv_a[r, :].astype(jnp.float32)
            att[r, :] = a
            v = hid_ref[r, :] + mod_ref[0, frame, :] * a
            x1[r, :] = v
            y, _inv = norm_rows(v)
            n2[at(c * 2 * rows + k * TPF, TPF), :] = (
                y * (1.0 + mod_ref[2, frame, :]) + mod_ref[1, frame, :]
            ).astype(bf16)
        copy_b(c).start()
        return 0

    lax.fori_loop(0, chunks, phase_b, 0)
    for w in weights:
        w.wait()

    def phase_c(c, _):
        copy_b(c).wait_recv()
        tok = at(c * 2 * rows, 2 * rows)
        n2t[:, tok] = n2[tok, :].T

        def up(i, _):
            cols = at(i * ft, ft)
            a, g = gelu_pair(dotf(n2[tok, :], wu_ref[:, cols]))
            act[tok, cols] = a.astype(bf16)
            dgl[tok, cols] = g.astype(bf16)
            return 0

        lax.fori_loop(0, ff // ft, up, 0)

        def down(i, _):
            cols = at(i * dt, dt)
            res = dotf(act[tok, :], wd_ref[cols, :], NT)
            out[at(c * rows, rows), cols] = res[:rows]
            send_c[at(c * rows, rows), cols] = res[rows:].astype(bf16)
            return 0

        lax.fori_loop(0, width // dt, down, 0)
        copy_c(c).start()
        return 0

    lax.fori_loop(0, chunks, phase_c, 0)

    ghead_ref[...] = jnp.zeros_like(ghead_ref)
    loss_ref[...] = jnp.zeros_like(loss_ref)

    def phase_d(c, _):
        copy_c(c).wait_recv()
        for k in range(rows // TPF):
            r = at(c * rows + k * TPF, TPF)
            frame = pl.ds(c * (rows // TPF) + k, 1)
            o = out[r, :] + recv_c[r, :].astype(jnp.float32)
            gate = mod_ref[3, frame, :]
            y, inv = norm_rows(x1[r, :] + gate * o)
            fn = y.astype(bf16)
            misfit = dotf(fn, head_ref[...], NT) - noise_ref[r, :]
            weighted = tw_ref[r, :] * misfit
            loss_ref[...] += weighted * misfit
            d_pred = (2.0 * gs_ref[0] * weighted).astype(bf16)
            ghead_ref[...] += dotf(d_pred, fn, TN)
            d_x2 = norm_rows_back(dotf(d_pred, head_ref[...]), y, inv)
            dx2[r, :] = d_x2
            dmod_ref[3, frame, :] = jnp.sum(d_x2 * o, axis=0, keepdims=True)
            dout[at(c * 2 * rows + k * TPF, TPF), :] = (gate * d_x2).astype(bf16)
        copy_d(c).start()
        return 0

    lax.fori_loop(0, chunks, phase_d, 0)

    def phase_e(c, _):
        copy_d(c).wait_recv()
        tok = at(c * 2 * rows, 2 * rows)
        doutt[:, tok] = dout[tok, :].T

        def down(i, _):
            cols = at(i * ft, ft)
            g = dotf(dout[tok, :], wd_ref[:, cols]) * dgl[tok, cols].astype(jnp.float32)
            dgl[tok, cols] = g.astype(bf16)
            return 0

        lax.fori_loop(0, ff // ft, down, 0)

        def up(i, _):
            cols = at(i * dt, dt)
            res = dotf(dgl[tok, :], wu_ref[cols, :], NT)
            out[at(c * rows, rows), cols] = res[:rows]
            send_e[at(c * rows, rows), cols] = res[rows:].astype(bf16)
            return 0

        lax.fori_loop(0, width // dt, up, 0)
        copy_e(c).start()
        return 0

    lax.fori_loop(0, chunks, phase_e, 0)

    def phase_f(c, _):
        copy_e(c).wait_recv()
        for k in range(rows // TPF):
            r = at(c * rows + k * TPF, TPF)
            frame = pl.ds(c * (rows // TPF) + k, 1)
            g = out[r, :] + recv_e[r, :].astype(jnp.float32)
            y, inv = norm_rows(x1[r, :])
            dmod_ref[1, frame, :] = jnp.sum(g, axis=0, keepdims=True)
            dmod_ref[2, frame, :] = jnp.sum(g * y, axis=0, keepdims=True)
            d_x1 = dx2[r, :] + norm_rows_back(g * (1.0 + mod_ref[2, frame, :]), y, inv)
            dx1_ref[r, :] = d_x1
            dmod_ref[0, frame, :] = jnp.sum(d_x1 * att[r, :], axis=0, keepdims=True)
            datt[at(h * half + c * rows + k * TPF, TPF), :] = (mod_ref[0, frame, :] * d_x1).astype(
                bf16
            )
        copy_f(c).start()
        return 0

    lax.fori_loop(0, chunks, phase_f, 0)

    def weight_grads(left, right, target):
        def put(slot, i):
            return pltpu.make_async_copy(
                stage.at[slot], target.at[at(i * dt, dt), pl.ds(0, ff)], gsem.at[slot]
            )

        def tile(i, _):
            slot = lax.rem(i, 2)

            @pl.when(i >= 2)
            def _():
                put(slot, i - 2).wait()

            def cols_of(j, _):
                cols = at(j * ft, ft)
                stage[slot, :, cols] = dotf(left[at(i * dt, dt), :], right[:, cols]).astype(bf16)
                return 0

            lax.fori_loop(0, ff // ft, cols_of, 0)
            put(slot, i).start()
            return 0

        lax.fori_loop(0, width // dt, tile, 0)
        for i in (width // dt - 2, width // dt - 1):
            put(i % 2, i).wait()

    weight_grads(n2t, dgl, up_hbm)
    weight_grads(doutt, act, rest_hbm)

    def own_mix(c, _):
        tok = at(h * half + c * rows, rows)
        datt_t[:, tok] = datt[tok, :].T
        dmix_ref[tok, :] = dotf(datt[tok, :], wo_ref[...]).astype(bf16)
        return 0

    lax.fori_loop(0, chunks, own_mix, 0)

    def phase_g(c, _):
        tok = at((1 - h) * half + c * rows, rows)
        theirs = datt.at[tok]
        copy(theirs, theirs, 5, c, x_peer).wait_recv()
        datt_t[:, tok] = datt[tok, :].T
        dmix_ref[tok, :] = dotf(datt[tok, :], wo_ref[...]).astype(bf16)
        return 0

    lax.fori_loop(0, chunks, phase_g, 0)

    def grad_out(i, _):
        d = at(i * dt, dt)
        go_ref[d, :] = dotf(datt_t[d, :], o_ref[...].astype(bf16)).astype(bf16)
        return 0

    lax.fori_loop(0, width // dt, grad_out, 0)
    gh_t[...] = ghead_ref[...].T.astype(bf16)
    ends = [
        pltpu.make_async_copy(go_ref, rest_hbm.at[:, pl.ds(ff, e)], gsem.at[2]),
        pltpu.make_async_copy(gh_t, rest_hbm.at[:, pl.ds(ff + e, 128)], gsem.at[3]),
    ]
    for one in ends:
        one.start()
    for one in ends:
        one.wait()
    def sent(c, _):
        for one in (copy_a, copy_b, copy_c, copy_d, copy_e, copy_f):
            one(c).wait_send()
        return 0

    lax.fori_loop(0, chunks, sent, 0)


def mid_block(o, wo, hid, mod, noise, tw, head, gs, wu, wd, tp, cid):
    tok, e = o.shape
    half, width = hid.shape
    ff = wu.shape[1]
    own_frames = half // TPF
    f32, bf16 = jnp.float32, jnp.bfloat16
    vm = pl.BlockSpec(memory_space=pltpu.VMEM)
    anym = pl.BlockSpec(memory_space=pl.ANY)
    V = pltpu.VMEM
    return pl.pallas_call(
        functools.partial(mid_kernel, tp=tp),
        in_specs=[vm] * 7 + [pl.BlockSpec(memory_space=pltpu.SMEM), anym, anym],
        out_specs=[vm] * 4 + [anym] * 2,
        out_shape=[
            jax.ShapeDtypeStruct((tok, e), bf16),
            jax.ShapeDtypeStruct((half, width), f32),
            jax.ShapeDtypeStruct((4, own_frames, width), f32),
            jax.ShapeDtypeStruct((TPF, 128), f32),
            jax.ShapeDtypeStruct((width, ff), bf16),
            jax.ShapeDtypeStruct((width, ff + e + 128), bf16),
        ],
        scratch_shapes=[
            V((width, ff), bf16), V((width, ff), bf16),
            V((half, width), f32), V((half, width), f32), V((half, width), f32),
            V((half, width), f32),
            V((2 * half, width), bf16), V((width, 2 * half), bf16),
            V((2 * half, ff), bf16), V((2 * half, ff), bf16),
            V((2 * half, width), bf16), V((width, 2 * half), bf16),
            V((tok, width), bf16), V((width, tok), bf16),
            V((half, width), bf16), V((half, width), bf16),
            V((half, width), bf16), V((half, width), bf16),
            V((half, width), bf16), V((half, width), bf16),
            V((2, 256, ff), bf16), V((128, width), f32), V((width, e), bf16),
            V((width, 128), bf16),
            pltpu.SemaphoreType.DMA((2,)), pltpu.SemaphoreType.DMA((4,)),
            pltpu.SemaphoreType.DMA((6, half // 128)), pltpu.SemaphoreType.DMA((6, half // 128)),
        ],
        compiler_params=pltpu.CompilerParams(
            vmem_limit_bytes=62 << 20, collective_id=cid, has_side_effects=True
        ),
        cost_estimate=pl.CostEstimate(
            flops=4 * 10**10, bytes_accessed=3 * 10**7, transcendentals=2 * 10**6
        ),
        name="feed_forward",
    )(o, wo, hid, mod, noise, tw, head, gs, wu, wd)


def split_three(v):
    high = v.astype(jnp.bfloat16)
    left = v - high.astype(jnp.float32)
    middle = left.astype(jnp.bfloat16)
    return high, middle, (left - middle.astype(jnp.float32)).astype(jnp.bfloat16)


def turn_back(g, cosine, sine, rot):
    parts = split_three(g * sine)
    return (g * cosine + sum(dotf(p, rot, NT) for p in parts)).astype(jnp.bfloat16)


def tail_kernel(
    dq_ref, n1_ref, w_ref, cos_ref, sin_ref, rot_ref, hid_ref, scale_ref, dx1_ref, inp_ref,
    dk_hbm, dv_hbm,
    gq_ref, gin_ref, dss_ref,
    own, near, yrecv, zrecv, n1t, dproj, send_x, recv_x, part,
    lsem, s_near, r_near, s_y, r_y, s_z, r_z, s_x, r_x,
):
    f = lax.axis_index("frames")
    h = lax.axis_index("mp")
    n = lax.axis_size("frames")
    core = lax.rem(f, 2)
    odd = lax.rem(lax.div(f, 2), 2)
    core_peer = {"frames": f + 1 - 2 * core}
    y_peer = {"frames": f + 2 - 4 * odd}
    before = {"frames": lax.rem(f - 4 + n, n)}
    after = {"frames": lax.rem(f + 4, n)}
    x_peer = {"mp": 1 - h}
    tok, e = dq_ref.shape
    width = n1_ref.shape[1]
    half = tok // 2
    rows = 256
    chunks = tok // rows
    f32, bf16 = jnp.float32, jnp.bfloat16
    MESH = pl.DeviceIdType.MESH
    sides = (dk_hbm, dv_hbm)
    share = width // n

    def at(start, size):
        return pl.ds(pl.multiple_of(start, size), size)

    loads = [
        pltpu.make_async_copy(
            sides[s].at[pl.ds(b * tok, tok)], own.at[s, j], lsem.at[s, j]
        )
        for s in range(2)
        for j, b in enumerate((4, 2, 0))
    ]
    for one in loads:
        one.start()

    barrier = pltpu.get_barrier_semaphore()
    for peer in (core_peer, y_peer, x_peer):
        pl.semaphore_signal(barrier, inc=1, device_id=peer, device_id_type=MESH)

    @pl.when(f >= 4)
    def _():
        pl.semaphore_signal(barrier, inc=1, device_id=before, device_id_type=MESH)

    @pl.when(f + 4 < n)
    def _():
        pl.semaphore_signal(barrier, inc=1, device_id=after, device_id_type=MESH)

    pl.semaphore_wait(barrier, 3 + jnp.where(f >= 4, 1, 0) + jnp.where(f + 4 < n, 1, 0))

    def rows_of(i):
        return lax.rem(i + (chunks // 2) * (1 - h), chunks) * rows

    def remote(src, dst, send, recv, peer):
        return pltpu.make_async_remote_copy(
            src_ref=src, dst_ref=dst, send_sem=send, recv_sem=recv, device_id=peer,
            device_id_type=MESH,
        )

    def near_copy(i, s, j):
        b = (3, 1)[j]
        return remote(
            sides[s].at[at(b * tok + rows_of(i), rows)],
            near.at[s, j, at(rows_of(i), rows)],
            s_near.at[s, j, i], r_near.at[s, j, i], core_peer,
        )

    def y_copy(i, s):
        r = at(rows_of(i), rows)
        return remote(own.at[s, 1, r], yrecv.at[s, r], s_y.at[s, i], r_y.at[s, i], y_peer)

    def z_copy(i, s):
        r = at(rows_of(i), rows)
        return remote(own.at[s, 2, r], zrecv.at[s, r], s_z.at[s, i], r_z.at[s, i], before)

    def x_copy(i):
        r = at(i * rows, rows)
        return remote(send_x.at[r], recv_x.at[r], s_x.at[i], r_x.at[i], x_peer)

    def start_near(i, _):
        for s in range(2):
            for j in range(2):
                near_copy(i, s, j).start()
        return 0

    lax.fori_loop(0, chunks, start_near, 0)

    @pl.when(f + 4 >= n)
    def _():
        zrecv[...] = jnp.zeros_like(zrecv)

    for one in loads:
        one.wait()
    low_core = core == 0

    def combine(i, _):
        r = at(rows_of(i), rows)
        for s in range(2):
            for j in range(2):
                near_copy(i, s, j).wait_recv()
            n3 = near[s, 0, r, :].astype(f32)
            n1_ = near[s, 1, r, :].astype(f32)
            own[s, 1, r, :] = (
                own[s, 1, r, :].astype(f32) + jnp.where(low_core, n1_, n3)
            ).astype(bf16)
            y_copy(i, s).start()
            own[s, 2, r, :] = (
                own[s, 2, r, :].astype(f32) + jnp.where(low_core, 0.0, n1_)
            ).astype(bf16)

            @pl.when((odd == 0) & (f >= 4))
            def _():
                z_copy(i, s).start()

        return 0

    lax.fori_loop(0, chunks, combine, 0)

    def turned(g, r, k):
        for b in range(e // 256):
            cols = slice(b * 256, (b + 1) * 256)
            dproj[k, r, cols] = turn_back(
                g[:, cols], cos_ref[r, :], sin_ref[r, :], rot_ref[...]
            )

    def relay(i, _):
        r = at(rows_of(i), rows)
        turned(dq_ref[r, :], r, 0)
        n1t[:, r] = n1_ref[r, :].T

        @pl.when(odd == 1)
        def _():
            for s in range(2):
                y_copy(i, s).wait_recv()

                @pl.when(f >= 4)
                def _():
                    own[s, 2, r, :] = (
                        own[s, 2, r, :].astype(f32) + yrecv[s, r, :].astype(f32)
                    ).astype(bf16)
                    z_copy(i, s).start()

        return 0

    lax.fori_loop(0, chunks, relay, 0)

    def grads(k):
        def tile(i, _):
            res = dotf(n1t[at(i * 256, 256), :], dproj[k]).astype(bf16)
            for q in range(256 // share):
                j = i * (256 // share // 4) + q // 4
                gq_ref[q % 2, (q // 2) % 2, k, at(j * share, share), :] = res[
                    q * share : (q + 1) * share
                ]
            return 0

        lax.fori_loop(0, width // 256, tile, 0)

    grads(0)

    def finish(i, _):
        r = at(rows_of(i), rows)
        for s in range(2):

            @pl.when(odd == 0)
            def _():
                y_copy(i, s).wait_recv()

            @pl.when(f + 4 < n)
            def _():
                z_copy(i, s).wait_recv()

            total = (
                own[s, 0, r, :].astype(f32)
                + jnp.where(low_core, near[s, 0, r, :].astype(f32), 0.0)
                + jnp.where(odd == 0, yrecv[s, r, :].astype(f32), 0.0)
                + zrecv[s, r, :].astype(f32)
            )
            if s == 0:
                turned(total, r, 1)
            else:
                dproj[2, r, :] = total.astype(bf16)

        def cols_of(j, _):
            cols = at(j * 256, 256)
            res = sum(dotf(dproj[k, r, :], w_ref[k, cols, :], NT) for k in range(3))

            @pl.when(i < chunks // 2)
            def _():
                send_x[at(i * rows, rows), cols] = res.astype(bf16)

            @pl.when(i >= chunks // 2)
            def _():
                part[at((i - chunks // 2) * rows, rows), cols] = res

            return 0

        lax.fori_loop(0, width // 256, cols_of, 0)

        @pl.when(i < chunks // 2)
        def _():
            x_copy(i).start()

        return 0

    lax.fori_loop(0, chunks, finish, 0)
    grads(1)
    grads(2)
    gin_ref[...] = jnp.zeros_like(gin_ref)

    def norm_back(i, _):
        x_copy(i).wait_recv()
        for k in range(rows // TPF):
            r = at(i * rows + k * TPF, TPF)
            frame = pl.ds(i * (rows // TPF) + k, 1)
            g = part[r, :] + recv_x[r, :].astype(f32)
            y, inv = norm_rows(hid_ref[r, :])
            dss_ref[0, frame, :] = jnp.sum(g, axis=0, keepdims=True)
            dss_ref[1, frame, :] = jnp.sum(g * y, axis=0, keepdims=True)
            d_hid = dx1_ref[r, :] + norm_rows_back(g * (1.0 + scale_ref[frame, :]), y, inv)
            gin_ref[...] += dotf(inp_ref[r, :], d_hid.astype(bf16), TN)
        return 0

    lax.fori_loop(0, half // rows, norm_back, 0)

    def sent(i, _):
        for s in range(2):
            for j in range(2):
                near_copy(i, s, j).wait_send()
            y_copy(i, s).wait_send()

            @pl.when(f >= 4)
            def _():
                z_copy(i, s).wait_send()

        @pl.when(i < chunks // 2)
        def _():
            x_copy(i).wait_send()

        return 0

    lax.fori_loop(0, chunks, sent, 0)


def tail_block(dq, n1, w, cosine, sine, rot, hid, scale, dx1, inp, dk, dv, cid):
    tok, e = dq.shape
    width = n1.shape[1]
    half = tok // 2
    f32, bf16 = jnp.float32, jnp.bfloat16
    vm = pl.BlockSpec(memory_space=pltpu.VMEM)
    anym = pl.BlockSpec(memory_space=pl.ANY)
    V = pltpu.VMEM
    D_ = pltpu.SemaphoreType.DMA
    chunks = tok // 256
    return pl.pallas_call(
        tail_kernel,
        in_specs=[vm] * 10 + [anym] * 2,
        out_specs=[vm] * 3,
        out_shape=[
            jax.ShapeDtypeStruct((2, 2, 3, width // 4, e), bf16),
            jax.ShapeDtypeStruct((128, width), f32),
            jax.ShapeDtypeStruct((2, half // TPF, width), f32),
        ],
        scratch_shapes=[
            V((2, 3, tok, e), bf16), V((2, 2, tok, e), bf16), V((2, tok, e), bf16),
            V((2, tok, e), bf16), V((width, tok), bf16), V((3, tok, e), bf16),
            V((half, width), bf16), V((half, width), bf16), V((half, width), f32),
            D_((2, 3)), D_((2, 2, chunks)), D_((2, 2, chunks)), D_((2, chunks)), D_((2, chunks)),
            D_((2, chunks)), D_((2, chunks)), D_((chunks // 2,)), D_((chunks // 2,)),
        ],
        compiler_params=pltpu.CompilerParams(
            vmem_limit_bytes=56 << 20, collective_id=cid, has_side_effects=True
        ),
        cost_estimate=pl.CostEstimate(
            flops=2 * 10**10, bytes_accessed=3 * 10**7, transcendentals=0
        ),
        name="projection_backward",
    )(dq, n1, w, cosine, sine, rot, hid, scale, dx1, inp, dk, dv)


def proj_kernel(
    inp_ref, win_ref, mod_ref, w_ref, cos_ref, sin_ref, rot_ref,
    n1_ref, hid_ref, q_ref, k_hbm, v_hbm,
    kv, wr,
    lsem, s_core, r_core, s_y, r_y, s_z, r_z,
):
    f = lax.axis_index("frames")
    h = lax.axis_index("mp")
    n = lax.axis_size("frames")
    core = lax.rem(f, 2)
    odd = lax.rem(lax.div(f, 2), 2)
    core_peer = {"frames": f + 1 - 2 * core}
    y_peer = {"frames": f + 2 - 4 * odd}
    before = {"frames": lax.rem(f - 4 + n, n)}
    after = {"frames": lax.rem(f + 4, n)}
    tok, width = n1_ref.shape
    e = q_ref.shape[1]
    half = tok // 2
    rows = 256
    chunks = tok // rows
    bf16 = jnp.bfloat16
    MESH = pl.DeviceIdType.MESH
    sides = (k_hbm, v_hbm)
    has_z = f >= 4
    has_next = f + 4 < n
    has_y = has_z | (odd == 1)

    def at(start, size):
        return pl.ds(pl.multiple_of(start, size), size)

    barrier = pltpu.get_barrier_semaphore()
    for peer in (core_peer, y_peer):
        pl.semaphore_signal(barrier, inc=1, device_id=peer, device_id_type=MESH)

    @pl.when(has_z)
    def _():
        pl.semaphore_signal(barrier, inc=1, device_id=before, device_id_type=MESH)

    @pl.when(has_next)
    def _():
        pl.semaphore_signal(barrier, inc=1, device_id=after, device_id_type=MESH)

    def embed(i, _):
        for k in range(2):
            r = at(i * 2 * TPF + k * TPF, TPF)
            frame = pl.ds(i * 2 + k, 1)
            v = dotf(inp_ref[r, :], win_ref[...])
            y, _inv = norm_rows(v)
            n1_ref[r, :] = (y * (1.0 + mod_ref[1, frame, :]) + mod_ref[0, frame, :]).astype(bf16)

            @pl.when(lax.div(i * 2 * TPF, half) == h)
            def _():
                hid_ref[at(lax.rem(i * 2 * TPF, half) + k * TPF, TPF), :] = v

        return 0

    lax.fori_loop(0, tok // (2 * TPF), embed, 0)

    def turn_weights(i, _):
        d = at(i * 256, 256)
        for k in range(2):
            for b in range(e // 256):
                cols = slice(b * 256, (b + 1) * 256)
                wr[k, d, cols] = dotf(w_ref[k, d, cols], rot_ref[...]).astype(bf16)
        return 0

    lax.fori_loop(0, width // 256, turn_weights, 0)
    pl.semaphore_wait(barrier, 2 + jnp.where(has_z, 1, 0) + jnp.where(has_next, 1, 0))

    def remote(src, dst, send, recv, peer):
        return pltpu.make_async_remote_copy(
            src_ref=src, dst_ref=dst, send_sem=send, recv_sem=recv, device_id=peer,
            device_id_type=MESH,
        )

    def block(s, b, i):
        return sides[s].at[at(b * tok + i * rows, rows)]

    def mine(s, i):
        return kv.at[s, at(i * rows, rows)]

    def keep(s, i):
        return pltpu.make_async_copy(mine(s, i), block(s, 4, i), lsem.at[s, i])

    def z_copy(s, i):
        return remote(mine(s, i), block(s, 0, i), s_z.at[s, i], r_z.at[s, i], after)

    def y_copy(s, i, src):
        return remote(src, block(s, 2, i), s_y.at[s, i], r_y.at[s, i], y_peer)

    def core_copy(s, i, j, src):
        return remote(
            src, block(s, (3, 1)[j], i), s_core.at[j, s, i], r_core.at[j, s, i], core_peer
        )

    def rotated(r, k):
        cosine, sine = cos_ref[r, :], sin_ref[r, :]
        parts = []
        for b in range(e // 256):
            cols = slice(b * 256, (b + 1) * 256)
            plain = dotf(n1_ref[r, :], w_ref[k, :, cols])
            turned = dotf(n1_ref[r, :], wr[k, :, cols])
            parts.append((plain * cosine + turned * sine).astype(bf16))
        return parts

    def own_chunk(i, _):
        r = at(i * rows, rows)
        for b, part in enumerate(rotated(r, 1)):
            kv[0, r, b * 256 : (b + 1) * 256] = part
        kv[1, r, :] = dotf(n1_ref[r, :], w_ref[2]).astype(bf16)
        for s in range(2):
            keep(s, i).start()

            @pl.when(has_next)
            def _():
                z_copy(s, i).start()

            @pl.when(odd == 0)
            def _():
                y_copy(s, i, mine(s, i)).start()

            @pl.when(core == 0)
            def _():
                core_copy(s, i, 0, mine(s, i)).start()

        return 0

    lax.fori_loop(0, chunks, own_chunk, 0)

    def queries(i, _):
        r = at(i * rows, rows)
        for b, part in enumerate(rotated(r, 0)):
            q_ref[r, b * 256 : (b + 1) * 256] = part
        return 0

    lax.fori_loop(0, chunks, queries, 0)

    def from_z(i, _):
        @pl.when(has_z)
        def _():
            for s in range(2):
                z_copy(s, i).wait_recv()

                @pl.when(odd == 1)
                def _():
                    y_copy(s, i, block(s, 0, i)).start()

                @pl.when(core == 1)
                def _():
                    core_copy(s, i, 1, block(s, 0, i)).start()

        return 0

    lax.fori_loop(0, chunks, from_z, 0)

    def from_y(i, _):
        @pl.when(has_y)
        def _():
            for s in range(2):
                y_copy(s, i, mine(s, i)).wait_recv()

                @pl.when(core == 1)
                def _():
                    core_copy(s, i, 0, block(s, 2, i)).start()

                @pl.when(core == 0)
                def _():
                    core_copy(s, i, 1, block(s, 2, i)).start()

        return 0

    lax.fori_loop(0, chunks, from_y, 0)

    def ended(i, _):
        for s in range(2):
            keep(s, i).wait()

            @pl.when((core == 1) | has_y)
            def _():
                core_copy(s, i, 0, mine(s, i)).wait_recv()

            @pl.when(((core == 1) & has_y) | has_z)
            def _():
                core_copy(s, i, 1, mine(s, i)).wait_recv()

            @pl.when(has_next)
            def _():
                z_copy(s, i).wait_send()

            @pl.when((odd == 0) | has_z)
            def _():
                y_copy(s, i, mine(s, i)).wait_send()

            @pl.when((core == 0) | has_y)
            def _():
                core_copy(s, i, 0, mine(s, i)).wait_send()

            @pl.when(((core == 0) & has_y) | has_z)
            def _():
                core_copy(s, i, 1, mine(s, i)).wait_send()

        return 0

    lax.fori_loop(0, chunks, ended, 0)


def proj_block(inp, win, mod, w, cosine, sine, rot, reach, cid):
    tok = inp.shape[0]
    width, e = w.shape[1:]
    f32, bf16 = jnp.float32, jnp.bfloat16
    vm = pl.BlockSpec(memory_space=pltpu.VMEM)
    anym = pl.BlockSpec(memory_space=pl.ANY)
    V = pltpu.VMEM
    D_ = pltpu.SemaphoreType.DMA
    chunks = tok // 256
    return pl.pallas_call(
        proj_kernel,
        in_specs=[vm] * 7,
        out_specs=[vm] * 3 + [anym] * 2,
        out_shape=[
            jax.ShapeDtypeStruct((tok, width), bf16),
            jax.ShapeDtypeStruct((tok // 2, width), f32),
            jax.ShapeDtypeStruct((tok, e), bf16),
            jax.ShapeDtypeStruct(((reach + 1) * tok, e), bf16),
            jax.ShapeDtypeStruct(((reach + 1) * tok, e), bf16),
        ],
        scratch_shapes=[
            V((2, tok, e), bf16), V((2, width, e), bf16),
            D_((2, chunks)), D_((2, 2, chunks)), D_((2, 2, chunks)), D_((2, chunks)),
            D_((2, chunks)), D_((2, chunks)), D_((2, chunks)),
        ],
        compiler_params=pltpu.CompilerParams(
            vmem_limit_bytes=48 << 20, collective_id=cid, has_side_effects=True
        ),
        cost_estimate=pl.CostEstimate(
            flops=6 * 10**10, bytes_accessed=3 * 10**7, transcendentals=0
        ),
        name="projection_forward",
    )(inp, win, mod, w, cosine, sine, rot)


def last_kernel(
    g_hbm, gin_ref, dm_ref, cond_ref, wm_ref, loss_ref,
    sq_ref, sin_ref, smod_ref, dct_ref,
    g_own, g_in, near, near_in, side, side_in, far, far_in, ends, ends_peer, dm_peer, dm,
    dc_send, dc_peer,
    lsem, s_x, r_x, s_g, r_g, s_f, r_f, s_d, r_d, s_dz, r_dz,
):
    f = lax.axis_index("frames")
    h = lax.axis_index("mp")
    n = lax.axis_size("frames")
    nj = n // 4
    core = lax.rem(f, 2)
    y = lax.rem(lax.div(f, 2), 2)
    j = lax.div(f, 4)
    core_peer = {"frames": f + 1 - 2 * core}
    y_peer = {"frames": f + 2 - 4 * y}
    x_peer = {"mp": 1 - h}
    f32, bf16 = jnp.float32, jnp.bfloat16
    MESH = pl.DeviceIdType.MESH
    rows = g_hbm.shape[3] // nj

    def z_peer(t):
        return {"frames": lax.rem(f + 4 * t, n)}

    def from_j(t):
        return lax.rem(j - t + nj, nj)

    def at(start, size):
        return pl.ds(pl.multiple_of(start, size), size)

    load = pltpu.make_async_copy(g_hbm.at[core], g_own, lsem.at[0])
    load.start()
    barrier = pltpu.get_barrier_semaphore()
    for peer in [core_peer, y_peer, x_peer] + [z_peer(t) for t in range(1, nj)]:
        pl.semaphore_signal(barrier, inc=1, device_id=peer, device_id_type=MESH)
    pl.semaphore_wait(barrier, 2 + nj)

    def remote(src, dst, send, recv, peer):
        return pltpu.make_async_remote_copy(
            src_ref=src, dst_ref=dst, send_sem=send, recv_sem=recv, device_id=peer,
            device_id_type=MESH,
        )

    dm_x = remote(dm_ref.at[1 - h], dm_peer, s_x.at[0], r_x.at[0], x_peer)
    dm_x.start()
    core_g = remote(g_hbm.at[1 - core], near, s_g.at[0], r_g.at[0], core_peer)
    core_in = remote(gin_ref.at[1 - core], near_in, s_g.at[1], r_g.at[1], core_peer)
    core_g.start()
    core_in.start()

    dm_x.wait_recv()
    mine = dm_ref[h]
    theirs = dm_peer[...]
    low = h == 0
    dm[core, y, j] = jnp.concatenate(
        [jnp.where(low, mine, theirs), jnp.where(low, theirs, mine)], axis=0
    ).astype(bf16)

    def dm_z(t, src):
        block = dm.at[core, y, src]
        return remote(block, block, s_dz.at[0, t], r_dz.at[0, t], z_peer(t))

    for t in range(1, nj):
        dm_z(t, j).start()
    load.wait()
    core_g.wait_recv()
    core_in.wait_recv()

    def add_near(i, _):
        for s in range(2):
            for k in range(g_own.shape[1]):
                r = at(i * rows, rows)
                g_own[s, k, r, :] = (
                    g_own[s, k, r, :].astype(f32) + near[s, k, r, :].astype(f32)
                ).astype(bf16)
        return 0

    lax.fori_loop(0, nj, add_near, 0)
    g_in[...] = (gin_ref[core].astype(f32) + near_in[...].astype(f32)).astype(bf16)
    for t in range(1, nj):
        dm_z(t, from_j(t)).wait_recv()

    def dm_y(side_index):
        block = dm.at[core, side_index]
        return remote(block, block, s_d.at[0], r_d.at[0], y_peer)

    dm_y(y).start()
    y_g = remote(g_own.at[1 - y], side, s_g.at[2], r_g.at[2], y_peer)
    y_in = remote(g_in.at[1 - y], side_in, s_g.at[3], r_g.at[3], y_peer)
    y_g.start()
    y_in.start()
    dm_y(1 - y).wait_recv()

    def dm_core(core_index):
        block = dm.at[core_index]
        return remote(block, block, s_d.at[1], r_d.at[1], core_peer)

    dm_core(core).start()
    y_g.wait_recv()
    y_in.wait_recv()

    def add_side(i, _):
        for k in range(g_own.shape[1]):
            r = at(i * rows, rows)
            side[k, r, :] = (
                g_own[y, k, r, :].astype(f32) + side[k, r, :].astype(f32)
            ).astype(bf16)
        return 0

    lax.fori_loop(0, nj, add_side, 0)
    side_in[...] = (g_in[y].astype(f32) + side_in[...].astype(f32)).astype(bf16)

    def far_g(t):
        there = at(lax.rem(j + t, nj) * rows, rows)
        return remote(
            side.at[:, there], far.at[t - 1], s_f.at[0, t], r_f.at[0, t], z_peer(t)
        )

    def far_i(t):
        there = at(lax.rem(j + t, nj) * rows, rows)
        return remote(
            side_in.at[there], far_in.at[t - 1], s_f.at[1, t], r_f.at[1, t], z_peer(t)
        )

    for t in range(1, nj):
        far_g(t).start()
        far_i(t).start()

    dm_core(1 - core).wait_recv()
    frames = dm.shape[0] * dm.shape[1] * dm.shape[2] * dm.shape[3]
    wide = dm.shape[4]
    every = dm[...].reshape(frames, wide)
    part = dotf(wm_ref[...], every, NT)
    dc_send[:rows, :] = part
    dc_send[rows:, :] = jnp.broadcast_to(jnp.sum(loss_ref[...]), (8, frames))
    dc_x = remote(dc_send, dc_peer, s_x.at[1], r_x.at[1], x_peer)
    dc_x.start()

    def mod_cols(i, _):
        cols = at(i * 512, 512)
        block = dm[:, :, :, :, cols].reshape(frames, 512)
        res = dotf(cond_ref[...], block)
        smod_ref[:, cols] = res[:rows] + res[rows : 2 * rows] + res[2 * rows :]
        return 0

    lax.fori_loop(0, wide // 512, mod_cols, 0)
    dc_x.wait_recv()
    total = dc_send[...] + dc_peer[...]
    dct_ref[core, y, j, :rows, :] = total[:rows].astype(bf16)
    pieces = [p[:1].astype(f32) for p in split_three(total[rows:])]
    dct_ref[core, y, j, rows:, :] = jnp.concatenate(
        pieces + [jnp.zeros((13, frames), f32)], axis=0
    ).astype(bf16)

    def dc_z(t, src):
        block = dct_ref.at[core, y, src]
        return remote(block, block, s_dz.at[1, t], r_dz.at[1, t], z_peer(t))

    for t in range(1, nj):
        dc_z(t, j).start()
    for t in range(1, nj):
        dc_z(t, from_j(t)).wait_recv()

    def dc_y(side_index):
        block = dct_ref.at[core, side_index]
        return remote(block, block, s_d.at[2], r_d.at[2], y_peer)

    dc_y(y).start()

    here = at(j * rows, rows)
    for t in range(1, nj):
        far_g(t).wait_recv()
        far_i(t).wait_recv()
    for k in range(sq_ref.shape[0]):
        sq_ref[k] = side[k, here, :].astype(f32) + sum(
            far[t, k].astype(f32) for t in range(nj - 1)
        )
    ends[...] = side_in[here, :].astype(f32) + sum(
        far_in[t].astype(f32) for t in range(nj - 1)
    )
    ends_x = remote(ends, ends_peer, s_x.at[2], r_x.at[2], x_peer)
    ends_x.start()
    dc_y(1 - y).wait_recv()

    def dc_core(core_index):
        block = dct_ref.at[core_index]
        return remote(block, block, s_d.at[3], r_d.at[3], core_peer)

    dc_core(core).start()
    ends_x.wait_recv()
    sin_ref[...] = ends[...] + ends_peer[...]
    dc_core(1 - core).wait_recv()

    for one in (dm_x, core_g, core_in, y_g, y_in, dc_x, ends_x):
        one.wait_send()
    for one in (dm_y(y), dm_core(core), dc_y(y), dc_core(core)):
        one.wait_send()
    for t in range(1, nj):
        for one in (dm_z(t, j), dc_z(t, j), far_g(t), far_i(t)):
            one.wait_send()


def last_block(g, gin, dm, cond, wm, loss, cid):
    _, _, kinds, block_rows, e = g.shape
    n = lax.axis_size("frames")
    nj = n // 4
    rows = block_rows // nj
    own_frames, wide = dm.shape[1:]
    frames = n * 2 * own_frames
    f32, bf16 = jnp.float32, jnp.bfloat16
    vm = pl.BlockSpec(memory_space=pltpu.VMEM)
    anym = pl.BlockSpec(memory_space=pl.ANY)
    V = pltpu.VMEM
    D_ = pltpu.SemaphoreType.DMA
    return pl.pallas_call(
        last_kernel,
        in_specs=[anym] + [vm] * 5,
        out_specs=[vm] * 4,
        out_shape=[
            jax.ShapeDtypeStruct((kinds, rows, e), f32),
            jax.ShapeDtypeStruct((rows, 128), f32),
            jax.ShapeDtypeStruct((rows, wide), f32),
            jax.ShapeDtypeStruct((2, 2, nj, rows + 16, frames), bf16),
        ],
        scratch_shapes=[
            V((2, kinds, block_rows, e), bf16), V((2, block_rows, 128), bf16),
            V((2, kinds, block_rows, e), bf16), V((2, block_rows, 128), bf16),
            V((kinds, block_rows, e), bf16), V((block_rows, 128), bf16),
            V((nj - 1, kinds, rows, e), bf16), V((nj - 1, rows, 128), bf16),
            V((rows, 128), f32), V((rows, 128), f32),
            V((own_frames, wide), f32), V((2, 2, nj, 2 * own_frames, wide), bf16),
            V((rows + 8, frames), f32), V((rows + 8, frames), f32),
            D_((1,)), D_((3,)), D_((3,)), D_((4,)), D_((4,)), D_((2, nj)), D_((2, nj)),
            D_((4,)), D_((4,)), D_((2, nj)), D_((2, nj)),
        ],
        compiler_params=pltpu.CompilerParams(
            vmem_limit_bytes=48 << 20, collective_id=cid, has_side_effects=True
        ),
        cost_estimate=pl.CostEstimate(
            flops=2 * 10**10, bytes_accessed=2 * 10**7, transcendentals=0
        ),
        name="weight_sums",
    )(g, gin, dm, cond, wm, loss)


def per_device(
    latents,
    noise,
    levels,
    clip_ids,
    clean_flags,
    attn_weights,
    mlp_weights,
    mod_weight,
    small_weights,
    attn_moment,
    mlp_moment,
    mod_moment,
    small_moment,
    attn_average,
    mlp_average,
    mod_average,
    small_average,
):
    frame_count = latents.shape[0]
    tok_count = frame_count * TPF
    patch_side = GRID // 2
    frames_total = clip_ids.shape[0]
    tokens_total = frames_total * TPF
    width_local = attn_weights.shape[2]
    heads_local = width_local // HD
    key_span = (REACH + 1) * tok_count
    device = lax.axis_index("frames")
    mp_index = lax.axis_index("mp")
    first_frame = device * frame_count
    scale_qk = HD ** (-0.5)
    w_attn = lax.all_gather(attn_weights.astype(jnp.bfloat16), "frames", axis=1, tiled=True)
    w_mlp = lax.all_gather(mlp_weights.astype(jnp.bfloat16), "frames", axis=1, tiled=True)
    low_mod = mod_weight.astype(jnp.bfloat16)
    w_mod = lax.all_gather(low_mod, "frames", axis=0, tiled=True)
    small_low = lax.all_gather(
        small_weights.astype(jnp.bfloat16), ("frames", "mp"), axis=1, tiled=True
    )
    levels_all = lax.all_gather(levels, "frames", axis=0, tiled=True)
    small_full = small_low.astype(jnp.float32)
    noised_all = (1 - clean_flags).astype(jnp.float32)
    noised_count = jnp.sum(noised_all)
    noised = lax.dynamic_slice_in_dim(noised_all, first_frame, frame_count)
    level_eff = levels * noised
    signal_scale = jnp.repeat(jnp.cos(0.5 * math.pi * level_eff), TPF)
    noise_scale = jnp.repeat(jnp.sin(0.5 * math.pi * level_eff), TPF)
    noise_patches = patchify(noise)
    inputs = signal_scale[:, None] * patchify(latents) + noise_scale[:, None] * noise_patches
    in_clip_all = clip_positions(clip_ids)
    in_clip = jnp.repeat(
        lax.dynamic_slice_in_dim(in_clip_all, first_frame, frame_count), TPF
    ).astype(jnp.float32)
    within = jnp.arange(tok_count, dtype=jnp.int32) % TPF
    angles = rotary_angles(
        in_clip,
        (within // patch_side).astype(jnp.float32),
        (within % patch_side).astype(jnp.float32),
        HD,
    )
    cosine_table = jnp.tile(jnp.cos(angles), (1, 4))
    sine_table = jnp.tile(jnp.sin(angles), (1, 4))
    turn_four = jnp.asarray(np.kron(np.eye(4, dtype=np.float32), rotation_matrix(HD)), jnp.bfloat16)
    clip_start = (
        lax.dynamic_slice_in_dim(
            jnp.arange(frames_total, dtype=jnp.int32) - in_clip_all, first_frame, frame_count
        )
        - first_frame
        + REACH * frame_count
    )
    features_all = time_features(levels_all * noised_all)
    pre_one = jnp.dot(features_all, small_full[:FREQ], precision=HIGH)
    first_all = jax.nn.silu(pre_one)
    pre_two = jnp.dot(first_all, small_full[FREQ : FREQ + D], precision=HIGH)
    conditioning_all = jax.nn.silu(pre_two)
    placed = jnp.asarray(
        np.arange(frames_total)
        .reshape(-1, 2, 2, frame_count)
        .transpose(2, 1, 0, 3)
        .reshape(frames_total)
    )
    features_placed = features_all[placed]
    first_placed = first_all[placed]
    pre_two_t = pre_two[placed].T
    pre_one_own = lax.dynamic_slice_in_dim(
        pre_one,
        (device * lax.axis_size("mp") + mp_index) * small_weights.shape[1],
        small_weights.shape[1],
        1,
    )[placed].T
    cond_rows = lax.dynamic_slice_in_dim(
        conditioning_all, device * mod_weight.shape[0], mod_weight.shape[0], 1
    )[placed]
    cond_parts = jnp.concatenate([part.T for part in split_three(cond_rows)], axis=0)
    conditioning = lax.dynamic_slice_in_dim(conditioning_all, first_frame, frame_count)
    mod_full = w_mod.astype(jnp.float32)
    modulation = lax.all_gather(
        jnp.dot(conditioning, mod_full, precision=HIGH), "mp", axis=1, tiled=True
    )
    pieces = [
        modulation[:, None, piece_index * D : (piece_index + 1) * D] for piece_index in range(6)
    ]
    shift_one, scale_one, gate_one, shift_two, scale_two, gate_two = pieces
    w_in = small_low[FREQ + D : FREQ + D + P_SIZE]
    w_head = small_low[FREQ + D + P_SIZE :]
    inputs_low = inputs.astype(jnp.bfloat16)
    padding = ((0, 0), (0, 128 - P_SIZE))
    inputs_low = jnp.pad(inputs_low, padding)
    normed_one, hidden_half, queries, keys_wide, values_wide = proj_block(
        inputs_low,
        jnp.pad(w_in, ((0, 128 - P_SIZE), (0, 0))),
        jnp.stack([shift_one[:, 0], scale_one[:, 0]]),
        w_attn[:3],
        cosine_table,
        sine_table,
        turn_four,
        REACH,
        2,
    )
    heads_wide, log_totals = attn_fwd(queries, keys_wide, values_wide, clip_start)
    half = tok_count // 2
    own_frames = frame_count // 2

    def half_of(array, dim=0):
        size = array.shape[dim] // 2
        return lax.dynamic_slice_in_dim(array, mp_index * size, size, dim)

    token_weight = jnp.repeat(noised, TPF) / (TPF * P_SIZE)
    grad_scale = 1.0 / jnp.maximum(noised_count, 1.0)
    mod_mid = jnp.stack(
        [half_of(piece[:, 0]) for piece in (gate_one, shift_two, scale_two, gate_two)]
    )
    d_mixed, d_shaped_one, d_mod_mid, loss_parts, grad_up, grad_rest = mid_block(
        heads_wide,
        w_attn[3],
        hidden_half,
        mod_mid,
        jnp.pad(half_of(noise_patches), padding),
        jnp.broadcast_to(half_of(token_weight)[:, None], (half, 128)),
        jnp.pad(w_head, ((0, 128 - P_SIZE), (0, 0))),
        grad_scale.reshape(1),
        w_mlp[0],
        w_mlp[1],
        TP_AXIS,
        0,
    )
    sum_up = lax.psum_scatter(grad_up, "frames", scatter_dimension=0, tiled=True)
    sum_rest = lax.psum_scatter(grad_rest, "frames", scatter_dimension=0, tiled=True)
    d_queries, keys_grad_wide, values_grad_wide = attn_bwd(
        queries, keys_wide, values_wide, d_mixed, heads_wide, log_totals, clip_start
    )
    d_queries, sum_up = lax.optimization_barrier((d_queries, sum_up))
    grad_qkv, grad_in, d_first_mods = tail_block(
        d_queries,
        normed_one,
        w_attn[:3],
        cosine_table,
        sine_table,
        turn_four,
        hidden_half,
        half_of(scale_one[:, 0]),
        d_shaped_one,
        half_of(inputs_low),
        keys_grad_wide,
        values_grad_wide,
        1,
    )
    d_first_mods, sum_rest = lax.optimization_barrier((d_first_mods, sum_rest))
    frame_groups = frames_total // (4 * frame_count)
    mod_rows = mod_weight.shape[0]
    small_cols = small_weights.shape[1]

    def by_place(array, dim):
        shape = array.shape
        size = shape[dim] // (4 * frame_groups)
        split = array.reshape(shape[:dim] + (frame_groups, 2, 2, size) + shape[dim + 1 :])
        order = list(range(split.ndim))
        order[dim], order[dim + 2] = dim + 2, dim
        return split.transpose(order)

    in_columns = by_place(grad_in.T, 0).reshape(2, 2, D // 4, 128).astype(jnp.bfloat16)
    d_mods = jnp.stack(
        [
            jnp.concatenate([d_first_mods[0], d_first_mods[1], d_mod_mid[0]], axis=1),
            jnp.concatenate([d_mod_mid[1], d_mod_mid[2], d_mod_mid[3]], axis=1),
        ]
    )
    sum_qkv, sum_in, sum_mod, d_cond_rows = last_block(
        grad_qkv, in_columns, d_mods, cond_parts, low_mod, loss_parts, 3
    )
    loss_sum = jnp.sum(d_cond_rows[:, :, :, mod_rows : mod_rows + 3, 0].astype(jnp.float32))
    d_cond_t = (
        d_cond_rows[:, :, :, :mod_rows, :].transpose(2, 1, 0, 3, 4).reshape(D, frames_total)
    ).astype(jnp.float32)
    d_pre_two = jax.vjp(jax.nn.silu, pre_two_t)[1](d_cond_t)[0]
    first_col = (device * lax.axis_size("mp") + mp_index) * small_cols
    d_pre_own = lax.dynamic_slice_in_dim(d_pre_two, first_col, small_cols, 0)
    grad_second = jnp.einsum("fi,jf->ij", first_placed, d_pre_own, precision=HIGH)
    second_rows = lax.dynamic_slice_in_dim(small_full, FREQ + first_col, small_cols, 0)
    d_first = jnp.einsum("kf,jk->jf", d_pre_two, second_rows, precision=HIGH)
    d_pre_one = jax.vjp(jax.nn.silu, pre_one_own)[1](d_first)[0]
    grad_first = jnp.einsum("fi,jf->ij", features_placed, d_pre_one, precision=HIGH)
    ff_cols = mlp_weights.shape[2]
    sum_rest = sum_rest.astype(jnp.float32)
    sum_mlp = jnp.stack([sum_up.astype(jnp.float32), sum_rest[:, :ff_cols]])
    sum_attn = jnp.stack(
        [sum_qkv[0], sum_qkv[1], sum_qkv[2]]
        + [sum_rest[:, ff_cols : ff_cols + width_local]]
    )
    head_first = ff_cols + width_local
    head_part = sum_rest[:, head_first : head_first + P_SIZE]
    sum_head = head_part + lax.ppermute(head_part, "mp", [(0, 1), (1, 0)])
    sum_ends = half_of(jnp.concatenate([sum_in[:, :P_SIZE], sum_head], axis=1).T, 1)
    sum_small = jnp.concatenate([grad_first, grad_second, sum_ends], axis=0)
    learning_rate = 0.5 * math.sqrt(tokens_total * P_SIZE / D)
    attn_new, attn_moment_new, attn_average_new, attn_copy = update(
        attn_weights, sum_attn, attn_moment, attn_average, learning_rate
    )
    mlp_new, mlp_moment_new, mlp_average_new, mlp_copy = update(
        mlp_weights, sum_mlp, mlp_moment, mlp_average, learning_rate
    )
    mod_new, mod_moment_new, mod_average_new, mod_copy = update(
        mod_weight, sum_mod, mod_moment, mod_average, learning_rate
    )
    small_new, small_moment_new, small_average_new, small_copy = update(
        small_weights, sum_small, small_moment, small_average, learning_rate
    )
    return (
        loss_sum,
        noised_count,
        attn_new,
        attn_moment_new,
        attn_average_new,
        attn_copy,
        mlp_new,
        mlp_moment_new,
        mlp_average_new,
        mlp_copy,
        mod_new,
        mod_moment_new,
        mod_average_new,
        mod_copy,
        small_new,
        small_moment_new,
        small_average_new,
        small_copy,
    )


def solution(mesh):
    return jax.shard_map(
        per_device,
        mesh=mesh,
        in_specs=(
            P("frames", None),
            P("frames", None),
            P("frames"),
            P(),
            P(),
            P(None, "frames", "mp"),
            P(None, "frames", "mp"),
            P("frames", "mp"),
            P(None, ("frames", "mp")),
            P(None, "frames", "mp"),
            P(None, "frames", "mp"),
            P("frames", "mp"),
            P(None, ("frames", "mp")),
            P(None, "frames", "mp"),
            P(None, "frames", "mp"),
            P("frames", "mp"),
            P(None, ("frames", "mp")),
        ),
        out_specs=(
            P(),
            P(),
            P(None, "frames", "mp"),
            P(None, "frames", "mp"),
            P(None, "frames", "mp"),
            P(None, "frames", "mp"),
            P(None, "frames", "mp"),
            P(None, "frames", "mp"),
            P(None, "frames", "mp"),
            P(None, "frames", "mp"),
            P("frames", "mp"),
            P("frames", "mp"),
            P("frames", "mp"),
            P("frames", "mp"),
            P(None, ("frames", "mp")),
            P(None, ("frames", "mp")),
            P(None, ("frames", "mp")),
            P(None, ("frames", "mp")),
        ),
        check_vma=False,
    )
```

```python
import functools
import math

import jax
import jax.numpy as jnp
import numpy as np
from jax import lax
from jax.experimental import pallas as pl
from jax.experimental.pallas import tpu as pltpu
from jax.sharding import PartitionSpec as P

D = 1024
HD = 64
CH = 4
FREQ = 256
GRID = 16
P_SIZE = 16
TPF = 64
REACH = 4


HIGH = lax.Precision.HIGHEST
EPSILON = 1e-06
MOMENTUM = 0.5
EMA_DECAY = 0.5
TP_AXIS = "mp"


def rotation_matrix(head_width):
    groups = [head_width // 4, 3 * head_width // 8, 3 * head_width // 8]
    rotation = np.zeros((head_width, head_width), np.float32)
    offset = 0
    for group_size in groups:
        half_size = group_size // 2
        for pair_index in range(half_size):
            rotation[offset + half_size + pair_index, offset + pair_index] = -1.0
            rotation[offset + pair_index, offset + half_size + pair_index] = 1.0
        offset += group_size
    return rotation


def rotary_angles(frame_pos, row_pos, col_pos, head_width):
    pieces = []
    for position, group_size in (
        (frame_pos, head_width // 4),
        (row_pos, 3 * head_width // 8),
        (col_pos, 3 * head_width // 8),
    ):
        half_size = group_size // 2
        frequency = 10000.0 ** (-jnp.arange(half_size, dtype=jnp.float32) / half_size)
        phases = position[:, None] * frequency[None, :]
        pieces += [phases, phases]
    return jnp.concatenate(pieces, axis=1)


def clip_positions(clip_ids):
    frame_index = jnp.arange(clip_ids.shape[0], dtype=jnp.int32)
    starts_here = jnp.concatenate([jnp.ones((1,), bool), clip_ids[1:] != clip_ids[:-1]])
    clip_start = lax.cummax(jnp.where(starts_here, frame_index, 0), axis=0)
    return frame_index - clip_start


def patchify(frame_data):
    frame_total = frame_data.shape[0]
    patch_side = GRID // 2
    shaped = frame_data.reshape(frame_total, CH, patch_side, 2, patch_side, 2)
    return shaped.transpose(0, 2, 4, 1, 3, 5).reshape(frame_total * patch_side * patch_side, CH * 4)


def layer_norm(vector):
    row_mean = jnp.mean(vector, axis=-1, keepdims=True)
    centred = vector - row_mean
    variance = jnp.mean(centred * centred, axis=-1, keepdims=True)
    return centred * lax.rsqrt(variance + EPSILON)


def modulate_local(shaped, shift_rows, scale_rows):
    return layer_norm(shaped) * (1.0 + scale_rows) + shift_rows


def time_features(level_eff):
    half_size = FREQ // 2
    frequency = jnp.exp(-math.log(10000.0) * jnp.arange(half_size, dtype=jnp.float32) / half_size)
    phases = (level_eff * 1000.0)[:, None] * frequency[None, :]
    return jnp.concatenate([jnp.cos(phases), jnp.sin(phases)], axis=1)


NT=(((1,),(1,)),((),()))
NN=(((1,),(0,)),((),()))

def dotf(a,b,dims=NN):
    return lax.dot_general(a,b,dims,preferred_element_type=jnp.float32)

def split_pair(xT):
    r=lax.broadcasted_iota(jnp.int32,xT.shape,0)
    z=jnp.zeros_like(xT)
    return jnp.where(r<HD,xT,z), jnp.where(r<HD,z,xT)

def keep_of(t,TK,TQ,cs,qf):
    kf=lax.broadcasted_iota(jnp.int32,(TK,TQ),0)//TPF+t*(TK//TPF)
    return (kf>=cs)&(kf<=qf)

def fwd_kernel(lo_ref,mid_ref,hi_ref,q_ref,k_ref,v_ref,cs_ref,o_ref,lse_ref,vT,*,TQ,TK,W0,NQ):
    KS=k_ref.shape[0]
    def tr(i,_):
        s=pl.multiple_of(i*TK,TK)
        vT[:,pl.ds(s,TK)]=v_ref[pl.ds(s,TK),:].T
        return 0
    lax.fori_loop(lo_ref[0],KS//TK,tr,0)
    def qtile(j,_):
        qs=pl.multiple_of(j*TQ,TQ)
        qT=(q_ref[pl.ds(qs,TQ),:].T)*jnp.bfloat16(0.125)
        qA,qB=split_pair(qT)
        cs=cs_ref[0:1,pl.ds(qs,TQ)]
        qf=lax.broadcasted_iota(jnp.int32,(1,TQ),1)//TPF+(W0+j*(TQ//TPF))
        def step(t,carry,masked):
            ks=pl.multiple_of(t*TK,TK)
            kt=k_ref[pl.ds(ks,TK),:]
            out=[]
            if masked: keep=keep_of(t,TK,TQ,cs,qf)
            for h,(qh,(m,l,o)) in enumerate(zip((qA,qB),carry)):
                s=dotf(kt,qh)
                if masked: s=jnp.where(keep,s,-1e30)
                mn=jnp.maximum(m,jnp.max(s,axis=0,keepdims=True))
                a=jnp.exp(m-mn)
                p=jnp.exp(s-mn)
                l=l*a+jnp.sum(p,axis=0,keepdims=True)
                o=o*a+dotf(vT[h*HD:(h+1)*HD,pl.ds(ks,TK)],p.astype(jnp.bfloat16))
                out.append((mn,l,o))
            return tuple(out)
        init=tuple((jnp.full((1,TQ),-1e29,jnp.float32),jnp.zeros((1,TQ),jnp.float32),jnp.zeros((HD,TQ),jnp.float32)) for _ in range(2))
        c=lax.fori_loop(lo_ref[j],mid_ref[j],lambda t,c:step(t,c,True),init)
        c=lax.fori_loop(mid_ref[j],hi_ref[j],lambda t,c:step(t,c,False),c)
        c=lax.fori_loop(hi_ref[j],(W0*TPF+(j+1)*TQ+TK-1)//TK,lambda t,c:step(t,c,True),c)
        oT=jnp.concatenate([c[0][2]/c[0][1],c[1][2]/c[1][1]],axis=0)
        o_ref[pl.ds(qs,TQ),:]=oT.T.astype(o_ref.dtype)
        lse_ref[0,0:1,pl.ds(qs,TQ)]=c[0][0]+jnp.log(c[0][1])
        lse_ref[0,1:2,pl.ds(qs,TQ)]=c[1][0]+jnp.log(c[1][1])
        return 0
    lax.fori_loop(0,NQ,qtile,0)

def tile_bounds(cs_rel,TQ,TK,W0,NQ):
    fq=TQ//TPF; fk=TK//TPF
    j=jnp.arange(NQ)
    first=cs_rel[::fq]; last=cs_rel[fq-1::fq]
    lo=first//fk
    dg=(W0+j*fq+1)//fk
    mid=jnp.minimum((last+fk-1)//fk,dg)
    mid=jnp.maximum(mid,lo)
    hi=jnp.maximum(dg,mid)
    return lo.astype(jnp.int32),mid.astype(jnp.int32),hi.astype(jnp.int32)

def attn_fwd(q,k,v,cs_rel,TQ=512,TK=512):
    T,Wd=q.shape; KS=k.shape[0]; P=Wd//128
    W0=(KS-T)//TPF; NQ=T//TQ
    lo,mid,hi=tile_bounds(cs_rel,TQ,TK,W0,NQ)
    cs_tok=jnp.broadcast_to(jnp.repeat(cs_rel,TPF)[None,:],(8,T)).astype(jnp.int32)
    return pl.pallas_call(
        functools.partial(fwd_kernel,TQ=TQ,TK=TK,W0=W0,NQ=NQ),
        grid_spec=pltpu.PrefetchScalarGridSpec(num_scalar_prefetch=3,grid=(P,),
            in_specs=[pl.BlockSpec((T,128),lambda p,*_:(0,p)),pl.BlockSpec((KS,128),lambda p,*_:(0,p)),pl.BlockSpec((KS,128),lambda p,*_:(0,p)),pl.BlockSpec((8,T),lambda p,*_:(0,0))],
            out_specs=[pl.BlockSpec((T,128),lambda p,*_:(0,p)),pl.BlockSpec((1,8,T),lambda p,*_:(p,0,0))],
            scratch_shapes=[pltpu.VMEM((128,KS),jnp.bfloat16)]),
        out_shape=[jax.ShapeDtypeStruct((T,Wd),jnp.float32),jax.ShapeDtypeStruct((P,8,T),jnp.float32)],
        compiler_params=pltpu.CompilerParams(vmem_limit_bytes=48<<20),
        cost_estimate=pl.CostEstimate(flops=10**11,bytes_accessed=2*10**7,transcendentals=3*10**7),
        name="attn_forward",
    )(lo,mid,hi,q,k,v,cs_tok)

def bwd_kernel(lo_ref,mid_ref,hi_ref,q_ref,k_ref,v_ref,do_ref,o_ref,lse_ref,cs_ref,dq_ref,dk_ref,dv_ref,kT,dkT,dvT,*,TQ,TK,W0,NQ):
    KS=k_ref.shape[0]
    def tr(i,_):
        s=pl.multiple_of(i*TK,TK)
        kT[:,pl.ds(s,TK)]=k_ref[pl.ds(s,TK),:].T
        return 0
    lax.fori_loop(lo_ref[0],KS//TK,tr,0)
    dkT[...]=jnp.zeros_like(dkT); dvT[...]=jnp.zeros_like(dvT)
    def qtile(j,_):
        qs=pl.multiple_of(j*TQ,TQ)
        qT=(q_ref[pl.ds(qs,TQ),:].T)*jnp.bfloat16(0.125)
        qh=split_pair(qT)
        doT=do_ref[pl.ds(qs,TQ),:].T
        doh=split_pair(doT)
        oT=o_ref[pl.ds(qs,TQ),:].T
        prod=oT*doT.astype(jnp.float32)
        delta=(jnp.sum(prod[:HD],axis=0,keepdims=True),jnp.sum(prod[HD:],axis=0,keepdims=True))
        lse=(lse_ref[0,0:1,pl.ds(qs,TQ)],lse_ref[0,1:2,pl.ds(qs,TQ)])
        cs=cs_ref[0:1,pl.ds(qs,TQ)]
        qf=lax.broadcasted_iota(jnp.int32,(1,TQ),1)//TPF+(W0+j*(TQ//TPF))
        def step(t,carry,masked):
            ks=pl.multiple_of(t*TK,TK)
            kt=k_ref[pl.ds(ks,TK),:]; vt=v_ref[pl.ds(ks,TK),:]
            out=[]
            if masked: keep=keep_of(t,TK,TQ,cs,qf)
            for h in range(2):
                r=slice(h*HD,(h+1)*HD)
                s=dotf(kt,qh[h])
                p=jnp.exp(s-lse[h])
                if masked: p=jnp.where(keep,p,0.0)
                dp=dotf(vt,doh[h])
                ds=(p*(dp-delta[h])).astype(jnp.bfloat16)
                pb=p.astype(jnp.bfloat16)
                dvT[r,pl.ds(ks,TK)]+=dotf(doT[r],pb,NT)
                dkT[r,pl.ds(ks,TK)]+=dotf(qT[r],ds,NT)
                out.append(carry[h]+dotf(kT[r,pl.ds(ks,TK)],ds))
            return tuple(out)
        init=(jnp.zeros((HD,TQ),jnp.float32),)*2
        c=lax.fori_loop(lo_ref[j],mid_ref[j],lambda t,c:step(t,c,True),init)
        c=lax.fori_loop(mid_ref[j],hi_ref[j],lambda t,c:step(t,c,False),c)
        c=lax.fori_loop(hi_ref[j],(W0*TPF+(j+1)*TQ+TK-1)//TK,lambda t,c:step(t,c,True),c)
        dq_ref[pl.ds(qs,TQ),:]=(jnp.concatenate(c,axis=0)*0.125).T
        return 0
    lax.fori_loop(0,NQ,qtile,0)
    def back(i,_):
        s=pl.multiple_of(i*TK,TK)
        dk_ref[pl.ds(s,TK),:]=dkT[:,pl.ds(s,TK)].T.astype(dk_ref.dtype)
        dv_ref[pl.ds(s,TK),:]=dvT[:,pl.ds(s,TK)].T.astype(dv_ref.dtype)
        return 0
    lax.fori_loop(0,KS//TK,back,0)

def attn_bwd(q,k,v,do,o,lse,cs_rel,TQ=512,TK=512,out_dt=jnp.bfloat16):
    T,Wd=q.shape; KS=k.shape[0]; P=Wd//128
    W0=(KS-T)//TPF; NQ=T//TQ
    lo,mid,hi=tile_bounds(cs_rel,TQ,TK,W0,NQ)
    cs_tok=jnp.broadcast_to(jnp.repeat(cs_rel,TPF)[None,:],(8,T)).astype(jnp.int32)
    tb=pl.BlockSpec((T,128),lambda p,*_:(0,p)); kb=pl.BlockSpec((KS,128),lambda p,*_:(0,p))
    return pl.pallas_call(
        functools.partial(bwd_kernel,TQ=TQ,TK=TK,W0=W0,NQ=NQ),
        grid_spec=pltpu.PrefetchScalarGridSpec(num_scalar_prefetch=3,grid=(P,),
            in_specs=[tb,kb,kb,tb,tb,pl.BlockSpec((1,8,T),lambda p,*_:(p,0,0)),pl.BlockSpec((8,T),lambda p,*_:(0,0))],
            out_specs=[tb,kb,kb],
            scratch_shapes=[pltpu.VMEM((128,KS),jnp.bfloat16),pltpu.VMEM((128,KS),jnp.float32),pltpu.VMEM((128,KS),jnp.float32)]),
        out_shape=[jax.ShapeDtypeStruct((T,Wd),jnp.float32),jax.ShapeDtypeStruct((KS,Wd),out_dt),jax.ShapeDtypeStruct((KS,Wd),out_dt)],
        compiler_params=pltpu.CompilerParams(vmem_limit_bytes=56<<20),
        cost_estimate=pl.CostEstimate(flops=2*10**11,bytes_accessed=5*10**7,transcendentals=3*10**7),
        name="attn_backward",
    )(lo,mid,hi,q,k,v,do,o,lse,cs_tok)


def update(weight, gradient, moment, average, learning_rate):
    moment_new = MOMENTUM * moment + gradient
    weight_new = weight - learning_rate * (gradient + MOMENTUM * moment_new)
    average_new = EMA_DECAY * average + (1.0 - EMA_DECAY) * weight_new
    return (weight_new, moment_new, average_new, weight_new.astype(jnp.bfloat16))


TN = (((0,), (0,)), ((), ()))


def norm_rows(v):
    centred = v - jnp.mean(v, axis=-1, keepdims=True)
    inverse = lax.rsqrt(jnp.mean(centred * centred, axis=-1, keepdims=True) + EPSILON)
    return centred * inverse, inverse


def norm_rows_back(grad, normed, inverse):
    return inverse * (
        grad
        - jnp.mean(grad, axis=-1, keepdims=True)
        - normed * jnp.mean(grad * normed, axis=-1, keepdims=True)
    )


def gelu_pair(x):
    c = math.sqrt(2.0 / math.pi)
    sq = x * x
    t = jnp.tanh(c * (x + 0.044715 * (x * sq)))
    half = 0.5 * (1.0 + t)
    return x * half, half + (0.5 * c) * x * (1.0 - t * t) * (1.0 + 0.134145 * sq)


def mid_kernel(
    o_ref, wo_ref, hid_ref, mod_ref, noise_ref, tw_ref, head_ref, gs_ref, wu_hbm, wd_hbm,
    dmix_ref, dx1_ref, dmod_ref, loss_ref, up_hbm, rest_hbm,
    wu_ref, wd_ref, att, x1, out, dx2, n2, n2t, act, dgl, dout, doutt, datt, datt_t,
    send_a, recv_a, send_c, recv_c, send_e, recv_e, stage, ghead_ref, go_ref, gh_t,
    wsem, gsem, ssem, rsem, *, tp,
):
    f = lax.axis_index("frames")
    h = lax.axis_index("mp")
    bf16 = jnp.bfloat16
    x_peer = {"mp": 1 - h}
    tp_peer = {"frames": f + 1 - 2 * lax.rem(f, 2)} if tp == "core" else x_peer
    half = hid_ref.shape[0]
    rows = 128
    chunks = half // rows
    width = hid_ref.shape[1]
    ff = wu_hbm.shape[1]
    e = o_ref.shape[1]
    ft = 512
    dt = 256

    weights = [
        pltpu.make_async_copy(wu_hbm, wu_ref, wsem.at[0]),
        pltpu.make_async_copy(wd_hbm, wd_ref, wsem.at[1]),
    ]
    for w in weights:
        w.start()

    barrier = pltpu.get_barrier_semaphore()
    pl.semaphore_signal(barrier, inc=1, device_id=x_peer, device_id_type=pl.DeviceIdType.MESH)
    if tp == "core":
        pl.semaphore_signal(barrier, inc=1, device_id=tp_peer, device_id_type=pl.DeviceIdType.MESH)
    pl.semaphore_wait(barrier, 2 if tp == "core" else 1)

    def at(start, size):
        return pl.ds(pl.multiple_of(start, size), size)

    def copy(src, dst, phase, c, peer):
        return pltpu.make_async_remote_copy(
            src_ref=src, dst_ref=dst, send_sem=ssem.at[phase, c], recv_sem=rsem.at[phase, c],
            device_id=peer, device_id_type=pl.DeviceIdType.MESH,
        )

    def copy_a(c):
        return copy(send_a.at[at(c * rows, rows)], recv_a.at[at(c * rows, rows)], 0, c, x_peer)

    def copy_b(c):
        return copy(
            n2.at[at(c * 2 * rows, rows)], n2.at[at(c * 2 * rows + rows, rows)], 1, c, tp_peer
        )

    def copy_c(c):
        return copy(send_c.at[at(c * rows, rows)], recv_c.at[at(c * rows, rows)], 2, c, tp_peer)

    def copy_d(c):
        return copy(
            dout.at[at(c * 2 * rows, rows)], dout.at[at(c * 2 * rows + rows, rows)], 3, c, tp_peer
        )

    def copy_e(c):
        return copy(send_e.at[at(c * rows, rows)], recv_e.at[at(c * rows, rows)], 4, c, tp_peer)

    def copy_f(c):
        mine = datt.at[at(h * half + c * rows, rows)]
        return copy(mine, mine, 5, c, x_peer)

    def phase_a(c, _):
        part = o_ref[at((1 - h) * half + c * rows, rows), :].astype(bf16)
        send_a[at(c * rows, rows), :] = dotf(part, wo_ref[...], NT).astype(bf16)
        copy_a(c).start()
        return 0

    lax.fori_loop(0, chunks, phase_a, 0)

    def phase_b(c, _):
        part = o_ref[at(h * half + c * rows, rows), :].astype(bf16)
        att[at(c * rows, rows), :] = dotf(part, wo_ref[...], NT)
        copy_a(c).wait_recv()
        for k in range(rows // TPF):
            r = at(c * rows + k * TPF, TPF)
            frame = pl.ds(c * (rows // TPF) + k, 1)
            a = att[r, :] + recv_a[r, :].astype(jnp.float32)
            att[r, :] = a
            v = hid_ref[r, :] + mod_ref[0, frame, :] * a
            x1[r, :] = v
            y, _inv = norm_rows(v)
            n2[at(c * 2 * rows + k * TPF, TPF), :] = (
                y * (1.0 + mod_ref[2, frame, :]) + mod_ref[1, frame, :]
            ).astype(bf16)
        copy_b(c).start()
        return 0

    lax.fori_loop(0, chunks, phase_b, 0)
    for w in weights:
        w.wait()

    def phase_c(c, _):
        copy_b(c).wait_recv()
        tok = at(c * 2 * rows, 2 * rows)
        n2t[:, tok] = n2[tok, :].T

        def up(i, _):
            cols = at(i * ft, ft)
            a, g = gelu_pair(dotf(n2[tok, :], wu_ref[:, cols]))
            act[tok, cols] = a.astype(bf16)
            dgl[tok, cols] = g.astype(bf16)
            return 0

        lax.fori_loop(0, ff // ft, up, 0)

        def down(i, _):
            cols = at(i * dt, dt)
            res = dotf(act[tok, :], wd_ref[cols, :], NT)
            out[at(c * rows, rows), cols] = res[:rows]
            send_c[at(c * rows, rows), cols] = res[rows:].astype(bf16)
            return 0

        lax.fori_loop(0, width // dt, down, 0)
        copy_c(c).start()
        return 0

    lax.fori_loop(0, chunks, phase_c, 0)

    ghead_ref[...] = jnp.zeros_like(ghead_ref)
    loss_ref[...] = jnp.zeros_like(loss_ref)

    def phase_d(c, _):
        copy_c(c).wait_recv()
        for k in range(rows // TPF):
            r = at(c * rows + k * TPF, TPF)
            frame = pl.ds(c * (rows // TPF) + k, 1)
            o = out[r, :] + recv_c[r, :].astype(jnp.float32)
            gate = mod_ref[3, frame, :]
            y, inv = norm_rows(x1[r, :] + gate * o)
            fn = y.astype(bf16)
            misfit = dotf(fn, head_ref[...], NT) - noise_ref[r, :]
            weighted = tw_ref[r, :] * misfit
            loss_ref[...] += weighted * misfit
            d_pred = (2.0 * gs_ref[0] * weighted).astype(bf16)
            ghead_ref[...] += dotf(d_pred, fn, TN)
            d_x2 = norm_rows_back(dotf(d_pred, head_ref[...]), y, inv)
            dx2[r, :] = d_x2
            dmod_ref[3, frame, :] = jnp.sum(d_x2 * o, axis=0, keepdims=True)
            dout[at(c * 2 * rows + k * TPF, TPF), :] = (gate * d_x2).astype(bf16)
        copy_d(c).start()
        return 0

    lax.fori_loop(0, chunks, phase_d, 0)

    def phase_e(c, _):
        copy_d(c).wait_recv()
        tok = at(c * 2 * rows, 2 * rows)
        doutt[:, tok] = dout[tok, :].T

        def down(i, _):
            cols = at(i * ft, ft)
            g = dotf(dout[tok, :], wd_ref[:, cols]) * dgl[tok, cols].astype(jnp.float32)
            dgl[tok, cols] = g.astype(bf16)
            return 0

        lax.fori_loop(0, ff // ft, down, 0)

        def up(i, _):
            cols = at(i * dt, dt)
            res = dotf(dgl[tok, :], wu_ref[cols, :], NT)
            out[at(c * rows, rows), cols] = res[:rows]
            send_e[at(c * rows, rows), cols] = res[rows:].astype(bf16)
            return 0

        lax.fori_loop(0, width // dt, up, 0)
        copy_e(c).start()
        return 0

    lax.fori_loop(0, chunks, phase_e, 0)

    def phase_f(c, _):
        copy_e(c).wait_recv()
        for k in range(rows // TPF):
            r = at(c * rows + k * TPF, TPF)
            frame = pl.ds(c * (rows // TPF) + k, 1)
            g = out[r, :] + recv_e[r, :].astype(jnp.float32)
            y, inv = norm_rows(x1[r, :])
            dmod_ref[1, frame, :] = jnp.sum(g, axis=0, keepdims=True)
            dmod_ref[2, frame, :] = jnp.sum(g * y, axis=0, keepdims=True)
            d_x1 = dx2[r, :] + norm_rows_back(g * (1.0 + mod_ref[2, frame, :]), y, inv)
            dx1_ref[r, :] = d_x1
            dmod_ref[0, frame, :] = jnp.sum(d_x1 * att[r, :], axis=0, keepdims=True)
            datt[at(h * half + c * rows + k * TPF, TPF), :] = (mod_ref[0, frame, :] * d_x1).astype(
                bf16
            )
        copy_f(c).start()
        return 0

    lax.fori_loop(0, chunks, phase_f, 0)

    def weight_grads(left, right, target):
        def put(slot, i):
            return pltpu.make_async_copy(
                stage.at[slot], target.at[at(i * dt, dt), pl.ds(0, ff)], gsem.at[slot]
            )

        def tile(i, _):
            slot = lax.rem(i, 2)

            @pl.when(i >= 2)
            def _():
                put(slot, i - 2).wait()

            def cols_of(j, _):
                cols = at(j * ft, ft)
                stage[slot, :, cols] = dotf(left[at(i * dt, dt), :], right[:, cols]).astype(bf16)
                return 0

            lax.fori_loop(0, ff // ft, cols_of, 0)
            put(slot, i).start()
            return 0

        lax.fori_loop(0, width // dt, tile, 0)
        for i in (width // dt - 2, width // dt - 1):
            put(i % 2, i).wait()

    weight_grads(n2t, dgl, up_hbm)
    weight_grads(doutt, act, rest_hbm)

    def own_mix(c, _):
        tok = at(h * half + c * rows, rows)
        datt_t[:, tok] = datt[tok, :].T
        dmix_ref[tok, :] = dotf(datt[tok, :], wo_ref[...]).astype(bf16)
        return 0

    lax.fori_loop(0, chunks, own_mix, 0)

    def phase_g(c, _):
        tok = at((1 - h) * half + c * rows, rows)
        theirs = datt.at[tok]
        copy(theirs, theirs, 5, c, x_peer).wait_recv()
        datt_t[:, tok] = datt[tok, :].T
        dmix_ref[tok, :] = dotf(datt[tok, :], wo_ref[...]).astype(bf16)
        return 0

    lax.fori_loop(0, chunks, phase_g, 0)

    def grad_out(i, _):
        d = at(i * dt, dt)
        go_ref[d, :] = dotf(datt_t[d, :], o_ref[...].astype(bf16)).astype(bf16)
        return 0

    lax.fori_loop(0, width // dt, grad_out, 0)
    gh_t[...] = ghead_ref[...].T.astype(bf16)
    ends = [
        pltpu.make_async_copy(go_ref, rest_hbm.at[:, pl.ds(ff, e)], gsem.at[2]),
        pltpu.make_async_copy(gh_t, rest_hbm.at[:, pl.ds(ff + e, 128)], gsem.at[3]),
    ]
    for one in ends:
        one.start()
    for one in ends:
        one.wait()
    def sent(c, _):
        for one in (copy_a, copy_b, copy_c, copy_d, copy_e, copy_f):
            one(c).wait_send()
        return 0

    lax.fori_loop(0, chunks, sent, 0)


def mid_block(o, wo, hid, mod, noise, tw, head, gs, wu, wd, tp, cid):
    tok, e = o.shape
    half, width = hid.shape
    ff = wu.shape[1]
    own_frames = half // TPF
    f32, bf16 = jnp.float32, jnp.bfloat16
    vm = pl.BlockSpec(memory_space=pltpu.VMEM)
    anym = pl.BlockSpec(memory_space=pl.ANY)
    V = pltpu.VMEM
    return pl.pallas_call(
        functools.partial(mid_kernel, tp=tp),
        in_specs=[vm] * 7 + [pl.BlockSpec(memory_space=pltpu.SMEM), anym, anym],
        out_specs=[vm] * 4 + [anym] * 2,
        out_shape=[
            jax.ShapeDtypeStruct((tok, e), bf16),
            jax.ShapeDtypeStruct((half, width), f32),
            jax.ShapeDtypeStruct((4, own_frames, width), f32),
            jax.ShapeDtypeStruct((TPF, 128), f32),
            jax.ShapeDtypeStruct((width, ff), bf16),
            jax.ShapeDtypeStruct((width, ff + e + 128), bf16),
        ],
        scratch_shapes=[
            V((width, ff), bf16), V((width, ff), bf16),
            V((half, width), f32), V((half, width), f32), V((half, width), f32),
            V((half, width), f32),
            V((2 * half, width), bf16), V((width, 2 * half), bf16),
            V((2 * half, ff), bf16), V((2 * half, ff), bf16),
            V((2 * half, width), bf16), V((width, 2 * half), bf16),
            V((tok, width), bf16), V((width, tok), bf16),
            V((half, width), bf16), V((half, width), bf16),
            V((half, width), bf16), V((half, width), bf16),
            V((half, width), bf16), V((half, width), bf16),
            V((2, 256, ff), bf16), V((128, width), f32), V((width, e), bf16),
            V((width, 128), bf16),
            pltpu.SemaphoreType.DMA((2,)), pltpu.SemaphoreType.DMA((4,)),
            pltpu.SemaphoreType.DMA((6, half // 128)), pltpu.SemaphoreType.DMA((6, half // 128)),
        ],
        compiler_params=pltpu.CompilerParams(
            vmem_limit_bytes=62 << 20, collective_id=cid, has_side_effects=True
        ),
        cost_estimate=pl.CostEstimate(
            flops=4 * 10**10, bytes_accessed=3 * 10**7, transcendentals=2 * 10**6
        ),
        name="feed_forward",
    )(o, wo, hid, mod, noise, tw, head, gs, wu, wd)


def split_three(v):
    high = v.astype(jnp.bfloat16)
    left = v - high.astype(jnp.float32)
    middle = left.astype(jnp.bfloat16)
    return high, middle, (left - middle.astype(jnp.float32)).astype(jnp.bfloat16)


def turn_back(g, cosine, sine, rot):
    parts = split_three(g * sine)
    return (g * cosine + sum(dotf(p, rot, NT) for p in parts)).astype(jnp.bfloat16)


def tail_kernel(
    dq_ref, n1_ref, w_ref, cos_ref, sin_ref, rot_ref, hid_ref, scale_ref, dx1_ref, inp_ref,
    dk_hbm, dv_hbm,
    gq_ref, gin_ref, dss_ref,
    own, near, yrecv, zrecv, n1t, dproj, send_x, recv_x, part,
    lsem, s_near, r_near, s_y, r_y, s_z, r_z, s_x, r_x,
):
    f = lax.axis_index("frames")
    h = lax.axis_index("mp")
    n = lax.axis_size("frames")
    core = lax.rem(f, 2)
    odd = lax.rem(lax.div(f, 2), 2)
    core_peer = {"frames": f + 1 - 2 * core}
    y_peer = {"frames": f + 2 - 4 * odd}
    before = {"frames": lax.rem(f - 4 + n, n)}
    after = {"frames": lax.rem(f + 4, n)}
    x_peer = {"mp": 1 - h}
    tok, e = dq_ref.shape
    width = n1_ref.shape[1]
    half = tok // 2
    rows = 256
    chunks = tok // rows
    f32, bf16 = jnp.float32, jnp.bfloat16
    MESH = pl.DeviceIdType.MESH
    sides = (dk_hbm, dv_hbm)
    share = width // n

    def at(start, size):
        return pl.ds(pl.multiple_of(start, size), size)

    loads = [
        pltpu.make_async_copy(
            sides[s].at[pl.ds(b * tok, tok)], own.at[s, j], lsem.at[s, j]
        )
        for s in range(2)
        for j, b in enumerate((4, 2, 0))
    ]
    for one in loads:
        one.start()

    barrier = pltpu.get_barrier_semaphore()
    for peer in (core_peer, y_peer, x_peer):
        pl.semaphore_signal(barrier, inc=1, device_id=peer, device_id_type=MESH)

    @pl.when(f >= 4)
    def _():
        pl.semaphore_signal(barrier, inc=1, device_id=before, device_id_type=MESH)

    @pl.when(f + 4 < n)
    def _():
        pl.semaphore_signal(barrier, inc=1, device_id=after, device_id_type=MESH)

    pl.semaphore_wait(barrier, 3 + jnp.where(f >= 4, 1, 0) + jnp.where(f + 4 < n, 1, 0))

    def rows_of(i):
        return lax.rem(i + (chunks // 2) * (1 - h), chunks) * rows

    def remote(src, dst, send, recv, peer):
        return pltpu.make_async_remote_copy(
            src_ref=src, dst_ref=dst, send_sem=send, recv_sem=recv, device_id=peer,
            device_id_type=MESH,
        )

    def near_copy(i, s, j):
        b = (3, 1)[j]
        return remote(
            sides[s].at[at(b * tok + rows_of(i), rows)],
            near.at[s, j, at(rows_of(i), rows)],
            s_near.at[s, j, i], r_near.at[s, j, i], core_peer,
        )

    def y_copy(i, s):
        r = at(rows_of(i), rows)
        return remote(own.at[s, 1, r], yrecv.at[s, r], s_y.at[s, i], r_y.at[s, i], y_peer)

    def z_copy(i, s):
        r = at(rows_of(i), rows)
        return remote(own.at[s, 2, r], zrecv.at[s, r], s_z.at[s, i], r_z.at[s, i], before)

    def x_copy(i):
        r = at(i * rows, rows)
        return remote(send_x.at[r], recv_x.at[r], s_x.at[i], r_x.at[i], x_peer)

    def start_near(i, _):
        for s in range(2):
            for j in range(2):
                near_copy(i, s, j).start()
        return 0

    lax.fori_loop(0, chunks, start_near, 0)

    @pl.when(f + 4 >= n)
    def _():
        zrecv[...] = jnp.zeros_like(zrecv)

    for one in loads:
        one.wait()
    low_core = core == 0

    def combine(i, _):
        r = at(rows_of(i), rows)
        for s in range(2):
            for j in range(2):
                near_copy(i, s, j).wait_recv()
            n3 = near[s, 0, r, :].astype(f32)
            n1_ = near[s, 1, r, :].astype(f32)
            own[s, 1, r, :] = (
                own[s, 1, r, :].astype(f32) + jnp.where(low_core, n1_, n3)
            ).astype(bf16)
            y_copy(i, s).start()
            own[s, 2, r, :] = (
                own[s, 2, r, :].astype(f32) + jnp.where(low_core, 0.0, n1_)
            ).astype(bf16)

            @pl.when((odd == 0) & (f >= 4))
            def _():
                z_copy(i, s).start()

        return 0

    lax.fori_loop(0, chunks, combine, 0)

    def turned(g, r, k):
        for b in range(e // 256):
            cols = slice(b * 256, (b + 1) * 256)
            dproj[k, r, cols] = turn_back(
                g[:, cols], cos_ref[r, :], sin_ref[r, :], rot_ref[...]
            )

    def relay(i, _):
        r = at(rows_of(i), rows)
        turned(dq_ref[r, :], r, 0)
        n1t[:, r] = n1_ref[r, :].T

        @pl.when(odd == 1)
        def _():
            for s in range(2):
                y_copy(i, s).wait_recv()

                @pl.when(f >= 4)
                def _():
                    own[s, 2, r, :] = (
                        own[s, 2, r, :].astype(f32) + yrecv[s, r, :].astype(f32)
                    ).astype(bf16)
                    z_copy(i, s).start()

        return 0

    lax.fori_loop(0, chunks, relay, 0)

    def grads(k):
        def tile(i, _):
            res = dotf(n1t[at(i * 256, 256), :], dproj[k]).astype(bf16)
            for q in range(256 // share):
                j = i * (256 // share // 4) + q // 4
                gq_ref[q % 2, (q // 2) % 2, k, at(j * share, share), :] = res[
                    q * share : (q + 1) * share
                ]
            return 0

        lax.fori_loop(0, width // 256, tile, 0)

    grads(0)

    def finish(i, _):
        r = at(rows_of(i), rows)
        for s in range(2):

            @pl.when(odd == 0)
            def _():
                y_copy(i, s).wait_recv()

            @pl.when(f + 4 < n)
            def _():
                z_copy(i, s).wait_recv()

            total = (
                own[s, 0, r, :].astype(f32)
                + jnp.where(low_core, near[s, 0, r, :].astype(f32), 0.0)
                + jnp.where(odd == 0, yrecv[s, r, :].astype(f32), 0.0)
                + zrecv[s, r, :].astype(f32)
            )
            if s == 0:
                turned(total, r, 1)
            else:
                dproj[2, r, :] = total.astype(bf16)

        def cols_of(j, _):
            cols = at(j * 256, 256)
            res = sum(dotf(dproj[k, r, :], w_ref[k, cols, :], NT) for k in range(3))

            @pl.when(i < chunks // 2)
            def _():
                send_x[at(i * rows, rows), cols] = res.astype(bf16)

            @pl.when(i >= chunks // 2)
            def _():
                part[at((i - chunks // 2) * rows, rows), cols] = res

            return 0

        lax.fori_loop(0, width // 256, cols_of, 0)

        @pl.when(i < chunks // 2)
        def _():
            x_copy(i).start()

        return 0

    lax.fori_loop(0, chunks, finish, 0)
    grads(1)
    grads(2)
    gin_ref[...] = jnp.zeros_like(gin_ref)

    def norm_back(i, _):
        x_copy(i).wait_recv()
        for k in range(rows // TPF):
            r = at(i * rows + k * TPF, TPF)
            frame = pl.ds(i * (rows // TPF) + k, 1)
            g = part[r, :] + recv_x[r, :].astype(f32)
            y, inv = norm_rows(hid_ref[r, :])
            dss_ref[0, frame, :] = jnp.sum(g, axis=0, keepdims=True)
            dss_ref[1, frame, :] = jnp.sum(g * y, axis=0, keepdims=True)
            d_hid = dx1_ref[r, :] + norm_rows_back(g * (1.0 + scale_ref[frame, :]), y, inv)
            gin_ref[...] += dotf(inp_ref[r, :], d_hid.astype(bf16), TN)
        return 0

    lax.fori_loop(0, half // rows, norm_back, 0)

    def sent(i, _):
        for s in range(2):
            for j in range(2):
                near_copy(i, s, j).wait_send()
            y_copy(i, s).wait_send()

            @pl.when(f >= 4)
            def _():
                z_copy(i, s).wait_send()

        @pl.when(i < chunks // 2)
        def _():
            x_copy(i).wait_send()

        return 0

    lax.fori_loop(0, chunks, sent, 0)


def tail_block(dq, n1, w, cosine, sine, rot, hid, scale, dx1, inp, dk, dv, cid):
    tok, e = dq.shape
    width = n1.shape[1]
    half = tok // 2
    f32, bf16 = jnp.float32, jnp.bfloat16
    vm = pl.BlockSpec(memory_space=pltpu.VMEM)
    anym = pl.BlockSpec(memory_space=pl.ANY)
    V = pltpu.VMEM
    D_ = pltpu.SemaphoreType.DMA
    chunks = tok // 256
    return pl.pallas_call(
        tail_kernel,
        in_specs=[vm] * 10 + [anym] * 2,
        out_specs=[vm] * 3,
        out_shape=[
            jax.ShapeDtypeStruct((2, 2, 3, width // 4, e), bf16),
            jax.ShapeDtypeStruct((128, width), f32),
            jax.ShapeDtypeStruct((2, half // TPF, width), f32),
        ],
        scratch_shapes=[
            V((2, 3, tok, e), bf16), V((2, 2, tok, e), bf16), V((2, tok, e), bf16),
            V((2, tok, e), bf16), V((width, tok), bf16), V((3, tok, e), bf16),
            V((half, width), bf16), V((half, width), bf16), V((half, width), f32),
            D_((2, 3)), D_((2, 2, chunks)), D_((2, 2, chunks)), D_((2, chunks)), D_((2, chunks)),
            D_((2, chunks)), D_((2, chunks)), D_((chunks // 2,)), D_((chunks // 2,)),
        ],
        compiler_params=pltpu.CompilerParams(
            vmem_limit_bytes=56 << 20, collective_id=cid, has_side_effects=True
        ),
        cost_estimate=pl.CostEstimate(
            flops=2 * 10**10, bytes_accessed=3 * 10**7, transcendentals=0
        ),
        name="projection_backward",
    )(dq, n1, w, cosine, sine, rot, hid, scale, dx1, inp, dk, dv)


def proj_kernel(
    inp_ref, win_ref, mod_ref, w_ref, cos_ref, sin_ref, rot_ref,
    n1_ref, hid_ref, q_ref, k_hbm, v_hbm,
    kv, wr,
    lsem, s_core, r_core, s_y, r_y, s_z, r_z,
):
    f = lax.axis_index("frames")
    h = lax.axis_index("mp")
    n = lax.axis_size("frames")
    core = lax.rem(f, 2)
    odd = lax.rem(lax.div(f, 2), 2)
    core_peer = {"frames": f + 1 - 2 * core}
    y_peer = {"frames": f + 2 - 4 * odd}
    before = {"frames": lax.rem(f - 4 + n, n)}
    after = {"frames": lax.rem(f + 4, n)}
    tok, width = n1_ref.shape
    e = q_ref.shape[1]
    half = tok // 2
    rows = 256
    chunks = tok // rows
    bf16 = jnp.bfloat16
    MESH = pl.DeviceIdType.MESH
    sides = (k_hbm, v_hbm)
    has_z = f >= 4
    has_next = f + 4 < n
    has_y = has_z | (odd == 1)

    def at(start, size):
        return pl.ds(pl.multiple_of(start, size), size)

    barrier = pltpu.get_barrier_semaphore()
    for peer in (core_peer, y_peer):
        pl.semaphore_signal(barrier, inc=1, device_id=peer, device_id_type=MESH)

    @pl.when(has_z)
    def _():
        pl.semaphore_signal(barrier, inc=1, device_id=before, device_id_type=MESH)

    @pl.when(has_next)
    def _():
        pl.semaphore_signal(barrier, inc=1, device_id=after, device_id_type=MESH)

    def embed(i, _):
        for k in range(2):
            r = at(i * 2 * TPF + k * TPF, TPF)
            frame = pl.ds(i * 2 + k, 1)
            v = dotf(inp_ref[r, :], win_ref[...])
            y, _inv = norm_rows(v)
            n1_ref[r, :] = (y * (1.0 + mod_ref[1, frame, :]) + mod_ref[0, frame, :]).astype(bf16)

            @pl.when(lax.div(i * 2 * TPF, half) == h)
            def _():
                hid_ref[at(lax.rem(i * 2 * TPF, half) + k * TPF, TPF), :] = v

        return 0

    lax.fori_loop(0, tok // (2 * TPF), embed, 0)

    def turn_weights(i, _):
        d = at(i * 256, 256)
        for k in range(2):
            for b in range(e // 256):
                cols = slice(b * 256, (b + 1) * 256)
                wr[k, d, cols] = dotf(w_ref[k, d, cols], rot_ref[...]).astype(bf16)
        return 0

    lax.fori_loop(0, width // 256, turn_weights, 0)
    pl.semaphore_wait(barrier, 2 + jnp.where(has_z, 1, 0) + jnp.where(has_next, 1, 0))

    def remote(src, dst, send, recv, peer):
        return pltpu.make_async_remote_copy(
            src_ref=src, dst_ref=dst, send_sem=send, recv_sem=recv, device_id=peer,
            device_id_type=MESH,
        )

    def block(s, b, i):
        return sides[s].at[at(b * tok + i * rows, rows)]

    def mine(s, i):
        return kv.at[s, at(i * rows, rows)]

    def keep(s, i):
        return pltpu.make_async_copy(mine(s, i), block(s, 4, i), lsem.at[s, i])

    def z_copy(s, i):
        return remote(mine(s, i), block(s, 0, i), s_z.at[s, i], r_z.at[s, i], after)

    def y_copy(s, i, src):
        return remote(src, block(s, 2, i), s_y.at[s, i], r_y.at[s, i], y_peer)

    def core_copy(s, i, j, src):
        return remote(
            src, block(s, (3, 1)[j], i), s_core.at[j, s, i], r_core.at[j, s, i], core_peer
        )

    def rotated(r, k):
        cosine, sine = cos_ref[r, :], sin_ref[r, :]
        parts = []
        for b in range(e // 256):
            cols = slice(b * 256, (b + 1) * 256)
            plain = dotf(n1_ref[r, :], w_ref[k, :, cols])
            turned = dotf(n1_ref[r, :], wr[k, :, cols])
            parts.append((plain * cosine + turned * sine).astype(bf16))
        return parts

    def own_chunk(i, _):
        r = at(i * rows, rows)
        for b, part in enumerate(rotated(r, 1)):
            kv[0, r, b * 256 : (b + 1) * 256] = part
        kv[1, r, :] = dotf(n1_ref[r, :], w_ref[2]).astype(bf16)
        for s in range(2):
            keep(s, i).start()

            @pl.when(has_next)
            def _():
                z_copy(s, i).start()

            @pl.when(odd == 0)
            def _():
                y_copy(s, i, mine(s, i)).start()

            @pl.when(core == 0)
            def _():
                core_copy(s, i, 0, mine(s, i)).start()

        return 0

    lax.fori_loop(0, chunks, own_chunk, 0)

    def queries(i, _):
        r = at(i * rows, rows)
        for b, part in enumerate(rotated(r, 0)):
            q_ref[r, b * 256 : (b + 1) * 256] = part
        return 0

    lax.fori_loop(0, chunks, queries, 0)

    def from_z(i, _):
        @pl.when(has_z)
        def _():
            for s in range(2):
                z_copy(s, i).wait_recv()

                @pl.when(odd == 1)
                def _():
                    y_copy(s, i, block(s, 0, i)).start()

                @pl.when(core == 1)
                def _():
                    core_copy(s, i, 1, block(s, 0, i)).start()

        return 0

    lax.fori_loop(0, chunks, from_z, 0)

    def from_y(i, _):
        @pl.when(has_y)
        def _():
            for s in range(2):
                y_copy(s, i, mine(s, i)).wait_recv()

                @pl.when(core == 1)
                def _():
                    core_copy(s, i, 0, block(s, 2, i)).start()

                @pl.when(core == 0)
                def _():
                    core_copy(s, i, 1, block(s, 2, i)).start()

        return 0

    lax.fori_loop(0, chunks, from_y, 0)

    def ended(i, _):
        for s in range(2):
            keep(s, i).wait()

            @pl.when((core == 1) | has_y)
            def _():
                core_copy(s, i, 0, mine(s, i)).wait_recv()

            @pl.when(((core == 1) & has_y) | has_z)
            def _():
                core_copy(s, i, 1, mine(s, i)).wait_recv()

            @pl.when(has_next)
            def _():
                z_copy(s, i).wait_send()

            @pl.when((odd == 0) | has_z)
            def _():
                y_copy(s, i, mine(s, i)).wait_send()

            @pl.when((core == 0) | has_y)
            def _():
                core_copy(s, i, 0, mine(s, i)).wait_send()

            @pl.when(((core == 0) & has_y) | has_z)
            def _():
                core_copy(s, i, 1, mine(s, i)).wait_send()

        return 0

    lax.fori_loop(0, chunks, ended, 0)


def proj_block(inp, win, mod, w, cosine, sine, rot, reach, cid):
    tok = inp.shape[0]
    width, e = w.shape[1:]
    f32, bf16 = jnp.float32, jnp.bfloat16
    vm = pl.BlockSpec(memory_space=pltpu.VMEM)
    anym = pl.BlockSpec(memory_space=pl.ANY)
    V = pltpu.VMEM
    D_ = pltpu.SemaphoreType.DMA
    chunks = tok // 256
    return pl.pallas_call(
        proj_kernel,
        in_specs=[vm] * 7,
        out_specs=[vm] * 3 + [anym] * 2,
        out_shape=[
            jax.ShapeDtypeStruct((tok, width), bf16),
            jax.ShapeDtypeStruct((tok // 2, width), f32),
            jax.ShapeDtypeStruct((tok, e), bf16),
            jax.ShapeDtypeStruct(((reach + 1) * tok, e), bf16),
            jax.ShapeDtypeStruct(((reach + 1) * tok, e), bf16),
        ],
        scratch_shapes=[
            V((2, tok, e), bf16), V((2, width, e), bf16),
            D_((2, chunks)), D_((2, 2, chunks)), D_((2, 2, chunks)), D_((2, chunks)),
            D_((2, chunks)), D_((2, chunks)), D_((2, chunks)),
        ],
        compiler_params=pltpu.CompilerParams(
            vmem_limit_bytes=48 << 20, collective_id=cid, has_side_effects=True
        ),
        cost_estimate=pl.CostEstimate(
            flops=6 * 10**10, bytes_accessed=3 * 10**7, transcendentals=0
        ),
        name="projection_forward",
    )(inp, win, mod, w, cosine, sine, rot)


def last_kernel(
    g_hbm, gin_ref, dm_ref, cond_ref, wm_ref, loss_ref,
    sq_ref, sin_ref, smod_ref, dct_ref,
    g_own, g_in, near, near_in, side, side_in, far, far_in, ends, ends_peer, dm_peer, dm,
    dc_send, dc_peer,
    lsem, s_x, r_x, s_g, r_g, s_f, r_f, s_d, r_d, s_dz, r_dz,
):
    f = lax.axis_index("frames")
    h = lax.axis_index("mp")
    n = lax.axis_size("frames")
    nj = n // 4
    core = lax.rem(f, 2)
    y = lax.rem(lax.div(f, 2), 2)
    j = lax.div(f, 4)
    core_peer = {"frames": f + 1 - 2 * core}
    y_peer = {"frames": f + 2 - 4 * y}
    x_peer = {"mp": 1 - h}
    f32, bf16 = jnp.float32, jnp.bfloat16
    MESH = pl.DeviceIdType.MESH
    rows = g_hbm.shape[3] // nj

    def z_peer(t):
        return {"frames": lax.rem(f + 4 * t, n)}

    def from_j(t):
        return lax.rem(j - t + nj, nj)

    def at(start, size):
        return pl.ds(pl.multiple_of(start, size), size)

    load = pltpu.make_async_copy(g_hbm.at[core], g_own, lsem.at[0])
    load.start()
    barrier = pltpu.get_barrier_semaphore()
    for peer in [core_peer, y_peer, x_peer] + [z_peer(t) for t in range(1, nj)]:
        pl.semaphore_signal(barrier, inc=1, device_id=peer, device_id_type=MESH)
    pl.semaphore_wait(barrier, 2 + nj)

    def remote(src, dst, send, recv, peer):
        return pltpu.make_async_remote_copy(
            src_ref=src, dst_ref=dst, send_sem=send, recv_sem=recv, device_id=peer,
            device_id_type=MESH,
        )

    dm_x = remote(dm_ref.at[1 - h], dm_peer, s_x.at[0], r_x.at[0], x_peer)
    dm_x.start()
    core_g = remote(g_hbm.at[1 - core], near, s_g.at[0], r_g.at[0], core_peer)
    core_in = remote(gin_ref.at[1 - core], near_in, s_g.at[1], r_g.at[1], core_peer)
    core_g.start()
    core_in.start()

    dm_x.wait_recv()
    mine = dm_ref[h]
    theirs = dm_peer[...]
    low = h == 0
    dm[core, y, j] = jnp.concatenate(
        [jnp.where(low, mine, theirs), jnp.where(low, theirs, mine)], axis=0
    ).astype(bf16)

    def dm_z(t, src):
        block = dm.at[core, y, src]
        return remote(block, block, s_dz.at[0, t], r_dz.at[0, t], z_peer(t))

    for t in range(1, nj):
        dm_z(t, j).start()
    load.wait()
    core_g.wait_recv()
    core_in.wait_recv()

    def add_near(i, _):
        for s in range(2):
            for k in range(g_own.shape[1]):
                r = at(i * rows, rows)
                g_own[s, k, r, :] = (
                    g_own[s, k, r, :].astype(f32) + near[s, k, r, :].astype(f32)
                ).astype(bf16)
        return 0

    lax.fori_loop(0, nj, add_near, 0)
    g_in[...] = (gin_ref[core].astype(f32) + near_in[...].astype(f32)).astype(bf16)
    for t in range(1, nj):
        dm_z(t, from_j(t)).wait_recv()

    def dm_y(side_index):
        block = dm.at[core, side_index]
        return remote(block, block, s_d.at[0], r_d.at[0], y_peer)

    dm_y(y).start()
    y_g = remote(g_own.at[1 - y], side, s_g.at[2], r_g.at[2], y_peer)
    y_in = remote(g_in.at[1 - y], side_in, s_g.at[3], r_g.at[3], y_peer)
    y_g.start()
    y_in.start()
    dm_y(1 - y).wait_recv()

    def dm_core(core_index):
        block = dm.at[core_index]
        return remote(block, block, s_d.at[1], r_d.at[1], core_peer)

    dm_core(core).start()
    y_g.wait_recv()
    y_in.wait_recv()

    def add_side(i, _):
        for k in range(g_own.shape[1]):
            r = at(i * rows, rows)
            side[k, r, :] = (
                g_own[y, k, r, :].astype(f32) + side[k, r, :].astype(f32)
            ).astype(bf16)
        return 0

    lax.fori_loop(0, nj, add_side, 0)
    side_in[...] = (g_in[y].astype(f32) + side_in[...].astype(f32)).astype(bf16)

    def far_g(t):
        there = at(lax.rem(j + t, nj) * rows, rows)
        return remote(
            side.at[:, there], far.at[t - 1], s_f.at[0, t], r_f.at[0, t], z_peer(t)
        )

    def far_i(t):
        there = at(lax.rem(j + t, nj) * rows, rows)
        return remote(
            side_in.at[there], far_in.at[t - 1], s_f.at[1, t], r_f.at[1, t], z_peer(t)
        )

    for t in range(1, nj):
        far_g(t).start()
        far_i(t).start()

    dm_core(1 - core).wait_recv()
    frames = dm.shape[0] * dm.shape[1] * dm.shape[2] * dm.shape[3]
    wide = dm.shape[4]
    every = dm[...].reshape(frames, wide)
    part = dotf(wm_ref[...], every, NT)
    dc_send[:rows, :] = part
    dc_send[rows:, :] = jnp.broadcast_to(jnp.sum(loss_ref[...]), (8, frames))
    dc_x = remote(dc_send, dc_peer, s_x.at[1], r_x.at[1], x_peer)
    dc_x.start()

    def mod_cols(i, _):
        cols = at(i * 512, 512)
        block = dm[:, :, :, :, cols].reshape(frames, 512)
        res = dotf(cond_ref[...], block)
        smod_ref[:, cols] = res[:rows] + res[rows : 2 * rows] + res[2 * rows :]
        return 0

    lax.fori_loop(0, wide // 512, mod_cols, 0)
    dc_x.wait_recv()
    total = dc_send[...] + dc_peer[...]
    dct_ref[core, y, j, :rows, :] = total[:rows].astype(bf16)
    pieces = [p[:1].astype(f32) for p in split_three(total[rows:])]
    dct_ref[core, y, j, rows:, :] = jnp.concatenate(
        pieces + [jnp.zeros((13, frames), f32)], axis=0
    ).astype(bf16)

    def dc_z(t, src):
        block = dct_ref.at[core, y, src]
        return remote(block, block, s_dz.at[1, t], r_dz.at[1, t], z_peer(t))

    for t in range(1, nj):
        dc_z(t, j).start()
    for t in range(1, nj):
        dc_z(t, from_j(t)).wait_recv()

    def dc_y(side_index):
        block = dct_ref.at[core, side_index]
        return remote(block, block, s_d.at[2], r_d.at[2], y_peer)

    dc_y(y).start()

    here = at(j * rows, rows)
    for t in range(1, nj):
        far_g(t).wait_recv()
        far_i(t).wait_recv()
    for k in range(sq_ref.shape[0]):
        sq_ref[k] = side[k, here, :].astype(f32) + sum(
            far[t, k].astype(f32) for t in range(nj - 1)
        )
    ends[...] = side_in[here, :].astype(f32) + sum(
        far_in[t].astype(f32) for t in range(nj - 1)
    )
    ends_x = remote(ends, ends_peer, s_x.at[2], r_x.at[2], x_peer)
    ends_x.start()
    dc_y(1 - y).wait_recv()

    def dc_core(core_index):
        block = dct_ref.at[core_index]
        return remote(block, block, s_d.at[3], r_d.at[3], core_peer)

    dc_core(core).start()
    ends_x.wait_recv()
    sin_ref[...] = ends[...] + ends_peer[...]
    dc_core(1 - core).wait_recv()

    for one in (dm_x, core_g, core_in, y_g, y_in, dc_x, ends_x):
        one.wait_send()
    for one in (dm_y(y), dm_core(core), dc_y(y), dc_core(core)):
        one.wait_send()
    for t in range(1, nj):
        for one in (dm_z(t, j), dc_z(t, j), far_g(t), far_i(t)):
            one.wait_send()


def last_block(g, gin, dm, cond, wm, loss, cid):
    _, _, kinds, block_rows, e = g.shape
    n = lax.axis_size("frames")
    nj = n // 4
    rows = block_rows // nj
    own_frames, wide = dm.shape[1:]
    frames = n * 2 * own_frames
    f32, bf16 = jnp.float32, jnp.bfloat16
    vm = pl.BlockSpec(memory_space=pltpu.VMEM)
    anym = pl.BlockSpec(memory_space=pl.ANY)
    V = pltpu.VMEM
    D_ = pltpu.SemaphoreType.DMA
    return pl.pallas_call(
        last_kernel,
        in_specs=[anym] + [vm] * 5,
        out_specs=[vm] * 4,
        out_shape=[
            jax.ShapeDtypeStruct((kinds, rows, e), f32),
            jax.ShapeDtypeStruct((rows, 128), f32),
            jax.ShapeDtypeStruct((rows, wide), f32),
            jax.ShapeDtypeStruct((2, 2, nj, rows + 16, frames), bf16),
        ],
        scratch_shapes=[
            V((2, kinds, block_rows, e), bf16), V((2, block_rows, 128), bf16),
            V((2, kinds, block_rows, e), bf16), V((2, block_rows, 128), bf16),
            V((kinds, block_rows, e), bf16), V((block_rows, 128), bf16),
            V((nj - 1, kinds, rows, e), bf16), V((nj - 1, rows, 128), bf16),
            V((rows, 128), f32), V((rows, 128), f32),
            V((own_frames, wide), f32), V((2, 2, nj, 2 * own_frames, wide), bf16),
            V((rows + 8, frames), f32), V((rows + 8, frames), f32),
            D_((1,)), D_((3,)), D_((3,)), D_((4,)), D_((4,)), D_((2, nj)), D_((2, nj)),
            D_((4,)), D_((4,)), D_((2, nj)), D_((2, nj)),
        ],
        compiler_params=pltpu.CompilerParams(
            vmem_limit_bytes=48 << 20, collective_id=cid, has_side_effects=True
        ),
        cost_estimate=pl.CostEstimate(
            flops=2 * 10**10, bytes_accessed=2 * 10**7, transcendentals=0
        ),
        name="weight_sums",
    )(g, gin, dm, cond, wm, loss)


def front_kernel(
    small_ref, feat_ref, wm_ref, w_ref,
    st_ref, feats_ref, pre1_ref, pre2_ref, wout_ref, ends_ref, mod_ref,
    wcol, mods,
    s_x, r_x, s_z, r_z, s_y, r_y, s_c, r_c, s_a, r_a, s_m, r_m,
):
    f = lax.axis_index("frames")
    h = lax.axis_index("mp")
    n = lax.axis_size("frames")
    nj = n // 4
    c = lax.rem(f, 2)
    y = lax.rem(lax.div(f, 2), 2)
    j = lax.div(f, 4)
    f32, bf16 = jnp.float32, jnp.bfloat16
    MESH = pl.DeviceIdType.MESH
    x_peer = {"mp": 1 - h}
    core_peer = {"frames": f + 1 - 2 * c}
    y_peer = {"frames": f + 2 - 4 * y}
    offsets = [
        (tj, ty, tc) for tj in range(nj) for ty in range(2) for tc in range(2)
    ][1:]

    def place(tj, ty, tc):
        return (
            lax.rem(j + tj, nj),
            y + ty - 2 * y * ty,
            c + tc - 2 * c * tc,
        )

    def peer_of(spot):
        return {"frames": 4 * spot[0] + 2 * spot[1] + spot[2]}

    def from_j(t):
        return lax.rem(j - t + nj, nj)

    def remote(src, dst, send, recv, peer):
        return pltpu.make_async_remote_copy(
            src_ref=src, dst_ref=dst, send_sem=send, recv_sem=recv, device_id=peer,
            device_id_type=MESH,
        )

    barrier = pltpu.get_barrier_semaphore()
    for o in offsets:
        pl.semaphore_signal(barrier, inc=1, device_id=peer_of(place(*o)), device_id_type=MESH)
    pl.semaphore_signal(barrier, inc=1, device_id=x_peer, device_id_type=MESH)
    pl.semaphore_wait(barrier, n)

    class Gather:
        def __init__(self, block, k):
            self.block, self.k = block, k

        def over_z(self, t, jj):
            b = self.block(jj, y, c)
            return remote(
                b, b, s_z.at[self.k, t], r_z.at[self.k, t], {"frames": lax.rem(f + 4 * t, n)}
            )

        def over_y(self, t, yy):
            b = self.block(from_j(t), yy, c)
            return remote(b, b, s_y.at[self.k, t], r_y.at[self.k, t], y_peer)

        def over_core(self, t, same, yy, cc):
            b = self.block(from_j(t), yy, cc)
            return remote(
                b, b, s_c.at[self.k, same, t], r_c.at[self.k, same, t], core_peer
            )

        def start(self):
            for t in range(1, nj):
                self.over_z(t, j).start()
            self.over_y(0, y).start()
            self.over_core(0, 0, y, c).start()

        def pass_z(self):
            for t in range(1, nj):
                self.over_z(t, from_j(t)).wait_recv()
                self.over_y(t, y).start()
                self.over_core(t, 0, y, c).start()

        def pass_y(self):
            for t in range(nj):
                self.over_y(t, 1 - y).wait_recv()
                self.over_core(t, 1, 1 - y, c).start()

        def finish(self):
            for t in range(nj):
                self.over_core(t, 0, y, 1 - c).wait_recv()
                self.over_core(t, 1, 1 - y, 1 - c).wait_recv()

        def sent(self):
            for t in range(1, nj):
                self.over_z(t, j).wait_send()
            for t in range(nj):
                self.over_y(t, y).wait_send()
                self.over_core(t, 0, y, c).wait_send()
                self.over_core(t, 1, 1 - y, c).wait_send()

    small = Gather(lambda a, b, d: st_ref.at[a, b, d], 0)
    feats = Gather(lambda a, b, d: feats_ref.at[d, b, a], 1)
    weights = Gather(lambda a, b, d: wout_ref.at[:, a, b, d], 2)

    small_x = remote(small_ref, st_ref.at[j, y, c, h], s_x.at[0], r_x.at[0], x_peer)
    small_x.start()
    feats_ref[c, y, j] = feat_ref[...]
    feats.start()

    def column_copy(i, spot, slot):
        return remote(
            wm_ref.at[spot[2], spot[1], spot[0]], wcol.at[slot[0], slot[1], slot[2]],
            s_a.at[i], r_a.at[i], peer_of(spot),
        )

    def source(o):
        return place((nj - o[0]) % nj, o[1], o[2])

    for i, o in enumerate(offsets):
        column_copy(i, place(*o), (j, y, c)).start()
    st_ref[j, y, c, h] = small_ref[...]
    wout_ref[:, j, y, c] = w_ref[...]
    wcol[j, y, c] = wm_ref[c, y, j]
    remote(
        small_ref, st_ref.at[j, y, c, 1 - h], s_x.at[0], r_x.at[0], x_peer
    ).wait_recv()
    small.start()
    feats.pass_z()
    small.pass_z()
    weights.start()
    feats.pass_y()
    small.pass_y()
    feats.finish()
    small.finish()

    total = st_ref.shape[0] * 4
    width = total * 2 * st_ref.shape[4]
    frames = feats_ref.shape[2] * 4 * feats_ref.shape[3]
    inner = feats_ref.shape[4]

    def exact(left, right, dims):
        m = left.shape[0]
        res = dotf(jnp.concatenate(split_three(left), axis=0), right, dims)
        return res[:m] + res[m : 2 * m] + res[2 * m :]

    def silu(v):
        return v * jax.nn.sigmoid(v)

    table = st_ref[...].reshape(width, st_ref.shape[5])
    fv = feats_ref[...].reshape(frames, inner)
    pre1 = exact(fv, table[:, :inner], NT)
    pre1_ref[...] = pre1
    pre2 = exact(silu(pre1), table[:, inner : inner + width], NT)
    pre2_ref[...] = pre2
    ends_ref[...] = table[:, inner + width : inner + width + 128].T
    for i, o in enumerate(offsets):
        column_copy(i, place(*o), source(o)).wait_recv()
    cols = wcol[...].reshape(width, wcol.shape[4])
    mods[...] = exact(silu(pre2), cols, NN).reshape(mods.shape)

    def mods_copy(i, spot, slot):
        return remote(
            mods.at[spot[2], spot[1], spot[0]], mod_ref.at[h, slot[2], slot[1], slot[0]],
            s_m.at[i], r_m.at[i], peer_of(spot),
        )

    for i, o in enumerate(offsets):
        mods_copy(i, place(*o), (j, y, c)).start()
    mod_ref[h, c, y, j] = mods[c, y, j]
    weights.pass_z()
    for i, o in enumerate(offsets):
        mods_copy(i, place(*o), source(o)).wait_recv()
    mods_x = remote(mod_ref.at[h], mod_ref.at[h], s_x.at[1], r_x.at[1], x_peer)
    mods_x.start()
    weights.pass_y()
    weights.finish()
    theirs = mod_ref.at[1 - h]
    remote(theirs, theirs, s_x.at[1], r_x.at[1], x_peer).wait_recv()

    small_x.wait_send()
    mods_x.wait_send()
    for g in (small, feats, weights):
        g.sent()
    for i, o in enumerate(offsets):
        column_copy(i, place(*o), (j, y, c)).wait_send()
        mods_copy(i, place(*o), (j, y, c)).wait_send()


def front_block(small, feat, wm, w, cid):
    n = lax.axis_size("frames")
    nj = n // 4
    cols, lanes = small.shape
    own_frames, inner = feat.shape
    frames = n * own_frames
    kinds, rows, e = w.shape
    wide = wm.shape[-1]
    width = rows * n
    f32, bf16 = jnp.float32, jnp.bfloat16
    vm = pl.BlockSpec(memory_space=pltpu.VMEM)
    V = pltpu.VMEM
    D_ = pltpu.SemaphoreType.DMA
    return pl.pallas_call(
        front_kernel,
        in_specs=[vm] * 4,
        out_specs=[vm] * 7,
        out_shape=[
            jax.ShapeDtypeStruct((nj, 2, 2, 2, cols, lanes), bf16),
            jax.ShapeDtypeStruct((2, 2, nj, own_frames, inner), f32),
            jax.ShapeDtypeStruct((frames, width), f32),
            jax.ShapeDtypeStruct((frames, width), f32),
            jax.ShapeDtypeStruct((kinds, nj, 2, 2, rows, e), bf16),
            jax.ShapeDtypeStruct((128, width), bf16),
            jax.ShapeDtypeStruct((2, 2, 2, nj, own_frames, wide), f32),
        ],
        scratch_shapes=[
            V((nj, 2, 2, rows, wide), bf16), V((2, 2, nj, own_frames, wide), f32),
            D_((2,)), D_((2,)), D_((3, nj)), D_((3, nj)), D_((3, nj)), D_((3, nj)),
            D_((3, 2, nj)), D_((3, 2, nj)), D_((n - 1,)), D_((n - 1,)), D_((n - 1,)),
            D_((n - 1,)),
        ],
        compiler_params=pltpu.CompilerParams(
            vmem_limit_bytes=48 << 20, collective_id=cid, has_side_effects=True
        ),
        cost_estimate=pl.CostEstimate(
            flops=4 * 10**10, bytes_accessed=2 * 10**7, transcendentals=0
        ),
        name="conditioning",
    )(small, feat, wm, w)


def per_device(
    latents,
    noise,
    levels,
    clip_ids,
    clean_flags,
    attn_weights,
    mlp_weights,
    mod_weight,
    small_weights,
    attn_moment,
    mlp_moment,
    mod_moment,
    small_moment,
    attn_average,
    mlp_average,
    mod_average,
    small_average,
):
    frame_count = latents.shape[0]
    tok_count = frame_count * TPF
    patch_side = GRID // 2
    frames_total = clip_ids.shape[0]
    tokens_total = frames_total * TPF
    width_local = attn_weights.shape[2]
    heads_local = width_local // HD
    key_span = (REACH + 1) * tok_count
    device = lax.axis_index("frames")
    mp_index = lax.axis_index("mp")
    first_frame = device * frame_count
    scale_qk = HD ** (-0.5)
    attn_low = attn_weights.astype(jnp.bfloat16)
    mlp_low = mlp_weights.astype(jnp.bfloat16)
    low_mod = mod_weight.astype(jnp.bfloat16)
    noised_all = (1 - clean_flags).astype(jnp.float32)
    noised_count = jnp.sum(noised_all)
    noised = lax.dynamic_slice_in_dim(noised_all, first_frame, frame_count)
    level_eff = levels * noised
    signal_scale = jnp.repeat(jnp.cos(0.5 * math.pi * level_eff), TPF)
    noise_scale = jnp.repeat(jnp.sin(0.5 * math.pi * level_eff), TPF)
    noise_patches = patchify(noise)
    inputs = signal_scale[:, None] * patchify(latents) + noise_scale[:, None] * noise_patches
    in_clip_all = clip_positions(clip_ids)
    in_clip = jnp.repeat(
        lax.dynamic_slice_in_dim(in_clip_all, first_frame, frame_count), TPF
    ).astype(jnp.float32)
    within = jnp.arange(tok_count, dtype=jnp.int32) % TPF
    angles = rotary_angles(
        in_clip,
        (within // patch_side).astype(jnp.float32),
        (within % patch_side).astype(jnp.float32),
        HD,
    )
    cosine_table = jnp.tile(jnp.cos(angles), (1, 4))
    sine_table = jnp.tile(jnp.sin(angles), (1, 4))
    turn_four = jnp.asarray(np.kron(np.eye(4, dtype=np.float32), rotation_matrix(HD)), jnp.bfloat16)
    clip_start = (
        lax.dynamic_slice_in_dim(
            jnp.arange(frames_total, dtype=jnp.int32) - in_clip_all, first_frame, frame_count
        )
        - first_frame
        + REACH * frame_count
    )
    peers = lax.axis_size("frames")
    frame_groups = peers // 4
    small_rows, small_cols = small_weights.shape
    mod_rows, mod_cols = mod_weight.shape
    mod_share = mod_cols // peers
    mod_wide = -(-mod_share // 128) * 128
    small_lanes = FREQ + D + 128
    small_t = jnp.pad(
        small_weights.astype(jnp.bfloat16).T, ((0, 0), (0, small_lanes - small_rows))
    )
    mod_blocks = jnp.pad(
        low_mod.reshape(mod_rows, frame_groups, 2, 2, mod_share).transpose(3, 2, 1, 0, 4),
        ((0, 0),) * 4 + ((0, mod_wide - mod_share),),
    )
    small_full, features_placed, pre_one, pre_two, w_qkv, end_rows, mod_parts = front_block(
        small_t, time_features(level_eff), mod_blocks, attn_low[:3], 4
    )
    w_qkv = w_qkv.reshape(3, D, width_local)
    w_out = lax.all_gather(attn_low[3], "frames", axis=0, tiled=True)
    w_up = lax.all_gather(mlp_low[0], "frames", axis=0, tiled=True)
    w_down = lax.all_gather(mlp_low[1], "frames", axis=0, tiled=True)
    features_placed = features_placed.reshape(frames_total, FREQ)
    first_placed = jax.nn.silu(pre_one)
    pre_two_t = pre_two.T
    first_col = (device * lax.axis_size("mp") + mp_index) * small_cols
    pre_one_own = lax.dynamic_slice_in_dim(pre_one, first_col, small_cols, 1).T
    cond_rows = jax.nn.silu(
        lax.dynamic_slice_in_dim(pre_two, device * mod_rows, mod_rows, 1)
    )
    cond_parts = jnp.concatenate([part.T for part in split_three(cond_rows)], axis=0)
    modulation = (
        mod_parts[..., :mod_share].transpose(4, 0, 3, 2, 1, 5).reshape(frame_count, 6 * D)
    )
    pieces = [
        modulation[:, None, piece_index * D : (piece_index + 1) * D] for piece_index in range(6)
    ]
    shift_one, scale_one, gate_one, shift_two, scale_two, gate_two = pieces
    inputs_low = inputs.astype(jnp.bfloat16)
    padding = ((0, 0), (0, 128 - P_SIZE))
    inputs_low = jnp.pad(inputs_low, padding)
    normed_one, hidden_half, queries, keys_wide, values_wide = proj_block(
        inputs_low,
        end_rows,
        jnp.stack([shift_one[:, 0], scale_one[:, 0]]),
        w_qkv,
        cosine_table,
        sine_table,
        turn_four,
        REACH,
        2,
    )
    heads_wide, log_totals = attn_fwd(queries, keys_wide, values_wide, clip_start)
    half = tok_count // 2
    own_frames = frame_count // 2

    def half_of(array, dim=0):
        size = array.shape[dim] // 2
        return lax.dynamic_slice_in_dim(array, mp_index * size, size, dim)

    token_weight = jnp.repeat(noised, TPF) / (TPF * P_SIZE)
    grad_scale = 1.0 / jnp.maximum(noised_count, 1.0)
    head_lanes = ((0, 0), (P_SIZE, 128 - 2 * P_SIZE))
    mod_mid = jnp.stack(
        [half_of(piece[:, 0]) for piece in (gate_one, shift_two, scale_two, gate_two)]
    )
    d_mixed, d_shaped_one, d_mod_mid, loss_parts, grad_up, grad_rest = mid_block(
        heads_wide,
        w_out,
        hidden_half,
        mod_mid,
        jnp.pad(half_of(noise_patches), head_lanes),
        jnp.pad(jnp.broadcast_to(half_of(token_weight)[:, None], (half, P_SIZE)), head_lanes),
        end_rows,
        grad_scale.reshape(1),
        w_up,
        w_down,
        TP_AXIS,
        0,
    )
    sum_up = lax.psum_scatter(grad_up, "frames", scatter_dimension=0, tiled=True)
    sum_rest = lax.psum_scatter(grad_rest, "frames", scatter_dimension=0, tiled=True)
    d_queries, keys_grad_wide, values_grad_wide = attn_bwd(
        queries, keys_wide, values_wide, d_mixed, heads_wide, log_totals, clip_start
    )
    d_queries, sum_up = lax.optimization_barrier((d_queries, sum_up))
    grad_qkv, grad_in, d_first_mods = tail_block(
        d_queries,
        normed_one,
        w_qkv,
        cosine_table,
        sine_table,
        turn_four,
        hidden_half,
        half_of(scale_one[:, 0]),
        d_shaped_one,
        half_of(inputs_low),
        keys_grad_wide,
        values_grad_wide,
        1,
    )
    d_first_mods, sum_rest = lax.optimization_barrier((d_first_mods, sum_rest))
    def by_place(array, dim):
        shape = array.shape
        size = shape[dim] // (4 * frame_groups)
        split = array.reshape(shape[:dim] + (frame_groups, 2, 2, size) + shape[dim + 1 :])
        order = list(range(split.ndim))
        order[dim], order[dim + 2] = dim + 2, dim
        return split.transpose(order)

    in_columns = by_place(grad_in.T, 0).reshape(2, 2, D // 4, 128).astype(jnp.bfloat16)
    d_mods = jnp.stack(
        [
            jnp.concatenate([d_first_mods[0], d_first_mods[1], d_mod_mid[0]], axis=1),
            jnp.concatenate([d_mod_mid[1], d_mod_mid[2], d_mod_mid[3]], axis=1),
        ]
    )
    sum_qkv, sum_in, sum_mod, d_cond_rows = last_block(
        grad_qkv, in_columns, d_mods, cond_parts, low_mod, loss_parts, 3
    )
    loss_sum = jnp.sum(d_cond_rows[:, :, :, mod_rows : mod_rows + 3, 0].astype(jnp.float32))
    d_cond_t = (
        d_cond_rows[:, :, :, :mod_rows, :].transpose(2, 1, 0, 3, 4).reshape(D, frames_total)
    ).astype(jnp.float32)
    d_pre_two = jax.vjp(jax.nn.silu, pre_two_t)[1](d_cond_t)[0]
    d_pre_own = lax.dynamic_slice_in_dim(d_pre_two, first_col, small_cols, 0)
    grad_second = jnp.einsum("fi,jf->ij", first_placed, d_pre_own, precision=HIGH)
    second_cols = lax.dynamic_slice_in_dim(
        small_full.reshape(D, small_lanes), FREQ + first_col, small_cols, 1
    ).astype(jnp.float32)
    d_first = jnp.einsum("kf,kj->jf", d_pre_two, second_cols, precision=HIGH)
    d_pre_one = jax.vjp(jax.nn.silu, pre_one_own)[1](d_first)[0]
    grad_first = jnp.einsum("fi,jf->ij", features_placed, d_pre_one, precision=HIGH)
    ff_cols = mlp_weights.shape[2]
    sum_rest = sum_rest.astype(jnp.float32)
    sum_mlp = jnp.stack([sum_up.astype(jnp.float32), sum_rest[:, :ff_cols]])
    sum_attn = jnp.stack(
        [sum_qkv[0], sum_qkv[1], sum_qkv[2]]
        + [sum_rest[:, ff_cols : ff_cols + width_local]]
    )
    head_first = ff_cols + width_local
    head_part = sum_rest[:, head_first + P_SIZE : head_first + 2 * P_SIZE]
    sum_head = head_part + lax.ppermute(head_part, "mp", [(0, 1), (1, 0)])
    sum_ends = half_of(jnp.concatenate([sum_in[:, :P_SIZE], sum_head], axis=1).T, 1)
    sum_small = jnp.concatenate([grad_first, grad_second, sum_ends], axis=0)
    learning_rate = 0.5 * math.sqrt(tokens_total * P_SIZE / D)
    attn_new, attn_moment_new, attn_average_new, attn_copy = update(
        attn_weights, sum_attn, attn_moment, attn_average, learning_rate
    )
    mlp_new, mlp_moment_new, mlp_average_new, mlp_copy = update(
        mlp_weights, sum_mlp, mlp_moment, mlp_average, learning_rate
    )
    mod_new, mod_moment_new, mod_average_new, mod_copy = update(
        mod_weight, sum_mod, mod_moment, mod_average, learning_rate
    )
    small_new, small_moment_new, small_average_new, small_copy = update(
        small_weights, sum_small, small_moment, small_average, learning_rate
    )
    return (
        loss_sum,
        noised_count,
        attn_new,
        attn_moment_new,
        attn_average_new,
        attn_copy,
        mlp_new,
        mlp_moment_new,
        mlp_average_new,
        mlp_copy,
        mod_new,
        mod_moment_new,
        mod_average_new,
        mod_copy,
        small_new,
        small_moment_new,
        small_average_new,
        small_copy,
    )


def solution(mesh):
    return jax.shard_map(
        per_device,
        mesh=mesh,
        in_specs=(
            P("frames", None),
            P("frames", None),
            P("frames"),
            P(),
            P(),
            P(None, "frames", "mp"),
            P(None, "frames", "mp"),
            P("frames", "mp"),
            P(None, ("frames", "mp")),
            P(None, "frames", "mp"),
            P(None, "frames", "mp"),
            P("frames", "mp"),
            P(None, ("frames", "mp")),
            P(None, "frames", "mp"),
            P(None, "frames", "mp"),
            P("frames", "mp"),
            P(None, ("frames", "mp")),
        ),
        out_specs=(
            P(),
            P(),
            P(None, "frames", "mp"),
            P(None, "frames", "mp"),
            P(None, "frames", "mp"),
            P(None, "frames", "mp"),
            P(None, "frames", "mp"),
            P(None, "frames", "mp"),
            P(None, "frames", "mp"),
            P(None, "frames", "mp"),
            P("frames", "mp"),
            P("frames", "mp"),
            P("frames", "mp"),
            P("frames", "mp"),
            P(None, ("frames", "mp")),
            P(None, ("frames", "mp")),
            P(None, ("frames", "mp")),
            P(None, ("frames", "mp")),
        ),
        check_vma=False,
    )
```

```python
import functools
import math

import jax
import jax.numpy as jnp
import numpy as np
from jax import lax
from jax.experimental import pallas as pl
from jax.experimental.pallas import tpu as pltpu
from jax.sharding import PartitionSpec as P

D = 1024
HD = 64
CH = 4
FREQ = 256
GRID = 16
P_SIZE = 16
TPF = 64
REACH = 4


HIGH = lax.Precision.HIGHEST
EPSILON = 1e-06
MOMENTUM = 0.5
EMA_DECAY = 0.5
TP_AXIS = "mp"


def rotation_matrix(head_width):
    groups = [head_width // 4, 3 * head_width // 8, 3 * head_width // 8]
    rotation = np.zeros((head_width, head_width), np.float32)
    offset = 0
    for group_size in groups:
        half_size = group_size // 2
        for pair_index in range(half_size):
            rotation[offset + half_size + pair_index, offset + pair_index] = -1.0
            rotation[offset + pair_index, offset + half_size + pair_index] = 1.0
        offset += group_size
    return rotation


def turn_phases(positions, group_size):
    half_size = group_size // 2
    frequency = 10000.0 ** (-np.arange(half_size, dtype=np.float32) / half_size)
    phases = positions[:, None] * frequency.astype(np.float32)[None, :]
    return [phases, phases]


def turn_table(frame_ref, patch_ref, first, count):
    lanes = lax.broadcasted_iota(jnp.int32, (1, patch_ref.shape[1]), 1)
    by_frame = lax.rem(lanes, HD) < HD // 4
    rows = [
        jnp.where(by_frame, frame_ref[pl.ds(first + k, 1), :], patch_ref[...])
        for k in range(count)
    ]
    return jnp.concatenate(rows, axis=0)


def clip_positions(clip_ids):
    frame_index = jnp.arange(clip_ids.shape[0], dtype=jnp.int32)
    starts_here = jnp.concatenate([jnp.ones((1,), bool), clip_ids[1:] != clip_ids[:-1]])
    clip_start = lax.cummax(jnp.where(starts_here, frame_index, 0), axis=0)
    return frame_index - clip_start


def patchify(frame_data):
    frame_total = frame_data.shape[0]
    patch_side = GRID // 2
    shaped = frame_data.reshape(frame_total, CH, patch_side, 2, patch_side, 2)
    return shaped.transpose(0, 2, 4, 1, 3, 5).reshape(frame_total * patch_side * patch_side, CH * 4)


def layer_norm(vector):
    row_mean = jnp.mean(vector, axis=-1, keepdims=True)
    centred = vector - row_mean
    variance = jnp.mean(centred * centred, axis=-1, keepdims=True)
    return centred * lax.rsqrt(variance + EPSILON)


def modulate_local(shaped, shift_rows, scale_rows):
    return layer_norm(shaped) * (1.0 + scale_rows) + shift_rows


def time_features(level_eff):
    half_size = FREQ // 2
    frequency = jnp.exp(-math.log(10000.0) * jnp.arange(half_size, dtype=jnp.float32) / half_size)
    phases = (level_eff * 1000.0)[:, None] * frequency[None, :]
    return jnp.concatenate([jnp.cos(phases), jnp.sin(phases)], axis=1)


NT=(((1,),(1,)),((),()))
NN=(((1,),(0,)),((),()))

def dotf(a,b,dims=NN):
    return lax.dot_general(a,b,dims,preferred_element_type=jnp.float32)

def split_pair(xT):
    r=lax.broadcasted_iota(jnp.int32,xT.shape,0)
    z=jnp.zeros_like(xT)
    return jnp.where(r<HD,xT,z), jnp.where(r<HD,z,xT)

def keep_of(t,TK,TQ,cs,qf):
    kf=lax.broadcasted_iota(jnp.int32,(TK,TQ),0)//TPF+t*(TK//TPF)
    return (kf>=cs)&(kf<=qf)

def fwd_kernel(lo_ref,mid_ref,hi_ref,q_ref,k_ref,v_ref,cs_ref,o_ref,lse_ref,vT,*,TQ,TK,W0,NQ):
    KS=k_ref.shape[0]
    def tr(i,_):
        s=pl.multiple_of(i*TK,TK)
        vT[:,pl.ds(s,TK)]=v_ref[pl.ds(s,TK),:].T
        return 0
    lax.fori_loop(lo_ref[0],KS//TK,tr,0)
    def qtile(j,_):
        qs=pl.multiple_of(j*TQ,TQ)
        qT=(q_ref[pl.ds(qs,TQ),:].T)*jnp.bfloat16(0.125)
        qA,qB=split_pair(qT)
        cs=cs_ref[0:1,pl.ds(qs,TQ)]
        qf=lax.broadcasted_iota(jnp.int32,(1,TQ),1)//TPF+(W0+j*(TQ//TPF))
        def step(t,carry,masked):
            ks=pl.multiple_of(t*TK,TK)
            kt=k_ref[pl.ds(ks,TK),:]
            out=[]
            if masked: keep=keep_of(t,TK,TQ,cs,qf)
            ones=jnp.ones((16,TK),jnp.bfloat16)
            both=[dotf(kt,qh) for qh in (qA,qB)]
            for h,(s,(m,l,o)) in enumerate(zip(both,carry)):
                if masked: s=jnp.where(keep,s,-1e30)
                mn=jnp.maximum(m,jnp.max(s,axis=0,keepdims=True))
                a=jnp.exp(m-mn)
                p=jnp.exp(s-mn)
                vh=jnp.concatenate([vT[h*HD:(h+1)*HD,pl.ds(ks,TK)],ones],axis=0)
                ov=dotf(vh,p.astype(jnp.bfloat16))
                l=l*a+ov[HD:HD+1]
                o=o*a+ov[:HD]
                out.append((mn,l,o))
            return tuple(out)
        init=tuple((jnp.full((1,TQ),-1e29,jnp.float32),jnp.zeros((1,TQ),jnp.float32),jnp.zeros((HD,TQ),jnp.float32)) for _ in range(2))
        c=lax.fori_loop(lo_ref[j],mid_ref[j],lambda t,c:step(t,c,True),init)
        c=lax.fori_loop(mid_ref[j],hi_ref[j],lambda t,c:step(t,c,False),c)
        c=lax.fori_loop(hi_ref[j],(W0*TPF+(j+1)*TQ+TK-1)//TK,lambda t,c:step(t,c,True),c)
        oT=jnp.concatenate([c[0][2]/c[0][1],c[1][2]/c[1][1]],axis=0)
        o_ref[pl.ds(qs,TQ),:]=oT.T.astype(o_ref.dtype)
        lse_ref[0,0:1,pl.ds(qs,TQ)]=c[0][0]+jnp.log(c[0][1])
        lse_ref[0,1:2,pl.ds(qs,TQ)]=c[1][0]+jnp.log(c[1][1])
        return 0
    lax.fori_loop(0,NQ,qtile,0)

def tile_bounds(cs_rel,TQ,TK,W0,NQ):
    fq=TQ//TPF; fk=TK//TPF
    j=jnp.arange(NQ)
    first=cs_rel[::fq]; last=cs_rel[fq-1::fq]
    lo=first//fk
    dg=(W0+j*fq+1)//fk
    mid=jnp.minimum((last+fk-1)//fk,dg)
    mid=jnp.maximum(mid,lo)
    hi=jnp.maximum(dg,mid)
    return lo.astype(jnp.int32),mid.astype(jnp.int32),hi.astype(jnp.int32)

def attn_fwd(q,k,v,cs_rel,TQ=512,TK=512):
    T,Wd=q.shape; KS=k.shape[0]; P=Wd//128
    W0=(KS-T)//TPF; NQ=T//TQ
    lo,mid,hi=tile_bounds(cs_rel,TQ,TK,W0,NQ)
    cs_tok=jnp.broadcast_to(jnp.repeat(cs_rel,TPF)[None,:],(8,T)).astype(jnp.int32)
    return pl.pallas_call(
        functools.partial(fwd_kernel,TQ=TQ,TK=TK,W0=W0,NQ=NQ),
        grid_spec=pltpu.PrefetchScalarGridSpec(num_scalar_prefetch=3,grid=(P,),
            in_specs=[pl.BlockSpec((T,128),lambda p,*_:(0,p)),pl.BlockSpec((KS,128),lambda p,*_:(0,p)),pl.BlockSpec((KS,128),lambda p,*_:(0,p)),pl.BlockSpec((8,T),lambda p,*_:(0,0))],
            out_specs=[pl.BlockSpec((T,128),lambda p,*_:(0,p)),pl.BlockSpec((1,8,T),lambda p,*_:(p,0,0))],
            scratch_shapes=[pltpu.VMEM((128,KS),jnp.bfloat16)]),
        out_shape=[jax.ShapeDtypeStruct((T,Wd),jnp.float32),jax.ShapeDtypeStruct((P,8,T),jnp.float32)],
        compiler_params=pltpu.CompilerParams(vmem_limit_bytes=48<<20),
        cost_estimate=pl.CostEstimate(flops=10**11,bytes_accessed=2*10**7,transcendentals=3*10**7),
        name="attn_forward",
    )(lo,mid,hi,q,k,v,cs_tok)

def bwd_kernel(lo_ref,mid_ref,hi_ref,q_ref,k_ref,v_ref,do_ref,o_ref,lse_ref,cs_ref,dq_ref,dk_ref,dv_ref,kT,dkT,dvT,*,TQ,TK,W0,NQ):
    KS=k_ref.shape[0]
    def tr(i,_):
        s=pl.multiple_of(i*TK,TK)
        kT[:,pl.ds(s,TK)]=k_ref[pl.ds(s,TK),:].T
        return 0
    lax.fori_loop(lo_ref[0],KS//TK,tr,0)
    dkT[...]=jnp.zeros_like(dkT); dvT[...]=jnp.zeros_like(dvT)
    def qtile(j,_):
        qs=pl.multiple_of(j*TQ,TQ)
        qT=(q_ref[pl.ds(qs,TQ),:].T)*jnp.bfloat16(0.125)
        qh=split_pair(qT)
        doT=do_ref[pl.ds(qs,TQ),:].T
        doh=split_pair(doT)
        oT=o_ref[pl.ds(qs,TQ),:].T
        prod=oT*doT.astype(jnp.float32)
        delta=(jnp.sum(prod[:HD],axis=0,keepdims=True),jnp.sum(prod[HD:],axis=0,keepdims=True))
        lse=(lse_ref[0,0:1,pl.ds(qs,TQ)],lse_ref[0,1:2,pl.ds(qs,TQ)])
        cs=cs_ref[0:1,pl.ds(qs,TQ)]
        qf=lax.broadcasted_iota(jnp.int32,(1,TQ),1)//TPF+(W0+j*(TQ//TPF))
        def step(t,carry,masked):
            ks=pl.multiple_of(t*TK,TK)
            kt=k_ref[pl.ds(ks,TK),:]; vt=v_ref[pl.ds(ks,TK),:]
            out=[]
            if masked: keep=keep_of(t,TK,TQ,cs,qf)
            for h in range(2):
                r=slice(h*HD,(h+1)*HD)
                s=dotf(kt,qh[h])
                p=jnp.exp(s-lse[h])
                if masked: p=jnp.where(keep,p,0.0)
                dp=dotf(vt,doh[h])
                ds=(p*(dp-delta[h])).astype(jnp.bfloat16)
                pb=p.astype(jnp.bfloat16)
                dvT[r,pl.ds(ks,TK)]+=dotf(doT[r],pb,NT)
                dkT[r,pl.ds(ks,TK)]+=dotf(qT[r],ds,NT)
                out.append(carry[h]+dotf(kT[r,pl.ds(ks,TK)],ds))
            return tuple(out)
        init=(jnp.zeros((HD,TQ),jnp.float32),)*2
        c=lax.fori_loop(lo_ref[j],mid_ref[j],lambda t,c:step(t,c,True),init)
        c=lax.fori_loop(mid_ref[j],hi_ref[j],lambda t,c:step(t,c,False),c)
        c=lax.fori_loop(hi_ref[j],(W0*TPF+(j+1)*TQ+TK-1)//TK,lambda t,c:step(t,c,True),c)
        dq_ref[pl.ds(qs,TQ),:]=(jnp.concatenate(c,axis=0)*0.125).T
        return 0
    lax.fori_loop(0,NQ,qtile,0)
    def back(i,_):
        s=pl.multiple_of(i*TK,TK)
        dk_ref[pl.ds(s,TK),:]=dkT[:,pl.ds(s,TK)].T.astype(dk_ref.dtype)
        dv_ref[pl.ds(s,TK),:]=dvT[:,pl.ds(s,TK)].T.astype(dv_ref.dtype)
        return 0
    lax.fori_loop(0,KS//TK,back,0)

def attn_bwd(q,k,v,do,o,lse,cs_rel,TQ=512,TK=512,out_dt=jnp.bfloat16):
    T,Wd=q.shape; KS=k.shape[0]; P=Wd//128
    W0=(KS-T)//TPF; NQ=T//TQ
    lo,mid,hi=tile_bounds(cs_rel,TQ,TK,W0,NQ)
    cs_tok=jnp.broadcast_to(jnp.repeat(cs_rel,TPF)[None,:],(8,T)).astype(jnp.int32)
    tb=pl.BlockSpec((T,128),lambda p,*_:(0,p)); kb=pl.BlockSpec((KS,128),lambda p,*_:(0,p))
    return pl.pallas_call(
        functools.partial(bwd_kernel,TQ=TQ,TK=TK,W0=W0,NQ=NQ),
        grid_spec=pltpu.PrefetchScalarGridSpec(num_scalar_prefetch=3,grid=(P,),
            in_specs=[tb,kb,kb,tb,tb,pl.BlockSpec((1,8,T),lambda p,*_:(p,0,0)),pl.BlockSpec((8,T),lambda p,*_:(0,0))],
            out_specs=[tb,kb,kb],
            scratch_shapes=[pltpu.VMEM((128,KS),jnp.bfloat16),pltpu.VMEM((128,KS),jnp.float32),pltpu.VMEM((128,KS),jnp.float32)]),
        out_shape=[jax.ShapeDtypeStruct((T,Wd),jnp.float32),jax.ShapeDtypeStruct((KS,Wd),out_dt),jax.ShapeDtypeStruct((KS,Wd),out_dt)],
        compiler_params=pltpu.CompilerParams(vmem_limit_bytes=56<<20),
        cost_estimate=pl.CostEstimate(flops=2*10**11,bytes_accessed=5*10**7,transcendentals=3*10**7),
        name="attn_backward",
    )(lo,mid,hi,q,k,v,do,o,lse,cs_tok)


def update(weight, gradient, moment, average, learning_rate):
    moment_new = MOMENTUM * moment + gradient
    weight_new = weight - learning_rate * (gradient + MOMENTUM * moment_new)
    average_new = EMA_DECAY * average + (1.0 - EMA_DECAY) * weight_new
    return (weight_new, moment_new, average_new, weight_new.astype(jnp.bfloat16))


TN = (((0,), (0,)), ((), ()))


def norm_rows(v):
    centred = v - jnp.mean(v, axis=-1, keepdims=True)
    inverse = lax.rsqrt(jnp.mean(centred * centred, axis=-1, keepdims=True) + EPSILON)
    return centred * inverse, inverse


def norm_rows_back(grad, normed, inverse):
    return inverse * (
        grad
        - jnp.mean(grad, axis=-1, keepdims=True)
        - normed * jnp.mean(grad * normed, axis=-1, keepdims=True)
    )


def gelu_pair(x):
    c = math.sqrt(2.0 / math.pi)
    sq = x * x
    t = jnp.tanh(c * (x + 0.044715 * (x * sq)))
    half = 0.5 * (1.0 + t)
    return x * half, half + (0.5 * c) * x * (1.0 - t * t) * (1.0 + 0.134145 * sq)


def mid_kernel(
    o_ref, hid_ref, mod_ref, noise_ref, tw_ref, head_ref, gs_ref, wu_hbm, wd_hbm, wa_hbm,
    dmix_ref, dx1_ref, dmod_ref, loss_ref, up_hbm, rest_hbm,
    wo_ref, wu_ref, wd_ref, att, x1, out, dx2, n2, n2t, act, dgl, dout, doutt, datt, datt_t,
    send_a, recv_a, send_c, recv_c, send_e, recv_e, stage, ghead_ref, go_ref, gh_t,
    wsem, gsem, ssem, rsem, *, tp,
):
    f = lax.axis_index("frames")
    h = lax.axis_index("mp")
    bf16 = jnp.bfloat16
    x_peer = {"mp": 1 - h}
    tp_peer = {"frames": f + 1 - 2 * lax.rem(f, 2)} if tp == "core" else x_peer
    half = hid_ref.shape[0]
    rows = 128
    chunks = half // rows
    width = hid_ref.shape[1]
    ff = wu_hbm.shape[1]
    e = o_ref.shape[1]
    ft = 512
    dt = 256

    weights = [
        pltpu.make_async_copy(wu_hbm, wu_ref, wsem.at[0]),
        pltpu.make_async_copy(wd_hbm, wd_ref, wsem.at[1]),
    ]
    load_out = pltpu.make_async_copy(wa_hbm.at[3], wo_ref, wsem.at[2])
    load_out.start()
    for w in weights:
        w.start()

    barrier = pltpu.get_barrier_semaphore()
    pl.semaphore_signal(barrier, inc=1, device_id=x_peer, device_id_type=pl.DeviceIdType.MESH)
    if tp == "core":
        pl.semaphore_signal(barrier, inc=1, device_id=tp_peer, device_id_type=pl.DeviceIdType.MESH)
    pl.semaphore_wait(barrier, 2 if tp == "core" else 1)

    def at(start, size):
        return pl.ds(pl.multiple_of(start, size), size)

    def copy(src, dst, phase, c, peer):
        return pltpu.make_async_remote_copy(
            src_ref=src, dst_ref=dst, send_sem=ssem.at[phase, c], recv_sem=rsem.at[phase, c],
            device_id=peer, device_id_type=pl.DeviceIdType.MESH,
        )

    def copy_a(c):
        return copy(send_a.at[at(c * rows, rows)], recv_a.at[at(c * rows, rows)], 0, c, x_peer)

    def copy_b(c):
        return copy(
            n2.at[at(c * 2 * rows, rows)], n2.at[at(c * 2 * rows + rows, rows)], 1, c, tp_peer
        )

    def copy_c(c):
        return copy(send_c.at[at(c * rows, rows)], recv_c.at[at(c * rows, rows)], 2, c, tp_peer)

    def copy_d(c):
        return copy(
            dout.at[at(c * 2 * rows, rows)], dout.at[at(c * 2 * rows + rows, rows)], 3, c, tp_peer
        )

    def copy_e(c):
        return copy(send_e.at[at(c * rows, rows)], recv_e.at[at(c * rows, rows)], 4, c, tp_peer)

    def copy_f(c):
        mine = datt.at[at(h * half + c * rows, rows)]
        return copy(mine, mine, 5, c, x_peer)

    load_out.wait()

    def phase_a(c, _):
        part = o_ref[at((1 - h) * half + c * rows, rows), :].astype(bf16)
        send_a[at(c * rows, rows), :] = dotf(part, wo_ref[...], NT).astype(bf16)
        copy_a(c).start()
        return 0

    lax.fori_loop(0, chunks, phase_a, 0)

    def phase_b(c, _):
        part = o_ref[at(h * half + c * rows, rows), :].astype(bf16)
        att[at(c * rows, rows), :] = dotf(part, wo_ref[...], NT)
        copy_a(c).wait_recv()
        for k in range(rows // TPF):
            r = at(c * rows + k * TPF, TPF)
            frame = pl.ds(c * (rows // TPF) + k, 1)
            a = att[r, :] + recv_a[r, :].astype(jnp.float32)
            att[r, :] = a
            v = hid_ref[r, :] + mod_ref[0, frame, :] * a
            x1[r, :] = v
            y, _inv = norm_rows(v)
            n2[at(c * 2 * rows + k * TPF, TPF), :] = (
                y * (1.0 + mod_ref[2, frame, :]) + mod_ref[1, frame, :]
            ).astype(bf16)
        copy_b(c).start()
        return 0

    lax.fori_loop(0, chunks, phase_b, 0)
    for w in weights:
        w.wait()

    def phase_c(c, _):
        copy_b(c).wait_recv()
        tok = at(c * 2 * rows, 2 * rows)
        n2t[:, tok] = n2[tok, :].T

        def up(i, _):
            cols = at(i * ft, ft)
            a, g = gelu_pair(dotf(n2[tok, :], wu_ref[:, cols]))
            act[tok, cols] = a.astype(bf16)
            dgl[tok, cols] = g.astype(bf16)
            return 0

        lax.fori_loop(0, ff // ft, up, 0)

        def down(i, _):
            cols = at(i * dt, dt)
            res = dotf(act[tok, :], wd_ref[cols, :], NT)
            out[at(c * rows, rows), cols] = res[:rows]
            send_c[at(c * rows, rows), cols] = res[rows:].astype(bf16)
            return 0

        lax.fori_loop(0, width // dt, down, 0)
        copy_c(c).start()
        return 0

    lax.fori_loop(0, chunks, phase_c, 0)

    ghead_ref[...] = jnp.zeros_like(ghead_ref)
    loss_ref[...] = jnp.zeros_like(loss_ref)

    def phase_d(c, _):
        copy_c(c).wait_recv()
        for k in range(rows // TPF):
            r = at(c * rows + k * TPF, TPF)
            frame = pl.ds(c * (rows // TPF) + k, 1)
            o = out[r, :] + recv_c[r, :].astype(jnp.float32)
            gate = mod_ref[3, frame, :]
            y, inv = norm_rows(x1[r, :] + gate * o)
            fn = y.astype(bf16)
            misfit = dotf(fn, head_ref[...], NT) - noise_ref[r, :]
            weighted = tw_ref[r, :] * misfit
            loss_ref[...] += weighted * misfit
            d_pred = (2.0 * gs_ref[0] * weighted).astype(bf16)
            ghead_ref[...] += dotf(d_pred, fn, TN)
            d_x2 = norm_rows_back(dotf(d_pred, head_ref[...]), y, inv)
            dx2[r, :] = d_x2
            dmod_ref[3, frame, :] = jnp.sum(d_x2 * o, axis=0, keepdims=True)
            dout[at(c * 2 * rows + k * TPF, TPF), :] = (gate * d_x2).astype(bf16)
        copy_d(c).start()
        return 0

    lax.fori_loop(0, chunks, phase_d, 0)

    def phase_e(c, _):
        copy_d(c).wait_recv()
        tok = at(c * 2 * rows, 2 * rows)
        doutt[:, tok] = dout[tok, :].T

        def down(i, _):
            cols = at(i * ft, ft)
            g = dotf(dout[tok, :], wd_ref[:, cols]) * dgl[tok, cols].astype(jnp.float32)
            dgl[tok, cols] = g.astype(bf16)
            return 0

        lax.fori_loop(0, ff // ft, down, 0)

        def up(i, _):
            cols = at(i * dt, dt)
            res = dotf(dgl[tok, :], wu_ref[cols, :], NT)
            out[at(c * rows, rows), cols] = res[:rows]
            send_e[at(c * rows, rows), cols] = res[rows:].astype(bf16)
            return 0

        lax.fori_loop(0, width // dt, up, 0)
        copy_e(c).start()
        return 0

    lax.fori_loop(0, chunks, phase_e, 0)

    def phase_f(c, _):
        copy_e(c).wait_recv()
        for k in range(rows // TPF):
            r = at(c * rows + k * TPF, TPF)
            frame = pl.ds(c * (rows // TPF) + k, 1)
            g = out[r, :] + recv_e[r, :].astype(jnp.float32)
            y, inv = norm_rows(x1[r, :])
            dmod_ref[1, frame, :] = jnp.sum(g, axis=0, keepdims=True)
            dmod_ref[2, frame, :] = jnp.sum(g * y, axis=0, keepdims=True)
            d_x1 = dx2[r, :] + norm_rows_back(g * (1.0 + mod_ref[2, frame, :]), y, inv)
            dx1_ref[r, :] = d_x1
            dmod_ref[0, frame, :] = jnp.sum(d_x1 * att[r, :], axis=0, keepdims=True)
            datt[at(h * half + c * rows + k * TPF, TPF), :] = (mod_ref[0, frame, :] * d_x1).astype(
                bf16
            )
        copy_f(c).start()
        return 0

    lax.fori_loop(0, chunks, phase_f, 0)

    def weight_grads(left, right, target):
        def put(slot, i):
            return pltpu.make_async_copy(
                stage.at[slot], target.at[at(i * dt, dt), pl.ds(0, ff)], gsem.at[slot]
            )

        def tile(i, _):
            slot = lax.rem(i, 2)

            @pl.when(i >= 2)
            def _():
                put(slot, i - 2).wait()

            def cols_of(j, _):
                cols = at(j * ft, ft)
                stage[slot, :, cols] = dotf(left[at(i * dt, dt), :], right[:, cols]).astype(bf16)
                return 0

            lax.fori_loop(0, ff // ft, cols_of, 0)
            put(slot, i).start()
            return 0

        lax.fori_loop(0, width // dt, tile, 0)
        for i in (width // dt - 2, width // dt - 1):
            put(i % 2, i).wait()

    weight_grads(n2t, dgl, up_hbm)
    weight_grads(doutt, act, rest_hbm)

    def own_mix(c, _):
        tok = at(h * half + c * rows, rows)
        datt_t[:, tok] = datt[tok, :].T
        dmix_ref[tok, :] = dotf(datt[tok, :], wo_ref[...]).astype(bf16)
        return 0

    lax.fori_loop(0, chunks, own_mix, 0)

    def phase_g(c, _):
        tok = at((1 - h) * half + c * rows, rows)
        theirs = datt.at[tok]
        copy(theirs, theirs, 5, c, x_peer).wait_recv()
        datt_t[:, tok] = datt[tok, :].T
        dmix_ref[tok, :] = dotf(datt[tok, :], wo_ref[...]).astype(bf16)
        return 0

    lax.fori_loop(0, chunks, phase_g, 0)

    def grad_out(i, _):
        d = at(i * dt, dt)
        go_ref[d, :] = dotf(datt_t[d, :], o_ref[...].astype(bf16)).astype(bf16)
        return 0

    lax.fori_loop(0, width // dt, grad_out, 0)
    gh_t[...] = ghead_ref[...].T.astype(bf16)
    ends = [
        pltpu.make_async_copy(go_ref, rest_hbm.at[:, pl.ds(ff, e)], gsem.at[2]),
        pltpu.make_async_copy(gh_t, rest_hbm.at[:, pl.ds(ff + e, 128)], gsem.at[3]),
    ]
    for one in ends:
        one.start()
    for one in ends:
        one.wait()
    def sent(c, _):
        for one in (copy_a, copy_b, copy_c, copy_d, copy_e, copy_f):
            one(c).wait_send()
        return 0

    lax.fori_loop(0, chunks, sent, 0)


def mid_block(o, hid, mod, noise, tw, head, gs, wu, wd, wa, tp, cid):
    tok, e = o.shape
    half, width = hid.shape
    ff = wu.shape[1]
    own_frames = half // TPF
    f32, bf16 = jnp.float32, jnp.bfloat16
    vm = pl.BlockSpec(memory_space=pltpu.VMEM)
    anym = pl.BlockSpec(memory_space=pl.ANY)
    V = pltpu.VMEM
    return pl.pallas_call(
        functools.partial(mid_kernel, tp=tp),
        in_specs=[vm] * 6 + [pl.BlockSpec(memory_space=pltpu.SMEM), anym, anym, anym],
        out_specs=[vm] * 4 + [anym] * 2,
        out_shape=[
            jax.ShapeDtypeStruct((tok, e), bf16),
            jax.ShapeDtypeStruct((half, width), f32),
            jax.ShapeDtypeStruct((4, own_frames, width), f32),
            jax.ShapeDtypeStruct((TPF, 128), f32),
            jax.ShapeDtypeStruct((width, ff), bf16),
            jax.ShapeDtypeStruct((width, ff + e + 128), bf16),
        ],
        scratch_shapes=[
            V((width, e), bf16), V((width, ff), bf16), V((width, ff), bf16),
            V((half, width), f32), V((half, width), f32), V((half, width), f32),
            V((half, width), f32),
            V((2 * half, width), bf16), V((width, 2 * half), bf16),
            V((2 * half, ff), bf16), V((2 * half, ff), bf16),
            V((2 * half, width), bf16), V((width, 2 * half), bf16),
            V((tok, width), bf16), V((width, tok), bf16),
            V((half, width), bf16), V((half, width), bf16),
            V((half, width), bf16), V((half, width), bf16),
            V((half, width), bf16), V((half, width), bf16),
            V((2, 256, ff), bf16), V((128, width), f32), V((width, e), bf16),
            V((width, 128), bf16),
            pltpu.SemaphoreType.DMA((3,)), pltpu.SemaphoreType.DMA((4,)),
            pltpu.SemaphoreType.DMA((6, half // 128)), pltpu.SemaphoreType.DMA((6, half // 128)),
        ],
        compiler_params=pltpu.CompilerParams(
            vmem_limit_bytes=62 << 20, collective_id=cid, has_side_effects=True
        ),
        cost_estimate=pl.CostEstimate(
            flops=4 * 10**10, bytes_accessed=3 * 10**7, transcendentals=2 * 10**6
        ),
        name="feed_forward",
    )(o, hid, mod, noise, tw, head, gs, wu, wd, wa)


def split_three(v):
    high = v.astype(jnp.bfloat16)
    left = v - high.astype(jnp.float32)
    middle = left.astype(jnp.bfloat16)
    return high, middle, (left - middle.astype(jnp.float32)).astype(jnp.bfloat16)


def turn_back(g, cosine, sine, rot):
    parts = split_three(g * sine)
    return (g * cosine + sum(dotf(p, rot, NT) for p in parts)).astype(jnp.bfloat16)


def tail_kernel(
    dq_ref, n1_ref, w_ref, fcos_ref, fsin_ref, pcos_ref, psin_ref, rot_ref, hid_ref, scale_ref, dx1_ref, inp_ref,
    dk_hbm, dv_hbm,
    gq_ref, gin_ref, dss_ref,
    own, near, yrecv, zrecv, n1t, dproj, send_x, recv_x, part,
    lsem, s_near, r_near, s_y, r_y, s_z, r_z, s_x, r_x,
):
    f = lax.axis_index("frames")
    h = lax.axis_index("mp")
    n = lax.axis_size("frames")
    core = lax.rem(f, 2)
    odd = lax.rem(lax.div(f, 2), 2)
    core_peer = {"frames": f + 1 - 2 * core}
    y_peer = {"frames": f + 2 - 4 * odd}
    before = {"frames": lax.rem(f - 4 + n, n)}
    after = {"frames": lax.rem(f + 4, n)}
    x_peer = {"mp": 1 - h}
    tok, e = dq_ref.shape
    width = n1_ref.shape[1]
    half = tok // 2
    rows = 256
    chunks = tok // rows
    f32, bf16 = jnp.float32, jnp.bfloat16
    MESH = pl.DeviceIdType.MESH
    sides = (dk_hbm, dv_hbm)
    share = width // n

    def at(start, size):
        return pl.ds(pl.multiple_of(start, size), size)

    loads = [
        pltpu.make_async_copy(
            sides[s].at[pl.ds(b * tok, tok)], own.at[s, j], lsem.at[s, j]
        )
        for s in range(2)
        for j, b in enumerate((4, 2, 0))
    ]
    for one in loads:
        one.start()

    barrier = pltpu.get_barrier_semaphore()
    for peer in (core_peer, y_peer, x_peer):
        pl.semaphore_signal(barrier, inc=1, device_id=peer, device_id_type=MESH)

    @pl.when(f >= 4)
    def _():
        pl.semaphore_signal(barrier, inc=1, device_id=before, device_id_type=MESH)

    @pl.when(f + 4 < n)
    def _():
        pl.semaphore_signal(barrier, inc=1, device_id=after, device_id_type=MESH)

    pl.semaphore_wait(barrier, 3 + jnp.where(f >= 4, 1, 0) + jnp.where(f + 4 < n, 1, 0))

    def rows_of(i):
        return lax.rem(i + (chunks // 2) * (1 - h), chunks) * rows

    def remote(src, dst, send, recv, peer):
        return pltpu.make_async_remote_copy(
            src_ref=src, dst_ref=dst, send_sem=send, recv_sem=recv, device_id=peer,
            device_id_type=MESH,
        )

    def near_copy(i, s, j):
        b = (3, 1)[j]
        return remote(
            sides[s].at[at(b * tok + rows_of(i), rows)],
            near.at[s, j, at(rows_of(i), rows)],
            s_near.at[s, j, i], r_near.at[s, j, i], core_peer,
        )

    def y_copy(i, s):
        r = at(rows_of(i), rows)
        return remote(own.at[s, 1, r], yrecv.at[s, r], s_y.at[s, i], r_y.at[s, i], y_peer)

    def z_copy(i, s):
        r = at(rows_of(i), rows)
        return remote(own.at[s, 2, r], zrecv.at[s, r], s_z.at[s, i], r_z.at[s, i], before)

    def x_copy(i):
        r = at(i * rows, rows)
        return remote(send_x.at[r], recv_x.at[r], s_x.at[i], r_x.at[i], x_peer)

    def start_near(i, _):
        for s in range(2):
            for j in range(2):
                near_copy(i, s, j).start()
        return 0

    lax.fori_loop(0, chunks, start_near, 0)

    @pl.when(f + 4 >= n)
    def _():
        zrecv[...] = jnp.zeros_like(zrecv)

    for one in loads:
        one.wait()
    low_core = core == 0

    def combine(i, _):
        r = at(rows_of(i), rows)
        for s in range(2):
            for j in range(2):
                near_copy(i, s, j).wait_recv()
            n3 = near[s, 0, r, :].astype(f32)
            n1_ = near[s, 1, r, :].astype(f32)
            own[s, 1, r, :] = (
                own[s, 1, r, :].astype(f32) + jnp.where(low_core, n1_, n3)
            ).astype(bf16)
            y_copy(i, s).start()
            own[s, 2, r, :] = (
                own[s, 2, r, :].astype(f32) + jnp.where(low_core, 0.0, n1_)
            ).astype(bf16)

            @pl.when((odd == 0) & (f >= 4))
            def _():
                z_copy(i, s).start()

        return 0

    lax.fori_loop(0, chunks, combine, 0)

    def turned(g, r, first, k):
        cosine = turn_table(fcos_ref, pcos_ref, first, rows // TPF)
        sine = turn_table(fsin_ref, psin_ref, first, rows // TPF)
        for b in range(e // 256):
            cols = slice(b * 256, (b + 1) * 256)
            dproj[k, r, cols] = turn_back(
                g[:, cols], cosine, sine, rot_ref[...]
            )

    def relay(i, _):
        r = at(rows_of(i), rows)
        turned(dq_ref[r, :], r, lax.div(rows_of(i), TPF), 0)
        n1t[:, r] = n1_ref[r, :].T

        @pl.when(odd == 1)
        def _():
            for s in range(2):
                y_copy(i, s).wait_recv()

                @pl.when(f >= 4)
                def _():
                    own[s, 2, r, :] = (
                        own[s, 2, r, :].astype(f32) + yrecv[s, r, :].astype(f32)
                    ).astype(bf16)
                    z_copy(i, s).start()

        return 0

    lax.fori_loop(0, chunks, relay, 0)

    def grads(k):
        def tile(i, _):
            res = dotf(n1t[at(i * 256, 256), :], dproj[k]).astype(bf16)
            for q in range(256 // share):
                j = i * (256 // share // 4) + q // 4
                gq_ref[q % 2, (q // 2) % 2, k, at(j * share, share), :] = res[
                    q * share : (q + 1) * share
                ]
            return 0

        lax.fori_loop(0, width // 256, tile, 0)

    grads(0)

    def finish(i, _):
        r = at(rows_of(i), rows)
        for s in range(2):

            @pl.when(odd == 0)
            def _():
                y_copy(i, s).wait_recv()

            @pl.when(f + 4 < n)
            def _():
                z_copy(i, s).wait_recv()

            total = (
                own[s, 0, r, :].astype(f32)
                + jnp.where(low_core, near[s, 0, r, :].astype(f32), 0.0)
                + jnp.where(odd == 0, yrecv[s, r, :].astype(f32), 0.0)
                + zrecv[s, r, :].astype(f32)
            )
            if s == 0:
                turned(total, r, lax.div(rows_of(i), TPF), 1)
            else:
                dproj[2, r, :] = total.astype(bf16)

        def cols_of(j, _):
            cols = at(j * 256, 256)
            res = sum(dotf(dproj[k, r, :], w_ref[k, cols, :], NT) for k in range(3))

            @pl.when(i < chunks // 2)
            def _():
                send_x[at(i * rows, rows), cols] = res.astype(bf16)

            @pl.when(i >= chunks // 2)
            def _():
                part[at((i - chunks // 2) * rows, rows), cols] = res

            return 0

        lax.fori_loop(0, width // 256, cols_of, 0)

        @pl.when(i < chunks // 2)
        def _():
            x_copy(i).start()

        return 0

    lax.fori_loop(0, chunks, finish, 0)
    grads(1)
    grads(2)
    gin_ref[...] = jnp.zeros_like(gin_ref)

    def norm_back(i, _):
        x_copy(i).wait_recv()
        for k in range(rows // TPF):
            r = at(i * rows + k * TPF, TPF)
            frame = pl.ds(i * (rows // TPF) + k, 1)
            g = part[r, :] + recv_x[r, :].astype(f32)
            y, inv = norm_rows(hid_ref[r, :])
            dss_ref[0, frame, :] = jnp.sum(g, axis=0, keepdims=True)
            dss_ref[1, frame, :] = jnp.sum(g * y, axis=0, keepdims=True)
            d_hid = dx1_ref[r, :] + norm_rows_back(g * (1.0 + scale_ref[frame, :]), y, inv)
            gin_ref[...] += dotf(inp_ref[r, :], d_hid.astype(bf16), TN)
        return 0

    lax.fori_loop(0, half // rows, norm_back, 0)

    def sent(i, _):
        for s in range(2):
            for j in range(2):
                near_copy(i, s, j).wait_send()
            y_copy(i, s).wait_send()

            @pl.when(f >= 4)
            def _():
                z_copy(i, s).wait_send()

        @pl.when(i < chunks // 2)
        def _():
            x_copy(i).wait_send()

        return 0

    lax.fori_loop(0, chunks, sent, 0)


def tail_block(dq, n1, w, tables, rot, hid, scale, dx1, inp, dk, dv, cid):
    tok, e = dq.shape
    width = n1.shape[1]
    half = tok // 2
    f32, bf16 = jnp.float32, jnp.bfloat16
    vm = pl.BlockSpec(memory_space=pltpu.VMEM)
    anym = pl.BlockSpec(memory_space=pl.ANY)
    V = pltpu.VMEM
    D_ = pltpu.SemaphoreType.DMA
    chunks = tok // 256
    return pl.pallas_call(
        tail_kernel,
        in_specs=[vm] * 12 + [anym] * 2,
        out_specs=[vm] * 3,
        out_shape=[
            jax.ShapeDtypeStruct((2, 2, 3, width // 4, e), bf16),
            jax.ShapeDtypeStruct((128, width), f32),
            jax.ShapeDtypeStruct((2, half // TPF, width), f32),
        ],
        scratch_shapes=[
            V((2, 3, tok, e), bf16), V((2, 2, tok, e), bf16), V((2, tok, e), bf16),
            V((2, tok, e), bf16), V((width, tok), bf16), V((3, tok, e), bf16),
            V((half, width), bf16), V((half, width), bf16), V((half, width), f32),
            D_((2, 3)), D_((2, 2, chunks)), D_((2, 2, chunks)), D_((2, chunks)), D_((2, chunks)),
            D_((2, chunks)), D_((2, chunks)), D_((chunks // 2,)), D_((chunks // 2,)),
        ],
        compiler_params=pltpu.CompilerParams(
            vmem_limit_bytes=56 << 20, collective_id=cid, has_side_effects=True
        ),
        cost_estimate=pl.CostEstimate(
            flops=2 * 10**10, bytes_accessed=3 * 10**7, transcendentals=0
        ),
        name="projection_backward",
    )(dq, n1, w, *tables, rot, hid, scale, dx1, inp, dk, dv)


def proj_kernel(
    inp_ref, win_ref, mod_ref, w_ref, fcos_ref, fsin_ref, pcos_ref, psin_ref, rot_ref,
    n1_ref, hid_ref, q_ref, k_hbm, v_hbm,
    kv, wr,
    lsem, s_core, r_core, s_y, r_y, s_z, r_z,
):
    f = lax.axis_index("frames")
    h = lax.axis_index("mp")
    n = lax.axis_size("frames")
    core = lax.rem(f, 2)
    odd = lax.rem(lax.div(f, 2), 2)
    core_peer = {"frames": f + 1 - 2 * core}
    y_peer = {"frames": f + 2 - 4 * odd}
    before = {"frames": lax.rem(f - 4 + n, n)}
    after = {"frames": lax.rem(f + 4, n)}
    tok, width = n1_ref.shape
    e = q_ref.shape[1]
    half = tok // 2
    rows = 256
    chunks = tok // rows
    bf16 = jnp.bfloat16
    MESH = pl.DeviceIdType.MESH
    sides = (k_hbm, v_hbm)
    has_z = f >= 4
    has_next = f + 4 < n
    has_y = has_z | (odd == 1)

    def at(start, size):
        return pl.ds(pl.multiple_of(start, size), size)

    barrier = pltpu.get_barrier_semaphore()
    for peer in (core_peer, y_peer):
        pl.semaphore_signal(barrier, inc=1, device_id=peer, device_id_type=MESH)

    @pl.when(has_z)
    def _():
        pl.semaphore_signal(barrier, inc=1, device_id=before, device_id_type=MESH)

    @pl.when(has_next)
    def _():
        pl.semaphore_signal(barrier, inc=1, device_id=after, device_id_type=MESH)

    def embed(i, _):
        for k in range(2):
            r = at(i * 2 * TPF + k * TPF, TPF)
            frame = pl.ds(i * 2 + k, 1)
            v = dotf(inp_ref[r, :], win_ref[...])
            y, _inv = norm_rows(v)
            n1_ref[r, :] = (y * (1.0 + mod_ref[1, frame, :]) + mod_ref[0, frame, :]).astype(bf16)

            @pl.when(lax.div(i * 2 * TPF, half) == h)
            def _():
                hid_ref[at(lax.rem(i * 2 * TPF, half) + k * TPF, TPF), :] = v

        return 0

    lax.fori_loop(0, tok // (2 * TPF), embed, 0)

    def turn_weights(i, _):
        d = at(i * 256, 256)
        for k in range(2):
            for b in range(e // 256):
                cols = slice(b * 256, (b + 1) * 256)
                wr[k, d, cols] = dotf(w_ref[k, d, cols], rot_ref[...]).astype(bf16)
        return 0

    lax.fori_loop(0, width // 256, turn_weights, 0)
    pl.semaphore_wait(barrier, 2 + jnp.where(has_z, 1, 0) + jnp.where(has_next, 1, 0))

    def remote(src, dst, send, recv, peer):
        return pltpu.make_async_remote_copy(
            src_ref=src, dst_ref=dst, send_sem=send, recv_sem=recv, device_id=peer,
            device_id_type=MESH,
        )

    def block(s, b, i):
        return sides[s].at[at(b * tok + i * rows, rows)]

    def mine(s, i):
        return kv.at[s, at(i * rows, rows)]

    def keep(s, i):
        return pltpu.make_async_copy(mine(s, i), block(s, 4, i), lsem.at[s, i])

    def z_copy(s, i):
        return remote(mine(s, i), block(s, 0, i), s_z.at[s, i], r_z.at[s, i], after)

    def y_copy(s, i, src):
        return remote(src, block(s, 2, i), s_y.at[s, i], r_y.at[s, i], y_peer)

    def core_copy(s, i, j, src):
        return remote(
            src, block(s, (3, 1)[j], i), s_core.at[j, s, i], r_core.at[j, s, i], core_peer
        )

    def rotated(r, i, k):
        frames = rows // TPF
        cosine = turn_table(fcos_ref, pcos_ref, i * frames, frames)
        sine = turn_table(fsin_ref, psin_ref, i * frames, frames)
        parts = []
        for b in range(e // 256):
            cols = slice(b * 256, (b + 1) * 256)
            plain = dotf(n1_ref[r, :], w_ref[k, :, cols])
            turned = dotf(n1_ref[r, :], wr[k, :, cols])
            parts.append((plain * cosine + turned * sine).astype(bf16))
        return parts

    def own_chunk(i, _):
        r = at(i * rows, rows)
        for b, part in enumerate(rotated(r, i, 1)):
            kv[0, r, b * 256 : (b + 1) * 256] = part
        kv[1, r, :] = dotf(n1_ref[r, :], w_ref[2]).astype(bf16)
        for s in range(2):
            keep(s, i).start()

            @pl.when(has_next)
            def _():
                z_copy(s, i).start()

            @pl.when(odd == 0)
            def _():
                y_copy(s, i, mine(s, i)).start()

            @pl.when(core == 0)
            def _():
                core_copy(s, i, 0, mine(s, i)).start()

        return 0

    lax.fori_loop(0, chunks, own_chunk, 0)

    def queries(i, _):
        r = at(i * rows, rows)
        for b, part in enumerate(rotated(r, i, 0)):
            q_ref[r, b * 256 : (b + 1) * 256] = part
        return 0

    lax.fori_loop(0, chunks, queries, 0)

    def from_z(i, _):
        @pl.when(has_z)
        def _():
            for s in range(2):
                z_copy(s, i).wait_recv()

                @pl.when(odd == 1)
                def _():
                    y_copy(s, i, block(s, 0, i)).start()

                @pl.when(core == 1)
                def _():
                    core_copy(s, i, 1, block(s, 0, i)).start()

        return 0

    lax.fori_loop(0, chunks, from_z, 0)

    def from_y(i, _):
        @pl.when(has_y)
        def _():
            for s in range(2):
                y_copy(s, i, mine(s, i)).wait_recv()

                @pl.when(core == 1)
                def _():
                    core_copy(s, i, 0, block(s, 2, i)).start()

                @pl.when(core == 0)
                def _():
                    core_copy(s, i, 1, block(s, 2, i)).start()

        return 0

    lax.fori_loop(0, chunks, from_y, 0)

    def ended(i, _):
        for s in range(2):
            keep(s, i).wait()

            @pl.when((core == 1) | has_y)
            def _():
                core_copy(s, i, 0, mine(s, i)).wait_recv()

            @pl.when(((core == 1) & has_y) | has_z)
            def _():
                core_copy(s, i, 1, mine(s, i)).wait_recv()

            @pl.when(has_next)
            def _():
                z_copy(s, i).wait_send()

            @pl.when((odd == 0) | has_z)
            def _():
                y_copy(s, i, mine(s, i)).wait_send()

            @pl.when((core == 0) | has_y)
            def _():
                core_copy(s, i, 0, mine(s, i)).wait_send()

            @pl.when(((core == 0) & has_y) | has_z)
            def _():
                core_copy(s, i, 1, mine(s, i)).wait_send()

        return 0

    lax.fori_loop(0, chunks, ended, 0)


def proj_block(inp, win, mod, w, tables, rot, reach, cid):
    tok = inp.shape[0]
    width, e = w.shape[1:]
    f32, bf16 = jnp.float32, jnp.bfloat16
    vm = pl.BlockSpec(memory_space=pltpu.VMEM)
    anym = pl.BlockSpec(memory_space=pl.ANY)
    V = pltpu.VMEM
    D_ = pltpu.SemaphoreType.DMA
    chunks = tok // 256
    return pl.pallas_call(
        proj_kernel,
        in_specs=[vm] * 9,
        out_specs=[vm] * 3 + [anym] * 2,
        out_shape=[
            jax.ShapeDtypeStruct((tok, width), bf16),
            jax.ShapeDtypeStruct((tok // 2, width), f32),
            jax.ShapeDtypeStruct((tok, e), bf16),
            jax.ShapeDtypeStruct(((reach + 1) * tok, e), bf16),
            jax.ShapeDtypeStruct(((reach + 1) * tok, e), bf16),
        ],
        scratch_shapes=[
            V((2, tok, e), bf16), V((2, width, e), bf16),
            D_((2, chunks)), D_((2, 2, chunks)), D_((2, 2, chunks)), D_((2, chunks)),
            D_((2, chunks)), D_((2, chunks)), D_((2, chunks)),
        ],
        compiler_params=pltpu.CompilerParams(
            vmem_limit_bytes=48 << 20, collective_id=cid, has_side_effects=True
        ),
        cost_estimate=pl.CostEstimate(
            flops=6 * 10**10, bytes_accessed=3 * 10**7, transcendentals=0
        ),
        name="projection_forward",
    )(inp, win, mod, w, *tables, rot)


def last_kernel(
    g_hbm, gin_ref, dm_ref, cond_ref, wm_ref, loss_ref,
    sq_ref, sin_ref, smod_ref, dct_ref,
    g_own, g_in, near, near_in, side, side_in, far, far_in, ends, ends_peer, dm_peer, dm,
    dc_send, dc_peer,
    lsem, s_x, r_x, s_g, r_g, s_f, r_f, s_d, r_d, s_dz, r_dz,
):
    f = lax.axis_index("frames")
    h = lax.axis_index("mp")
    n = lax.axis_size("frames")
    nj = n // 4
    core = lax.rem(f, 2)
    y = lax.rem(lax.div(f, 2), 2)
    j = lax.div(f, 4)
    core_peer = {"frames": f + 1 - 2 * core}
    y_peer = {"frames": f + 2 - 4 * y}
    x_peer = {"mp": 1 - h}
    f32, bf16 = jnp.float32, jnp.bfloat16
    MESH = pl.DeviceIdType.MESH
    rows = g_hbm.shape[3] // nj

    def z_peer(t):
        return {"frames": lax.rem(f + 4 * t, n)}

    def from_j(t):
        return lax.rem(j - t + nj, nj)

    def at(start, size):
        return pl.ds(pl.multiple_of(start, size), size)

    load = pltpu.make_async_copy(g_hbm.at[core], g_own, lsem.at[0])
    load.start()
    barrier = pltpu.get_barrier_semaphore()
    for peer in [core_peer, y_peer, x_peer] + [z_peer(t) for t in range(1, nj)]:
        pl.semaphore_signal(barrier, inc=1, device_id=peer, device_id_type=MESH)
    pl.semaphore_wait(barrier, 2 + nj)

    def remote(src, dst, send, recv, peer):
        return pltpu.make_async_remote_copy(
            src_ref=src, dst_ref=dst, send_sem=send, recv_sem=recv, device_id=peer,
            device_id_type=MESH,
        )

    dm_x = remote(dm_ref.at[1 - h], dm_peer, s_x.at[0], r_x.at[0], x_peer)
    dm_x.start()
    core_g = remote(g_hbm.at[1 - core], near, s_g.at[0], r_g.at[0], core_peer)
    core_in = remote(gin_ref.at[1 - core], near_in, s_g.at[1], r_g.at[1], core_peer)
    core_g.start()
    core_in.start()

    dm_x.wait_recv()
    mine = dm_ref[h]
    theirs = dm_peer[...]
    low = h == 0
    dm[core, y, j] = jnp.concatenate(
        [jnp.where(low, mine, theirs), jnp.where(low, theirs, mine)], axis=0
    ).astype(bf16)

    def dm_z(t, src):
        block = dm.at[core, y, src]
        return remote(block, block, s_dz.at[0, t], r_dz.at[0, t], z_peer(t))

    for t in range(1, nj):
        dm_z(t, j).start()
    load.wait()
    core_g.wait_recv()
    core_in.wait_recv()

    def add_near(i, _):
        for s in range(2):
            for k in range(g_own.shape[1]):
                r = at(i * rows, rows)
                g_own[s, k, r, :] = (
                    g_own[s, k, r, :].astype(f32) + near[s, k, r, :].astype(f32)
                ).astype(bf16)
        return 0

    lax.fori_loop(0, nj, add_near, 0)
    g_in[...] = (gin_ref[core].astype(f32) + near_in[...].astype(f32)).astype(bf16)
    for t in range(1, nj):
        dm_z(t, from_j(t)).wait_recv()

    def dm_y(side_index):
        block = dm.at[core, side_index]
        return remote(block, block, s_d.at[0], r_d.at[0], y_peer)

    dm_y(y).start()
    y_g = remote(g_own.at[1 - y], side, s_g.at[2], r_g.at[2], y_peer)
    y_in = remote(g_in.at[1 - y], side_in, s_g.at[3], r_g.at[3], y_peer)
    y_g.start()
    y_in.start()
    dm_y(1 - y).wait_recv()

    def dm_core(core_index):
        block = dm.at[core_index]
        return remote(block, block, s_d.at[1], r_d.at[1], core_peer)

    dm_core(core).start()
    y_g.wait_recv()
    y_in.wait_recv()

    def add_side(i, _):
        for k in range(g_own.shape[1]):
            r = at(i * rows, rows)
            side[k, r, :] = (
                g_own[y, k, r, :].astype(f32) + side[k, r, :].astype(f32)
            ).astype(bf16)
        return 0

    lax.fori_loop(0, nj, add_side, 0)
    side_in[...] = (g_in[y].astype(f32) + side_in[...].astype(f32)).astype(bf16)

    def far_g(t):
        there = at(lax.rem(j + t, nj) * rows, rows)
        return remote(
            side.at[:, there], far.at[t - 1], s_f.at[0, t], r_f.at[0, t], z_peer(t)
        )

    def far_i(t):
        there = at(lax.rem(j + t, nj) * rows, rows)
        return remote(
            side_in.at[there], far_in.at[t - 1], s_f.at[1, t], r_f.at[1, t], z_peer(t)
        )

    for t in range(1, nj):
        far_g(t).start()
        far_i(t).start()

    dm_core(1 - core).wait_recv()
    frames = dm.shape[0] * dm.shape[1] * dm.shape[2] * dm.shape[3]
    wide = dm.shape[4]
    every = dm[...].reshape(frames, wide)
    part = dotf(wm_ref[...], every, NT)
    dc_send[:rows, :] = part
    dc_send[rows:, :] = jnp.broadcast_to(jnp.sum(loss_ref[...]), (8, frames))
    dc_x = remote(dc_send, dc_peer, s_x.at[1], r_x.at[1], x_peer)
    dc_x.start()

    def mod_cols(i, _):
        cols = at(i * 512, 512)
        block = dm[:, :, :, :, cols].reshape(frames, 512)
        res = dotf(cond_ref[...], block)
        smod_ref[:, cols] = res[:rows] + res[rows : 2 * rows] + res[2 * rows :]
        return 0

    lax.fori_loop(0, wide // 512, mod_cols, 0)
    dc_x.wait_recv()
    total = dc_send[...] + dc_peer[...]
    dct_ref[core, y, j, :rows, :] = total[:rows].astype(bf16)
    pieces = [p[:1].astype(f32) for p in split_three(total[rows:])]
    dct_ref[core, y, j, rows:, :] = jnp.concatenate(
        pieces + [jnp.zeros((13, frames), f32)], axis=0
    ).astype(bf16)

    def dc_z(t, src):
        block = dct_ref.at[core, y, src]
        return remote(block, block, s_dz.at[1, t], r_dz.at[1, t], z_peer(t))

    for t in range(1, nj):
        dc_z(t, j).start()
    for t in range(1, nj):
        dc_z(t, from_j(t)).wait_recv()

    def dc_y(side_index):
        block = dct_ref.at[core, side_index]
        return remote(block, block, s_d.at[2], r_d.at[2], y_peer)

    dc_y(y).start()

    here = at(j * rows, rows)
    for t in range(1, nj):
        far_g(t).wait_recv()
        far_i(t).wait_recv()
    for k in range(sq_ref.shape[0]):
        sq_ref[k] = side[k, here, :].astype(f32) + sum(
            far[t, k].astype(f32) for t in range(nj - 1)
        )
    ends[...] = side_in[here, :].astype(f32) + sum(
        far_in[t].astype(f32) for t in range(nj - 1)
    )
    ends_x = remote(ends, ends_peer, s_x.at[2], r_x.at[2], x_peer)
    ends_x.start()
    dc_y(1 - y).wait_recv()

    def dc_core(core_index):
        block = dct_ref.at[core_index]
        return remote(block, block, s_d.at[3], r_d.at[3], core_peer)

    dc_core(core).start()
    ends_x.wait_recv()
    sin_ref[...] = ends[...] + ends_peer[...]
    dc_core(1 - core).wait_recv()

    for one in (dm_x, core_g, core_in, y_g, y_in, dc_x, ends_x):
        one.wait_send()
    for one in (dm_y(y), dm_core(core), dc_y(y), dc_core(core)):
        one.wait_send()
    for t in range(1, nj):
        for one in (dm_z(t, j), dc_z(t, j), far_g(t), far_i(t)):
            one.wait_send()


def last_block(g, gin, dm, cond, wm, loss, cid):
    _, _, kinds, block_rows, e = g.shape
    n = lax.axis_size("frames")
    nj = n // 4
    rows = block_rows // nj
    own_frames, wide = dm.shape[1:]
    frames = n * 2 * own_frames
    f32, bf16 = jnp.float32, jnp.bfloat16
    vm = pl.BlockSpec(memory_space=pltpu.VMEM)
    anym = pl.BlockSpec(memory_space=pl.ANY)
    V = pltpu.VMEM
    D_ = pltpu.SemaphoreType.DMA
    return pl.pallas_call(
        last_kernel,
        in_specs=[anym] + [vm] * 5,
        out_specs=[vm] * 4,
        out_shape=[
            jax.ShapeDtypeStruct((kinds, rows, e), f32),
            jax.ShapeDtypeStruct((rows, 128), f32),
            jax.ShapeDtypeStruct((rows, wide), f32),
            jax.ShapeDtypeStruct((2, 2, nj, rows + 16, frames), bf16),
        ],
        scratch_shapes=[
            V((2, kinds, block_rows, e), bf16), V((2, block_rows, 128), bf16),
            V((2, kinds, block_rows, e), bf16), V((2, block_rows, 128), bf16),
            V((kinds, block_rows, e), bf16), V((block_rows, 128), bf16),
            V((nj - 1, kinds, rows, e), bf16), V((nj - 1, rows, 128), bf16),
            V((rows, 128), f32), V((rows, 128), f32),
            V((own_frames, wide), f32), V((2, 2, nj, 2 * own_frames, wide), bf16),
            V((rows + 8, frames), f32), V((rows + 8, frames), f32),
            D_((1,)), D_((3,)), D_((3,)), D_((4,)), D_((4,)), D_((2, nj)), D_((2, nj)),
            D_((4,)), D_((4,)), D_((2, nj)), D_((2, nj)),
        ],
        compiler_params=pltpu.CompilerParams(
            vmem_limit_bytes=48 << 20, collective_id=cid, has_side_effects=True
        ),
        cost_estimate=pl.CostEstimate(
            flops=2 * 10**10, bytes_accessed=2 * 10**7, transcendentals=0
        ),
        name="weight_sums",
    )(g, gin, dm, cond, wm, loss)


def front_kernel(
    small_ref, feat_ref, wm_ref, w_ref,
    st_ref, feats_ref, pre1_ref, pre2_ref, wout_ref, ends_ref, mod_ref,
    wcol, mods,
    s_x, r_x, s_z, r_z, s_y, r_y, s_c, r_c, s_a, r_a, s_m, r_m,
):
    f = lax.axis_index("frames")
    h = lax.axis_index("mp")
    n = lax.axis_size("frames")
    nj = n // 4
    c = lax.rem(f, 2)
    y = lax.rem(lax.div(f, 2), 2)
    j = lax.div(f, 4)
    f32, bf16 = jnp.float32, jnp.bfloat16
    MESH = pl.DeviceIdType.MESH
    x_peer = {"mp": 1 - h}
    core_peer = {"frames": f + 1 - 2 * c}
    y_peer = {"frames": f + 2 - 4 * y}
    offsets = [
        (tj, ty, tc) for tj in range(nj) for ty in range(2) for tc in range(2)
    ][1:]

    def place(tj, ty, tc):
        return (
            lax.rem(j + tj, nj),
            y + ty - 2 * y * ty,
            c + tc - 2 * c * tc,
        )

    def peer_of(spot):
        return {"frames": 4 * spot[0] + 2 * spot[1] + spot[2]}

    def from_j(t):
        return lax.rem(j - t + nj, nj)

    def remote(src, dst, send, recv, peer):
        return pltpu.make_async_remote_copy(
            src_ref=src, dst_ref=dst, send_sem=send, recv_sem=recv, device_id=peer,
            device_id_type=MESH,
        )

    barrier = pltpu.get_barrier_semaphore()
    for o in offsets:
        pl.semaphore_signal(barrier, inc=1, device_id=peer_of(place(*o)), device_id_type=MESH)
    pl.semaphore_signal(barrier, inc=1, device_id=x_peer, device_id_type=MESH)
    pl.semaphore_wait(barrier, n)

    class Gather:
        def __init__(self, block, k):
            self.block, self.k = block, k

        def over_z(self, t, jj):
            b = self.block(jj, y, c)
            return remote(
                b, b, s_z.at[self.k, t], r_z.at[self.k, t], {"frames": lax.rem(f + 4 * t, n)}
            )

        def over_y(self, t, yy):
            b = self.block(from_j(t), yy, c)
            return remote(b, b, s_y.at[self.k, t], r_y.at[self.k, t], y_peer)

        def over_core(self, t, same, yy, cc):
            b = self.block(from_j(t), yy, cc)
            return remote(
                b, b, s_c.at[self.k, same, t], r_c.at[self.k, same, t], core_peer
            )

        def start(self):
            for t in range(1, nj):
                self.over_z(t, j).start()
            self.over_y(0, y).start()
            self.over_core(0, 0, y, c).start()

        def pass_z(self):
            for t in range(1, nj):
                self.over_z(t, from_j(t)).wait_recv()
                self.over_y(t, y).start()
                self.over_core(t, 0, y, c).start()

        def pass_y(self):
            for t in range(nj):
                self.over_y(t, 1 - y).wait_recv()
                self.over_core(t, 1, 1 - y, c).start()

        def finish(self):
            for t in range(nj):
                self.over_core(t, 0, y, 1 - c).wait_recv()
                self.over_core(t, 1, 1 - y, 1 - c).wait_recv()

        def sent(self):
            for t in range(1, nj):
                self.over_z(t, j).wait_send()
            for t in range(nj):
                self.over_y(t, y).wait_send()
                self.over_core(t, 0, y, c).wait_send()
                self.over_core(t, 1, 1 - y, c).wait_send()

    small = Gather(lambda a, b, d: st_ref.at[a, b, d], 0)
    feats = Gather(lambda a, b, d: feats_ref.at[d, b, a], 1)
    weights = Gather(lambda a, b, d: wout_ref.at[:, a, b, d], 2)

    small_x = remote(small_ref, st_ref.at[j, y, c, h], s_x.at[0], r_x.at[0], x_peer)
    small_x.start()
    feats_ref[c, y, j] = feat_ref[...]
    feats.start()

    def column_copy(i, spot, slot):
        return remote(
            wm_ref.at[spot[2], spot[1], spot[0]], wcol.at[slot[0], slot[1], slot[2]],
            s_a.at[i], r_a.at[i], peer_of(spot),
        )

    def source(o):
        return place((nj - o[0]) % nj, o[1], o[2])

    for i, o in enumerate(offsets):
        column_copy(i, place(*o), (j, y, c)).start()
    st_ref[j, y, c, h] = small_ref[...]
    wout_ref[:, j, y, c] = w_ref[...]
    wcol[j, y, c] = wm_ref[c, y, j]
    remote(
        small_ref, st_ref.at[j, y, c, 1 - h], s_x.at[0], r_x.at[0], x_peer
    ).wait_recv()
    small.start()
    feats.pass_z()
    small.pass_z()
    weights.start()
    feats.pass_y()
    small.pass_y()
    feats.finish()
    small.finish()

    total = st_ref.shape[0] * 4
    width = total * 2 * st_ref.shape[4]
    frames = feats_ref.shape[2] * 4 * feats_ref.shape[3]
    inner = feats_ref.shape[4]

    def exact(left, right, dims):
        m = left.shape[0]
        res = dotf(jnp.concatenate(split_three(left), axis=0), right, dims)
        return res[:m] + res[m : 2 * m] + res[2 * m :]

    def silu(v):
        return v * jax.nn.sigmoid(v)

    table = st_ref[...].reshape(width, st_ref.shape[5])
    fv = feats_ref[...].reshape(frames, inner)
    pre1 = exact(fv, table[:, :inner], NT)
    pre1_ref[...] = pre1
    pre2 = exact(silu(pre1), table[:, inner : inner + width], NT)
    pre2_ref[...] = pre2
    ends_ref[...] = table[:, inner + width : inner + width + 128].T
    for i, o in enumerate(offsets):
        column_copy(i, place(*o), source(o)).wait_recv()
    cols = wcol[...].reshape(width, wcol.shape[4])
    mods[...] = exact(silu(pre2), cols, NN).reshape(mods.shape)

    def mods_copy(i, spot, slot):
        return remote(
            mods.at[spot[2], spot[1], spot[0]], mod_ref.at[h, slot[2], slot[1], slot[0]],
            s_m.at[i], r_m.at[i], peer_of(spot),
        )

    for i, o in enumerate(offsets):
        mods_copy(i, place(*o), (j, y, c)).start()
    mod_ref[h, c, y, j] = mods[c, y, j]
    weights.pass_z()
    for i, o in enumerate(offsets):
        mods_copy(i, place(*o), source(o)).wait_recv()
    mods_x = remote(mod_ref.at[h], mod_ref.at[h], s_x.at[1], r_x.at[1], x_peer)
    mods_x.start()
    weights.pass_y()
    weights.finish()
    theirs = mod_ref.at[1 - h]
    remote(theirs, theirs, s_x.at[1], r_x.at[1], x_peer).wait_recv()

    small_x.wait_send()
    mods_x.wait_send()
    for g in (small, feats, weights):
        g.sent()
    for i, o in enumerate(offsets):
        column_copy(i, place(*o), (j, y, c)).wait_send()
        mods_copy(i, place(*o), (j, y, c)).wait_send()


def front_block(small, feat, wm, w, cid):
    n = lax.axis_size("frames")
    nj = n // 4
    cols, lanes = small.shape
    own_frames, inner = feat.shape
    frames = n * own_frames
    kinds, rows, e = w.shape
    wide = wm.shape[-1]
    width = rows * n
    f32, bf16 = jnp.float32, jnp.bfloat16
    vm = pl.BlockSpec(memory_space=pltpu.VMEM)
    V = pltpu.VMEM
    D_ = pltpu.SemaphoreType.DMA
    return pl.pallas_call(
        front_kernel,
        in_specs=[vm] * 4,
        out_specs=[vm] * 7,
        out_shape=[
            jax.ShapeDtypeStruct((nj, 2, 2, 2, cols, lanes), bf16),
            jax.ShapeDtypeStruct((2, 2, nj, own_frames, inner), f32),
            jax.ShapeDtypeStruct((frames, width), f32),
            jax.ShapeDtypeStruct((frames, width), f32),
            jax.ShapeDtypeStruct((kinds, nj, 2, 2, rows, e), bf16),
            jax.ShapeDtypeStruct((128, width), bf16),
            jax.ShapeDtypeStruct((2, 2, 2, nj, own_frames, wide), f32),
        ],
        scratch_shapes=[
            V((nj, 2, 2, rows, wide), bf16), V((2, 2, nj, own_frames, wide), f32),
            D_((2,)), D_((2,)), D_((3, nj)), D_((3, nj)), D_((3, nj)), D_((3, nj)),
            D_((3, 2, nj)), D_((3, 2, nj)), D_((n - 1,)), D_((n - 1,)), D_((n - 1,)),
            D_((n - 1,)),
        ],
        compiler_params=pltpu.CompilerParams(
            vmem_limit_bytes=48 << 20, collective_id=cid, has_side_effects=True
        ),
        cost_estimate=pl.CostEstimate(
            flops=4 * 10**10, bytes_accessed=2 * 10**7, transcendentals=0
        ),
        name="conditioning",
    )(small, feat, wm, w)


def per_device(
    latents,
    noise,
    levels,
    clip_ids,
    clean_flags,
    attn_weights,
    mlp_weights,
    mod_weight,
    small_weights,
    attn_moment,
    mlp_moment,
    mod_moment,
    small_moment,
    attn_average,
    mlp_average,
    mod_average,
    small_average,
):
    frame_count = latents.shape[0]
    tok_count = frame_count * TPF
    patch_side = GRID // 2
    frames_total = clip_ids.shape[0]
    tokens_total = frames_total * TPF
    width_local = attn_weights.shape[2]
    heads_local = width_local // HD
    key_span = (REACH + 1) * tok_count
    device = lax.axis_index("frames")
    mp_index = lax.axis_index("mp")
    first_frame = device * frame_count
    scale_qk = HD ** (-0.5)
    attn_low = attn_weights.astype(jnp.bfloat16)
    mlp_low = mlp_weights.astype(jnp.bfloat16)
    low_mod = mod_weight.astype(jnp.bfloat16)
    noised_all = (1 - clean_flags).astype(jnp.float32)
    noised_count = jnp.sum(noised_all)
    noised = lax.dynamic_slice_in_dim(noised_all, first_frame, frame_count)
    level_eff = levels * noised
    signal_scale = jnp.repeat(jnp.cos(0.5 * math.pi * level_eff), TPF)
    noise_scale = jnp.repeat(jnp.sin(0.5 * math.pi * level_eff), TPF)
    noise_patches = patchify(noise)
    inputs = signal_scale[:, None] * patchify(latents) + noise_scale[:, None] * noise_patches
    in_clip_all = clip_positions(clip_ids)
    in_clip = lax.dynamic_slice_in_dim(in_clip_all, first_frame, frame_count).astype(jnp.float32)
    within = np.arange(TPF)
    patch_zero = np.zeros((TPF, HD // 4), np.float32)
    patch_angles = np.concatenate(
        [patch_zero]
        + turn_phases((within // patch_side).astype(np.float32), 3 * HD // 8)
        + turn_phases((within % patch_side).astype(np.float32), 3 * HD // 8),
        axis=1,
    )
    patch_angles = np.tile(patch_angles, (1, 4))
    frame_angles = jnp.tile(
        jnp.concatenate(
            turn_phases(in_clip, HD // 4) + [jnp.zeros((frame_count, 3 * HD // 4))], axis=1
        ),
        (1, 4),
    )
    tables = (
        jnp.cos(frame_angles),
        jnp.sin(frame_angles),
        jnp.asarray(np.cos(patch_angles), jnp.float32),
        jnp.asarray(np.sin(patch_angles), jnp.float32),
    )
    turn_four = jnp.asarray(np.kron(np.eye(4, dtype=np.float32), rotation_matrix(HD)), jnp.bfloat16)
    clip_start = (
        lax.dynamic_slice_in_dim(
            jnp.arange(frames_total, dtype=jnp.int32) - in_clip_all, first_frame, frame_count
        )
        - first_frame
        + REACH * frame_count
    )
    peers = lax.axis_size("frames")
    frame_groups = peers // 4
    small_rows, small_cols = small_weights.shape
    mod_rows, mod_cols = mod_weight.shape
    mod_share = mod_cols // peers
    mod_wide = -(-mod_share // 128) * 128
    small_lanes = FREQ + D + 128
    small_t = jnp.pad(
        small_weights.astype(jnp.bfloat16).T, ((0, 0), (0, small_lanes - small_rows))
    )
    mod_blocks = jnp.pad(
        low_mod.reshape(mod_rows, frame_groups, 2, 2, mod_share).transpose(3, 2, 1, 0, 4),
        ((0, 0),) * 4 + ((0, mod_wide - mod_share),),
    )
    small_full, features_placed, pre_one, pre_two, w_qkv, end_rows, mod_parts = front_block(
        small_t, time_features(level_eff), mod_blocks, attn_low, 4
    )
    w_qkv, up_low = lax.optimization_barrier((w_qkv, mlp_low[0]))
    w_up = lax.all_gather(up_low, "frames", axis=0, tiled=True)
    w_qkv = w_qkv.reshape(4, D, width_local)
    features_placed = features_placed.reshape(frames_total, FREQ)
    first_placed = jax.nn.silu(pre_one)
    pre_two_t = pre_two.T
    first_col = (device * lax.axis_size("mp") + mp_index) * small_cols
    pre_one_own = lax.dynamic_slice_in_dim(pre_one, first_col, small_cols, 1).T
    cond_rows = jax.nn.silu(
        lax.dynamic_slice_in_dim(pre_two, device * mod_rows, mod_rows, 1)
    )
    cond_parts = jnp.concatenate([part.T for part in split_three(cond_rows)], axis=0)
    modulation = (
        mod_parts[..., :mod_share].transpose(4, 0, 3, 2, 1, 5).reshape(frame_count, 6 * D)
    )
    pieces = [
        modulation[:, None, piece_index * D : (piece_index + 1) * D] for piece_index in range(6)
    ]
    shift_one, scale_one, gate_one, shift_two, scale_two, gate_two = pieces
    inputs_low = inputs.astype(jnp.bfloat16)
    padding = ((0, 0), (0, 128 - P_SIZE))
    inputs_low = jnp.pad(inputs_low, padding)
    normed_one, hidden_half, queries, keys_wide, values_wide = proj_block(
        inputs_low,
        end_rows,
        jnp.stack([shift_one[:, 0], scale_one[:, 0]]),
        w_qkv,
        tables,
        turn_four,
        REACH,
        2,
    )
    down_low = mlp_low[1]
    queries, down_low = lax.optimization_barrier((queries, down_low))
    w_down = lax.all_gather(down_low, "frames", axis=0, tiled=True)
    heads_wide, log_totals = attn_fwd(queries, keys_wide, values_wide, clip_start)
    half = tok_count // 2
    own_frames = frame_count // 2

    def half_of(array, dim=0):
        size = array.shape[dim] // 2
        return lax.dynamic_slice_in_dim(array, mp_index * size, size, dim)

    token_weight = jnp.repeat(noised, TPF) / (TPF * P_SIZE)
    grad_scale = 1.0 / jnp.maximum(noised_count, 1.0)
    head_lanes = ((0, 0), (P_SIZE, 128 - 2 * P_SIZE))
    mod_mid = jnp.stack(
        [half_of(piece[:, 0]) for piece in (gate_one, shift_two, scale_two, gate_two)]
    )
    d_mixed, d_shaped_one, d_mod_mid, loss_parts, grad_up, grad_rest = mid_block(
        heads_wide,
        hidden_half,
        mod_mid,
        jnp.pad(half_of(noise_patches), head_lanes),
        jnp.pad(jnp.broadcast_to(half_of(token_weight)[:, None], (half, P_SIZE)), head_lanes),
        end_rows,
        grad_scale.reshape(1),
        w_up,
        w_down,
        w_qkv,
        TP_AXIS,
        0,
    )
    sum_up = lax.psum_scatter(grad_up, "frames", scatter_dimension=0, tiled=True)
    sum_rest = lax.psum_scatter(grad_rest, "frames", scatter_dimension=0, tiled=True)
    d_queries, keys_grad_wide, values_grad_wide = attn_bwd(
        queries, keys_wide, values_wide, d_mixed, heads_wide, log_totals, clip_start
    )
    d_queries, sum_up = lax.optimization_barrier((d_queries, sum_up))
    grad_qkv, grad_in, d_first_mods = tail_block(
        d_queries,
        normed_one,
        w_qkv,
        tables,
        turn_four,
        hidden_half,
        half_of(scale_one[:, 0]),
        d_shaped_one,
        half_of(inputs_low),
        keys_grad_wide,
        values_grad_wide,
        1,
    )
    d_first_mods, sum_rest = lax.optimization_barrier((d_first_mods, sum_rest))
    def by_place(array, dim):
        shape = array.shape
        size = shape[dim] // (4 * frame_groups)
        split = array.reshape(shape[:dim] + (frame_groups, 2, 2, size) + shape[dim + 1 :])
        order = list(range(split.ndim))
        order[dim], order[dim + 2] = dim + 2, dim
        return split.transpose(order)

    in_columns = by_place(grad_in.T, 0).reshape(2, 2, D // 4, 128).astype(jnp.bfloat16)
    d_mods = jnp.stack(
        [
            jnp.concatenate([d_first_mods[0], d_first_mods[1], d_mod_mid[0]], axis=1),
            jnp.concatenate([d_mod_mid[1], d_mod_mid[2], d_mod_mid[3]], axis=1),
        ]
    )
    sum_qkv, sum_in, sum_mod, d_cond_rows = last_block(
        grad_qkv, in_columns, d_mods, cond_parts, low_mod, loss_parts, 3
    )
    loss_sum = jnp.sum(d_cond_rows[:, :, :, mod_rows : mod_rows + 3, 0].astype(jnp.float32))
    d_cond_t = (
        d_cond_rows[:, :, :, :mod_rows, :].transpose(2, 1, 0, 3, 4).reshape(D, frames_total)
    ).astype(jnp.float32)
    d_pre_two = jax.vjp(jax.nn.silu, pre_two_t)[1](d_cond_t)[0]
    d_pre_own = lax.dynamic_slice_in_dim(d_pre_two, first_col, small_cols, 0)
    grad_second = jnp.einsum("fi,jf->ij", first_placed, d_pre_own, precision=HIGH)
    second_cols = lax.dynamic_slice_in_dim(
        small_full.reshape(D, small_lanes), FREQ + first_col, small_cols, 1
    ).astype(jnp.float32)
    d_first = jnp.einsum("kf,kj->jf", d_pre_two, second_cols, precision=HIGH)
    d_pre_one = jax.vjp(jax.nn.silu, pre_one_own)[1](d_first)[0]
    grad_first = jnp.einsum("fi,jf->ij", features_placed, d_pre_one, precision=HIGH)
    ff_cols = mlp_weights.shape[2]
    sum_rest = sum_rest.astype(jnp.float32)
    sum_mlp = jnp.stack([sum_up.astype(jnp.float32), sum_rest[:, :ff_cols]])
    sum_attn = jnp.stack(
        [sum_qkv[0], sum_qkv[1], sum_qkv[2]]
        + [sum_rest[:, ff_cols : ff_cols + width_local]]
    )
    head_first = ff_cols + width_local
    head_part = sum_rest[:, head_first + P_SIZE : head_first + 2 * P_SIZE]
    sum_head = head_part + lax.ppermute(head_part, "mp", [(0, 1), (1, 0)])
    sum_ends = half_of(jnp.concatenate([sum_in[:, :P_SIZE], sum_head], axis=1).T, 1)
    sum_small = jnp.concatenate([grad_first, grad_second, sum_ends], axis=0)
    learning_rate = 0.5 * math.sqrt(tokens_total * P_SIZE / D)
    attn_new, attn_moment_new, attn_average_new, attn_copy = update(
        attn_weights, sum_attn, attn_moment, attn_average, learning_rate
    )
    mlp_new, mlp_moment_new, mlp_average_new, mlp_copy = update(
        mlp_weights, sum_mlp, mlp_moment, mlp_average, learning_rate
    )
    mod_new, mod_moment_new, mod_average_new, mod_copy = update(
        mod_weight, sum_mod, mod_moment, mod_average, learning_rate
    )
    small_new, small_moment_new, small_average_new, small_copy = update(
        small_weights, sum_small, small_moment, small_average, learning_rate
    )
    return (
        loss_sum,
        noised_count,
        attn_new,
        attn_moment_new,
        attn_average_new,
        attn_copy,
        mlp_new,
        mlp_moment_new,
        mlp_average_new,
        mlp_copy,
        mod_new,
        mod_moment_new,
        mod_average_new,
        mod_copy,
        small_new,
        small_moment_new,
        small_average_new,
        small_copy,
    )


def solution(mesh):
    return jax.shard_map(
        per_device,
        mesh=mesh,
        in_specs=(
            P("frames", None),
            P("frames", None),
            P("frames"),
            P(),
            P(),
            P(None, "frames", "mp"),
            P(None, "frames", "mp"),
            P("frames", "mp"),
            P(None, ("frames", "mp")),
            P(None, "frames", "mp"),
            P(None, "frames", "mp"),
            P("frames", "mp"),
            P(None, ("frames", "mp")),
            P(None, "frames", "mp"),
            P(None, "frames", "mp"),
            P("frames", "mp"),
            P(None, ("frames", "mp")),
        ),
        out_specs=(
            P(),
            P(),
            P(None, "frames", "mp"),
            P(None, "frames", "mp"),
            P(None, "frames", "mp"),
            P(None, "frames", "mp"),
            P(None, "frames", "mp"),
            P(None, "frames", "mp"),
            P(None, "frames", "mp"),
            P(None, "frames", "mp"),
            P("frames", "mp"),
            P("frames", "mp"),
            P("frames", "mp"),
            P("frames", "mp"),
            P(None, ("frames", "mp")),
            P(None, ("frames", "mp")),
            P(None, ("frames", "mp")),
            P(None, ("frames", "mp")),
        ),
        check_vma=False,
    )
```

```python
import functools
import math

import jax
import jax.numpy as jnp
import numpy as np
from jax import lax
from jax.experimental import pallas as pl
from jax.experimental.pallas import tpu as pltpu
from jax.sharding import PartitionSpec as P

D = 1024
HD = 64
CH = 4
FREQ = 256
GRID = 16
P_SIZE = 16
TPF = 64
REACH = 4


HIGH = lax.Precision.HIGHEST
EPSILON = 1e-06
MOMENTUM = 0.5
EMA_DECAY = 0.5
TP_AXIS = "mp"


def rotation_matrix(head_width):
    groups = [head_width // 4, 3 * head_width // 8, 3 * head_width // 8]
    rotation = np.zeros((head_width, head_width), np.float32)
    offset = 0
    for group_size in groups:
        half_size = group_size // 2
        for pair_index in range(half_size):
            rotation[offset + half_size + pair_index, offset + pair_index] = -1.0
            rotation[offset + pair_index, offset + half_size + pair_index] = 1.0
        offset += group_size
    return rotation


def turn_phases(positions, group_size):
    half_size = group_size // 2
    frequency = 10000.0 ** (-np.arange(half_size, dtype=np.float32) / half_size)
    phases = positions[:, None] * frequency.astype(np.float32)[None, :]
    return [phases, phases]


def turn_table(frame_ref, patch_ref, first, count):
    lanes = lax.broadcasted_iota(jnp.int32, (1, patch_ref.shape[1]), 1)
    by_frame = lax.rem(lanes, HD) < HD // 4
    rows = [
        jnp.where(by_frame, frame_ref[pl.ds(first + k, 1), :], patch_ref[...])
        for k in range(count)
    ]
    return jnp.concatenate(rows, axis=0)


def clip_positions(clip_ids):
    frame_index = jnp.arange(clip_ids.shape[0], dtype=jnp.int32)
    starts_here = jnp.concatenate([jnp.ones((1,), bool), clip_ids[1:] != clip_ids[:-1]])
    clip_start = lax.cummax(jnp.where(starts_here, frame_index, 0), axis=0)
    return frame_index - clip_start


def patchify(frame_data):
    frame_total = frame_data.shape[0]
    patch_side = GRID // 2
    shaped = frame_data.reshape(frame_total, CH, patch_side, 2, patch_side, 2)
    return shaped.transpose(0, 2, 4, 1, 3, 5).reshape(frame_total * patch_side * patch_side, CH * 4)


def layer_norm(vector):
    row_mean = jnp.mean(vector, axis=-1, keepdims=True)
    centred = vector - row_mean
    variance = jnp.mean(centred * centred, axis=-1, keepdims=True)
    return centred * lax.rsqrt(variance + EPSILON)


def modulate_local(shaped, shift_rows, scale_rows):
    return layer_norm(shaped) * (1.0 + scale_rows) + shift_rows


def time_features(level_eff):
    half_size = FREQ // 2
    frequency = jnp.exp(-math.log(10000.0) * jnp.arange(half_size, dtype=jnp.float32) / half_size)
    phases = (level_eff * 1000.0)[:, None] * frequency[None, :]
    return jnp.concatenate([jnp.cos(phases), jnp.sin(phases)], axis=1)


NT=(((1,),(1,)),((),()))
NN=(((1,),(0,)),((),()))

def dotf(a,b,dims=NN):
    return lax.dot_general(a,b,dims,preferred_element_type=jnp.float32)

def split_pair(xT):
    r=lax.broadcasted_iota(jnp.int32,xT.shape,0)
    z=jnp.zeros_like(xT)
    return jnp.where(r<HD,xT,z), jnp.where(r<HD,z,xT)

def keep_of(t,TK,TQ,cs,qf):
    kf=lax.broadcasted_iota(jnp.int32,(TK,TQ),0)//TPF+t*(TK//TPF)
    return (kf>=cs)&(kf<=qf)

def fwd_kernel(lo_ref,mid_ref,hi_ref,q_ref,k_ref,v_ref,cs_ref,o_ref,ol_ref,lse_ref,vT,*,TQ,TK,W0,NQ):
    KS=k_ref.shape[0]
    def tr(i,_):
        s=pl.multiple_of(i*TK,TK)
        vT[:,pl.ds(s,TK)]=v_ref[pl.ds(s,TK),:].T
        return 0
    lax.fori_loop(lo_ref[0],KS//TK,tr,0)
    def qtile(j,_):
        qs=pl.multiple_of(j*TQ,TQ)
        qT=(q_ref[pl.ds(qs,TQ),:].T)*jnp.bfloat16(0.125)
        qA,qB=split_pair(qT)
        cs=cs_ref[0:1,pl.ds(qs,TQ)]
        qf=lax.broadcasted_iota(jnp.int32,(1,TQ),1)//TPF+(W0+j*(TQ//TPF))
        def step(t,carry,masked):
            ks=pl.multiple_of(t*TK,TK)
            kt=k_ref[pl.ds(ks,TK),:]
            out=[]
            if masked: keep=keep_of(t,TK,TQ,cs,qf)
            ones=jnp.ones((16,TK),jnp.bfloat16)
            both=[dotf(kt,qh) for qh in (qA,qB)]
            for h,(s,(m,l,o)) in enumerate(zip(both,carry)):
                if masked: s=jnp.where(keep,s,-1e30)
                mn=jnp.maximum(m,jnp.max(s,axis=0,keepdims=True))
                a=jnp.exp(m-mn)
                p=jnp.exp(s-mn)
                vh=jnp.concatenate([vT[h*HD:(h+1)*HD,pl.ds(ks,TK)],ones],axis=0)
                ov=dotf(vh,p.astype(jnp.bfloat16))
                l=l*a+ov[HD:HD+1]
                o=o*a+ov[:HD]
                out.append((mn,l,o))
            return tuple(out)
        init=tuple((jnp.full((1,TQ),-1e29,jnp.float32),jnp.zeros((1,TQ),jnp.float32),jnp.zeros((HD,TQ),jnp.float32)) for _ in range(2))
        c=lax.fori_loop(lo_ref[j],mid_ref[j],lambda t,c:step(t,c,True),init)
        c=lax.fori_loop(mid_ref[j],hi_ref[j],lambda t,c:step(t,c,False),c)
        c=lax.fori_loop(hi_ref[j],(W0*TPF+(j+1)*TQ+TK-1)//TK,lambda t,c:step(t,c,True),c)
        oT=jnp.concatenate([c[0][2]/c[0][1],c[1][2]/c[1][1]],axis=0)
        o_nat=oT.T
        o_ref[pl.ds(qs,TQ),:]=o_nat
        ol_ref[pl.ds(qs,TQ),:]=o_nat.astype(jnp.bfloat16)
        lse_ref[0,0:1,pl.ds(qs,TQ)]=c[0][0]+jnp.log(c[0][1])
        lse_ref[0,1:2,pl.ds(qs,TQ)]=c[1][0]+jnp.log(c[1][1])
        return 0
    lax.fori_loop(0,NQ,qtile,0)

def tile_bounds(cs_rel,TQ,TK,W0,NQ):
    fq=TQ//TPF; fk=TK//TPF
    j=jnp.arange(NQ)
    first=cs_rel[::fq]; last=cs_rel[fq-1::fq]
    lo=first//fk
    dg=(W0+j*fq+1)//fk
    mid=jnp.minimum((last+fk-1)//fk,dg)
    mid=jnp.maximum(mid,lo)
    hi=jnp.maximum(dg,mid)
    return lo.astype(jnp.int32),mid.astype(jnp.int32),hi.astype(jnp.int32)

def attn_fwd(q,k,v,cs_rel,TQ=512,TK=512):
    T,Wd=q.shape; KS=k.shape[0]; P=Wd//128
    W0=(KS-T)//TPF; NQ=T//TQ
    lo,mid,hi=tile_bounds(cs_rel,TQ,TK,W0,NQ)
    cs_tok=jnp.broadcast_to(jnp.repeat(cs_rel,TPF)[None,:],(8,T)).astype(jnp.int32)
    return pl.pallas_call(
        functools.partial(fwd_kernel,TQ=TQ,TK=TK,W0=W0,NQ=NQ),
        grid_spec=pltpu.PrefetchScalarGridSpec(num_scalar_prefetch=3,grid=(P,),
            in_specs=[pl.BlockSpec((T,128),lambda p,*_:(0,p)),pl.BlockSpec((KS,128),lambda p,*_:(0,p)),pl.BlockSpec((KS,128),lambda p,*_:(0,p)),pl.BlockSpec((8,T),lambda p,*_:(0,0))],
            out_specs=[pl.BlockSpec((T,128),lambda p,*_:(0,p)),pl.BlockSpec((T,128),lambda p,*_:(0,p)),pl.BlockSpec((1,8,T),lambda p,*_:(p,0,0))],
            scratch_shapes=[pltpu.VMEM((128,KS),jnp.bfloat16)]),
        out_shape=[jax.ShapeDtypeStruct((T,Wd),jnp.float32),jax.ShapeDtypeStruct((T,Wd),jnp.bfloat16),jax.ShapeDtypeStruct((P,8,T),jnp.float32)],
        compiler_params=pltpu.CompilerParams(vmem_limit_bytes=48<<20),
        cost_estimate=pl.CostEstimate(flops=10**11,bytes_accessed=2*10**7,transcendentals=3*10**7),
        name="attn_forward",
    )(lo,mid,hi,q,k,v,cs_tok)

def bwd_kernel(lo_ref,mid_ref,hi_ref,q_ref,k_ref,v_ref,do_ref,o_ref,lse_ref,cs_ref,dq_ref,dk_ref,dv_ref,kT,dkT,dvT,*,TQ,TK,W0,NQ):
    KS=k_ref.shape[0]
    def tr(i,_):
        s=pl.multiple_of(i*TK,TK)
        kT[:,pl.ds(s,TK)]=k_ref[pl.ds(s,TK),:].T
        return 0
    lax.fori_loop(lo_ref[0],KS//TK,tr,0)
    dkT[...]=jnp.zeros_like(dkT); dvT[...]=jnp.zeros_like(dvT)
    def qtile(j,_):
        qs=pl.multiple_of(j*TQ,TQ)
        qT=(q_ref[pl.ds(qs,TQ),:].T)*jnp.bfloat16(0.125)
        qh=split_pair(qT)
        doT=do_ref[pl.ds(qs,TQ),:].T
        doh=split_pair(doT)
        oT=o_ref[pl.ds(qs,TQ),:].T
        prod=oT*doT.astype(jnp.float32)
        delta=(jnp.sum(prod[:HD],axis=0,keepdims=True),jnp.sum(prod[HD:],axis=0,keepdims=True))
        lse=(lse_ref[0,0:1,pl.ds(qs,TQ)],lse_ref[0,1:2,pl.ds(qs,TQ)])
        cs=cs_ref[0:1,pl.ds(qs,TQ)]
        qf=lax.broadcasted_iota(jnp.int32,(1,TQ),1)//TPF+(W0+j*(TQ//TPF))
        def step(t,carry,masked):
            ks=pl.multiple_of(t*TK,TK)
            kt=k_ref[pl.ds(ks,TK),:]; vt=v_ref[pl.ds(ks,TK),:]
            out=[]
            if masked: keep=keep_of(t,TK,TQ,cs,qf)
            for h in range(2):
                r=slice(h*HD,(h+1)*HD)
                s=dotf(kt,qh[h])
                p=jnp.exp(s-lse[h])
                if masked: p=jnp.where(keep,p,0.0)
                dp=dotf(vt,doh[h])
                ds=(p*(dp-delta[h])).astype(jnp.bfloat16)
                pb=p.astype(jnp.bfloat16)
                dvT[r,pl.ds(ks,TK)]+=dotf(doT[r],pb,NT)
                dkT[r,pl.ds(ks,TK)]+=dotf(qT[r],ds,NT)
                out.append(carry[h]+dotf(kT[r,pl.ds(ks,TK)],ds))
            return tuple(out)
        init=(jnp.zeros((HD,TQ),jnp.float32),)*2
        c=lax.fori_loop(lo_ref[j],mid_ref[j],lambda t,c:step(t,c,True),init)
        c=lax.fori_loop(mid_ref[j],hi_ref[j],lambda t,c:step(t,c,False),c)
        c=lax.fori_loop(hi_ref[j],(W0*TPF+(j+1)*TQ+TK-1)//TK,lambda t,c:step(t,c,True),c)
        dq_ref[pl.ds(qs,TQ),:]=(jnp.concatenate(c,axis=0)*0.125).T
        return 0
    lax.fori_loop(0,NQ,qtile,0)
    def back(i,_):
        s=pl.multiple_of(i*TK,TK)
        dk_ref[pl.ds(s,TK),:]=dkT[:,pl.ds(s,TK)].T.astype(dk_ref.dtype)
        dv_ref[pl.ds(s,TK),:]=dvT[:,pl.ds(s,TK)].T.astype(dv_ref.dtype)
        return 0
    lax.fori_loop(0,KS//TK,back,0)

def attn_bwd(q,k,v,do,o,lse,cs_rel,TQ=512,TK=512,out_dt=jnp.bfloat16):
    T,Wd=q.shape; KS=k.shape[0]; P=Wd//128
    W0=(KS-T)//TPF; NQ=T//TQ
    lo,mid,hi=tile_bounds(cs_rel,TQ,TK,W0,NQ)
    cs_tok=jnp.broadcast_to(jnp.repeat(cs_rel,TPF)[None,:],(8,T)).astype(jnp.int32)
    tb=pl.BlockSpec((T,128),lambda p,*_:(0,p)); kb=pl.BlockSpec((KS,128),lambda p,*_:(0,p))
    return pl.pallas_call(
        functools.partial(bwd_kernel,TQ=TQ,TK=TK,W0=W0,NQ=NQ),
        grid_spec=pltpu.PrefetchScalarGridSpec(num_scalar_prefetch=3,grid=(P,),
            in_specs=[tb,kb,kb,tb,tb,pl.BlockSpec((1,8,T),lambda p,*_:(p,0,0)),pl.BlockSpec((8,T),lambda p,*_:(0,0))],
            out_specs=[tb,kb,kb],
            scratch_shapes=[pltpu.VMEM((128,KS),jnp.bfloat16),pltpu.VMEM((128,KS),jnp.float32),pltpu.VMEM((128,KS),jnp.float32)]),
        out_shape=[jax.ShapeDtypeStruct((T,Wd),jnp.float32),jax.ShapeDtypeStruct((KS,Wd),out_dt),jax.ShapeDtypeStruct((KS,Wd),out_dt)],
        compiler_params=pltpu.CompilerParams(vmem_limit_bytes=56<<20),
        cost_estimate=pl.CostEstimate(flops=2*10**11,bytes_accessed=5*10**7,transcendentals=3*10**7),
        name="attn_backward",
    )(lo,mid,hi,q,k,v,do,o,lse,cs_tok)


def update(weight, gradient, moment, average, learning_rate):
    moment_new = MOMENTUM * moment + gradient
    weight_new = weight - learning_rate * (gradient + MOMENTUM * moment_new)
    average_new = EMA_DECAY * average + (1.0 - EMA_DECAY) * weight_new
    return (weight_new, moment_new, average_new, weight_new.astype(jnp.bfloat16))


TN = (((0,), (0,)), ((), ()))


def norm_rows(v):
    centred = v - jnp.mean(v, axis=-1, keepdims=True)
    inverse = lax.rsqrt(jnp.mean(centred * centred, axis=-1, keepdims=True) + EPSILON)
    return centred * inverse, inverse


def norm_rows_back(grad, normed, inverse):
    return inverse * (
        grad
        - jnp.mean(grad, axis=-1, keepdims=True)
        - normed * jnp.mean(grad * normed, axis=-1, keepdims=True)
    )


def gelu_pair(x):
    c = math.sqrt(2.0 / math.pi)
    sq = x * x
    t = jnp.tanh(c * (x + 0.044715 * (x * sq)))
    half = 0.5 * (1.0 + t)
    return x * half, half + (0.5 * c) * x * (1.0 - t * t) * (1.0 + 0.134145 * sq)


def mid_kernel(
    o_hbm, hid_ref, mod_ref, noise_ref, tw_ref, head_ref, gs_ref, wu_hbm, wd_hbm, wa_hbm,
    dmix_hbm, dx1_ref, dmod_ref, loss_ref, rest_hbm,
    o_ref, dmix_ref, wo_ref, wu_ref, wd_ref, att, x1, out, dx2, n2, n2t, act, dgl, dout, doutt, datt, datt_t,
    send_a, recv_a, send_c, recv_c, send_e, recv_e, stage, ghead_ref, go_ref, gh_t,
    wsem, gsem, ssem, rsem, o_sem, m_sem, s_m, r_m, *, tp,
):
    f = lax.axis_index("frames")
    h = lax.axis_index("mp")
    bf16 = jnp.bfloat16
    x_peer = {"mp": 1 - h}
    tp_peer = x_peer
    core = lax.rem(f, 2)
    core_peer = {"frames": f + 1 - 2 * core}
    half = hid_ref.shape[0]
    rows = 128
    chunks = half // rows
    width = hid_ref.shape[1]
    ff = wu_hbm.shape[1]
    e = o_ref.shape[1]
    ft = 512
    dt = 256

    weights = [
        pltpu.make_async_copy(wu_hbm, wu_ref, wsem.at[0]),
        pltpu.make_async_copy(wd_hbm, wd_ref, wsem.at[1]),
    ]
    load_out = pltpu.make_async_copy(wa_hbm.at[3], wo_ref, wsem.at[2])
    load_out.start()
    for w in weights:
        w.start()

    barrier = pltpu.get_barrier_semaphore()
    for peer in (x_peer, core_peer):
        pl.semaphore_signal(barrier, inc=1, device_id=peer, device_id_type=pl.DeviceIdType.MESH)
    pl.semaphore_wait(barrier, 2)
    tok_all = o_ref.shape[0]
    eh = e // 2

    def at(start, size):
        return pl.ds(pl.multiple_of(start, size), size)

    def copy(src, dst, phase, c, peer):
        return pltpu.make_async_remote_copy(
            src_ref=src, dst_ref=dst, send_sem=ssem.at[phase, c], recv_sem=rsem.at[phase, c],
            device_id=peer, device_id_type=pl.DeviceIdType.MESH,
        )

    def copy_a(c):
        return copy(send_a.at[at(c * rows, rows)], recv_a.at[at(c * rows, rows)], 0, c, x_peer)

    def copy_b(c):
        return copy(
            n2.at[at(c * 2 * rows, rows)], n2.at[at(c * 2 * rows + rows, rows)], 1, c, tp_peer
        )

    def copy_c(c):
        return copy(send_c.at[at(c * rows, rows)], recv_c.at[at(c * rows, rows)], 2, c, tp_peer)

    def copy_d(c):
        return copy(
            dout.at[at(c * 2 * rows, rows)], dout.at[at(c * 2 * rows + rows, rows)], 3, c, tp_peer
        )

    def copy_e(c):
        return copy(send_e.at[at(c * rows, rows)], recv_e.at[at(c * rows, rows)], 4, c, tp_peer)

    def copy_f(c):
        mine = datt.at[at(h * half + c * rows, rows)]
        return copy(mine, mine, 5, c, x_peer)

    def lanes(k):
        return pl.ds(pl.multiple_of(k * eh, eh), eh)

    mine_o = pltpu.make_async_copy(
        o_hbm.at[at(core * tok_all, tok_all)], o_ref.at[:, lanes(core)], o_sem.at[0]
    )

    def give_o(k):
        return pltpu.make_async_remote_copy(
            src_ref=o_hbm.at[at((1 - core) * tok_all, tok_all)], dst_ref=o_ref.at[:, lanes(k)],
            send_sem=o_sem.at[1], recv_sem=o_sem.at[2], device_id=core_peer,
            device_id_type=pl.DeviceIdType.MESH,
        )

    give_o(core).start()
    mine_o.start()
    load_out.wait()
    mine_o.wait()
    give_o(1 - core).wait_recv()

    def mix_keep(rows_at, i):
        return pltpu.make_async_copy(
            dmix_ref.at[at(rows_at, rows), lanes(core)],
            dmix_hbm.at[at(core * tok_all + rows_at, rows)],
            m_sem.at[i],
        )

    def mix_give(rows_at, i, k):
        return pltpu.make_async_remote_copy(
            src_ref=dmix_ref.at[at(rows_at, rows), lanes(1 - core)],
            dst_ref=dmix_hbm.at[at(k * tok_all + rows_at, rows)],
            send_sem=s_m.at[i], recv_sem=r_m.at[i], device_id=core_peer,
            device_id_type=pl.DeviceIdType.MESH,
        )

    def phase_a(c, _):
        part = o_ref[at((1 - h) * half + c * rows, rows), :]
        send_a[at(c * rows, rows), :] = dotf(part, wo_ref[...], NT).astype(bf16)
        copy_a(c).start()
        return 0

    lax.fori_loop(0, chunks, phase_a, 0)

    def phase_b(c, _):
        part = o_ref[at(h * half + c * rows, rows), :]
        att[at(c * rows, rows), :] = dotf(part, wo_ref[...], NT)
        copy_a(c).wait_recv()
        for k in range(rows // TPF):
            r = at(c * rows + k * TPF, TPF)
            frame = pl.ds(c * (rows // TPF) + k, 1)
            a = att[r, :] + recv_a[r, :].astype(jnp.float32)
            att[r, :] = a
            v = hid_ref[r, :] + mod_ref[0, frame, :] * a
            x1[r, :] = v
            y, _inv = norm_rows(v)
            n2[at(c * 2 * rows + k * TPF, TPF), :] = (
                y * (1.0 + mod_ref[2, frame, :]) + mod_ref[1, frame, :]
            ).astype(bf16)
        copy_b(c).start()
        return 0

    lax.fori_loop(0, chunks, phase_b, 0)
    for w in weights:
        w.wait()

    def phase_c(c, _):
        copy_b(c).wait_recv()
        tok = at(c * 2 * rows, 2 * rows)
        n2t[:, tok] = n2[tok, :].T

        def up(i, _):
            cols = at(i * ft, ft)
            a, g = gelu_pair(dotf(n2[tok, :], wu_ref[:, cols]))
            act[tok, cols] = a.astype(bf16)
            dgl[tok, cols] = g.astype(bf16)
            return 0

        lax.fori_loop(0, ff // ft, up, 0)

        def down(i, _):
            cols = at(i * dt, dt)
            res = dotf(act[tok, :], wd_ref[cols, :], NT)
            out[at(c * rows, rows), cols] = res[:rows]
            send_c[at(c * rows, rows), cols] = res[rows:].astype(bf16)
            return 0

        lax.fori_loop(0, width // dt, down, 0)
        copy_c(c).start()
        return 0

    lax.fori_loop(0, chunks, phase_c, 0)

    ghead_ref[...] = jnp.zeros_like(ghead_ref)
    loss_ref[...] = jnp.zeros_like(loss_ref)

    def phase_d(c, _):
        copy_c(c).wait_recv()
        for k in range(rows // TPF):
            r = at(c * rows + k * TPF, TPF)
            frame = pl.ds(c * (rows // TPF) + k, 1)
            o = out[r, :] + recv_c[r, :].astype(jnp.float32)
            gate = mod_ref[3, frame, :]
            y, inv = norm_rows(x1[r, :] + gate * o)
            fn = y.astype(bf16)
            misfit = dotf(fn, head_ref[...], NT) - noise_ref[r, :]
            weighted = tw_ref[r, :] * misfit
            loss_ref[...] += weighted * misfit
            d_pred = (2.0 * gs_ref[0] * weighted).astype(bf16)
            ghead_ref[...] += dotf(d_pred, fn, TN)
            d_x2 = norm_rows_back(dotf(d_pred, head_ref[...]), y, inv)
            dx2[r, :] = d_x2
            dmod_ref[3, frame, :] = jnp.sum(d_x2 * o, axis=0, keepdims=True)
            dout[at(c * 2 * rows + k * TPF, TPF), :] = (gate * d_x2).astype(bf16)
        copy_d(c).start()
        return 0

    lax.fori_loop(0, chunks, phase_d, 0)

    def phase_e(c, _):
        copy_d(c).wait_recv()
        tok = at(c * 2 * rows, 2 * rows)
        doutt[:, tok] = dout[tok, :].T

        def down(i, _):
            cols = at(i * ft, ft)
            g = dotf(dout[tok, :], wd_ref[:, cols]) * dgl[tok, cols].astype(jnp.float32)
            dgl[tok, cols] = g.astype(bf16)
            return 0

        lax.fori_loop(0, ff // ft, down, 0)

        def up(i, _):
            cols = at(i * dt, dt)
            res = dotf(dgl[tok, :], wu_ref[cols, :], NT)
            out[at(c * rows, rows), cols] = res[:rows]
            send_e[at(c * rows, rows), cols] = res[rows:].astype(bf16)
            return 0

        lax.fori_loop(0, width // dt, up, 0)
        copy_e(c).start()
        return 0

    lax.fori_loop(0, chunks, phase_e, 0)

    def phase_f(c, _):
        copy_e(c).wait_recv()
        for k in range(rows // TPF):
            r = at(c * rows + k * TPF, TPF)
            frame = pl.ds(c * (rows // TPF) + k, 1)
            g = out[r, :] + recv_e[r, :].astype(jnp.float32)
            y, inv = norm_rows(x1[r, :])
            dmod_ref[1, frame, :] = jnp.sum(g, axis=0, keepdims=True)
            dmod_ref[2, frame, :] = jnp.sum(g * y, axis=0, keepdims=True)
            d_x1 = dx2[r, :] + norm_rows_back(g * (1.0 + mod_ref[2, frame, :]), y, inv)
            dx1_ref[r, :] = d_x1
            dmod_ref[0, frame, :] = jnp.sum(d_x1 * att[r, :], axis=0, keepdims=True)
            datt[at(h * half + c * rows + k * TPF, TPF), :] = (mod_ref[0, frame, :] * d_x1).astype(
                bf16
            )
        copy_f(c).start()
        return 0

    lax.fori_loop(0, chunks, phase_f, 0)

    def weight_grads(left, right, start):
        def put(slot, i):
            return pltpu.make_async_copy(
                stage.at[slot], rest_hbm.at[at(i * dt, dt), pl.ds(start, ff)], gsem.at[slot]
            )

        def tile(i, _):
            slot = lax.rem(i, 2)

            @pl.when(i >= 2)
            def _():
                put(slot, i - 2).wait()

            def cols_of(j, _):
                cols = at(j * ft, ft)
                stage[slot, :, cols] = dotf(left[at(i * dt, dt), :], right[:, cols]).astype(bf16)
                return 0

            lax.fori_loop(0, ff // ft, cols_of, 0)
            put(slot, i).start()
            return 0

        lax.fori_loop(0, width // dt, tile, 0)
        for i in (width // dt - 2, width // dt - 1):
            put(i % 2, i).wait()

    weight_grads(n2t, dgl, 0)
    weight_grads(doutt, act, ff)

    def own_mix(c, _):
        first = h * half + c * rows
        tok = at(first, rows)
        datt_t[:, tok] = datt[tok, :].T
        dmix_ref[tok, :] = dotf(datt[tok, :], wo_ref[...]).astype(bf16)
        mix_keep(first, c).start()
        mix_give(first, c, core).start()
        return 0

    lax.fori_loop(0, chunks, own_mix, 0)

    def phase_g(c, _):
        tok = at((1 - h) * half + c * rows, rows)
        theirs = datt.at[tok]
        copy(theirs, theirs, 5, c, x_peer).wait_recv()
        datt_t[:, tok] = datt[tok, :].T
        dmix_ref[tok, :] = dotf(datt[tok, :], wo_ref[...]).astype(bf16)
        first = (1 - h) * half + c * rows
        mix_keep(first, chunks + c).start()
        mix_give(first, chunks + c, core).start()
        return 0

    lax.fori_loop(0, chunks, phase_g, 0)

    def grad_out(i, _):
        d = at(i * dt, dt)
        go_ref[d, :] = dotf(datt_t[d, :], o_ref[...]).astype(bf16)
        return 0

    lax.fori_loop(0, width // dt, grad_out, 0)
    gh_t[...] = ghead_ref[...].T.astype(bf16)
    ends = [
        pltpu.make_async_copy(go_ref, rest_hbm.at[:, pl.ds(2 * ff, e)], gsem.at[2]),
        pltpu.make_async_copy(gh_t, rest_hbm.at[:, pl.ds(2 * ff + e, 128)], gsem.at[3]),
    ]
    for one in ends:
        one.start()
    for one in ends:
        one.wait()
    def sent(c, _):
        for one in (copy_a, copy_b, copy_c, copy_d, copy_e, copy_f):
            one(c).wait_send()
        for side in range(2):
            first = (h if side == 0 else 1 - h) * half + c * rows
            i = side * chunks + c
            mix_keep(first, i).wait()
            mix_give(first, i, core).wait_send()
            mix_give(first, i, 1 - core).wait_recv()
        return 0

    lax.fori_loop(0, chunks, sent, 0)
    give_o(core).wait_send()


def mid_block(o, hid, mod, noise, tw, head, gs, wu, wd, wa, tp, cid):
    tok, e = o.shape[0] // 2, 2 * o.shape[1]
    half, width = hid.shape
    ff = wu.shape[1]
    own_frames = half // TPF
    f32, bf16 = jnp.float32, jnp.bfloat16
    vm = pl.BlockSpec(memory_space=pltpu.VMEM)
    anym = pl.BlockSpec(memory_space=pl.ANY)
    V = pltpu.VMEM
    return pl.pallas_call(
        functools.partial(mid_kernel, tp=tp),
        in_specs=[anym] + [vm] * 5 + [pl.BlockSpec(memory_space=pltpu.SMEM), anym, anym, anym],
        out_specs=[anym] + [vm] * 3 + [anym],
        out_shape=[
            jax.ShapeDtypeStruct((2 * tok, e // 2), bf16),
            jax.ShapeDtypeStruct((half, width), f32),
            jax.ShapeDtypeStruct((4, own_frames, width), f32),
            jax.ShapeDtypeStruct((TPF, 128), f32),
            jax.ShapeDtypeStruct((width, 2 * ff + e + 128), bf16),
        ],
        scratch_shapes=[
            V((tok, e), bf16), V((tok, e), bf16),
            V((width, e), bf16), V((width, ff), bf16), V((width, ff), bf16),
            V((half, width), f32), V((half, width), f32), V((half, width), f32),
            V((half, width), f32),
            V((2 * half, width), bf16), V((width, 2 * half), bf16),
            V((2 * half, ff), bf16), V((2 * half, ff), bf16),
            V((2 * half, width), bf16), V((width, 2 * half), bf16),
            V((tok, width), bf16), V((width, tok), bf16),
            V((half, width), bf16), V((half, width), bf16),
            V((half, width), bf16), V((half, width), bf16),
            V((half, width), bf16), V((half, width), bf16),
            V((2, 256, ff), bf16), V((128, width), f32), V((width, e), bf16),
            V((width, 128), bf16),
            pltpu.SemaphoreType.DMA((3,)), pltpu.SemaphoreType.DMA((4,)),
            pltpu.SemaphoreType.DMA((6, half // 128)), pltpu.SemaphoreType.DMA((6, half // 128)),
            pltpu.SemaphoreType.DMA((3,)), pltpu.SemaphoreType.DMA((2 * half // 128,)),
            pltpu.SemaphoreType.DMA((2 * half // 128,)), pltpu.SemaphoreType.DMA((2 * half // 128,)),
        ],
        compiler_params=pltpu.CompilerParams(
            vmem_limit_bytes=62 << 20, collective_id=cid, has_side_effects=True
        ),
        cost_estimate=pl.CostEstimate(
            flops=4 * 10**10, bytes_accessed=3 * 10**7, transcendentals=2 * 10**6
        ),
        name="feed_forward",
    )(o, hid, mod, noise, tw, head, gs, wu, wd, wa)


def split_three(v):
    high = v.astype(jnp.bfloat16)
    left = v - high.astype(jnp.float32)
    middle = left.astype(jnp.bfloat16)
    return high, middle, (left - middle.astype(jnp.float32)).astype(jnp.bfloat16)


def turn_back(g, cosine, sine, rot):
    parts = split_three(g * sine)
    return (g * cosine + sum(dotf(p, rot, NT) for p in parts)).astype(jnp.bfloat16)


def tail_kernel(
    dq_ref, n1_ref, w_ref, fcos_ref, fsin_ref, pcos_ref, psin_ref, rot_ref, hid_ref, scale_ref, dx1_ref, inp_ref,
    dk_hbm, dv_hbm,
    gq_ref, gin_ref, dss_ref,
    relayed, own, yrecv, zrecv, give, n1t, dproj, send_x, recv_x, part,
    lsem, s_d, r_d, s_y, r_y, s_z, r_z, s_x, r_x,
):
    f = lax.axis_index("frames")
    h = lax.axis_index("mp")
    n = lax.axis_size("frames")
    core = lax.rem(f, 2)
    odd = lax.rem(lax.div(f, 2), 2)
    core_peer = {"frames": f + 1 - 2 * core}
    y_peer = {"frames": f + 2 - 4 * odd}
    before = {"frames": lax.rem(f - 4 + n, n)}
    after = {"frames": lax.rem(f + 4, n)}
    x_peer = {"mp": 1 - h}
    tok, width = n1_ref.shape
    eh = dq_ref.shape[1]
    half = tok // 2
    rows = 256
    f32, bf16 = jnp.float32, jnp.bfloat16
    MESH = pl.DeviceIdType.MESH
    sides = (dk_hbm, dv_hbm)
    share = width // n

    def at(start, size):
        return pl.ds(pl.multiple_of(start, size), size)

    loads = [
        pltpu.make_async_copy(
            sides[s].at[pl.ds(b * 2 * tok, 2 * tok)], (own, relayed)[j].at[s], lsem.at[s, j]
        )
        for s in range(2)
        for j, b in enumerate((2, 0))
    ]
    for one in loads:
        one.start()

    barrier = pltpu.get_barrier_semaphore()
    for peer in (core_peer, y_peer, x_peer):
        pl.semaphore_signal(barrier, inc=1, device_id=peer, device_id_type=MESH)

    @pl.when(f >= 4)
    def _():
        pl.semaphore_signal(barrier, inc=1, device_id=before, device_id_type=MESH)

    @pl.when(f + 4 < n)
    def _():
        pl.semaphore_signal(barrier, inc=1, device_id=after, device_id_type=MESH)

    pl.semaphore_wait(barrier, 3 + jnp.where(f >= 4, 1, 0) + jnp.where(f + 4 < n, 1, 0))

    def half_at(i2):
        return lax.rem(i2 + 1 - h, 2) * half

    def rows_of(i2, tc):
        return tc * tok + half_at(i2)

    def remote(src, dst, send, recv, peer):
        return pltpu.make_async_remote_copy(
            src_ref=src, dst_ref=dst, send_sem=send, recv_sem=recv, device_id=peer,
            device_id_type=MESH,
        )

    def y_copy(i2, tc, s):
        first = rows_of(i2, tc)
        i = 2 * i2 + tc
        return remote(
            sides[s].at[at(2 * tok + first, half)], yrecv.at[s, at(first, half)],
            s_y.at[s, i], r_y.at[s, i], y_peer,
        )

    def z_copy(i2, tc, s):
        r = at(rows_of(i2, tc), half)
        i = 2 * i2 + tc
        return remote(relayed.at[s, r], zrecv.at[s, r], s_z.at[s, i], r_z.at[s, i], before)

    def d_copy(k, i2, tc):
        r = at(half_at(i2), half)
        return remote(
            give.at[k, r], dproj.at[k, r, pl.ds(tc * eh, eh)], s_d.at[k, i2], r_d.at[k, i2],
            core_peer,
        )

    def x_copy(i):
        r = at(i * rows, rows)
        return remote(send_x.at[r], recv_x.at[r], s_x.at[i], r_x.at[i], x_peer)

    for one in loads:
        one.wait()

    def start_far(i2, _):
        for tc in range(2):
            for s in range(2):
                y_copy(i2, tc, s).start()

                @pl.when((odd == 0) & (f >= 4))
                def _():
                    z_copy(i2, tc, s).start()

        return 0

    lax.fori_loop(0, 2, start_far, 0)

    @pl.when(f + 4 >= n)
    def _():
        zrecv[...] = jnp.zeros_like(zrecv)

    def settle(k, i2, tc, value):
        r = at(half_at(i2), half)

        @pl.when(core == tc)
        def _():
            dproj[k, r, tc * eh : (tc + 1) * eh] = value

        @pl.when(core != tc)
        def _():
            give[k, r, :] = value
            d_copy(k, i2, 1 - tc).start()

    def arrived(k, i2):
        for tc in range(2):

            @pl.when(core == tc)
            def _():
                d_copy(k, i2, 1 - tc).wait_recv()

    def turned(g, i2, tc):
        first = tc * (tok // TPF) + lax.div(half_at(i2), TPF)
        cosine = turn_table(fcos_ref, pcos_ref, first, half // TPF)
        sine = turn_table(fsin_ref, psin_ref, first, half // TPF)
        return turn_back(g, cosine, sine, rot_ref[...])

    def relay(i2, _):
        for tc in range(2):
            r = at(rows_of(i2, tc), half)
            settle(0, i2, tc, turned(dq_ref[r, :], i2, tc))

            @pl.when(odd == 1)
            def _():
                for s in range(2):
                    y_copy(i2, tc, s).wait_recv()

                    @pl.when(f >= 4)
                    def _():
                        relayed[s, r, :] = (
                            relayed[s, r, :].astype(f32) + yrecv[s, r, :].astype(f32)
                        ).astype(bf16)
                        z_copy(i2, tc, s).start()

        for b in range(2):
            r = at(half_at(i2) + b * rows, rows)
            n1t[:, r] = n1_ref[r, :].T
        return 0

    lax.fori_loop(0, 2, relay, 0)
    for i2 in range(2):
        arrived(0, i2)

    def grads(k):
        def tile(i, _):
            res = dotf(n1t[at(i * 256, 256), :], dproj[k]).astype(bf16)
            for q in range(256 // share):
                j = i * (256 // share // 4) + q // 4
                gq_ref[q % 2, (q // 2) % 2, k, at(j * share, share), :] = res[
                    q * share : (q + 1) * share
                ]
            return 0

        lax.fori_loop(0, width // 256, tile, 0)

    grads(0)

    def finish(i2, _):
        for tc in range(2):
            r = at(rows_of(i2, tc), half)
            for s in range(2):

                @pl.when(odd == 0)
                def _():
                    y_copy(i2, tc, s).wait_recv()

                @pl.when(f + 4 < n)
                def _():
                    z_copy(i2, tc, s).wait_recv()

                total = (
                    own[s, r, :].astype(f32)
                    + jnp.where(odd == 0, yrecv[s, r, :].astype(f32), 0.0)
                    + zrecv[s, r, :].astype(f32)
                )
                if s == 0:
                    settle(1, i2, tc, turned(total, i2, tc))
                else:
                    settle(2, i2, tc, total.astype(bf16))

        arrived(1, i2)
        arrived(2, i2)

        def block_of(q, _):
            b = lax.div(q, width // 256)
            cols = at(lax.rem(q, width // 256) * 256, 256)
            r = at(half_at(i2) + b * rows, rows)
            res = sum(dotf(dproj[k, r, :], w_ref[k, cols, :], NT) for k in range(3))

            @pl.when(i2 == 0)
            def _():
                send_x[at(b * rows, rows), cols] = res.astype(bf16)

            @pl.when((i2 == 0) & (lax.rem(q, width // 256) == width // 256 - 1))
            def _():
                x_copy(b).start()

            @pl.when(i2 == 1)
            def _():
                part[at(b * rows, rows), cols] = res

            return 0

        lax.fori_loop(0, half // rows * (width // 256), block_of, 0)
        return 0

    lax.fori_loop(0, 2, finish, 0)
    grads(1)
    grads(2)
    gin_ref[...] = jnp.zeros_like(gin_ref)

    def norm_back(i, _):
        x_copy(i).wait_recv()
        for k in range(rows // TPF):
            r = at(i * rows + k * TPF, TPF)
            frame = pl.ds(i * (rows // TPF) + k, 1)
            g = part[r, :] + recv_x[r, :].astype(f32)
            y, inv = norm_rows(hid_ref[r, :])
            dss_ref[0, frame, :] = jnp.sum(g, axis=0, keepdims=True)
            dss_ref[1, frame, :] = jnp.sum(g * y, axis=0, keepdims=True)
            d_hid = dx1_ref[r, :] + norm_rows_back(g * (1.0 + scale_ref[frame, :]), y, inv)
            gin_ref[...] += dotf(inp_ref[r, :], d_hid.astype(bf16), TN)
        return 0

    lax.fori_loop(0, half // rows, norm_back, 0)

    def sent(i2, _):
        for tc in range(2):
            for s in range(2):
                y_copy(i2, tc, s).wait_send()

                @pl.when(f >= 4)
                def _():
                    z_copy(i2, tc, s).wait_send()

            @pl.when(core != tc)
            def _():
                for k in range(3):
                    d_copy(k, i2, 1 - tc).wait_send()

        x_copy(i2).wait_send()
        return 0

    lax.fori_loop(0, half // rows, sent, 0)


def tail_block(dq, n1, w, tables, rot, hid, scale, dx1, inp, dk, dv, cid):
    tok, width = n1.shape
    e = 2 * dq.shape[1]
    half = tok // 2
    f32, bf16 = jnp.float32, jnp.bfloat16
    vm = pl.BlockSpec(memory_space=pltpu.VMEM)
    anym = pl.BlockSpec(memory_space=pl.ANY)
    V = pltpu.VMEM
    D_ = pltpu.SemaphoreType.DMA
    return pl.pallas_call(
        tail_kernel,
        in_specs=[vm] * 12 + [anym] * 2,
        out_specs=[vm] * 3,
        out_shape=[
            jax.ShapeDtypeStruct((2, 2, 3, width // 4, e), bf16),
            jax.ShapeDtypeStruct((128, width), f32),
            jax.ShapeDtypeStruct((2, half // TPF, width), f32),
        ],
        scratch_shapes=[
            V((2, tok * 2, e // 2), bf16), V((2, tok * 2, e // 2), bf16),
            V((2, tok * 2, e // 2), bf16), V((2, tok * 2, e // 2), bf16),
            V((3, tok, e // 2), bf16), V((width, tok), bf16), V((3, tok, e), bf16),
            V((half, width), bf16), V((half, width), bf16), V((half, width), f32),
            D_((2, 2)), D_((3, 2)), D_((3, 2)), D_((2, 4)), D_((2, 4)),
            D_((2, 4)), D_((2, 4)), D_((half // 256,)), D_((half // 256,)),
        ],
        compiler_params=pltpu.CompilerParams(
            vmem_limit_bytes=56 << 20, collective_id=cid, has_side_effects=True
        ),
        cost_estimate=pl.CostEstimate(
            flops=10**9, bytes_accessed=10**6, transcendentals=0
        ),
        name="projection_backward",
    )(dq, n1, w, *tables, rot, hid, scale, dx1, inp, dk, dv)


def proj_kernel(
    inp_ref, win_ref, mod_ref, w_ref, fcos_ref, fsin_ref, pcos_ref, psin_ref, rot_ref,
    n1_ref, hid_ref, q_hbm, k_hbm, v_hbm,
    kv, give, q_keep, wr,
    lsem, qsem, s_core, r_core, s_y, r_y, s_z, r_z,
):
    f = lax.axis_index("frames")
    h = lax.axis_index("mp")
    n = lax.axis_size("frames")
    core = lax.rem(f, 2)
    odd = lax.rem(lax.div(f, 2), 2)
    core_peer = {"frames": f + 1 - 2 * core}
    y_peer = {"frames": f + 2 - 4 * odd}
    before = {"frames": lax.rem(f - 4 + n, n)}
    after = {"frames": lax.rem(f + 4, n)}
    tok, width = n1_ref.shape
    e = w_ref.shape[2]
    eh = e // 2
    low_core = core == 0
    half = tok // 2
    rows = 256
    chunks = tok // rows
    bf16 = jnp.bfloat16
    MESH = pl.DeviceIdType.MESH
    sides = (k_hbm, v_hbm)
    has_z = f >= 4
    has_next = f + 4 < n
    has_y = has_z | (odd == 1)

    def at(start, size):
        return pl.ds(pl.multiple_of(start, size), size)

    barrier = pltpu.get_barrier_semaphore()
    for peer in (core_peer, y_peer):
        pl.semaphore_signal(barrier, inc=1, device_id=peer, device_id_type=MESH)

    @pl.when(has_z)
    def _():
        pl.semaphore_signal(barrier, inc=1, device_id=before, device_id_type=MESH)

    @pl.when(has_next)
    def _():
        pl.semaphore_signal(barrier, inc=1, device_id=after, device_id_type=MESH)

    def embed(i, _):
        for k in range(2):
            r = at(i * 2 * TPF + k * TPF, TPF)
            frame = pl.ds(i * 2 + k, 1)
            v = dotf(inp_ref[r, :], win_ref[...])
            y, _inv = norm_rows(v)
            n1_ref[r, :] = (y * (1.0 + mod_ref[1, frame, :]) + mod_ref[0, frame, :]).astype(bf16)

            @pl.when(lax.div(i * 2 * TPF, half) == h)
            def _():
                hid_ref[at(lax.rem(i * 2 * TPF, half) + k * TPF, TPF), :] = v

        return 0

    lax.fori_loop(0, tok // (2 * TPF), embed, 0)

    def turn_weights(i, _):
        d = at(i * 256, 256)
        for k in range(2):
            for b in range(e // 256):
                cols = slice(b * 256, (b + 1) * 256)
                wr[k, d, cols] = dotf(w_ref[k, d, cols], rot_ref[...]).astype(bf16)
        return 0

    lax.fori_loop(0, width // 256, turn_weights, 0)
    pl.semaphore_wait(barrier, 2 + jnp.where(has_z, 1, 0) + jnp.where(has_next, 1, 0))

    def remote(src, dst, send, recv, peer):
        return pltpu.make_async_remote_copy(
            src_ref=src, dst_ref=dst, send_sem=send, recv_sem=recv, device_id=peer,
            device_id_type=MESH,
        )

    def block(s, b, i):
        return sides[s].at[at(b * tok + i * rows, rows)]

    def mine(s, tc, i):
        return kv.at[s, tc, at(i * rows, rows)]

    def keep(s, tc, i):
        return pltpu.make_async_copy(mine(s, tc, i), block(s, 4 + tc, i), lsem.at[s, tc, i])

    def z_copy(s, tc, i):
        return remote(
            mine(s, tc, i), block(s, tc, i), s_z.at[s, tc, i], r_z.at[s, tc, i], after
        )

    def y_copy(s, tc, i, src):
        return remote(src, block(s, 2 + tc, i), s_y.at[s, tc, i], r_y.at[s, tc, i], y_peer)

    def core_copy(s, i, tc):
        return remote(
            give.at[s, at(i * rows, rows)], mine(s, tc, i), s_core.at[s, i], r_core.at[s, i],
            core_peer,
        )

    def q_rows(tc, i):
        return q_hbm.at[at(tc * tok + i * rows, rows)]

    def q_own(i):
        return pltpu.make_async_copy(
            q_keep.at[at(i * rows, rows)], q_rows(core, i), qsem.at[i]
        )

    def q_copy(i, tc):
        return remote(
            give.at[2, at(i * rows, rows)], q_rows(tc, i), s_core.at[2, i], r_core.at[2, i],
            core_peer,
        )

    def onward(s, tc, i):
        keep(s, tc, i).start()

        @pl.when(has_next)
        def _():
            z_copy(s, tc, i).start()

        @pl.when(odd == 0)
        def _():
            y_copy(s, tc, i, mine(s, tc, i)).start()

    def rotated(r, i, k):
        frames = rows // TPF
        first = core * (tok // TPF) + i * frames
        cosine = turn_table(fcos_ref, pcos_ref, first, frames)
        sine = turn_table(fsin_ref, psin_ref, first, frames)
        parts = []
        for b in range(e // 256):
            cols = slice(b * 256, (b + 1) * 256)
            plain = dotf(n1_ref[r, :], w_ref[k, :, cols])
            turned = dotf(n1_ref[r, :], wr[k, :, cols])
            parts.append((plain * cosine + turned * sine).astype(bf16))
        return parts

    def own_chunk(i, _):
        r = at(i * rows, rows)
        keys = rotated(r, i, 1)
        values = dotf(n1_ref[r, :], w_ref[2]).astype(bf16)
        for s, pair in enumerate((keys, (values[:, :eh], values[:, eh:]))):
            kv[s, core, r, :] = jnp.where(low_core, pair[0], pair[1])
            give[s, r, :] = jnp.where(low_core, pair[1], pair[0])
            core_copy(s, i, core).start()
            onward(s, core, i)
        return 0

    lax.fori_loop(0, chunks, own_chunk, 0)

    def from_core(i, _):
        for s in range(2):
            core_copy(s, i, 1 - core).wait_recv()
            onward(s, 1 - core, i)
        return 0

    lax.fori_loop(0, chunks, from_core, 0)

    def queries(i, _):
        r = at(i * rows, rows)
        pair = rotated(r, i, 0)
        q_keep[r, :] = jnp.where(low_core, pair[0], pair[1])
        give[2, r, :] = jnp.where(low_core, pair[1], pair[0])
        q_own(i).start()
        q_copy(i, core).start()
        return 0

    lax.fori_loop(0, chunks, queries, 0)

    def from_z(g, _):
        tc = lax.rem(core + lax.div(g, chunks), 2)
        i = lax.rem(g, chunks)

        @pl.when(has_z)
        def _():
            for s in range(2):
                z_copy(s, tc, i).wait_recv()

                @pl.when(odd == 1)
                def _():
                    y_copy(s, tc, i, block(s, tc, i)).start()

        return 0

    lax.fori_loop(0, 2 * chunks, from_z, 0)

    def ended(i, _):
        q_own(i).wait()
        q_copy(i, 1 - core).wait_recv()
        q_copy(i, core).wait_send()
        for s in range(2):
            core_copy(s, i, core).wait_send()
            for tc in range(2):
                keep(s, tc, i).wait()

                @pl.when(has_y)
                def _():
                    y_copy(s, tc, i, mine(s, tc, i)).wait_recv()

                @pl.when(has_next)
                def _():
                    z_copy(s, tc, i).wait_send()

                @pl.when((odd == 0) | has_z)
                def _():
                    y_copy(s, tc, i, mine(s, tc, i)).wait_send()

        return 0

    lax.fori_loop(0, chunks, ended, 0)


def proj_block(inp, win, mod, w, tables, rot, reach, cid):
    tok = inp.shape[0]
    width, e = w.shape[1:]
    f32, bf16 = jnp.float32, jnp.bfloat16
    vm = pl.BlockSpec(memory_space=pltpu.VMEM)
    anym = pl.BlockSpec(memory_space=pl.ANY)
    V = pltpu.VMEM
    D_ = pltpu.SemaphoreType.DMA
    chunks = tok // 256
    return pl.pallas_call(
        proj_kernel,
        in_specs=[vm] * 9,
        out_specs=[vm] * 2 + [anym] * 3,
        out_shape=[
            jax.ShapeDtypeStruct((tok, width), bf16),
            jax.ShapeDtypeStruct((tok // 2, width), f32),
            jax.ShapeDtypeStruct((2 * tok, e // 2), bf16),
            jax.ShapeDtypeStruct(((reach + 2) * tok, e // 2), bf16),
            jax.ShapeDtypeStruct(((reach + 2) * tok, e // 2), bf16),
        ],
        scratch_shapes=[
            V((2, 2, tok, e // 2), bf16), V((3, tok, e // 2), bf16), V((tok, e // 2), bf16),
            V((2, width, e), bf16),
            D_((2, 2, chunks)), D_((chunks,)), D_((3, chunks)), D_((3, chunks)),
            D_((2, 2, chunks)), D_((2, 2, chunks)), D_((2, 2, chunks)), D_((2, 2, chunks)),
        ],
        compiler_params=pltpu.CompilerParams(
            vmem_limit_bytes=48 << 20, collective_id=cid, has_side_effects=True
        ),
        cost_estimate=pl.CostEstimate(
            flops=6 * 10**10, bytes_accessed=3 * 10**7, transcendentals=0
        ),
        name="projection_forward",
    )(inp, win, mod, w, *tables, rot)


def last_kernel(
    g_hbm, gin_ref, dm_ref, cond_ref, wm_ref, loss_ref,
    sq_ref, sin_ref, smod_ref, dct_ref,
    g_own, g_in, near, near_in, side, side_in, far, far_in, ends, ends_peer, dm_peer, dm,
    dc_send, dc_peer,
    lsem, s_x, r_x, s_g, r_g, s_f, r_f, s_d, r_d, s_dz, r_dz,
):
    f = lax.axis_index("frames")
    h = lax.axis_index("mp")
    n = lax.axis_size("frames")
    nj = n // 4
    core = lax.rem(f, 2)
    y = lax.rem(lax.div(f, 2), 2)
    j = lax.div(f, 4)
    core_peer = {"frames": f + 1 - 2 * core}
    y_peer = {"frames": f + 2 - 4 * y}
    x_peer = {"mp": 1 - h}
    f32, bf16 = jnp.float32, jnp.bfloat16
    MESH = pl.DeviceIdType.MESH
    rows = g_hbm.shape[3] // nj

    def z_peer(t):
        return {"frames": lax.rem(f + 4 * t, n)}

    def from_j(t):
        return lax.rem(j - t + nj, nj)

    def at(start, size):
        return pl.ds(pl.multiple_of(start, size), size)

    load = pltpu.make_async_copy(g_hbm.at[core], g_own, lsem.at[0])
    load.start()
    barrier = pltpu.get_barrier_semaphore()
    for peer in [core_peer, y_peer, x_peer] + [z_peer(t) for t in range(1, nj)]:
        pl.semaphore_signal(barrier, inc=1, device_id=peer, device_id_type=MESH)
    pl.semaphore_wait(barrier, 2 + nj)

    def remote(src, dst, send, recv, peer):
        return pltpu.make_async_remote_copy(
            src_ref=src, dst_ref=dst, send_sem=send, recv_sem=recv, device_id=peer,
            device_id_type=MESH,
        )

    dm_x = remote(dm_ref.at[1 - h], dm_peer, s_x.at[0], r_x.at[0], x_peer)
    dm_x.start()
    core_g = remote(g_hbm.at[1 - core], near, s_g.at[0], r_g.at[0], core_peer)
    core_in = remote(gin_ref.at[1 - core], near_in, s_g.at[1], r_g.at[1], core_peer)
    core_g.start()
    core_in.start()

    dm_x.wait_recv()
    mine = dm_ref[h]
    theirs = dm_peer[...]
    low = h == 0
    dm[core, y, j] = jnp.concatenate(
        [jnp.where(low, mine, theirs), jnp.where(low, theirs, mine)], axis=0
    ).astype(bf16)

    def dm_z(t, src):
        block = dm.at[core, y, src]
        return remote(block, block, s_dz.at[0, t], r_dz.at[0, t], z_peer(t))

    for t in range(1, nj):
        dm_z(t, j).start()
    load.wait()
    core_g.wait_recv()
    core_in.wait_recv()

    def add_near(i, _):
        for s in range(2):
            for k in range(g_own.shape[1]):
                r = at(i * rows, rows)
                g_own[s, k, r, :] = (
                    g_own[s, k, r, :].astype(f32) + near[s, k, r, :].astype(f32)
                ).astype(bf16)
        return 0

    lax.fori_loop(0, nj, add_near, 0)
    g_in[...] = (gin_ref[core].astype(f32) + near_in[...].astype(f32)).astype(bf16)
    for t in range(1, nj):
        dm_z(t, from_j(t)).wait_recv()

    def dm_y(side_index):
        block = dm.at[core, side_index]
        return remote(block, block, s_d.at[0], r_d.at[0], y_peer)

    dm_y(y).start()
    y_g = remote(g_own.at[1 - y], side, s_g.at[2], r_g.at[2], y_peer)
    y_in = remote(g_in.at[1 - y], side_in, s_g.at[3], r_g.at[3], y_peer)
    y_g.start()
    y_in.start()
    dm_y(1 - y).wait_recv()

    def dm_core(core_index):
        block = dm.at[core_index]
        return remote(block, block, s_d.at[1], r_d.at[1], core_peer)

    dm_core(core).start()
    y_g.wait_recv()
    y_in.wait_recv()

    def add_side(i, _):
        for k in range(g_own.shape[1]):
            r = at(i * rows, rows)
            side[k, r, :] = (
                g_own[y, k, r, :].astype(f32) + side[k, r, :].astype(f32)
            ).astype(bf16)
        return 0

    lax.fori_loop(0, nj, add_side, 0)
    side_in[...] = (g_in[y].astype(f32) + side_in[...].astype(f32)).astype(bf16)

    def far_g(t):
        there = at(lax.rem(j + t, nj) * rows, rows)
        return remote(
            side.at[:, there], far.at[t - 1], s_f.at[0, t], r_f.at[0, t], z_peer(t)
        )

    def far_i(t):
        there = at(lax.rem(j + t, nj) * rows, rows)
        return remote(
            side_in.at[there], far_in.at[t - 1], s_f.at[1, t], r_f.at[1, t], z_peer(t)
        )

    for t in range(1, nj):
        far_g(t).start()
        far_i(t).start()

    dm_core(1 - core).wait_recv()
    frames = dm.shape[0] * dm.shape[1] * dm.shape[2] * dm.shape[3]
    wide = dm.shape[4]
    every = dm[...].reshape(frames, wide)
    part = dotf(wm_ref[...], every, NT)
    dc_send[:rows, :] = part
    dc_send[rows:, :] = jnp.broadcast_to(jnp.sum(loss_ref[...]), (8, frames))
    dc_x = remote(dc_send, dc_peer, s_x.at[1], r_x.at[1], x_peer)
    dc_x.start()

    def mod_cols(i, _):
        cols = at(i * 512, 512)
        block = dm[:, :, :, :, cols].reshape(frames, 512)
        res = dotf(cond_ref[...], block)
        smod_ref[:, cols] = res[:rows] + res[rows : 2 * rows] + res[2 * rows :]
        return 0

    lax.fori_loop(0, wide // 512, mod_cols, 0)
    dc_x.wait_recv()
    total = dc_send[...] + dc_peer[...]
    dct_ref[core, y, j, :rows, :] = total[:rows].astype(bf16)
    pieces = [p[:1].astype(f32) for p in split_three(total[rows:])]
    dct_ref[core, y, j, rows:, :] = jnp.concatenate(
        pieces + [jnp.zeros((13, frames), f32)], axis=0
    ).astype(bf16)

    def dc_z(t, src):
        block = dct_ref.at[core, y, src]
        return remote(block, block, s_dz.at[1, t], r_dz.at[1, t], z_peer(t))

    for t in range(1, nj):
        dc_z(t, j).start()
    for t in range(1, nj):
        dc_z(t, from_j(t)).wait_recv()

    def dc_y(side_index):
        block = dct_ref.at[core, side_index]
        return remote(block, block, s_d.at[2], r_d.at[2], y_peer)

    dc_y(y).start()

    here = at(j * rows, rows)
    for t in range(1, nj):
        far_g(t).wait_recv()
        far_i(t).wait_recv()
    for k in range(sq_ref.shape[0]):
        sq_ref[k] = side[k, here, :].astype(f32) + sum(
            far[t, k].astype(f32) for t in range(nj - 1)
        )
    ends[...] = side_in[here, :].astype(f32) + sum(
        far_in[t].astype(f32) for t in range(nj - 1)
    )
    ends_x = remote(ends, ends_peer, s_x.at[2], r_x.at[2], x_peer)
    ends_x.start()
    dc_y(1 - y).wait_recv()

    def dc_core(core_index):
        block = dct_ref.at[core_index]
        return remote(block, block, s_d.at[3], r_d.at[3], core_peer)

    dc_core(core).start()
    ends_x.wait_recv()
    sin_ref[...] = ends[...] + ends_peer[...]
    dc_core(1 - core).wait_recv()

    for one in (dm_x, core_g, core_in, y_g, y_in, dc_x, ends_x):
        one.wait_send()
    for one in (dm_y(y), dm_core(core), dc_y(y), dc_core(core)):
        one.wait_send()
    for t in range(1, nj):
        for one in (dm_z(t, j), dc_z(t, j), far_g(t), far_i(t)):
            one.wait_send()


def last_block(g, gin, dm, cond, wm, loss, cid):
    _, _, kinds, block_rows, e = g.shape
    n = lax.axis_size("frames")
    nj = n // 4
    rows = block_rows // nj
    own_frames, wide = dm.shape[1:]
    frames = n * 2 * own_frames
    f32, bf16 = jnp.float32, jnp.bfloat16
    vm = pl.BlockSpec(memory_space=pltpu.VMEM)
    anym = pl.BlockSpec(memory_space=pl.ANY)
    V = pltpu.VMEM
    D_ = pltpu.SemaphoreType.DMA
    return pl.pallas_call(
        last_kernel,
        in_specs=[anym] + [vm] * 5,
        out_specs=[vm] * 4,
        out_shape=[
            jax.ShapeDtypeStruct((kinds, rows, e), f32),
            jax.ShapeDtypeStruct((rows, 128), f32),
            jax.ShapeDtypeStruct((rows, wide), f32),
            jax.ShapeDtypeStruct((2, 2, nj, rows + 16, frames), bf16),
        ],
        scratch_shapes=[
            V((2, kinds, block_rows, e), bf16), V((2, block_rows, 128), bf16),
            V((2, kinds, block_rows, e), bf16), V((2, block_rows, 128), bf16),
            V((kinds, block_rows, e), bf16), V((block_rows, 128), bf16),
            V((nj - 1, kinds, rows, e), bf16), V((nj - 1, rows, 128), bf16),
            V((rows, 128), f32), V((rows, 128), f32),
            V((own_frames, wide), f32), V((2, 2, nj, 2 * own_frames, wide), bf16),
            V((rows + 8, frames), f32), V((rows + 8, frames), f32),
            D_((1,)), D_((3,)), D_((3,)), D_((4,)), D_((4,)), D_((2, nj)), D_((2, nj)),
            D_((4,)), D_((4,)), D_((2, nj)), D_((2, nj)),
        ],
        compiler_params=pltpu.CompilerParams(
            vmem_limit_bytes=48 << 20, collective_id=cid, has_side_effects=True
        ),
        cost_estimate=pl.CostEstimate(
            flops=2 * 10**10, bytes_accessed=2 * 10**7, transcendentals=0
        ),
        name="weight_sums",
    )(g, gin, dm, cond, wm, loss)


def front_kernel(
    small_ref, feat_ref, wm_ref, w_ref,
    st_ref, feats_ref, pre1_ref, pre2_ref, wout_ref, ends_ref, mod_ref,
    wcol, mods,
    s_x, r_x, s_z, r_z, s_y, r_y, s_c, r_c, s_a, r_a, s_m, r_m,
):
    f = lax.axis_index("frames")
    h = lax.axis_index("mp")
    n = lax.axis_size("frames")
    nj = n // 4
    c = lax.rem(f, 2)
    y = lax.rem(lax.div(f, 2), 2)
    j = lax.div(f, 4)
    f32, bf16 = jnp.float32, jnp.bfloat16
    MESH = pl.DeviceIdType.MESH
    x_peer = {"mp": 1 - h}
    core_peer = {"frames": f + 1 - 2 * c}
    y_peer = {"frames": f + 2 - 4 * y}
    offsets = [
        (tj, ty, tc) for tj in range(nj) for ty in range(2) for tc in range(2)
    ][1:]

    def place(tj, ty, tc):
        return (
            lax.rem(j + tj, nj),
            y + ty - 2 * y * ty,
            c + tc - 2 * c * tc,
        )

    def peer_of(spot):
        return {"frames": 4 * spot[0] + 2 * spot[1] + spot[2]}

    def from_j(t):
        return lax.rem(j - t + nj, nj)

    def remote(src, dst, send, recv, peer):
        return pltpu.make_async_remote_copy(
            src_ref=src, dst_ref=dst, send_sem=send, recv_sem=recv, device_id=peer,
            device_id_type=MESH,
        )

    barrier = pltpu.get_barrier_semaphore()
    for o in offsets:
        pl.semaphore_signal(barrier, inc=1, device_id=peer_of(place(*o)), device_id_type=MESH)
    pl.semaphore_signal(barrier, inc=1, device_id=x_peer, device_id_type=MESH)
    pl.semaphore_wait(barrier, n)

    class Gather:
        def __init__(self, block, k):
            self.block, self.k = block, k

        def over_z(self, t, jj):
            b = self.block(jj, y, c)
            return remote(
                b, b, s_z.at[self.k, t], r_z.at[self.k, t], {"frames": lax.rem(f + 4 * t, n)}
            )

        def over_y(self, t, yy):
            b = self.block(from_j(t), yy, c)
            return remote(b, b, s_y.at[self.k, t], r_y.at[self.k, t], y_peer)

        def over_core(self, t, same, yy, cc):
            b = self.block(from_j(t), yy, cc)
            return remote(
                b, b, s_c.at[self.k, same, t], r_c.at[self.k, same, t], core_peer
            )

        def start(self):
            for t in range(1, nj):
                self.over_z(t, j).start()
            self.over_y(0, y).start()
            self.over_core(0, 0, y, c).start()

        def pass_z(self):
            for t in range(1, nj):
                self.over_z(t, from_j(t)).wait_recv()
                self.over_y(t, y).start()
                self.over_core(t, 0, y, c).start()

        def pass_y(self):
            for t in range(nj):
                self.over_y(t, 1 - y).wait_recv()
                self.over_core(t, 1, 1 - y, c).start()

        def finish(self):
            for t in range(nj):
                self.over_core(t, 0, y, 1 - c).wait_recv()
                self.over_core(t, 1, 1 - y, 1 - c).wait_recv()

        def sent(self):
            for t in range(1, nj):
                self.over_z(t, j).wait_send()
            for t in range(nj):
                self.over_y(t, y).wait_send()
                self.over_core(t, 0, y, c).wait_send()
                self.over_core(t, 1, 1 - y, c).wait_send()

    small = Gather(lambda a, b, d: st_ref.at[a, b, d], 0)
    feats = Gather(lambda a, b, d: feats_ref.at[d, b, a], 1)
    weights = Gather(lambda a, b, d: wout_ref.at[:, a, b, d], 2)

    small_x = remote(small_ref, st_ref.at[j, y, c, h], s_x.at[0], r_x.at[0], x_peer)
    small_x.start()
    feats_ref[c, y, j] = feat_ref[...]
    feats.start()

    def column_copy(i, spot, slot):
        return remote(
            wm_ref.at[spot[2], spot[1], spot[0]], wcol.at[slot[0], slot[1], slot[2]],
            s_a.at[i], r_a.at[i], peer_of(spot),
        )

    def source(o):
        return place((nj - o[0]) % nj, o[1], o[2])

    for i, o in enumerate(offsets):
        column_copy(i, place(*o), (j, y, c)).start()
    st_ref[j, y, c, h] = small_ref[...]
    wout_ref[:, j, y, c] = w_ref[...]
    wcol[j, y, c] = wm_ref[c, y, j]
    remote(
        small_ref, st_ref.at[j, y, c, 1 - h], s_x.at[0], r_x.at[0], x_peer
    ).wait_recv()
    small.start()
    feats.pass_z()
    small.pass_z()
    weights.start()
    feats.pass_y()
    small.pass_y()
    feats.finish()
    small.finish()

    total = st_ref.shape[0] * 4
    width = total * 2 * st_ref.shape[4]
    frames = feats_ref.shape[2] * 4 * feats_ref.shape[3]
    inner = feats_ref.shape[4]

    def exact(left, right, dims):
        m = left.shape[0]
        res = dotf(jnp.concatenate(split_three(left), axis=0), right, dims)
        return res[:m] + res[m : 2 * m] + res[2 * m :]

    def silu(v):
        return v * jax.nn.sigmoid(v)

    table = st_ref[...].reshape(width, st_ref.shape[5])
    fv = feats_ref[...].reshape(frames, inner)
    pre1 = exact(fv, table[:, :inner], NT)
    pre1_ref[...] = pre1
    pre2 = exact(silu(pre1), table[:, inner : inner + width], NT)
    pre2_ref[...] = pre2
    ends_ref[...] = table[:, inner + width : inner + width + 128].T
    for i, o in enumerate(offsets):
        column_copy(i, place(*o), source(o)).wait_recv()
    cols = wcol[...].reshape(width, wcol.shape[4])
    mods[...] = exact(silu(pre2), cols, NN).reshape(mods.shape)

    def mods_copy(i, spot, slot):
        return remote(
            mods.at[spot[2], spot[1], spot[0]], mod_ref.at[h, slot[2], slot[1], slot[0]],
            s_m.at[i], r_m.at[i], peer_of(spot),
        )

    for i, o in enumerate(offsets):
        mods_copy(i, place(*o), (j, y, c)).start()
    mod_ref[h, c, y, j] = mods[c, y, j]
    weights.pass_z()
    for i, o in enumerate(offsets):
        mods_copy(i, place(*o), source(o)).wait_recv()
    mods_x = remote(mod_ref.at[h], mod_ref.at[h], s_x.at[1], r_x.at[1], x_peer)
    mods_x.start()
    weights.pass_y()
    weights.finish()
    theirs = mod_ref.at[1 - h]
    remote(theirs, theirs, s_x.at[1], r_x.at[1], x_peer).wait_recv()

    small_x.wait_send()
    mods_x.wait_send()
    for g in (small, feats, weights):
        g.sent()
    for i, o in enumerate(offsets):
        column_copy(i, place(*o), (j, y, c)).wait_send()
        mods_copy(i, place(*o), (j, y, c)).wait_send()


def front_block(small, feat, wm, w, cid):
    n = lax.axis_size("frames")
    nj = n // 4
    cols, lanes = small.shape
    own_frames, inner = feat.shape
    frames = n * own_frames
    kinds, rows, e = w.shape
    wide = wm.shape[-1]
    width = rows * n
    f32, bf16 = jnp.float32, jnp.bfloat16
    vm = pl.BlockSpec(memory_space=pltpu.VMEM)
    V = pltpu.VMEM
    D_ = pltpu.SemaphoreType.DMA
    return pl.pallas_call(
        front_kernel,
        in_specs=[vm] * 4,
        out_specs=[vm] * 7,
        out_shape=[
            jax.ShapeDtypeStruct((nj, 2, 2, 2, cols, lanes), bf16),
            jax.ShapeDtypeStruct((2, 2, nj, own_frames, inner), f32),
            jax.ShapeDtypeStruct((frames, width), f32),
            jax.ShapeDtypeStruct((frames, width), f32),
            jax.ShapeDtypeStruct((kinds, nj, 2, 2, rows, e), bf16),
            jax.ShapeDtypeStruct((128, width), bf16),
            jax.ShapeDtypeStruct((2, 2, 2, nj, own_frames, wide), f32),
        ],
        scratch_shapes=[
            V((nj, 2, 2, rows, wide), bf16), V((2, 2, nj, own_frames, wide), f32),
            D_((2,)), D_((2,)), D_((3, nj)), D_((3, nj)), D_((3, nj)), D_((3, nj)),
            D_((3, 2, nj)), D_((3, 2, nj)), D_((n - 1,)), D_((n - 1,)), D_((n - 1,)),
            D_((n - 1,)),
        ],
        compiler_params=pltpu.CompilerParams(
            vmem_limit_bytes=48 << 20, collective_id=cid, has_side_effects=True
        ),
        cost_estimate=pl.CostEstimate(
            flops=4 * 10**10, bytes_accessed=2 * 10**7, transcendentals=0
        ),
        name="conditioning",
    )(small, feat, wm, w)


def per_device(
    latents,
    noise,
    levels,
    clip_ids,
    clean_flags,
    attn_weights,
    mlp_weights,
    mod_weight,
    small_weights,
    attn_moment,
    mlp_moment,
    mod_moment,
    small_moment,
    attn_average,
    mlp_average,
    mod_average,
    small_average,
):
    frame_count = latents.shape[0]
    tok_count = frame_count * TPF
    patch_side = GRID // 2
    frames_total = clip_ids.shape[0]
    tokens_total = frames_total * TPF
    width_local = attn_weights.shape[2]
    heads_local = width_local // HD
    key_span = (REACH + 1) * tok_count
    device = lax.axis_index("frames")
    mp_index = lax.axis_index("mp")
    first_frame = device * frame_count
    scale_qk = HD ** (-0.5)
    attn_low = attn_weights.astype(jnp.bfloat16)
    mlp_low = mlp_weights.astype(jnp.bfloat16)
    low_mod = mod_weight.astype(jnp.bfloat16)
    noised_all = (1 - clean_flags).astype(jnp.float32)
    noised_count = jnp.sum(noised_all)
    noised = lax.dynamic_slice_in_dim(noised_all, first_frame, frame_count)
    level_eff = levels * noised
    signal_scale = jnp.repeat(jnp.cos(0.5 * math.pi * level_eff), TPF)
    noise_scale = jnp.repeat(jnp.sin(0.5 * math.pi * level_eff), TPF)
    noise_patches = patchify(noise)
    inputs = signal_scale[:, None] * patchify(latents) + noise_scale[:, None] * noise_patches
    in_clip_all = clip_positions(clip_ids)
    chip_frames = 2 * frame_count
    chip_first = (device // 2) * chip_frames
    in_clip = lax.dynamic_slice_in_dim(in_clip_all, chip_first, chip_frames).astype(jnp.float32)
    within = np.arange(TPF)
    patch_zero = np.zeros((TPF, HD // 4), np.float32)
    patch_angles = np.concatenate(
        [patch_zero]
        + turn_phases((within // patch_side).astype(np.float32), 3 * HD // 8)
        + turn_phases((within % patch_side).astype(np.float32), 3 * HD // 8),
        axis=1,
    )
    patch_angles = np.tile(patch_angles, (1, 4))
    frame_angles = jnp.tile(
        jnp.concatenate(
            turn_phases(in_clip, HD // 4) + [jnp.zeros((chip_frames, 3 * HD // 4))], axis=1
        ),
        (1, 4),
    )
    tables = (
        jnp.cos(frame_angles),
        jnp.sin(frame_angles),
        jnp.asarray(np.cos(patch_angles), jnp.float32),
        jnp.asarray(np.sin(patch_angles), jnp.float32),
    )
    turn_four = jnp.asarray(np.kron(np.eye(4, dtype=np.float32), rotation_matrix(HD)), jnp.bfloat16)
    clip_start = (
        lax.dynamic_slice_in_dim(
            jnp.arange(frames_total, dtype=jnp.int32) - in_clip_all, chip_first, chip_frames
        )
        - chip_first
        + REACH * frame_count
    )
    peers = lax.axis_size("frames")
    frame_groups = peers // 4
    small_rows, small_cols = small_weights.shape
    mod_rows, mod_cols = mod_weight.shape
    mod_share = mod_cols // peers
    mod_wide = -(-mod_share // 128) * 128
    small_lanes = FREQ + D + 128
    small_t = jnp.pad(
        small_weights.astype(jnp.bfloat16).T, ((0, 0), (0, small_lanes - small_rows))
    )
    mod_blocks = jnp.pad(
        low_mod.reshape(mod_rows, frame_groups, 2, 2, mod_share).transpose(3, 2, 1, 0, 4),
        ((0, 0),) * 4 + ((0, mod_wide - mod_share),),
    )
    small_full, features_placed, pre_one, pre_two, w_qkv, end_rows, mod_parts = front_block(
        small_t, time_features(level_eff), mod_blocks, attn_low, 4
    )
    w_qkv, up_low = lax.optimization_barrier((w_qkv, mlp_low[0]))
    w_up = lax.all_gather(up_low, "frames", axis=0, tiled=True)
    w_qkv = w_qkv.reshape(4, D, width_local)
    features_placed = features_placed.reshape(frames_total, FREQ)
    first_placed = jax.nn.silu(pre_one)
    pre_two_t = pre_two.T
    first_col = (device * lax.axis_size("mp") + mp_index) * small_cols
    pre_one_own = lax.dynamic_slice_in_dim(pre_one, first_col, small_cols, 1).T
    cond_rows = jax.nn.silu(
        lax.dynamic_slice_in_dim(pre_two, device * mod_rows, mod_rows, 1)
    )
    cond_parts = jnp.concatenate([part.T for part in split_three(cond_rows)], axis=0)
    modulation = (
        mod_parts[..., :mod_share].transpose(4, 0, 3, 2, 1, 5).reshape(frame_count, 6 * D)
    )
    pieces = [
        modulation[:, None, piece_index * D : (piece_index + 1) * D] for piece_index in range(6)
    ]
    shift_one, scale_one, gate_one, shift_two, scale_two, gate_two = pieces
    inputs_low = inputs.astype(jnp.bfloat16)
    padding = ((0, 0), (0, 128 - P_SIZE))
    inputs_low = jnp.pad(inputs_low, padding)
    normed_one, hidden_half, queries, keys_wide, values_wide = proj_block(
        inputs_low,
        end_rows,
        jnp.stack([shift_one[:, 0], scale_one[:, 0]]),
        w_qkv,
        tables,
        turn_four,
        REACH,
        2,
    )
    down_low = mlp_low[1]
    queries, down_low = lax.optimization_barrier((queries, down_low))
    w_down = lax.all_gather(down_low, "frames", axis=0, tiled=True)
    heads_wide, heads_low, log_totals = attn_fwd(queries, keys_wide, values_wide, clip_start)
    half = tok_count // 2
    own_frames = frame_count // 2

    def half_of(array, dim=0):
        size = array.shape[dim] // 2
        return lax.dynamic_slice_in_dim(array, mp_index * size, size, dim)

    token_weight = jnp.repeat(noised, TPF) / (TPF * P_SIZE)
    grad_scale = 1.0 / jnp.maximum(noised_count, 1.0)
    head_lanes = ((0, 0), (P_SIZE, 128 - 2 * P_SIZE))
    mod_mid = jnp.stack(
        [half_of(piece[:, 0]) for piece in (gate_one, shift_two, scale_two, gate_two)]
    )
    d_mixed, d_shaped_one, d_mod_mid, loss_parts, grad_rest = mid_block(
        heads_low,
        hidden_half,
        mod_mid,
        jnp.pad(half_of(noise_patches), head_lanes),
        jnp.pad(jnp.broadcast_to(half_of(token_weight)[:, None], (half, P_SIZE)), head_lanes),
        end_rows,
        grad_scale.reshape(1),
        w_up,
        w_down,
        w_qkv,
        TP_AXIS,
        0,
    )
    sum_rest = lax.psum_scatter(grad_rest, "frames", scatter_dimension=0, tiled=True)
    d_queries, keys_grad_wide, values_grad_wide = attn_bwd(
        queries, keys_wide, values_wide, d_mixed, heads_wide, log_totals, clip_start
    )
    grad_qkv, grad_in, d_first_mods = tail_block(
        d_queries,
        normed_one,
        w_qkv,
        tables,
        turn_four,
        hidden_half,
        half_of(scale_one[:, 0]),
        d_shaped_one,
        half_of(inputs_low),
        keys_grad_wide,
        values_grad_wide,
        1,
    )
    d_first_mods, sum_rest = lax.optimization_barrier((d_first_mods, sum_rest))
    def by_place(array, dim):
        shape = array.shape
        size = shape[dim] // (4 * frame_groups)
        split = array.reshape(shape[:dim] + (frame_groups, 2, 2, size) + shape[dim + 1 :])
        order = list(range(split.ndim))
        order[dim], order[dim + 2] = dim + 2, dim
        return split.transpose(order)

    in_columns = by_place(grad_in.T, 0).reshape(2, 2, D // 4, 128).astype(jnp.bfloat16)
    d_mods = jnp.stack(
        [
            jnp.concatenate([d_first_mods[0], d_first_mods[1], d_mod_mid[0]], axis=1),
            jnp.concatenate([d_mod_mid[1], d_mod_mid[2], d_mod_mid[3]], axis=1),
        ]
    )
    sum_qkv, sum_in, sum_mod, d_cond_rows = last_block(
        grad_qkv, in_columns, d_mods, cond_parts, low_mod, loss_parts, 3
    )
    loss_sum = jnp.sum(d_cond_rows[:, :, :, mod_rows : mod_rows + 3, 0].astype(jnp.float32))
    d_cond_t = (
        d_cond_rows[:, :, :, :mod_rows, :].transpose(2, 1, 0, 3, 4).reshape(D, frames_total)
    ).astype(jnp.float32)
    d_pre_two = jax.vjp(jax.nn.silu, pre_two_t)[1](d_cond_t)[0]
    d_pre_own = lax.dynamic_slice_in_dim(d_pre_two, first_col, small_cols, 0)
    grad_second = jnp.einsum("fi,jf->ij", first_placed, d_pre_own, precision=HIGH)
    second_cols = lax.dynamic_slice_in_dim(
        small_full.reshape(D, small_lanes), FREQ + first_col, small_cols, 1
    ).astype(jnp.float32)
    d_first = jnp.einsum("kf,kj->jf", d_pre_two, second_cols, precision=HIGH)
    d_pre_one = jax.vjp(jax.nn.silu, pre_one_own)[1](d_first)[0]
    grad_first = jnp.einsum("fi,jf->ij", features_placed, d_pre_one, precision=HIGH)
    ff_cols = mlp_weights.shape[2]
    sum_rest = sum_rest.astype(jnp.float32)
    sum_mlp = jnp.stack([sum_rest[:, :ff_cols], sum_rest[:, ff_cols : 2 * ff_cols]])
    sum_attn = jnp.stack(
        [sum_qkv[0], sum_qkv[1], sum_qkv[2]]
        + [sum_rest[:, 2 * ff_cols : 2 * ff_cols + width_local]]
    )
    head_first = 2 * ff_cols + width_local
    head_part = sum_rest[:, head_first + P_SIZE : head_first + 2 * P_SIZE]
    sum_head = head_part + lax.ppermute(head_part, "mp", [(0, 1), (1, 0)])
    sum_ends = half_of(jnp.concatenate([sum_in[:, :P_SIZE], sum_head], axis=1).T, 1)
    sum_small = jnp.concatenate([grad_first, grad_second, sum_ends], axis=0)
    learning_rate = 0.5 * math.sqrt(tokens_total * P_SIZE / D)
    attn_new, attn_moment_new, attn_average_new, attn_copy = update(
        attn_weights, sum_attn, attn_moment, attn_average, learning_rate
    )
    mlp_new, mlp_moment_new, mlp_average_new, mlp_copy = update(
        mlp_weights, sum_mlp, mlp_moment, mlp_average, learning_rate
    )
    mod_new, mod_moment_new, mod_average_new, mod_copy = update(
        mod_weight, sum_mod, mod_moment, mod_average, learning_rate
    )
    small_new, small_moment_new, small_average_new, small_copy = update(
        small_weights, sum_small, small_moment, small_average, learning_rate
    )
    return (
        loss_sum,
        noised_count,
        attn_new,
        attn_moment_new,
        attn_average_new,
        attn_copy,
        mlp_new,
        mlp_moment_new,
        mlp_average_new,
        mlp_copy,
        mod_new,
        mod_moment_new,
        mod_average_new,
        mod_copy,
        small_new,
        small_moment_new,
        small_average_new,
        small_copy,
    )


def solution(mesh):
    return jax.shard_map(
        per_device,
        mesh=mesh,
        in_specs=(
            P("frames", None),
            P("frames", None),
            P("frames"),
            P(),
            P(),
            P(None, "frames", "mp"),
            P(None, "frames", "mp"),
            P("frames", "mp"),
            P(None, ("frames", "mp")),
            P(None, "frames", "mp"),
            P(None, "frames", "mp"),
            P("frames", "mp"),
            P(None, ("frames", "mp")),
            P(None, "frames", "mp"),
            P(None, "frames", "mp"),
            P("frames", "mp"),
            P(None, ("frames", "mp")),
        ),
        out_specs=(
            P(),
            P(),
            P(None, "frames", "mp"),
            P(None, "frames", "mp"),
            P(None, "frames", "mp"),
            P(None, "frames", "mp"),
            P(None, "frames", "mp"),
            P(None, "frames", "mp"),
            P(None, "frames", "mp"),
            P(None, "frames", "mp"),
            P("frames", "mp"),
            P("frames", "mp"),
            P("frames", "mp"),
            P("frames", "mp"),
            P(None, ("frames", "mp")),
            P(None, ("frames", "mp")),
            P(None, ("frames", "mp")),
            P(None, ("frames", "mp")),
        ),
        check_vma=False,
    )
```

```python
import functools
import math

import jax
import jax.numpy as jnp
import numpy as np
from jax import lax
from jax.experimental import pallas as pl
from jax.experimental.pallas import tpu as pltpu
from jax.sharding import PartitionSpec as P

D = 1024
HD = 64
CH = 4
FREQ = 256
GRID = 16
P_SIZE = 16
TPF = 64
REACH = 4


HIGH = lax.Precision.HIGHEST
EPSILON = 1e-06
MOMENTUM = 0.5
EMA_DECAY = 0.5
TP_AXIS = "mp"


def rotation_matrix(head_width):
    groups = [head_width // 4, 3 * head_width // 8, 3 * head_width // 8]
    rotation = np.zeros((head_width, head_width), np.float32)
    offset = 0
    for group_size in groups:
        half_size = group_size // 2
        for pair_index in range(half_size):
            rotation[offset + half_size + pair_index, offset + pair_index] = -1.0
            rotation[offset + pair_index, offset + half_size + pair_index] = 1.0
        offset += group_size
    return rotation


def turn_phases(positions, group_size):
    half_size = group_size // 2
    frequency = 10000.0 ** (-np.arange(half_size, dtype=np.float32) / half_size)
    phases = positions[:, None] * frequency.astype(np.float32)[None, :]
    return [phases, phases]


def turn_table(frame_ref, patch_ref, first, count):
    lanes = lax.broadcasted_iota(jnp.int32, (1, patch_ref.shape[1]), 1)
    by_frame = lax.rem(lanes, HD) < HD // 4
    rows = [
        jnp.where(by_frame, frame_ref[pl.ds(first + k, 1), :], patch_ref[...])
        for k in range(count)
    ]
    return jnp.concatenate(rows, axis=0)


def clip_positions(clip_ids):
    frame_index = jnp.arange(clip_ids.shape[0], dtype=jnp.int32)
    starts_here = jnp.concatenate([jnp.ones((1,), bool), clip_ids[1:] != clip_ids[:-1]])
    clip_start = lax.cummax(jnp.where(starts_here, frame_index, 0), axis=0)
    return frame_index - clip_start


def patchify(frame_data):
    frame_total = frame_data.shape[0]
    patch_side = GRID // 2
    shaped = frame_data.reshape(frame_total, CH, patch_side, 2, patch_side, 2)
    return shaped.transpose(0, 2, 4, 1, 3, 5).reshape(frame_total * patch_side * patch_side, CH * 4)


def layer_norm(vector):
    row_mean = jnp.mean(vector, axis=-1, keepdims=True)
    centred = vector - row_mean
    variance = jnp.mean(centred * centred, axis=-1, keepdims=True)
    return centred * lax.rsqrt(variance + EPSILON)


def modulate_local(shaped, shift_rows, scale_rows):
    return layer_norm(shaped) * (1.0 + scale_rows) + shift_rows


def time_features(level_eff):
    half_size = FREQ // 2
    frequency = jnp.exp(-math.log(10000.0) * jnp.arange(half_size, dtype=jnp.float32) / half_size)
    phases = (level_eff * 1000.0)[:, None] * frequency[None, :]
    return jnp.concatenate([jnp.cos(phases), jnp.sin(phases)], axis=1)


NT=(((1,),(1,)),((),()))
NN=(((1,),(0,)),((),()))

def dotf(a,b,dims=NN):
    return lax.dot_general(a,b,dims,preferred_element_type=jnp.float32)

def split_pair(xT):
    r=lax.broadcasted_iota(jnp.int32,xT.shape,0)
    z=jnp.zeros_like(xT)
    return jnp.where(r<HD,xT,z), jnp.where(r<HD,z,xT)

def keep_of(t,TK,TQ,cs,qf):
    kf=lax.broadcasted_iota(jnp.int32,(TK,TQ),0)//TPF+t*(TK//TPF)
    return (kf>=cs)&(kf<=qf)

def fwd_kernel(lo_ref,mid_ref,hi_ref,q_ref,k_ref,v_ref,cs_ref,o_ref,ol_ref,lse_ref,vT,*,TQ,TK,W0,NQ):
    KS=k_ref.shape[0]
    def tr(i,_):
        s=pl.multiple_of(i*TK,TK)
        vT[:,pl.ds(s,TK)]=v_ref[pl.ds(s,TK),:].T
        return 0
    lax.fori_loop(lo_ref[0],KS//TK,tr,0)
    def qtile(j,_):
        qs=pl.multiple_of(j*TQ,TQ)
        qT=(q_ref[pl.ds(qs,TQ),:].T)*jnp.bfloat16(0.125)
        qA,qB=split_pair(qT)
        cs=cs_ref[0:1,pl.ds(qs,TQ)]
        qf=lax.broadcasted_iota(jnp.int32,(1,TQ),1)//TPF+(W0+j*(TQ//TPF))
        def step(t,carry,masked):
            ks=pl.multiple_of(t*TK,TK)
            kt=k_ref[pl.ds(ks,TK),:]
            out=[]
            if masked: keep=keep_of(t,TK,TQ,cs,qf)
            ones=jnp.ones((16,TK),jnp.bfloat16)
            both=[dotf(kt,qh) for qh in (qA,qB)]
            for h,(s,(m,l,o)) in enumerate(zip(both,carry)):
                if masked: s=jnp.where(keep,s,-1e30)
                mn=jnp.maximum(m,jnp.max(s,axis=0,keepdims=True))
                a=jnp.exp(m-mn)
                p=jnp.exp(s-mn)
                vh=jnp.concatenate([vT[h*HD:(h+1)*HD,pl.ds(ks,TK)],ones],axis=0)
                ov=dotf(vh,p.astype(jnp.bfloat16))
                l=l*a+ov[HD:HD+1]
                o=o*a+ov[:HD]
                out.append((mn,l,o))
            return tuple(out)
        init=tuple((jnp.full((1,TQ),-1e29,jnp.float32),jnp.zeros((1,TQ),jnp.float32),jnp.zeros((HD,TQ),jnp.float32)) for _ in range(2))
        c=lax.fori_loop(lo_ref[j],mid_ref[j],lambda t,c:step(t,c,True),init)
        c=lax.fori_loop(mid_ref[j],hi_ref[j],lambda t,c:step(t,c,False),c)
        c=lax.fori_loop(hi_ref[j],(W0*TPF+(j+1)*TQ+TK-1)//TK,lambda t,c:step(t,c,True),c)
        oT=jnp.concatenate([c[0][2]/c[0][1],c[1][2]/c[1][1]],axis=0)
        o_nat=oT.T
        o_ref[pl.ds(qs,TQ),:]=o_nat
        ol_ref[pl.ds(qs,TQ),:]=o_nat.astype(jnp.bfloat16)
        lse_ref[0,0:1,pl.ds(qs,TQ)]=c[0][0]+jnp.log(c[0][1])
        lse_ref[0,1:2,pl.ds(qs,TQ)]=c[1][0]+jnp.log(c[1][1])
        return 0
    lax.fori_loop(0,NQ,qtile,0)

def tile_bounds(cs_rel,TQ,TK,W0,NQ):
    fq=TQ//TPF; fk=TK//TPF
    j=jnp.arange(NQ)
    first=cs_rel[::fq]; last=cs_rel[fq-1::fq]
    lo=first//fk
    dg=(W0+j*fq+1)//fk
    mid=jnp.minimum((last+fk-1)//fk,dg)
    mid=jnp.maximum(mid,lo)
    hi=jnp.maximum(dg,mid)
    return lo.astype(jnp.int32),mid.astype(jnp.int32),hi.astype(jnp.int32)

def attn_fwd(q,k,v,cs_rel,TQ=512,TK=512):
    T,Wd=q.shape; KS=k.shape[0]; P=Wd//128
    W0=(KS-T)//TPF; NQ=T//TQ
    lo,mid,hi=tile_bounds(cs_rel,TQ,TK,W0,NQ)
    cs_tok=jnp.broadcast_to(jnp.repeat(cs_rel,TPF)[None,:],(8,T)).astype(jnp.int32)
    return pl.pallas_call(
        functools.partial(fwd_kernel,TQ=TQ,TK=TK,W0=W0,NQ=NQ),
        grid_spec=pltpu.PrefetchScalarGridSpec(num_scalar_prefetch=3,grid=(P,),
            in_specs=[pl.BlockSpec((T,128),lambda p,*_:(0,p)),pl.BlockSpec((KS,128),lambda p,*_:(0,p)),pl.BlockSpec((KS,128),lambda p,*_:(0,p)),pl.BlockSpec((8,T),lambda p,*_:(0,0))],
            out_specs=[pl.BlockSpec((T,128),lambda p,*_:(0,p)),pl.BlockSpec((T,128),lambda p,*_:(0,p)),pl.BlockSpec((1,8,T),lambda p,*_:(p,0,0))],
            scratch_shapes=[pltpu.VMEM((128,KS),jnp.bfloat16)]),
        out_shape=[jax.ShapeDtypeStruct((T,Wd),jnp.float32),jax.ShapeDtypeStruct((T,Wd),jnp.bfloat16),jax.ShapeDtypeStruct((P,8,T),jnp.float32)],
        compiler_params=pltpu.CompilerParams(vmem_limit_bytes=48<<20),
        cost_estimate=pl.CostEstimate(flops=10**11,bytes_accessed=2*10**7,transcendentals=3*10**7),
        name="attn_forward",
    )(lo,mid,hi,q,k,v,cs_tok)

def bwd_kernel(lo_ref,mid_ref,hi_ref,q_ref,k_ref,v_ref,do_ref,o_ref,lse_ref,cs_ref,dq_ref,dk_ref,dv_ref,kT,dkT,dvT,*,TQ,TK,W0,NQ):
    KS=k_ref.shape[0]
    def tr(i,_):
        s=pl.multiple_of(i*TK,TK)
        kT[:,pl.ds(s,TK)]=k_ref[pl.ds(s,TK),:].T
        return 0
    lax.fori_loop(lo_ref[0],KS//TK,tr,0)
    dkT[...]=jnp.zeros_like(dkT); dvT[...]=jnp.zeros_like(dvT)
    def qtile(j,_):
        qs=pl.multiple_of(j*TQ,TQ)
        qT=(q_ref[pl.ds(qs,TQ),:].T)*jnp.bfloat16(0.125)
        qh=split_pair(qT)
        doT=do_ref[pl.ds(qs,TQ),:].T
        doh=split_pair(doT)
        oT=o_ref[pl.ds(qs,TQ),:].T
        prod=oT*doT.astype(jnp.float32)
        delta=(jnp.sum(prod[:HD],axis=0,keepdims=True),jnp.sum(prod[HD:],axis=0,keepdims=True))
        lse=(lse_ref[0,0:1,pl.ds(qs,TQ)],lse_ref[0,1:2,pl.ds(qs,TQ)])
        cs=cs_ref[0:1,pl.ds(qs,TQ)]
        qf=lax.broadcasted_iota(jnp.int32,(1,TQ),1)//TPF+(W0+j*(TQ//TPF))
        def step(t,carry,masked):
            ks=pl.multiple_of(t*TK,TK)
            kt=k_ref[pl.ds(ks,TK),:]; vt=v_ref[pl.ds(ks,TK),:]
            out=[]
            if masked: keep=keep_of(t,TK,TQ,cs,qf)
            for h in range(2):
                r=slice(h*HD,(h+1)*HD)
                s=dotf(kt,qh[h])
                p=jnp.exp(s-lse[h])
                if masked: p=jnp.where(keep,p,0.0)
                dp=dotf(vt,doh[h])
                ds=(p*(dp-delta[h])).astype(jnp.bfloat16)
                pb=p.astype(jnp.bfloat16)
                dvT[r,pl.ds(ks,TK)]+=dotf(doT[r],pb,NT)
                dkT[r,pl.ds(ks,TK)]+=dotf(qT[r],ds,NT)
                out.append(carry[h]+dotf(kT[r,pl.ds(ks,TK)],ds))
            return tuple(out)
        init=(jnp.zeros((HD,TQ),jnp.float32),)*2
        c=lax.fori_loop(lo_ref[j],mid_ref[j],lambda t,c:step(t,c,True),init)
        c=lax.fori_loop(mid_ref[j],hi_ref[j],lambda t,c:step(t,c,False),c)
        c=lax.fori_loop(hi_ref[j],(W0*TPF+(j+1)*TQ+TK-1)//TK,lambda t,c:step(t,c,True),c)
        dq_ref[pl.ds(qs,TQ),:]=(jnp.concatenate(c,axis=0)*0.125).T
        return 0
    lax.fori_loop(0,NQ,qtile,0)
    def back(i,_):
        s=pl.multiple_of(i*TK,TK)
        dk_ref[pl.ds(s,TK),:]=dkT[:,pl.ds(s,TK)].T.astype(dk_ref.dtype)
        dv_ref[pl.ds(s,TK),:]=dvT[:,pl.ds(s,TK)].T.astype(dv_ref.dtype)
        return 0
    lax.fori_loop(0,KS//TK,back,0)

def attn_bwd(q,k,v,do,o,lse,cs_rel,TQ=512,TK=512,out_dt=jnp.bfloat16):
    T,Wd=q.shape; KS=k.shape[0]; P=Wd//128
    W0=(KS-T)//TPF; NQ=T//TQ
    lo,mid,hi=tile_bounds(cs_rel,TQ,TK,W0,NQ)
    cs_tok=jnp.broadcast_to(jnp.repeat(cs_rel,TPF)[None,:],(8,T)).astype(jnp.int32)
    tb=pl.BlockSpec((T,128),lambda p,*_:(0,p)); kb=pl.BlockSpec((KS,128),lambda p,*_:(0,p))
    return pl.pallas_call(
        functools.partial(bwd_kernel,TQ=TQ,TK=TK,W0=W0,NQ=NQ),
        grid_spec=pltpu.PrefetchScalarGridSpec(num_scalar_prefetch=3,grid=(P,),
            in_specs=[tb,kb,kb,tb,tb,pl.BlockSpec((1,8,T),lambda p,*_:(p,0,0)),pl.BlockSpec((8,T),lambda p,*_:(0,0))],
            out_specs=[tb,kb,kb],
            scratch_shapes=[pltpu.VMEM((128,KS),jnp.bfloat16),pltpu.VMEM((128,KS),jnp.float32),pltpu.VMEM((128,KS),jnp.float32)]),
        out_shape=[jax.ShapeDtypeStruct((T,Wd),jnp.float32),jax.ShapeDtypeStruct((KS,Wd),out_dt),jax.ShapeDtypeStruct((KS,Wd),out_dt)],
        compiler_params=pltpu.CompilerParams(vmem_limit_bytes=56<<20),
        cost_estimate=pl.CostEstimate(flops=2*10**11,bytes_accessed=5*10**7,transcendentals=3*10**7),
        name="attn_backward",
    )(lo,mid,hi,q,k,v,do,o,lse,cs_tok)


def update(weight, gradient, moment, average, learning_rate):
    moment_new = MOMENTUM * moment + gradient
    weight_new = weight - learning_rate * (gradient + MOMENTUM * moment_new)
    average_new = EMA_DECAY * average + (1.0 - EMA_DECAY) * weight_new
    return (weight_new, moment_new, average_new, weight_new.astype(jnp.bfloat16))


TN = (((0,), (0,)), ((), ()))


def norm_rows(v):
    centred = v - jnp.mean(v, axis=-1, keepdims=True)
    inverse = lax.rsqrt(jnp.mean(centred * centred, axis=-1, keepdims=True) + EPSILON)
    return centred * inverse, inverse


def norm_rows_back(grad, normed, inverse):
    return inverse * (
        grad
        - jnp.mean(grad, axis=-1, keepdims=True)
        - normed * jnp.mean(grad * normed, axis=-1, keepdims=True)
    )


def gelu_pair(x):
    c = math.sqrt(2.0 / math.pi)
    sq = x * x
    t = jnp.tanh(c * (x + 0.044715 * (x * sq)))
    half = 0.5 * (1.0 + t)
    return x * half, half + (0.5 * c) * x * (1.0 - t * t) * (1.0 + 0.134145 * sq)


def mid_kernel(
    o_hbm, hid_ref, mod_ref, noise_ref, tw_ref, head_ref, gs_ref, wu_hbm, wd_hbm, wa_hbm,
    dmix_hbm, dx1_ref, dmod_ref, loss_ref, rest_hbm,
    o_ref, dmix_ref, wo_ref, wu_ref, wd_ref, att, x1, out, dx2, n2, n2t, act, dgl, dout, doutt, datt, datt_t,
    send_a, recv_a, send_c, recv_c, send_e, recv_e, stage, ghead_ref, go_ref, gh_t,
    wsem, gsem, ssem, rsem, o_sem, m_sem, s_m, r_m, *, tp,
):
    f = lax.axis_index("frames")
    h = lax.axis_index("mp")
    bf16 = jnp.bfloat16
    x_peer = {"mp": 1 - h}
    tp_peer = x_peer
    core = lax.rem(f, 2)
    core_peer = {"frames": f + 1 - 2 * core}
    half = hid_ref.shape[0]
    rows = 128
    chunks = half // rows
    width = hid_ref.shape[1]
    ff = wu_hbm.shape[1]
    e = o_ref.shape[1]
    ft = 512
    dt = 256

    weights = [
        pltpu.make_async_copy(wu_hbm, wu_ref, wsem.at[0]),
        pltpu.make_async_copy(wd_hbm, wd_ref, wsem.at[1]),
    ]
    load_out = pltpu.make_async_copy(wa_hbm.at[3], wo_ref, wsem.at[2])
    load_out.start()
    for w in weights:
        w.start()

    barrier = pltpu.get_barrier_semaphore()
    for peer in (x_peer, core_peer):
        pl.semaphore_signal(barrier, inc=1, device_id=peer, device_id_type=pl.DeviceIdType.MESH)
    pl.semaphore_wait(barrier, 2)
    tok_all = o_ref.shape[0]
    eh = e // 2

    def at(start, size):
        return pl.ds(pl.multiple_of(start, size), size)

    def frame_at(c, k):
        return pl.ds(h * (half // TPF) + c * (rows // TPF) + k, 1)

    def mod_row(i, c, k):
        return mod_ref[frame_at(c, k), (2 + i) * width : (3 + i) * width]

    def copy(src, dst, phase, c, peer):
        return pltpu.make_async_remote_copy(
            src_ref=src, dst_ref=dst, send_sem=ssem.at[phase, c], recv_sem=rsem.at[phase, c],
            device_id=peer, device_id_type=pl.DeviceIdType.MESH,
        )

    def copy_a(c):
        return copy(send_a.at[at(c * rows, rows)], recv_a.at[at(c * rows, rows)], 0, c, x_peer)

    def copy_b(c):
        return copy(
            n2.at[at(c * 2 * rows, rows)], n2.at[at(c * 2 * rows + rows, rows)], 1, c, tp_peer
        )

    def copy_c(c):
        return copy(send_c.at[at(c * rows, rows)], recv_c.at[at(c * rows, rows)], 2, c, tp_peer)

    def copy_d(c):
        return copy(
            dout.at[at(c * 2 * rows, rows)], dout.at[at(c * 2 * rows + rows, rows)], 3, c, tp_peer
        )

    def copy_e(c):
        return copy(send_e.at[at(c * rows, rows)], recv_e.at[at(c * rows, rows)], 4, c, tp_peer)

    def copy_f(c):
        mine = datt.at[at(h * half + c * rows, rows)]
        return copy(mine, mine, 5, c, x_peer)

    def lanes(k):
        return pl.ds(pl.multiple_of(k * eh, eh), eh)

    mine_o = pltpu.make_async_copy(
        o_hbm.at[at(core * tok_all, tok_all)], o_ref.at[:, lanes(core)], o_sem.at[0]
    )

    def give_o(k):
        return pltpu.make_async_remote_copy(
            src_ref=o_hbm.at[at((1 - core) * tok_all, tok_all)], dst_ref=o_ref.at[:, lanes(k)],
            send_sem=o_sem.at[1], recv_sem=o_sem.at[2], device_id=core_peer,
            device_id_type=pl.DeviceIdType.MESH,
        )

    give_o(core).start()
    mine_o.start()
    load_out.wait()
    mine_o.wait()
    give_o(1 - core).wait_recv()

    def mix_keep(rows_at, i):
        return pltpu.make_async_copy(
            dmix_ref.at[at(rows_at, rows), lanes(core)],
            dmix_hbm.at[at(core * tok_all + rows_at, rows)],
            m_sem.at[i],
        )

    def mix_give(rows_at, i, k):
        return pltpu.make_async_remote_copy(
            src_ref=dmix_ref.at[at(rows_at, rows), lanes(1 - core)],
            dst_ref=dmix_hbm.at[at(k * tok_all + rows_at, rows)],
            send_sem=s_m.at[i], recv_sem=r_m.at[i], device_id=core_peer,
            device_id_type=pl.DeviceIdType.MESH,
        )

    def phase_a(c, _):
        part = o_ref[at((1 - h) * half + c * rows, rows), :]
        send_a[at(c * rows, rows), :] = dotf(part, wo_ref[...], NT).astype(bf16)
        copy_a(c).start()
        return 0

    lax.fori_loop(0, chunks, phase_a, 0)

    def phase_b(c, _):
        part = o_ref[at(h * half + c * rows, rows), :]
        att[at(c * rows, rows), :] = dotf(part, wo_ref[...], NT)
        copy_a(c).wait_recv()
        for k in range(rows // TPF):
            r = at(c * rows + k * TPF, TPF)
            frame = pl.ds(c * (rows // TPF) + k, 1)
            a = att[r, :] + recv_a[r, :].astype(jnp.float32)
            att[r, :] = a
            v = hid_ref[r, :] + mod_row(0, c, k) * a
            x1[r, :] = v
            y, _inv = norm_rows(v)
            n2[at(c * 2 * rows + k * TPF, TPF), :] = (
                y * (1.0 + mod_row(2, c, k)) + mod_row(1, c, k)
            ).astype(bf16)
        copy_b(c).start()
        return 0

    lax.fori_loop(0, chunks, phase_b, 0)
    for w in weights:
        w.wait()

    def phase_c(c, _):
        copy_b(c).wait_recv()
        tok = at(c * 2 * rows, 2 * rows)
        n2t[:, tok] = n2[tok, :].T

        def up(i, _):
            cols = at(i * ft, ft)
            a, g = gelu_pair(dotf(n2[tok, :], wu_ref[:, cols]))
            act[tok, cols] = a.astype(bf16)
            dgl[tok, cols] = g.astype(bf16)
            return 0

        lax.fori_loop(0, ff // ft, up, 0)

        def down(i, _):
            cols = at(i * dt, dt)
            res = dotf(act[tok, :], wd_ref[cols, :], NT)
            out[at(c * rows, rows), cols] = res[:rows]
            send_c[at(c * rows, rows), cols] = res[rows:].astype(bf16)
            return 0

        lax.fori_loop(0, width // dt, down, 0)
        copy_c(c).start()
        return 0

    lax.fori_loop(0, chunks, phase_c, 0)

    ghead_ref[...] = jnp.zeros_like(ghead_ref)
    loss_ref[...] = jnp.zeros_like(loss_ref)

    def phase_d(c, _):
        copy_c(c).wait_recv()
        for k in range(rows // TPF):
            r = at(c * rows + k * TPF, TPF)
            frame = pl.ds(c * (rows // TPF) + k, 1)
            o = out[r, :] + recv_c[r, :].astype(jnp.float32)
            gate = mod_row(3, c, k)
            y, inv = norm_rows(x1[r, :] + gate * o)
            fn = y.astype(bf16)
            misfit = dotf(fn, head_ref[...], NT) - noise_ref[at(h * half + c * rows + k * TPF, TPF), :]
            weighted = tw_ref[frame_at(c, k), :] * misfit
            loss_ref[...] += weighted * misfit
            d_pred = (2.0 * gs_ref[0] * weighted).astype(bf16)
            ghead_ref[...] += dotf(d_pred, fn, TN)
            d_x2 = norm_rows_back(dotf(d_pred, head_ref[...]), y, inv)
            dx2[r, :] = d_x2
            dmod_ref[3, frame, :] = jnp.sum(d_x2 * o, axis=0, keepdims=True)
            dout[at(c * 2 * rows + k * TPF, TPF), :] = (gate * d_x2).astype(bf16)
        copy_d(c).start()
        return 0

    lax.fori_loop(0, chunks, phase_d, 0)

    def phase_e(c, _):
        copy_d(c).wait_recv()
        tok = at(c * 2 * rows, 2 * rows)
        doutt[:, tok] = dout[tok, :].T

        def down(i, _):
            cols = at(i * ft, ft)
            g = dotf(dout[tok, :], wd_ref[:, cols]) * dgl[tok, cols].astype(jnp.float32)
            dgl[tok, cols] = g.astype(bf16)
            return 0

        lax.fori_loop(0, ff // ft, down, 0)

        def up(i, _):
            cols = at(i * dt, dt)
            res = dotf(dgl[tok, :], wu_ref[cols, :], NT)
            out[at(c * rows, rows), cols] = res[:rows]
            send_e[at(c * rows, rows), cols] = res[rows:].astype(bf16)
            return 0

        lax.fori_loop(0, width // dt, up, 0)
        copy_e(c).start()
        return 0

    lax.fori_loop(0, chunks, phase_e, 0)

    def phase_f(c, _):
        copy_e(c).wait_recv()
        for k in range(rows // TPF):
            r = at(c * rows + k * TPF, TPF)
            frame = pl.ds(c * (rows // TPF) + k, 1)
            g = out[r, :] + recv_e[r, :].astype(jnp.float32)
            y, inv = norm_rows(x1[r, :])
            dmod_ref[1, frame, :] = jnp.sum(g, axis=0, keepdims=True)
            dmod_ref[2, frame, :] = jnp.sum(g * y, axis=0, keepdims=True)
            d_x1 = dx2[r, :] + norm_rows_back(g * (1.0 + mod_row(2, c, k)), y, inv)
            dx1_ref[r, :] = d_x1
            dmod_ref[0, frame, :] = jnp.sum(d_x1 * att[r, :], axis=0, keepdims=True)
            datt[at(h * half + c * rows + k * TPF, TPF), :] = (mod_row(0, c, k) * d_x1).astype(
                bf16
            )
        copy_f(c).start()
        return 0

    lax.fori_loop(0, chunks, phase_f, 0)

    def weight_grads(left, right, start):
        def put(slot, i):
            return pltpu.make_async_copy(
                stage.at[slot], rest_hbm.at[at(i * dt, dt), pl.ds(start, ff)], gsem.at[slot]
            )

        def tile(i, _):
            slot = lax.rem(i, 2)

            @pl.when(i >= 2)
            def _():
                put(slot, i - 2).wait()

            def cols_of(j, _):
                cols = at(j * ft, ft)
                stage[slot, :, cols] = dotf(left[at(i * dt, dt), :], right[:, cols]).astype(bf16)
                return 0

            lax.fori_loop(0, ff // ft, cols_of, 0)
            put(slot, i).start()
            return 0

        lax.fori_loop(0, width // dt, tile, 0)
        for i in (width // dt - 2, width // dt - 1):
            put(i % 2, i).wait()

    weight_grads(n2t, dgl, 0)
    weight_grads(doutt, act, ff)

    def own_mix(c, _):
        first = h * half + c * rows
        tok = at(first, rows)
        datt_t[:, tok] = datt[tok, :].T
        dmix_ref[tok, :] = dotf(datt[tok, :], wo_ref[...]).astype(bf16)
        mix_keep(first, c).start()
        mix_give(first, c, core).start()
        return 0

    lax.fori_loop(0, chunks, own_mix, 0)

    def phase_g(c, _):
        tok = at((1 - h) * half + c * rows, rows)
        theirs = datt.at[tok]
        copy(theirs, theirs, 5, c, x_peer).wait_recv()
        datt_t[:, tok] = datt[tok, :].T
        dmix_ref[tok, :] = dotf(datt[tok, :], wo_ref[...]).astype(bf16)
        first = (1 - h) * half + c * rows
        mix_keep(first, chunks + c).start()
        mix_give(first, chunks + c, core).start()
        return 0

    lax.fori_loop(0, chunks, phase_g, 0)

    def grad_out(i, _):
        d = at(i * dt, dt)
        go_ref[d, :] = dotf(datt_t[d, :], o_ref[...]).astype(bf16)
        return 0

    lax.fori_loop(0, width // dt, grad_out, 0)
    gh_t[...] = ghead_ref[...].T.astype(bf16)
    ends = [
        pltpu.make_async_copy(go_ref, rest_hbm.at[:, pl.ds(2 * ff, e)], gsem.at[2]),
        pltpu.make_async_copy(gh_t, rest_hbm.at[:, pl.ds(2 * ff + e, 128)], gsem.at[3]),
    ]
    for one in ends:
        one.start()
    for one in ends:
        one.wait()
    def sent(c, _):
        for one in (copy_a, copy_b, copy_c, copy_d, copy_e, copy_f):
            one(c).wait_send()
        for side in range(2):
            first = (h if side == 0 else 1 - h) * half + c * rows
            i = side * chunks + c
            mix_keep(first, i).wait()
            mix_give(first, i, core).wait_send()
            mix_give(first, i, 1 - core).wait_recv()
        return 0

    lax.fori_loop(0, chunks, sent, 0)
    give_o(core).wait_send()


def mid_block(o, hid, mod, noise, tw, head, gs, wu, wd, wa, tp, cid):
    tok, e = o.shape[0] // 2, 2 * o.shape[1]
    half, width = hid.shape
    ff = wu.shape[1]
    own_frames = half // TPF
    f32, bf16 = jnp.float32, jnp.bfloat16
    vm = pl.BlockSpec(memory_space=pltpu.VMEM)
    anym = pl.BlockSpec(memory_space=pl.ANY)
    V = pltpu.VMEM
    return pl.pallas_call(
        functools.partial(mid_kernel, tp=tp),
        in_specs=[anym] + [vm] * 5 + [pl.BlockSpec(memory_space=pltpu.SMEM), anym, anym, anym],
        out_specs=[anym] + [vm] * 3 + [anym],
        out_shape=[
            jax.ShapeDtypeStruct((2 * tok, e // 2), bf16),
            jax.ShapeDtypeStruct((half, width), f32),
            jax.ShapeDtypeStruct((4, own_frames, width), f32),
            jax.ShapeDtypeStruct((TPF, 128), f32),
            jax.ShapeDtypeStruct((width, 2 * ff + e + 128), bf16),
        ],
        scratch_shapes=[
            V((tok, e), bf16), V((tok, e), bf16),
            V((width, e), bf16), V((width, ff), bf16), V((width, ff), bf16),
            V((half, width), f32), V((half, width), f32), V((half, width), f32),
            V((half, width), f32),
            V((2 * half, width), bf16), V((width, 2 * half), bf16),
            V((2 * half, ff), bf16), V((2 * half, ff), bf16),
            V((2 * half, width), bf16), V((width, 2 * half), bf16),
            V((tok, width), bf16), V((width, tok), bf16),
            V((half, width), bf16), V((half, width), bf16),
            V((half, width), bf16), V((half, width), bf16),
            V((half, width), bf16), V((half, width), bf16),
            V((2, 256, ff), bf16), V((128, width), f32), V((width, e), bf16),
            V((width, 128), bf16),
            pltpu.SemaphoreType.DMA((3,)), pltpu.SemaphoreType.DMA((4,)),
            pltpu.SemaphoreType.DMA((6, half // 128)), pltpu.SemaphoreType.DMA((6, half // 128)),
            pltpu.SemaphoreType.DMA((3,)), pltpu.SemaphoreType.DMA((2 * half // 128,)),
            pltpu.SemaphoreType.DMA((2 * half // 128,)), pltpu.SemaphoreType.DMA((2 * half // 128,)),
        ],
        compiler_params=pltpu.CompilerParams(
            vmem_limit_bytes=62 << 20, collective_id=cid, has_side_effects=True
        ),
        cost_estimate=pl.CostEstimate(
            flops=4 * 10**10, bytes_accessed=3 * 10**7, transcendentals=2 * 10**6
        ),
        name="feed_forward",
    )(o, hid, mod, noise, tw, head, gs, wu, wd, wa)


def split_three(v):
    high = v.astype(jnp.bfloat16)
    left = v - high.astype(jnp.float32)
    middle = left.astype(jnp.bfloat16)
    return high, middle, (left - middle.astype(jnp.float32)).astype(jnp.bfloat16)


def turn_back(g, cosine, sine, rot):
    parts = split_three(g * sine)
    return (g * cosine + sum(dotf(p, rot, NT) for p in parts)).astype(jnp.bfloat16)


def tail_kernel(
    dq_ref, n1_ref, w_ref, fcos_ref, fsin_ref, pcos_ref, psin_ref, rot_ref, hid_ref, scale_ref, dx1_ref, inp_ref,
    dk_hbm, dv_hbm,
    gq_ref, gin_ref, dss_ref,
    relayed, own, yrecv, zrecv, give, n1t, dproj, send_x, recv_x, part,
    lsem, s_d, r_d, s_y, r_y, s_z, r_z, s_x, r_x,
):
    f = lax.axis_index("frames")
    h = lax.axis_index("mp")
    n = lax.axis_size("frames")
    core = lax.rem(f, 2)
    odd = lax.rem(lax.div(f, 2), 2)
    core_peer = {"frames": f + 1 - 2 * core}
    y_peer = {"frames": f + 2 - 4 * odd}
    before = {"frames": lax.rem(f - 4 + n, n)}
    after = {"frames": lax.rem(f + 4, n)}
    x_peer = {"mp": 1 - h}
    tok, width = n1_ref.shape
    eh = dq_ref.shape[1]
    half = tok // 2
    rows = 256
    f32, bf16 = jnp.float32, jnp.bfloat16
    MESH = pl.DeviceIdType.MESH
    sides = (dk_hbm, dv_hbm)
    share = width // n

    def at(start, size):
        return pl.ds(pl.multiple_of(start, size), size)

    loads = [
        pltpu.make_async_copy(
            sides[s].at[pl.ds(b * 2 * tok, 2 * tok)], (own, relayed)[j].at[s], lsem.at[s, j]
        )
        for s in range(2)
        for j, b in enumerate((2, 0))
    ]
    for one in loads:
        one.start()

    barrier = pltpu.get_barrier_semaphore()
    for peer in (core_peer, y_peer, x_peer):
        pl.semaphore_signal(barrier, inc=1, device_id=peer, device_id_type=MESH)

    @pl.when(f >= 4)
    def _():
        pl.semaphore_signal(barrier, inc=1, device_id=before, device_id_type=MESH)

    @pl.when(f + 4 < n)
    def _():
        pl.semaphore_signal(barrier, inc=1, device_id=after, device_id_type=MESH)

    pl.semaphore_wait(barrier, 3 + jnp.where(f >= 4, 1, 0) + jnp.where(f + 4 < n, 1, 0))

    def half_at(i2):
        return lax.rem(i2 + 1 - h, 2) * half

    def rows_of(i2, tc):
        return tc * tok + half_at(i2)

    def remote(src, dst, send, recv, peer):
        return pltpu.make_async_remote_copy(
            src_ref=src, dst_ref=dst, send_sem=send, recv_sem=recv, device_id=peer,
            device_id_type=MESH,
        )

    def y_copy(i2, tc, s):
        first = rows_of(i2, tc)
        i = 2 * i2 + tc
        return remote(
            sides[s].at[at(2 * tok + first, half)], yrecv.at[s, at(first, half)],
            s_y.at[s, i], r_y.at[s, i], y_peer,
        )

    def z_copy(i2, tc, s):
        r = at(rows_of(i2, tc), half)
        i = 2 * i2 + tc
        return remote(relayed.at[s, r], zrecv.at[s, r], s_z.at[s, i], r_z.at[s, i], before)

    def d_copy(k, i2, tc):
        r = at(half_at(i2), half)
        return remote(
            give.at[k, r], dproj.at[k, r, pl.ds(tc * eh, eh)], s_d.at[k, i2], r_d.at[k, i2],
            core_peer,
        )

    def x_copy(i):
        r = at(i * rows, rows)
        return remote(send_x.at[r], recv_x.at[r], s_x.at[i], r_x.at[i], x_peer)

    for one in loads:
        one.wait()

    def start_far(i2, _):
        for tc in range(2):
            for s in range(2):
                y_copy(i2, tc, s).start()

                @pl.when((odd == 0) & (f >= 4))
                def _():
                    z_copy(i2, tc, s).start()

        return 0

    lax.fori_loop(0, 2, start_far, 0)

    @pl.when(f + 4 >= n)
    def _():
        zrecv[...] = jnp.zeros_like(zrecv)

    def settle(k, i2, tc, value):
        r = at(half_at(i2), half)

        @pl.when(core == tc)
        def _():
            dproj[k, r, tc * eh : (tc + 1) * eh] = value

        @pl.when(core != tc)
        def _():
            give[k, r, :] = value
            d_copy(k, i2, 1 - tc).start()

    def arrived(k, i2):
        for tc in range(2):

            @pl.when(core == tc)
            def _():
                d_copy(k, i2, 1 - tc).wait_recv()

    def turned(g, i2, tc):
        first = tc * (tok // TPF) + lax.div(half_at(i2), TPF)
        cosine = turn_table(fcos_ref, pcos_ref, first, half // TPF)
        sine = turn_table(fsin_ref, psin_ref, first, half // TPF)
        return turn_back(g, cosine, sine, rot_ref[...])

    def relay(i2, _):
        for tc in range(2):
            r = at(rows_of(i2, tc), half)
            settle(0, i2, tc, turned(dq_ref[r, :], i2, tc))

            @pl.when(odd == 1)
            def _():
                for s in range(2):
                    y_copy(i2, tc, s).wait_recv()

                    @pl.when(f >= 4)
                    def _():
                        relayed[s, r, :] = (
                            relayed[s, r, :].astype(f32) + yrecv[s, r, :].astype(f32)
                        ).astype(bf16)
                        z_copy(i2, tc, s).start()

        for b in range(2):
            r = at(half_at(i2) + b * rows, rows)
            n1t[:, r] = n1_ref[r, :].T
        return 0

    lax.fori_loop(0, 2, relay, 0)
    for i2 in range(2):
        arrived(0, i2)

    def grads(k):
        def tile(i, _):
            res = dotf(n1t[at(i * 256, 256), :], dproj[k]).astype(bf16)
            for q in range(256 // share):
                j = i * (256 // share // 4) + q // 4
                gq_ref[q % 2, (q // 2) % 2, k, at(j * share, share), :] = res[
                    q * share : (q + 1) * share
                ]
            return 0

        lax.fori_loop(0, width // 256, tile, 0)

    grads(0)

    def finish(i2, _):
        for tc in range(2):
            r = at(rows_of(i2, tc), half)
            for s in range(2):

                @pl.when(odd == 0)
                def _():
                    y_copy(i2, tc, s).wait_recv()

                @pl.when(f + 4 < n)
                def _():
                    z_copy(i2, tc, s).wait_recv()

                total = (
                    own[s, r, :].astype(f32)
                    + jnp.where(odd == 0, yrecv[s, r, :].astype(f32), 0.0)
                    + zrecv[s, r, :].astype(f32)
                )
                if s == 0:
                    settle(1, i2, tc, turned(total, i2, tc))
                else:
                    settle(2, i2, tc, total.astype(bf16))

        arrived(1, i2)
        arrived(2, i2)

        def block_of(q, _):
            b = lax.div(q, width // 256)
            cols = at(lax.rem(q, width // 256) * 256, 256)
            r = at(half_at(i2) + b * rows, rows)
            res = sum(dotf(dproj[k, r, :], w_ref[k, cols, :], NT) for k in range(3))

            @pl.when(i2 == 0)
            def _():
                send_x[at(b * rows, rows), cols] = res.astype(bf16)

            @pl.when((i2 == 0) & (lax.rem(q, width // 256) == width // 256 - 1))
            def _():
                x_copy(b).start()

            @pl.when(i2 == 1)
            def _():
                part[at(b * rows, rows), cols] = res

            return 0

        lax.fori_loop(0, half // rows * (width // 256), block_of, 0)
        return 0

    lax.fori_loop(0, 2, finish, 0)
    grads(1)
    grads(2)
    gin_ref[...] = jnp.zeros_like(gin_ref)

    def norm_back(i, _):
        x_copy(i).wait_recv()
        for k in range(rows // TPF):
            r = at(i * rows + k * TPF, TPF)
            frame = pl.ds(i * (rows // TPF) + k, 1)
            first = h * (half // TPF) + i * (rows // TPF) + k
            g = part[r, :] + recv_x[r, :].astype(f32)
            y, inv = norm_rows(hid_ref[r, :])
            dss_ref[0, frame, :] = jnp.sum(g, axis=0, keepdims=True)
            dss_ref[1, frame, :] = jnp.sum(g * y, axis=0, keepdims=True)
            d_hid = dx1_ref[r, :] + norm_rows_back(g * (1.0 + scale_ref[pl.ds(first, 1), width : 2 * width]), y, inv)
            gin_ref[...] += dotf(inp_ref[at(first * TPF, TPF), :], d_hid.astype(bf16), TN)
        return 0

    lax.fori_loop(0, half // rows, norm_back, 0)

    def sent(i2, _):
        for tc in range(2):
            for s in range(2):
                y_copy(i2, tc, s).wait_send()

                @pl.when(f >= 4)
                def _():
                    z_copy(i2, tc, s).wait_send()

            @pl.when(core != tc)
            def _():
                for k in range(3):
                    d_copy(k, i2, 1 - tc).wait_send()

        x_copy(i2).wait_send()
        return 0

    lax.fori_loop(0, half // rows, sent, 0)


def tail_block(dq, n1, w, tables, rot, hid, scale, dx1, inp, dk, dv, cid):
    tok, width = n1.shape
    e = 2 * dq.shape[1]
    half = tok // 2
    f32, bf16 = jnp.float32, jnp.bfloat16
    vm = pl.BlockSpec(memory_space=pltpu.VMEM)
    anym = pl.BlockSpec(memory_space=pl.ANY)
    V = pltpu.VMEM
    D_ = pltpu.SemaphoreType.DMA
    return pl.pallas_call(
        tail_kernel,
        in_specs=[vm] * 12 + [anym] * 2,
        out_specs=[vm] * 3,
        out_shape=[
            jax.ShapeDtypeStruct((2, 2, 3, width // 4, e), bf16),
            jax.ShapeDtypeStruct((128, width), f32),
            jax.ShapeDtypeStruct((2, half // TPF, width), f32),
        ],
        scratch_shapes=[
            V((2, tok * 2, e // 2), bf16), V((2, tok * 2, e // 2), bf16),
            V((2, tok * 2, e // 2), bf16), V((2, tok * 2, e // 2), bf16),
            V((3, tok, e // 2), bf16), V((width, tok), bf16), V((3, tok, e), bf16),
            V((half, width), bf16), V((half, width), bf16), V((half, width), f32),
            D_((2, 2)), D_((3, 2)), D_((3, 2)), D_((2, 4)), D_((2, 4)),
            D_((2, 4)), D_((2, 4)), D_((half // 256,)), D_((half // 256,)),
        ],
        compiler_params=pltpu.CompilerParams(
            vmem_limit_bytes=56 << 20, collective_id=cid, has_side_effects=True
        ),
        cost_estimate=pl.CostEstimate(
            flops=10**9, bytes_accessed=10**6, transcendentals=0
        ),
        name="projection_backward",
    )(dq, n1, w, *tables, rot, hid, scale, dx1, inp, dk, dv)


def proj_kernel(
    inp_ref, win_ref, mod_ref, w_ref, fcos_ref, fsin_ref, pcos_ref, psin_ref, rot_ref,
    n1_ref, hid_ref, q_hbm, k_hbm, v_hbm,
    kv, give, q_keep, wr,
    lsem, qsem, s_core, r_core, s_y, r_y, s_z, r_z,
):
    f = lax.axis_index("frames")
    h = lax.axis_index("mp")
    n = lax.axis_size("frames")
    core = lax.rem(f, 2)
    odd = lax.rem(lax.div(f, 2), 2)
    core_peer = {"frames": f + 1 - 2 * core}
    y_peer = {"frames": f + 2 - 4 * odd}
    before = {"frames": lax.rem(f - 4 + n, n)}
    after = {"frames": lax.rem(f + 4, n)}
    tok, width = n1_ref.shape
    e = w_ref.shape[2]
    eh = e // 2
    low_core = core == 0
    half = tok // 2
    rows = 256
    chunks = tok // rows
    bf16 = jnp.bfloat16
    MESH = pl.DeviceIdType.MESH
    sides = (k_hbm, v_hbm)
    has_z = f >= 4
    has_next = f + 4 < n
    has_y = has_z | (odd == 1)

    def at(start, size):
        return pl.ds(pl.multiple_of(start, size), size)

    barrier = pltpu.get_barrier_semaphore()
    for peer in (core_peer, y_peer):
        pl.semaphore_signal(barrier, inc=1, device_id=peer, device_id_type=MESH)

    @pl.when(has_z)
    def _():
        pl.semaphore_signal(barrier, inc=1, device_id=before, device_id_type=MESH)

    @pl.when(has_next)
    def _():
        pl.semaphore_signal(barrier, inc=1, device_id=after, device_id_type=MESH)

    def embed(i, _):
        for k in range(2):
            r = at(i * 2 * TPF + k * TPF, TPF)
            frame = pl.ds(i * 2 + k, 1)
            v = dotf(inp_ref[r, :], win_ref[...])
            y, _inv = norm_rows(v)
            scale = 1.0 + mod_ref[frame, width : 2 * width]
            n1_ref[r, :] = (y * scale + mod_ref[frame, :width]).astype(bf16)

            @pl.when(lax.div(i * 2 * TPF, half) == h)
            def _():
                hid_ref[at(lax.rem(i * 2 * TPF, half) + k * TPF, TPF), :] = v

        return 0

    lax.fori_loop(0, tok // (2 * TPF), embed, 0)

    def turn_weights(i, _):
        d = at(i * 256, 256)
        for k in range(2):
            for b in range(e // 256):
                cols = slice(b * 256, (b + 1) * 256)
                wr[k, d, cols] = dotf(w_ref[k, d, cols], rot_ref[...]).astype(bf16)
        return 0

    lax.fori_loop(0, width // 256, turn_weights, 0)
    pl.semaphore_wait(barrier, 2 + jnp.where(has_z, 1, 0) + jnp.where(has_next, 1, 0))

    def remote(src, dst, send, recv, peer):
        return pltpu.make_async_remote_copy(
            src_ref=src, dst_ref=dst, send_sem=send, recv_sem=recv, device_id=peer,
            device_id_type=MESH,
        )

    def block(s, b, i):
        return sides[s].at[at(b * tok + i * rows, rows)]

    def mine(s, tc, i):
        return kv.at[s, tc, at(i * rows, rows)]

    def keep(s, tc, i):
        return pltpu.make_async_copy(mine(s, tc, i), block(s, 4 + tc, i), lsem.at[s, tc, i])

    def z_copy(s, tc, i):
        return remote(
            mine(s, tc, i), block(s, tc, i), s_z.at[s, tc, i], r_z.at[s, tc, i], after
        )

    def y_copy(s, tc, i, src):
        return remote(src, block(s, 2 + tc, i), s_y.at[s, tc, i], r_y.at[s, tc, i], y_peer)

    def core_copy(s, i, tc):
        return remote(
            give.at[s, at(i * rows, rows)], mine(s, tc, i), s_core.at[s, i], r_core.at[s, i],
            core_peer,
        )

    def q_rows(tc, i):
        return q_hbm.at[at(tc * tok + i * rows, rows)]

    def q_own(i):
        return pltpu.make_async_copy(
            q_keep.at[at(i * rows, rows)], q_rows(core, i), qsem.at[i]
        )

    def q_copy(i, tc):
        return remote(
            give.at[2, at(i * rows, rows)], q_rows(tc, i), s_core.at[2, i], r_core.at[2, i],
            core_peer,
        )

    def onward(s, tc, i):
        keep(s, tc, i).start()

        @pl.when(has_next)
        def _():
            z_copy(s, tc, i).start()

        @pl.when(odd == 0)
        def _():
            y_copy(s, tc, i, mine(s, tc, i)).start()

    def rotated(r, i, k):
        frames = rows // TPF
        first = core * (tok // TPF) + i * frames
        cosine = turn_table(fcos_ref, pcos_ref, first, frames)
        sine = turn_table(fsin_ref, psin_ref, first, frames)
        parts = []
        for b in range(e // 256):
            cols = slice(b * 256, (b + 1) * 256)
            plain = dotf(n1_ref[r, :], w_ref[k, :, cols])
            turned = dotf(n1_ref[r, :], wr[k, :, cols])
            parts.append((plain * cosine + turned * sine).astype(bf16))
        return parts

    def own_chunk(i, _):
        r = at(i * rows, rows)
        keys = rotated(r, i, 1)
        values = dotf(n1_ref[r, :], w_ref[2]).astype(bf16)
        for s, pair in enumerate((keys, (values[:, :eh], values[:, eh:]))):
            kv[s, core, r, :] = jnp.where(low_core, pair[0], pair[1])
            give[s, r, :] = jnp.where(low_core, pair[1], pair[0])
            core_copy(s, i, core).start()
            onward(s, core, i)
        return 0

    lax.fori_loop(0, chunks, own_chunk, 0)

    def from_core(i, _):
        for s in range(2):
            core_copy(s, i, 1 - core).wait_recv()
            onward(s, 1 - core, i)
        return 0

    lax.fori_loop(0, chunks, from_core, 0)

    def queries(i, _):
        r = at(i * rows, rows)
        pair = rotated(r, i, 0)
        q_keep[r, :] = jnp.where(low_core, pair[0], pair[1])
        give[2, r, :] = jnp.where(low_core, pair[1], pair[0])
        q_own(i).start()
        q_copy(i, core).start()
        return 0

    lax.fori_loop(0, chunks, queries, 0)

    def from_z(g, _):
        tc = lax.rem(core + lax.div(g, chunks), 2)
        i = lax.rem(g, chunks)

        @pl.when(has_z)
        def _():
            for s in range(2):
                z_copy(s, tc, i).wait_recv()

                @pl.when(odd == 1)
                def _():
                    y_copy(s, tc, i, block(s, tc, i)).start()

        return 0

    lax.fori_loop(0, 2 * chunks, from_z, 0)

    def ended(i, _):
        q_own(i).wait()
        q_copy(i, 1 - core).wait_recv()
        q_copy(i, core).wait_send()
        for s in range(2):
            core_copy(s, i, core).wait_send()
            for tc in range(2):
                keep(s, tc, i).wait()

                @pl.when(has_y)
                def _():
                    y_copy(s, tc, i, mine(s, tc, i)).wait_recv()

                @pl.when(has_next)
                def _():
                    z_copy(s, tc, i).wait_send()

                @pl.when((odd == 0) | has_z)
                def _():
                    y_copy(s, tc, i, mine(s, tc, i)).wait_send()

        return 0

    lax.fori_loop(0, chunks, ended, 0)


def proj_block(inp, win, mod, w, tables, rot, reach, cid):
    tok = inp.shape[0]
    width, e = w.shape[1:]
    f32, bf16 = jnp.float32, jnp.bfloat16
    vm = pl.BlockSpec(memory_space=pltpu.VMEM)
    anym = pl.BlockSpec(memory_space=pl.ANY)
    V = pltpu.VMEM
    D_ = pltpu.SemaphoreType.DMA
    chunks = tok // 256
    return pl.pallas_call(
        proj_kernel,
        in_specs=[vm] * 9,
        out_specs=[vm] * 2 + [anym] * 3,
        out_shape=[
            jax.ShapeDtypeStruct((tok, width), bf16),
            jax.ShapeDtypeStruct((tok // 2, width), f32),
            jax.ShapeDtypeStruct((2 * tok, e // 2), bf16),
            jax.ShapeDtypeStruct(((reach + 2) * tok, e // 2), bf16),
            jax.ShapeDtypeStruct(((reach + 2) * tok, e // 2), bf16),
        ],
        scratch_shapes=[
            V((2, 2, tok, e // 2), bf16), V((3, tok, e // 2), bf16), V((tok, e // 2), bf16),
            V((2, width, e), bf16),
            D_((2, 2, chunks)), D_((chunks,)), D_((3, chunks)), D_((3, chunks)),
            D_((2, 2, chunks)), D_((2, 2, chunks)), D_((2, 2, chunks)), D_((2, 2, chunks)),
        ],
        compiler_params=pltpu.CompilerParams(
            vmem_limit_bytes=48 << 20, collective_id=cid, has_side_effects=True
        ),
        cost_estimate=pl.CostEstimate(
            flops=6 * 10**10, bytes_accessed=3 * 10**7, transcendentals=0
        ),
        name="projection_forward",
    )(inp, win, mod, w, *tables, rot)


def last_kernel(
    g_hbm, gin_ref, dm_ref, cond_ref, wm_ref, loss_ref,
    sq_ref, sin_ref, smod_ref, dct_ref,
    g_own, g_in, near, near_in, side, side_in, far, far_in, ends, ends_peer, dm_peer, dm,
    dc_send, dc_peer,
    lsem, s_x, r_x, s_g, r_g, s_f, r_f, s_d, r_d, s_dz, r_dz,
):
    f = lax.axis_index("frames")
    h = lax.axis_index("mp")
    n = lax.axis_size("frames")
    nj = n // 4
    core = lax.rem(f, 2)
    y = lax.rem(lax.div(f, 2), 2)
    j = lax.div(f, 4)
    core_peer = {"frames": f + 1 - 2 * core}
    y_peer = {"frames": f + 2 - 4 * y}
    x_peer = {"mp": 1 - h}
    f32, bf16 = jnp.float32, jnp.bfloat16
    MESH = pl.DeviceIdType.MESH
    rows = g_hbm.shape[3] // nj

    def z_peer(t):
        return {"frames": lax.rem(f + 4 * t, n)}

    def from_j(t):
        return lax.rem(j - t + nj, nj)

    def at(start, size):
        return pl.ds(pl.multiple_of(start, size), size)

    load = pltpu.make_async_copy(g_hbm.at[core], g_own, lsem.at[0])
    load.start()
    barrier = pltpu.get_barrier_semaphore()
    for peer in [core_peer, y_peer, x_peer] + [z_peer(t) for t in range(1, nj)]:
        pl.semaphore_signal(barrier, inc=1, device_id=peer, device_id_type=MESH)
    pl.semaphore_wait(barrier, 2 + nj)

    def remote(src, dst, send, recv, peer):
        return pltpu.make_async_remote_copy(
            src_ref=src, dst_ref=dst, send_sem=send, recv_sem=recv, device_id=peer,
            device_id_type=MESH,
        )

    dm_x = remote(dm_ref.at[1 - h], dm_peer, s_x.at[0], r_x.at[0], x_peer)
    dm_x.start()
    core_g = remote(g_hbm.at[1 - core], near, s_g.at[0], r_g.at[0], core_peer)
    core_in = remote(gin_ref.at[1 - core], near_in, s_g.at[1], r_g.at[1], core_peer)
    core_g.start()
    core_in.start()

    dm_x.wait_recv()
    mine = dm_ref[h]
    theirs = dm_peer[...]
    low = h == 0
    dm[core, y, j] = jnp.concatenate(
        [jnp.where(low, mine, theirs), jnp.where(low, theirs, mine)], axis=0
    ).astype(bf16)

    def dm_z(t, src):
        block = dm.at[core, y, src]
        return remote(block, block, s_dz.at[0, t], r_dz.at[0, t], z_peer(t))

    for t in range(1, nj):
        dm_z(t, j).start()
    load.wait()
    core_g.wait_recv()
    core_in.wait_recv()

    def add_near(i, _):
        for s in range(2):
            for k in range(g_own.shape[1]):
                r = at(i * rows, rows)
                g_own[s, k, r, :] = (
                    g_own[s, k, r, :].astype(f32) + near[s, k, r, :].astype(f32)
                ).astype(bf16)
        return 0

    lax.fori_loop(0, nj, add_near, 0)
    g_in[...] = (gin_ref[core].astype(f32) + near_in[...].astype(f32)).astype(bf16)
    for t in range(1, nj):
        dm_z(t, from_j(t)).wait_recv()

    def dm_y(side_index):
        block = dm.at[core, side_index]
        return remote(block, block, s_d.at[0], r_d.at[0], y_peer)

    dm_y(y).start()
    y_g = remote(g_own.at[1 - y], side, s_g.at[2], r_g.at[2], y_peer)
    y_in = remote(g_in.at[1 - y], side_in, s_g.at[3], r_g.at[3], y_peer)
    y_g.start()
    y_in.start()
    dm_y(1 - y).wait_recv()

    def dm_core(core_index):
        block = dm.at[core_index]
        return remote(block, block, s_d.at[1], r_d.at[1], core_peer)

    dm_core(core).start()
    y_g.wait_recv()
    y_in.wait_recv()

    def add_side(i, _):
        for k in range(g_own.shape[1]):
            r = at(i * rows, rows)
            side[k, r, :] = (
                g_own[y, k, r, :].astype(f32) + side[k, r, :].astype(f32)
            ).astype(bf16)
        return 0

    lax.fori_loop(0, nj, add_side, 0)
    side_in[...] = (g_in[y].astype(f32) + side_in[...].astype(f32)).astype(bf16)

    def far_g(t):
        there = at(lax.rem(j + t, nj) * rows, rows)
        return remote(
            side.at[:, there], far.at[t - 1], s_f.at[0, t], r_f.at[0, t], z_peer(t)
        )

    def far_i(t):
        there = at(lax.rem(j + t, nj) * rows, rows)
        return remote(
            side_in.at[there], far_in.at[t - 1], s_f.at[1, t], r_f.at[1, t], z_peer(t)
        )

    for t in range(1, nj):
        far_g(t).start()
        far_i(t).start()

    dm_core(1 - core).wait_recv()
    frames = dm.shape[0] * dm.shape[1] * dm.shape[2] * dm.shape[3]
    wide = dm.shape[4]
    every = dm[...].reshape(frames, wide)
    part = dotf(wm_ref[...], every, NT)
    dc_send[:rows, :] = part
    dc_send[rows:, :] = jnp.broadcast_to(jnp.sum(loss_ref[...]), (8, frames))
    dc_x = remote(dc_send, dc_peer, s_x.at[1], r_x.at[1], x_peer)
    dc_x.start()

    def mod_cols(i, _):
        cols = at(i * 512, 512)
        block = dm[:, :, :, :, cols].reshape(frames, 512)
        res = dotf(cond_ref[...], block)
        smod_ref[:, cols] = res[:rows] + res[rows : 2 * rows] + res[2 * rows :]
        return 0

    lax.fori_loop(0, wide // 512, mod_cols, 0)
    dc_x.wait_recv()
    total = dc_send[...] + dc_peer[...]
    dct_ref[core, y, j, :rows, :] = total[:rows].astype(bf16)
    pieces = [p[:1].astype(f32) for p in split_three(total[rows:])]
    dct_ref[core, y, j, rows:, :] = jnp.concatenate(
        pieces + [jnp.zeros((13, frames), f32)], axis=0
    ).astype(bf16)

    def dc_z(t, src):
        block = dct_ref.at[core, y, src]
        return remote(block, block, s_dz.at[1, t], r_dz.at[1, t], z_peer(t))

    for t in range(1, nj):
        dc_z(t, j).start()
    for t in range(1, nj):
        dc_z(t, from_j(t)).wait_recv()

    def dc_y(side_index):
        block = dct_ref.at[core, side_index]
        return remote(block, block, s_d.at[2], r_d.at[2], y_peer)

    dc_y(y).start()

    here = at(j * rows, rows)
    for t in range(1, nj):
        far_g(t).wait_recv()
        far_i(t).wait_recv()
    for k in range(sq_ref.shape[0]):
        sq_ref[k] = side[k, here, :].astype(f32) + sum(
            far[t, k].astype(f32) for t in range(nj - 1)
        )
    ends[...] = side_in[here, :].astype(f32) + sum(
        far_in[t].astype(f32) for t in range(nj - 1)
    )
    ends_x = remote(ends, ends_peer, s_x.at[2], r_x.at[2], x_peer)
    ends_x.start()
    dc_y(1 - y).wait_recv()

    def dc_core(core_index):
        block = dct_ref.at[core_index]
        return remote(block, block, s_d.at[3], r_d.at[3], core_peer)

    dc_core(core).start()
    ends_x.wait_recv()
    sin_ref[...] = ends[...] + ends_peer[...]
    dc_core(1 - core).wait_recv()

    for one in (dm_x, core_g, core_in, y_g, y_in, dc_x, ends_x):
        one.wait_send()
    for one in (dm_y(y), dm_core(core), dc_y(y), dc_core(core)):
        one.wait_send()
    for t in range(1, nj):
        for one in (dm_z(t, j), dc_z(t, j), far_g(t), far_i(t)):
            one.wait_send()


def last_block(g, gin, dm, cond, wm, loss, cid):
    _, _, kinds, block_rows, e = g.shape
    n = lax.axis_size("frames")
    nj = n // 4
    rows = block_rows // nj
    own_frames, wide = dm.shape[1:]
    frames = n * 2 * own_frames
    f32, bf16 = jnp.float32, jnp.bfloat16
    vm = pl.BlockSpec(memory_space=pltpu.VMEM)
    anym = pl.BlockSpec(memory_space=pl.ANY)
    V = pltpu.VMEM
    D_ = pltpu.SemaphoreType.DMA
    return pl.pallas_call(
        last_kernel,
        in_specs=[anym] + [vm] * 5,
        out_specs=[vm] * 4,
        out_shape=[
            jax.ShapeDtypeStruct((kinds, rows, e), f32),
            jax.ShapeDtypeStruct((rows, 128), f32),
            jax.ShapeDtypeStruct((rows, wide), f32),
            jax.ShapeDtypeStruct((2, 2, nj, rows + 16, frames), bf16),
        ],
        scratch_shapes=[
            V((2, kinds, block_rows, e), bf16), V((2, block_rows, 128), bf16),
            V((2, kinds, block_rows, e), bf16), V((2, block_rows, 128), bf16),
            V((kinds, block_rows, e), bf16), V((block_rows, 128), bf16),
            V((nj - 1, kinds, rows, e), bf16), V((nj - 1, rows, 128), bf16),
            V((rows, 128), f32), V((rows, 128), f32),
            V((own_frames, wide), f32), V((2, 2, nj, 2 * own_frames, wide), bf16),
            V((rows + 8, frames), f32), V((rows + 8, frames), f32),
            D_((1,)), D_((3,)), D_((3,)), D_((4,)), D_((4,)), D_((2, nj)), D_((2, nj)),
            D_((4,)), D_((4,)), D_((2, nj)), D_((2, nj)),
        ],
        compiler_params=pltpu.CompilerParams(
            vmem_limit_bytes=48 << 20, collective_id=cid, has_side_effects=True
        ),
        cost_estimate=pl.CostEstimate(
            flops=2 * 10**10, bytes_accessed=2 * 10**7, transcendentals=0
        ),
        name="weight_sums",
    )(g, gin, dm, cond, wm, loss)


def front_kernel(
    small_ref, feat_ref, wm_ref, w_ref,
    st_ref, feats_ref, pre1_ref, pre2_ref, wout_ref, ends_ref, mod_ref,
    wcol, mods,
    s_x, r_x, s_z, r_z, s_y, r_y, s_c, r_c, s_a, r_a, s_m, r_m,
):
    f = lax.axis_index("frames")
    h = lax.axis_index("mp")
    n = lax.axis_size("frames")
    nj = n // 4
    c = lax.rem(f, 2)
    y = lax.rem(lax.div(f, 2), 2)
    j = lax.div(f, 4)
    f32, bf16 = jnp.float32, jnp.bfloat16
    MESH = pl.DeviceIdType.MESH
    x_peer = {"mp": 1 - h}
    core_peer = {"frames": f + 1 - 2 * c}
    y_peer = {"frames": f + 2 - 4 * y}
    offsets = [
        (tj, ty, tc) for tj in range(nj) for ty in range(2) for tc in range(2)
    ][1:]

    def place(tj, ty, tc):
        return (
            lax.rem(j + tj, nj),
            y + ty - 2 * y * ty,
            c + tc - 2 * c * tc,
        )

    def peer_of(spot):
        return {"frames": 4 * spot[0] + 2 * spot[1] + spot[2]}

    def from_j(t):
        return lax.rem(j - t + nj, nj)

    def remote(src, dst, send, recv, peer):
        return pltpu.make_async_remote_copy(
            src_ref=src, dst_ref=dst, send_sem=send, recv_sem=recv, device_id=peer,
            device_id_type=MESH,
        )

    barrier = pltpu.get_barrier_semaphore()
    for o in offsets:
        pl.semaphore_signal(barrier, inc=1, device_id=peer_of(place(*o)), device_id_type=MESH)
    pl.semaphore_signal(barrier, inc=1, device_id=x_peer, device_id_type=MESH)
    pl.semaphore_wait(barrier, n)

    class Gather:
        def __init__(self, block, k):
            self.block, self.k = block, k

        def over_z(self, t, jj):
            b = self.block(jj, y, c)
            return remote(
                b, b, s_z.at[self.k, t], r_z.at[self.k, t], {"frames": lax.rem(f + 4 * t, n)}
            )

        def over_y(self, t, yy):
            b = self.block(from_j(t), yy, c)
            return remote(b, b, s_y.at[self.k, t], r_y.at[self.k, t], y_peer)

        def over_core(self, t, same, yy, cc):
            b = self.block(from_j(t), yy, cc)
            return remote(
                b, b, s_c.at[self.k, same, t], r_c.at[self.k, same, t], core_peer
            )

        def start(self):
            for t in range(1, nj):
                self.over_z(t, j).start()
            self.over_y(0, y).start()
            self.over_core(0, 0, y, c).start()

        def pass_z(self):
            for t in range(1, nj):
                self.over_z(t, from_j(t)).wait_recv()
                self.over_y(t, y).start()
                self.over_core(t, 0, y, c).start()

        def pass_y(self):
            for t in range(nj):
                self.over_y(t, 1 - y).wait_recv()
                self.over_core(t, 1, 1 - y, c).start()

        def finish(self):
            for t in range(nj):
                self.over_core(t, 0, y, 1 - c).wait_recv()
                self.over_core(t, 1, 1 - y, 1 - c).wait_recv()

        def sent(self):
            for t in range(1, nj):
                self.over_z(t, j).wait_send()
            for t in range(nj):
                self.over_y(t, y).wait_send()
                self.over_core(t, 0, y, c).wait_send()
                self.over_core(t, 1, 1 - y, c).wait_send()

    small = Gather(lambda a, b, d: st_ref.at[a, b, d], 0)
    feats = Gather(lambda a, b, d: feats_ref.at[d, b, a], 1)
    weights = Gather(lambda a, b, d: wout_ref.at[:, a, b, d], 2)

    small_x = remote(small_ref, st_ref.at[j, y, c, h], s_x.at[0], r_x.at[0], x_peer)
    small_x.start()
    feats_ref[c, y, j] = feat_ref[...]
    feats.start()

    def column_copy(i, spot, slot):
        return remote(
            wm_ref.at[spot[2], spot[1], spot[0]], wcol.at[slot[0], slot[1], slot[2]],
            s_a.at[i], r_a.at[i], peer_of(spot),
        )

    def source(o):
        return place((nj - o[0]) % nj, o[1], o[2])

    for i, o in enumerate(offsets):
        column_copy(i, place(*o), (j, y, c)).start()
    st_ref[j, y, c, h] = small_ref[...]
    wout_ref[:, j, y, c] = w_ref[...]
    wcol[j, y, c] = wm_ref[c, y, j]
    remote(
        small_ref, st_ref.at[j, y, c, 1 - h], s_x.at[0], r_x.at[0], x_peer
    ).wait_recv()
    small.start()
    feats.pass_z()
    small.pass_z()
    weights.start()
    feats.pass_y()
    small.pass_y()
    feats.finish()
    small.finish()

    total = st_ref.shape[0] * 4
    width = total * 2 * st_ref.shape[4]
    frames = feats_ref.shape[2] * 4 * feats_ref.shape[3]
    inner = feats_ref.shape[4]

    def exact(left, right, dims):
        m = left.shape[0]
        res = dotf(jnp.concatenate(split_three(left), axis=0), right, dims)
        return res[:m] + res[m : 2 * m] + res[2 * m :]

    def silu(v):
        return v * jax.nn.sigmoid(v)

    table = st_ref[...].reshape(width, st_ref.shape[5])
    fv = feats_ref[...].reshape(frames, inner)
    pre1 = exact(fv, table[:, :inner], NT)
    pre1_ref[...] = pre1
    pre2 = exact(silu(pre1), table[:, inner : inner + width], NT)
    pre2_ref[...] = pre2
    ends_ref[...] = table[:, inner + width : inner + width + 128].T
    for i, o in enumerate(offsets):
        column_copy(i, place(*o), source(o)).wait_recv()
    cols = wcol[...].reshape(width, wcol.shape[4])
    mods[...] = exact(silu(pre2), cols, NN).reshape(mods.shape)

    def mods_copy(i, spot, slot):
        return remote(
            mods.at[spot[2], spot[1], spot[0]], mod_ref.at[h, slot[2], slot[1], slot[0]],
            s_m.at[i], r_m.at[i], peer_of(spot),
        )

    for i, o in enumerate(offsets):
        mods_copy(i, place(*o), (j, y, c)).start()
    mod_ref[h, c, y, j] = mods[c, y, j]
    weights.pass_z()
    for i, o in enumerate(offsets):
        mods_copy(i, place(*o), source(o)).wait_recv()
    mods_x = remote(mod_ref.at[h], mod_ref.at[h], s_x.at[1], r_x.at[1], x_peer)
    mods_x.start()
    weights.pass_y()
    weights.finish()
    theirs = mod_ref.at[1 - h]
    remote(theirs, theirs, s_x.at[1], r_x.at[1], x_peer).wait_recv()

    small_x.wait_send()
    mods_x.wait_send()
    for g in (small, feats, weights):
        g.sent()
    for i, o in enumerate(offsets):
        column_copy(i, place(*o), (j, y, c)).wait_send()
        mods_copy(i, place(*o), (j, y, c)).wait_send()


def front_block(small, feat, wm, w, cid):
    n = lax.axis_size("frames")
    nj = n // 4
    cols, lanes = small.shape
    own_frames, inner = feat.shape
    frames = n * own_frames
    kinds, rows, e = w.shape
    wide = wm.shape[-1]
    width = rows * n
    f32, bf16 = jnp.float32, jnp.bfloat16
    vm = pl.BlockSpec(memory_space=pltpu.VMEM)
    V = pltpu.VMEM
    D_ = pltpu.SemaphoreType.DMA
    return pl.pallas_call(
        front_kernel,
        in_specs=[vm] * 4,
        out_specs=[vm] * 7,
        out_shape=[
            jax.ShapeDtypeStruct((nj, 2, 2, 2, cols, lanes), bf16),
            jax.ShapeDtypeStruct((2, 2, nj, own_frames, inner), f32),
            jax.ShapeDtypeStruct((frames, width), f32),
            jax.ShapeDtypeStruct((frames, width), f32),
            jax.ShapeDtypeStruct((kinds, nj, 2, 2, rows, e), bf16),
            jax.ShapeDtypeStruct((128, width), bf16),
            jax.ShapeDtypeStruct((2, 2, 2, nj, own_frames, wide), f32),
        ],
        scratch_shapes=[
            V((nj, 2, 2, rows, wide), bf16), V((2, 2, nj, own_frames, wide), f32),
            D_((2,)), D_((2,)), D_((3, nj)), D_((3, nj)), D_((3, nj)), D_((3, nj)),
            D_((3, 2, nj)), D_((3, 2, nj)), D_((n - 1,)), D_((n - 1,)), D_((n - 1,)),
            D_((n - 1,)),
        ],
        compiler_params=pltpu.CompilerParams(
            vmem_limit_bytes=48 << 20, collective_id=cid, has_side_effects=True
        ),
        cost_estimate=pl.CostEstimate(
            flops=4 * 10**10, bytes_accessed=2 * 10**7, transcendentals=0
        ),
        name="conditioning",
    )(small, feat, wm, w)


def per_device(
    latents,
    noise,
    levels,
    clip_ids,
    clean_flags,
    attn_weights,
    mlp_weights,
    mod_weight,
    small_weights,
    attn_moment,
    mlp_moment,
    mod_moment,
    small_moment,
    attn_average,
    mlp_average,
    mod_average,
    small_average,
):
    frame_count = latents.shape[0]
    tok_count = frame_count * TPF
    patch_side = GRID // 2
    frames_total = clip_ids.shape[0]
    tokens_total = frames_total * TPF
    width_local = attn_weights.shape[2]
    heads_local = width_local // HD
    key_span = (REACH + 1) * tok_count
    device = lax.axis_index("frames")
    mp_index = lax.axis_index("mp")
    first_frame = device * frame_count
    scale_qk = HD ** (-0.5)
    attn_low = attn_weights.astype(jnp.bfloat16)
    mlp_low = mlp_weights.astype(jnp.bfloat16)
    low_mod = mod_weight.astype(jnp.bfloat16)
    noised_all = (1 - clean_flags).astype(jnp.float32)
    noised_count = jnp.sum(noised_all)
    noised = lax.dynamic_slice_in_dim(noised_all, first_frame, frame_count)
    level_eff = levels * noised
    signal_scale = jnp.cos(0.5 * math.pi * level_eff)
    noise_scale = jnp.sin(0.5 * math.pi * level_eff)
    noise_patches = patchify(noise)
    inputs = patchify(signal_scale[:, None] * latents + noise_scale[:, None] * noise)
    in_clip_all = clip_positions(clip_ids)
    chip_frames = 2 * frame_count
    chip_first = (device // 2) * chip_frames
    in_clip = lax.dynamic_slice_in_dim(in_clip_all, chip_first, chip_frames).astype(jnp.float32)
    within = np.arange(TPF)
    patch_zero = np.zeros((TPF, HD // 4), np.float32)
    patch_angles = np.concatenate(
        [patch_zero]
        + turn_phases((within // patch_side).astype(np.float32), 3 * HD // 8)
        + turn_phases((within % patch_side).astype(np.float32), 3 * HD // 8),
        axis=1,
    )
    patch_angles = np.tile(patch_angles, (1, 4))
    frame_angles = jnp.tile(
        jnp.concatenate(
            turn_phases(in_clip, HD // 4) + [jnp.zeros((chip_frames, 3 * HD // 4))], axis=1
        ),
        (1, 4),
    )
    tables = (
        jnp.cos(frame_angles),
        jnp.sin(frame_angles),
        jnp.asarray(np.cos(patch_angles), jnp.float32),
        jnp.asarray(np.sin(patch_angles), jnp.float32),
    )
    turn_four = jnp.asarray(np.kron(np.eye(4, dtype=np.float32), rotation_matrix(HD)), jnp.bfloat16)
    clip_start = (
        lax.dynamic_slice_in_dim(
            jnp.arange(frames_total, dtype=jnp.int32) - in_clip_all, chip_first, chip_frames
        )
        - chip_first
        + REACH * frame_count
    )
    peers = lax.axis_size("frames")
    frame_groups = peers // 4
    small_rows, small_cols = small_weights.shape
    mod_rows, mod_cols = mod_weight.shape
    mod_share = mod_cols // peers
    mod_wide = -(-mod_share // 128) * 128
    small_lanes = FREQ + D + 128
    small_t = jnp.pad(
        small_weights.astype(jnp.bfloat16).T, ((0, 0), (0, small_lanes - small_rows))
    )
    mod_blocks = jnp.pad(
        low_mod.reshape(mod_rows, frame_groups, 2, 2, mod_share).transpose(3, 2, 1, 0, 4),
        ((0, 0),) * 4 + ((0, mod_wide - mod_share),),
    )
    small_full, features_placed, pre_one, pre_two, w_qkv, end_rows, mod_parts = front_block(
        small_t, time_features(level_eff), mod_blocks, attn_low, 4
    )
    w_qkv, up_low = lax.optimization_barrier((w_qkv, mlp_low[0]))
    w_up = lax.all_gather(up_low, "frames", axis=0, tiled=True)
    w_qkv = w_qkv.reshape(4, D, width_local)
    features_placed = features_placed.reshape(frames_total, FREQ)
    first_placed = jax.nn.silu(pre_one)
    pre_two_t = pre_two.T
    first_col = (device * lax.axis_size("mp") + mp_index) * small_cols
    pre_one_own = lax.dynamic_slice_in_dim(pre_one, first_col, small_cols, 1).T
    cond_rows = jax.nn.silu(
        lax.dynamic_slice_in_dim(pre_two, device * mod_rows, mod_rows, 1)
    )
    cond_parts = jnp.concatenate([part.T for part in split_three(cond_rows)], axis=0)
    modulation = (
        mod_parts[..., :mod_share].transpose(4, 0, 3, 2, 1, 5).reshape(frame_count, 6 * D)
    )
    inputs_low = inputs.astype(jnp.bfloat16)
    padding = ((0, 0), (0, 128 - P_SIZE))
    inputs_low = jnp.pad(inputs_low, padding)
    normed_one, hidden_half, queries, keys_wide, values_wide = proj_block(
        inputs_low,
        end_rows,
        modulation,
        w_qkv,
        tables,
        turn_four,
        REACH,
        2,
    )
    down_low = mlp_low[1]
    queries, down_low, w_up = lax.optimization_barrier((queries, down_low, w_up))
    w_down = lax.all_gather(down_low, "frames", axis=0, tiled=True)
    heads_wide, heads_low, log_totals = attn_fwd(queries, keys_wide, values_wide, clip_start)
    half = tok_count // 2
    own_frames = frame_count // 2

    def half_of(array, dim=0):
        size = array.shape[dim] // 2
        return lax.dynamic_slice_in_dim(array, mp_index * size, size, dim)

    grad_scale = 1.0 / jnp.maximum(noised_count, 1.0)
    head_lanes = ((0, 0), (P_SIZE, 128 - 2 * P_SIZE))
    frame_weight = jnp.broadcast_to(noised[:, None] / (TPF * P_SIZE), (frame_count, P_SIZE))
    d_mixed, d_shaped_one, d_mod_mid, loss_parts, grad_rest = mid_block(
        heads_low,
        hidden_half,
        modulation,
        jnp.pad(noise_patches, head_lanes),
        jnp.pad(frame_weight, head_lanes),
        end_rows,
        grad_scale.reshape(1),
        w_up,
        w_down,
        w_qkv,
        TP_AXIS,
        0,
    )
    sum_rest = lax.psum_scatter(grad_rest, "frames", scatter_dimension=0, tiled=True)
    d_queries, keys_grad_wide, values_grad_wide = attn_bwd(
        queries, keys_wide, values_wide, d_mixed, heads_wide, log_totals, clip_start
    )
    grad_qkv, grad_in, d_first_mods = tail_block(
        d_queries,
        normed_one,
        w_qkv,
        tables,
        turn_four,
        hidden_half,
        modulation,
        d_shaped_one,
        inputs_low,
        keys_grad_wide,
        values_grad_wide,
        1,
    )
    d_first_mods, sum_rest = lax.optimization_barrier((d_first_mods, sum_rest))
    def by_place(array, dim):
        shape = array.shape
        size = shape[dim] // (4 * frame_groups)
        split = array.reshape(shape[:dim] + (frame_groups, 2, 2, size) + shape[dim + 1 :])
        order = list(range(split.ndim))
        order[dim], order[dim + 2] = dim + 2, dim
        return split.transpose(order)

    in_columns = by_place(grad_in.T, 0).reshape(2, 2, D // 4, 128).astype(jnp.bfloat16)
    d_mods = jnp.stack(
        [
            jnp.concatenate([d_first_mods[0], d_first_mods[1], d_mod_mid[0]], axis=1),
            jnp.concatenate([d_mod_mid[1], d_mod_mid[2], d_mod_mid[3]], axis=1),
        ]
    )
    sum_qkv, sum_in, sum_mod, d_cond_rows = last_block(
        grad_qkv, in_columns, d_mods, cond_parts, low_mod, loss_parts, 3
    )
    loss_sum = jnp.sum(d_cond_rows[:, :, :, mod_rows : mod_rows + 3, 0].astype(jnp.float32))
    d_cond_t = (
        d_cond_rows[:, :, :, :mod_rows, :].transpose(2, 1, 0, 3, 4).reshape(D, frames_total)
    ).astype(jnp.float32)
    d_pre_two = jax.vjp(jax.nn.silu, pre_two_t)[1](d_cond_t)[0]
    d_pre_own = lax.dynamic_slice_in_dim(d_pre_two, first_col, small_cols, 0)
    grad_second = jnp.einsum("fi,jf->ij", first_placed, d_pre_own, precision=HIGH)
    second_cols = lax.dynamic_slice_in_dim(
        small_full.reshape(D, small_lanes), FREQ + first_col, small_cols, 1
    ).astype(jnp.float32)
    d_first = jnp.einsum("kf,kj->jf", d_pre_two, second_cols, precision=HIGH)
    d_pre_one = jax.vjp(jax.nn.silu, pre_one_own)[1](d_first)[0]
    grad_first = jnp.einsum("fi,jf->ij", features_placed, d_pre_one, precision=HIGH)
    ff_cols = mlp_weights.shape[2]
    sum_rest = sum_rest.astype(jnp.float32)
    sum_mlp = jnp.stack([sum_rest[:, :ff_cols], sum_rest[:, ff_cols : 2 * ff_cols]])
    sum_attn = jnp.stack(
        [sum_qkv[0], sum_qkv[1], sum_qkv[2]]
        + [sum_rest[:, 2 * ff_cols : 2 * ff_cols + width_local]]
    )
    head_first = 2 * ff_cols + width_local
    head_part = sum_rest[:, head_first + P_SIZE : head_first + 2 * P_SIZE]
    sum_head = head_part + lax.ppermute(head_part, "mp", [(0, 1), (1, 0)])
    sum_ends = half_of(jnp.concatenate([sum_in[:, :P_SIZE], sum_head], axis=1).T, 1)
    sum_small = jnp.concatenate([grad_first, grad_second, sum_ends], axis=0)
    learning_rate = 0.5 * math.sqrt(tokens_total * P_SIZE / D)
    attn_new, attn_moment_new, attn_average_new, attn_copy = update(
        attn_weights, sum_attn, attn_moment, attn_average, learning_rate
    )
    mlp_new, mlp_moment_new, mlp_average_new, mlp_copy = update(
        mlp_weights, sum_mlp, mlp_moment, mlp_average, learning_rate
    )
    mod_new, mod_moment_new, mod_average_new, mod_copy = update(
        mod_weight, sum_mod, mod_moment, mod_average, learning_rate
    )
    small_new, small_moment_new, small_average_new, small_copy = update(
        small_weights, sum_small, small_moment, small_average, learning_rate
    )
    return (
        loss_sum,
        noised_count,
        attn_new,
        attn_moment_new,
        attn_average_new,
        attn_copy,
        mlp_new,
        mlp_moment_new,
        mlp_average_new,
        mlp_copy,
        mod_new,
        mod_moment_new,
        mod_average_new,
        mod_copy,
        small_new,
        small_moment_new,
        small_average_new,
        small_copy,
    )


def solution(mesh):
    return jax.shard_map(
        per_device,
        mesh=mesh,
        in_specs=(
            P("frames", None),
            P("frames", None),
            P("frames"),
            P(),
            P(),
            P(None, "frames", "mp"),
            P(None, "frames", "mp"),
            P("frames", "mp"),
            P(None, ("frames", "mp")),
            P(None, "frames", "mp"),
            P(None, "frames", "mp"),
            P("frames", "mp"),
            P(None, ("frames", "mp")),
            P(None, "frames", "mp"),
            P(None, "frames", "mp"),
            P("frames", "mp"),
            P(None, ("frames", "mp")),
        ),
        out_specs=(
            P(),
            P(),
            P(None, "frames", "mp"),
            P(None, "frames", "mp"),
            P(None, "frames", "mp"),
            P(None, "frames", "mp"),
            P(None, "frames", "mp"),
            P(None, "frames", "mp"),
            P(None, "frames", "mp"),
            P(None, "frames", "mp"),
            P("frames", "mp"),
            P("frames", "mp"),
            P("frames", "mp"),
            P("frames", "mp"),
            P(None, ("frames", "mp")),
            P(None, ("frames", "mp")),
            P(None, ("frames", "mp")),
            P(None, ("frames", "mp")),
        ),
        check_vma=False,
    )
```

```python
import functools
import math

import jax
import jax.numpy as jnp
import numpy as np
from jax import lax
from jax.experimental import pallas as pl
from jax.experimental.pallas import tpu as pltpu
from jax.sharding import PartitionSpec as P

D = 1024
HD = 64
CH = 4
FREQ = 256
GRID = 16
P_SIZE = 16
TPF = 64
REACH = 4


HIGH = lax.Precision.HIGHEST
EPSILON = 1e-06
MOMENTUM = 0.5
EMA_DECAY = 0.5
TP_AXIS = "mp"


def rotation_matrix(head_width):
    groups = [head_width // 4, 3 * head_width // 8, 3 * head_width // 8]
    rotation = np.zeros((head_width, head_width), np.float32)
    offset = 0
    for group_size in groups:
        half_size = group_size // 2
        for pair_index in range(half_size):
            rotation[offset + half_size + pair_index, offset + pair_index] = -1.0
            rotation[offset + pair_index, offset + half_size + pair_index] = 1.0
        offset += group_size
    return rotation


def turn_phases(positions, group_size):
    half_size = group_size // 2
    frequency = 10000.0 ** (-np.arange(half_size, dtype=np.float32) / half_size)
    phases = positions[:, None] * frequency.astype(np.float32)[None, :]
    return [phases, phases]


def turn_table(frame_ref, patch_ref, first, count):
    lanes = lax.broadcasted_iota(jnp.int32, (1, patch_ref.shape[1]), 1)
    by_frame = lax.rem(lanes, HD) < HD // 4
    rows = [
        jnp.where(by_frame, frame_ref[pl.ds(first + k, 1), :], patch_ref[...])
        for k in range(count)
    ]
    return jnp.concatenate(rows, axis=0)


def clip_positions(clip_ids):
    frame_index = jnp.arange(clip_ids.shape[0], dtype=jnp.int32)
    starts_here = jnp.concatenate([jnp.ones((1,), bool), clip_ids[1:] != clip_ids[:-1]])
    clip_start = lax.cummax(jnp.where(starts_here, frame_index, 0), axis=0)
    return frame_index - clip_start


def patchify(frame_data):
    frame_total = frame_data.shape[0]
    patch_side = GRID // 2
    shaped = frame_data.reshape(frame_total, CH, patch_side, 2, patch_side, 2)
    return shaped.transpose(0, 2, 4, 1, 3, 5).reshape(frame_total * patch_side * patch_side, CH * 4)


def layer_norm(vector):
    row_mean = jnp.mean(vector, axis=-1, keepdims=True)
    centred = vector - row_mean
    variance = jnp.mean(centred * centred, axis=-1, keepdims=True)
    return centred * lax.rsqrt(variance + EPSILON)


def modulate_local(shaped, shift_rows, scale_rows):
    return layer_norm(shaped) * (1.0 + scale_rows) + shift_rows


def time_features(level_eff):
    half_size = FREQ // 2
    frequency = jnp.exp(-math.log(10000.0) * jnp.arange(half_size, dtype=jnp.float32) / half_size)
    phases = (level_eff * 1000.0)[:, None] * frequency[None, :]
    return jnp.concatenate([jnp.cos(phases), jnp.sin(phases)], axis=1)


NT=(((1,),(1,)),((),()))
NN=(((1,),(0,)),((),()))

def dotf(a,b,dims=NN):
    return lax.dot_general(a,b,dims,preferred_element_type=jnp.float32)

def split_pair(xT):
    r=lax.broadcasted_iota(jnp.int32,xT.shape,0)
    z=jnp.zeros_like(xT)
    return jnp.where(r<HD,xT,z), jnp.where(r<HD,z,xT)

def keep_of(t,TK,TQ,cs,qf):
    kf=lax.broadcasted_iota(jnp.int32,(TK,TQ),0)//TPF+t*(TK//TPF)
    return (kf>=cs)&(kf<=qf)

def fwd_kernel(lo_ref,mid_ref,hi_ref,q_ref,k_ref,v_ref,cs_ref,o_ref,ol_ref,lse_ref,vT,*,TQ,TK,W0,NQ):
    KS=k_ref.shape[0]
    def tr(i,_):
        s=pl.multiple_of(i*TK,TK)
        vT[:,pl.ds(s,TK)]=v_ref[pl.ds(s,TK),:].T
        return 0
    lax.fori_loop(lo_ref[0],KS//TK,tr,0)
    def qtile(j,_):
        qs=pl.multiple_of(j*TQ,TQ)
        qT=(q_ref[pl.ds(qs,TQ),:].T)*jnp.bfloat16(0.125)
        qA,qB=split_pair(qT)
        cs=cs_ref[0:1,pl.ds(qs,TQ)]
        qf=lax.broadcasted_iota(jnp.int32,(1,TQ),1)//TPF+(W0+j*(TQ//TPF))
        def step(t,carry,masked):
            ks=pl.multiple_of(t*TK,TK)
            kt=k_ref[pl.ds(ks,TK),:]
            out=[]
            if masked: keep=keep_of(t,TK,TQ,cs,qf)
            ones=jnp.ones((16,TK),jnp.bfloat16)
            both=[dotf(kt,qh) for qh in (qA,qB)]
            for h,(s,(m,l,o)) in enumerate(zip(both,carry)):
                if masked: s=jnp.where(keep,s,-1e30)
                mn=jnp.maximum(m,jnp.max(s,axis=0,keepdims=True))
                a=jnp.exp(m-mn)
                p=jnp.exp(s-mn)
                vh=jnp.concatenate([vT[h*HD:(h+1)*HD,pl.ds(ks,TK)],ones],axis=0)
                ov=dotf(vh,p.astype(jnp.bfloat16))
                l=l*a+ov[HD:HD+1]
                o=o*a+ov[:HD]
                out.append((mn,l,o))
            return tuple(out)
        init=tuple((jnp.full((1,TQ),-1e29,jnp.float32),jnp.zeros((1,TQ),jnp.float32),jnp.zeros((HD,TQ),jnp.float32)) for _ in range(2))
        c=lax.fori_loop(lo_ref[j],mid_ref[j],lambda t,c:step(t,c,True),init)
        c=lax.fori_loop(mid_ref[j],hi_ref[j],lambda t,c:step(t,c,False),c)
        c=lax.fori_loop(hi_ref[j],(W0*TPF+(j+1)*TQ+TK-1)//TK,lambda t,c:step(t,c,True),c)
        oT=jnp.concatenate([c[0][2]/c[0][1],c[1][2]/c[1][1]],axis=0)
        o_nat=oT.T
        o_ref[pl.ds(qs,TQ),:]=o_nat
        ol_ref[pl.ds(qs,TQ),:]=o_nat.astype(jnp.bfloat16)
        lse_ref[0,0:1,pl.ds(qs,TQ)]=c[0][0]+jnp.log(c[0][1])
        lse_ref[0,1:2,pl.ds(qs,TQ)]=c[1][0]+jnp.log(c[1][1])
        return 0
    lax.fori_loop(0,NQ,qtile,0)

def tile_bounds(cs_rel,TQ,TK,W0,NQ):
    fq=TQ//TPF; fk=TK//TPF
    j=jnp.arange(NQ)
    first=cs_rel[::fq]; last=cs_rel[fq-1::fq]
    lo=first//fk
    dg=(W0+j*fq+1)//fk
    mid=jnp.minimum((last+fk-1)//fk,dg)
    mid=jnp.maximum(mid,lo)
    hi=jnp.maximum(dg,mid)
    return lo.astype(jnp.int32),mid.astype(jnp.int32),hi.astype(jnp.int32)

def attn_fwd(q,k,v,cs_rel,TQ=512,TK=512):
    T,Wd=q.shape; KS=k.shape[0]; P=Wd//128
    W0=(KS-T)//TPF; NQ=T//TQ
    lo,mid,hi=tile_bounds(cs_rel,TQ,TK,W0,NQ)
    cs_tok=jnp.broadcast_to(jnp.repeat(cs_rel,TPF)[None,:],(8,T)).astype(jnp.int32)
    return pl.pallas_call(
        functools.partial(fwd_kernel,TQ=TQ,TK=TK,W0=W0,NQ=NQ),
        grid_spec=pltpu.PrefetchScalarGridSpec(num_scalar_prefetch=3,grid=(P,),
            in_specs=[pl.BlockSpec((T,128),lambda p,*_:(0,p)),pl.BlockSpec((KS,128),lambda p,*_:(0,p)),pl.BlockSpec((KS,128),lambda p,*_:(0,p)),pl.BlockSpec((8,T),lambda p,*_:(0,0))],
            out_specs=[pl.BlockSpec((T,128),lambda p,*_:(0,p)),pl.BlockSpec((T,128),lambda p,*_:(0,p)),pl.BlockSpec((1,8,T),lambda p,*_:(p,0,0))],
            scratch_shapes=[pltpu.VMEM((128,KS),jnp.bfloat16)]),
        out_shape=[jax.ShapeDtypeStruct((T,Wd),jnp.float32),jax.ShapeDtypeStruct((T,Wd),jnp.bfloat16),jax.ShapeDtypeStruct((P,8,T),jnp.float32)],
        compiler_params=pltpu.CompilerParams(vmem_limit_bytes=48<<20),
        cost_estimate=pl.CostEstimate(flops=10**11,bytes_accessed=2*10**7,transcendentals=3*10**7),
        name="attn_forward",
    )(lo,mid,hi,q,k,v,cs_tok)

def bwd_kernel(lo_ref,mid_ref,hi_ref,q_ref,k_ref,v_ref,do_ref,o_ref,lse_ref,cs_ref,dq_ref,dk_ref,dv_ref,kT,dkT,dvT,*,TQ,TK,W0,NQ):
    KS=k_ref.shape[0]
    def tr(i,_):
        s=pl.multiple_of(i*TK,TK)
        kT[:,pl.ds(s,TK)]=k_ref[pl.ds(s,TK),:].T
        return 0
    lax.fori_loop(lo_ref[0],KS//TK,tr,0)
    dkT[...]=jnp.zeros_like(dkT); dvT[...]=jnp.zeros_like(dvT)
    def qtile(j,_):
        qs=pl.multiple_of(j*TQ,TQ)
        qT=(q_ref[pl.ds(qs,TQ),:].T)*jnp.bfloat16(0.125)
        qh=split_pair(qT)
        doT=do_ref[pl.ds(qs,TQ),:].T
        doh=split_pair(doT)
        oT=o_ref[pl.ds(qs,TQ),:].T
        prod=oT*doT.astype(jnp.float32)
        delta=(jnp.sum(prod[:HD],axis=0,keepdims=True),jnp.sum(prod[HD:],axis=0,keepdims=True))
        lse=(lse_ref[0,0:1,pl.ds(qs,TQ)],lse_ref[0,1:2,pl.ds(qs,TQ)])
        cs=cs_ref[0:1,pl.ds(qs,TQ)]
        qf=lax.broadcasted_iota(jnp.int32,(1,TQ),1)//TPF+(W0+j*(TQ//TPF))
        def step(t,carry,masked):
            ks=pl.multiple_of(t*TK,TK)
            kt=k_ref[pl.ds(ks,TK),:]; vt=v_ref[pl.ds(ks,TK),:]
            out=[]
            if masked: keep=keep_of(t,TK,TQ,cs,qf)
            for h in range(2):
                r=slice(h*HD,(h+1)*HD)
                s=dotf(kt,qh[h])
                p=jnp.exp(s-lse[h])
                if masked: p=jnp.where(keep,p,0.0)
                dp=dotf(vt,doh[h])
                ds=(p*(dp-delta[h])).astype(jnp.bfloat16)
                pb=p.astype(jnp.bfloat16)
                dvT[r,pl.ds(ks,TK)]+=dotf(doT[r],pb,NT)
                dkT[r,pl.ds(ks,TK)]+=dotf(qT[r],ds,NT)
                out.append(carry[h]+dotf(kT[r,pl.ds(ks,TK)],ds))
            return tuple(out)
        init=(jnp.zeros((HD,TQ),jnp.float32),)*2
        c=lax.fori_loop(lo_ref[j],mid_ref[j],lambda t,c:step(t,c,True),init)
        c=lax.fori_loop(mid_ref[j],hi_ref[j],lambda t,c:step(t,c,False),c)
        c=lax.fori_loop(hi_ref[j],(W0*TPF+(j+1)*TQ+TK-1)//TK,lambda t,c:step(t,c,True),c)
        dq_ref[pl.ds(qs,TQ),:]=(jnp.concatenate(c,axis=0)*0.125).T
        return 0
    lax.fori_loop(0,NQ,qtile,0)
    def back(i,_):
        s=pl.multiple_of(i*TK,TK)
        dk_ref[pl.ds(s,TK),:]=dkT[:,pl.ds(s,TK)].T.astype(dk_ref.dtype)
        dv_ref[pl.ds(s,TK),:]=dvT[:,pl.ds(s,TK)].T.astype(dv_ref.dtype)
        return 0
    lax.fori_loop(0,KS//TK,back,0)

def attn_bwd(q,k,v,do,o,lse,cs_rel,TQ=512,TK=512,out_dt=jnp.bfloat16):
    T,Wd=q.shape; KS=k.shape[0]; P=Wd//128
    W0=(KS-T)//TPF; NQ=T//TQ
    lo,mid,hi=tile_bounds(cs_rel,TQ,TK,W0,NQ)
    cs_tok=jnp.broadcast_to(jnp.repeat(cs_rel,TPF)[None,:],(8,T)).astype(jnp.int32)
    tb=pl.BlockSpec((T,128),lambda p,*_:(0,p)); kb=pl.BlockSpec((KS,128),lambda p,*_:(0,p))
    return pl.pallas_call(
        functools.partial(bwd_kernel,TQ=TQ,TK=TK,W0=W0,NQ=NQ),
        grid_spec=pltpu.PrefetchScalarGridSpec(num_scalar_prefetch=3,grid=(P,),
            in_specs=[tb,kb,kb,tb,tb,pl.BlockSpec((1,8,T),lambda p,*_:(p,0,0)),pl.BlockSpec((8,T),lambda p,*_:(0,0))],
            out_specs=[tb,kb,kb],
            scratch_shapes=[pltpu.VMEM((128,KS),jnp.bfloat16),pltpu.VMEM((128,KS),jnp.float32),pltpu.VMEM((128,KS),jnp.float32)]),
        out_shape=[jax.ShapeDtypeStruct((T,Wd),jnp.float32),jax.ShapeDtypeStruct((KS,Wd),out_dt),jax.ShapeDtypeStruct((KS,Wd),out_dt)],
        compiler_params=pltpu.CompilerParams(vmem_limit_bytes=56<<20),
        cost_estimate=pl.CostEstimate(flops=2*10**11,bytes_accessed=5*10**7,transcendentals=3*10**7),
        name="attn_backward",
    )(lo,mid,hi,q,k,v,do,o,lse,cs_tok)


def update(weight, gradient, moment, average, learning_rate):
    moment_new = MOMENTUM * moment + gradient
    weight_new = weight - learning_rate * (gradient + MOMENTUM * moment_new)
    average_new = EMA_DECAY * average + (1.0 - EMA_DECAY) * weight_new
    return (weight_new, moment_new, average_new, weight_new.astype(jnp.bfloat16))


TN = (((0,), (0,)), ((), ()))


def norm_rows(v):
    centred = v - jnp.mean(v, axis=-1, keepdims=True)
    inverse = lax.rsqrt(jnp.mean(centred * centred, axis=-1, keepdims=True) + EPSILON)
    return centred * inverse, inverse


def norm_rows_back(grad, normed, inverse):
    return inverse * (
        grad
        - jnp.mean(grad, axis=-1, keepdims=True)
        - normed * jnp.mean(grad * normed, axis=-1, keepdims=True)
    )


def gelu_pair(x):
    c = math.sqrt(2.0 / math.pi)
    sq = x * x
    t = jnp.tanh(c * (x + 0.044715 * (x * sq)))
    half = 0.5 * (1.0 + t)
    return x * half, half + (0.5 * c) * x * (1.0 - t * t) * (1.0 + 0.134145 * sq)


def mid_kernel(
    o_hbm, hid_ref, mod_ref, noise_ref, tw_ref, head_ref, gs_ref, wu_hbm, wd_hbm, wa_hbm, wox_hbm,
    dmix_hbm, dx1_ref, dmod_ref, loss_ref, rest_hbm,
    o_ref, dmix_ref, wo_ref, wox_ref, wu_ref, wd_ref, att, x1, out, dx2, n2, n2t, act, dgl, dout, doutt, datt, datt_t,
    recv_o, send_f, send_c, recv_c, send_e, recv_e, stage, ghead_ref, go_ref, gh_t,
    wsem, gsem, ssem, rsem, o_sem, m_sem, s_m, r_m, *, tp,
):
    f = lax.axis_index("frames")
    h = lax.axis_index("mp")
    bf16 = jnp.bfloat16
    x_peer = {"mp": 1 - h}
    tp_peer = x_peer
    core = lax.rem(f, 2)
    core_peer = {"frames": f + 1 - 2 * core}
    half = hid_ref.shape[0]
    rows = 128
    chunks = half // rows
    width = hid_ref.shape[1]
    ff = wu_hbm.shape[1]
    e = o_ref.shape[1]
    ft = 512
    dt = 256

    weights = [
        pltpu.make_async_copy(wu_hbm, wu_ref, wsem.at[0]),
        pltpu.make_async_copy(wd_hbm, wd_ref, wsem.at[1]),
    ]
    load_out = pltpu.make_async_copy(wa_hbm.at[3], wo_ref, wsem.at[2])
    load_far = pltpu.make_async_copy(wox_hbm, wox_ref, wsem.at[3])
    load_out.start()
    load_far.start()
    for w in weights:
        w.start()

    barrier = pltpu.get_barrier_semaphore()
    for peer in (x_peer, core_peer):
        pl.semaphore_signal(barrier, inc=1, device_id=peer, device_id_type=pl.DeviceIdType.MESH)
    pl.semaphore_wait(barrier, 2)
    tok_all = o_ref.shape[0]
    eh = e // 2

    def at(start, size):
        return pl.ds(pl.multiple_of(start, size), size)

    def frame_at(c, k):
        return pl.ds(h * (half // TPF) + c * (rows // TPF) + k, 1)

    def mod_row(i, c, k):
        return mod_ref[frame_at(c, k), (2 + i) * width : (3 + i) * width]

    def copy(src, dst, phase, c, peer):
        return pltpu.make_async_remote_copy(
            src_ref=src, dst_ref=dst, send_sem=ssem.at[phase, c], recv_sem=rsem.at[phase, c],
            device_id=peer, device_id_type=pl.DeviceIdType.MESH,
        )

    def copy_a(c):
        theirs = o_ref.at[at((1 - h) * half + c * rows, rows)]
        return copy(theirs, recv_o.at[at(c * rows, rows)], 0, c, x_peer)

    def copy_b(c):
        return copy(
            n2.at[at(c * 2 * rows, rows)], n2.at[at(c * 2 * rows + rows, rows)], 1, c, tp_peer
        )

    def copy_c(c):
        return copy(send_c.at[at(c * rows, rows)], recv_c.at[at(c * rows, rows)], 2, c, tp_peer)

    def copy_d(c):
        return copy(
            dout.at[at(c * 2 * rows, rows)], dout.at[at(c * 2 * rows + rows, rows)], 3, c, tp_peer
        )

    def copy_e(c):
        return copy(send_e.at[at(c * rows, rows)], recv_e.at[at(c * rows, rows)], 4, c, tp_peer)

    def copy_f(c):
        there = dmix_ref.at[at(h * half + c * rows, rows)]
        return copy(send_f.at[at(c * rows, rows)], there, 5, c, x_peer)

    def lanes(k):
        return pl.ds(pl.multiple_of(k * eh, eh), eh)

    mine_o = pltpu.make_async_copy(
        o_hbm.at[at(core * tok_all, tok_all)], o_ref.at[:, lanes(core)], o_sem.at[0]
    )

    def give_o(k):
        return pltpu.make_async_remote_copy(
            src_ref=o_hbm.at[at((1 - core) * tok_all, tok_all)], dst_ref=o_ref.at[:, lanes(k)],
            send_sem=o_sem.at[1], recv_sem=o_sem.at[2], device_id=core_peer,
            device_id_type=pl.DeviceIdType.MESH,
        )

    give_o(core).start()
    mine_o.start()
    load_out.wait()
    mine_o.wait()
    give_o(1 - core).wait_recv()

    def mix_keep(rows_at, i):
        return pltpu.make_async_copy(
            dmix_ref.at[at(rows_at, rows), lanes(core)],
            dmix_hbm.at[at(core * tok_all + rows_at, rows)],
            m_sem.at[i],
        )

    def mix_give(rows_at, i, k):
        return pltpu.make_async_remote_copy(
            src_ref=dmix_ref.at[at(rows_at, rows), lanes(1 - core)],
            dst_ref=dmix_hbm.at[at(k * tok_all + rows_at, rows)],
            send_sem=s_m.at[i], recv_sem=r_m.at[i], device_id=core_peer,
            device_id_type=pl.DeviceIdType.MESH,
        )

    def phase_a(c, _):
        copy_a(c).start()
        return 0

    lax.fori_loop(0, chunks, phase_a, 0)
    load_far.wait()

    def phase_b(c, _):
        part = o_ref[at(h * half + c * rows, rows), :]
        copy_a(c).wait_recv()
        att[at(c * rows, rows), :] = dotf(part, wo_ref[...], NT) + dotf(
            recv_o[at(c * rows, rows), :], wox_ref[...], NT
        )
        for k in range(rows // TPF):
            r = at(c * rows + k * TPF, TPF)
            frame = pl.ds(c * (rows // TPF) + k, 1)
            a = att[r, :]
            v = hid_ref[r, :] + mod_row(0, c, k) * a
            x1[r, :] = v
            y, _inv = norm_rows(v)
            n2[at(c * 2 * rows + k * TPF, TPF), :] = (
                y * (1.0 + mod_row(2, c, k)) + mod_row(1, c, k)
            ).astype(bf16)
        copy_b(c).start()
        return 0

    lax.fori_loop(0, chunks, phase_b, 0)
    for w in weights:
        w.wait()

    def phase_c(c, _):
        copy_b(c).wait_recv()
        tok = at(c * 2 * rows, 2 * rows)
        n2t[:, tok] = n2[tok, :].T

        def up(i, _):
            cols = at(i * ft, ft)
            a, g = gelu_pair(dotf(n2[tok, :], wu_ref[:, cols]))
            act[tok, cols] = a.astype(bf16)
            dgl[tok, cols] = g.astype(bf16)
            return 0

        lax.fori_loop(0, ff // ft, up, 0)

        def down(i, _):
            cols = at(i * dt, dt)
            res = dotf(act[tok, :], wd_ref[cols, :], NT)
            out[at(c * rows, rows), cols] = res[:rows]
            send_c[at(c * rows, rows), cols] = res[rows:].astype(bf16)
            return 0

        lax.fori_loop(0, width // dt, down, 0)
        copy_c(c).start()
        return 0

    lax.fori_loop(0, chunks, phase_c, 0)

    ghead_ref[...] = jnp.zeros_like(ghead_ref)
    loss_ref[...] = jnp.zeros_like(loss_ref)

    def phase_d(c, _):
        copy_c(c).wait_recv()
        for k in range(rows // TPF):
            r = at(c * rows + k * TPF, TPF)
            frame = pl.ds(c * (rows // TPF) + k, 1)
            o = out[r, :] + recv_c[r, :].astype(jnp.float32)
            gate = mod_row(3, c, k)
            y, inv = norm_rows(x1[r, :] + gate * o)
            fn = y.astype(bf16)
            misfit = dotf(fn, head_ref[...], NT) - noise_ref[at(h * half + c * rows + k * TPF, TPF), :]
            weighted = tw_ref[frame_at(c, k), :] * misfit
            loss_ref[...] += weighted * misfit
            d_pred = (2.0 * gs_ref[0] * weighted).astype(bf16)
            ghead_ref[...] += dotf(d_pred, fn, TN)
            d_x2 = norm_rows_back(dotf(d_pred, head_ref[...]), y, inv)
            dx2[r, :] = d_x2
            dmod_ref[3, frame, :] = jnp.sum(d_x2 * o, axis=0, keepdims=True)
            dout[at(c * 2 * rows + k * TPF, TPF), :] = (gate * d_x2).astype(bf16)
        copy_d(c).start()
        return 0

    lax.fori_loop(0, chunks, phase_d, 0)

    def phase_e(c, _):
        copy_d(c).wait_recv()
        tok = at(c * 2 * rows, 2 * rows)
        doutt[:, tok] = dout[tok, :].T

        def down(i, _):
            cols = at(i * ft, ft)
            g = dotf(dout[tok, :], wd_ref[:, cols]) * dgl[tok, cols].astype(jnp.float32)
            dgl[tok, cols] = g.astype(bf16)
            return 0

        lax.fori_loop(0, ff // ft, down, 0)

        def up(i, _):
            cols = at(i * dt, dt)
            res = dotf(dgl[tok, :], wu_ref[cols, :], NT)
            out[at(c * rows, rows), cols] = res[:rows]
            send_e[at(c * rows, rows), cols] = res[rows:].astype(bf16)
            return 0

        lax.fori_loop(0, width // dt, up, 0)
        copy_e(c).start()
        return 0

    lax.fori_loop(0, chunks, phase_e, 0)

    def phase_f(c, _):
        copy_e(c).wait_recv()
        for k in range(rows // TPF):
            r = at(c * rows + k * TPF, TPF)
            frame = pl.ds(c * (rows // TPF) + k, 1)
            g = out[r, :] + recv_e[r, :].astype(jnp.float32)
            y, inv = norm_rows(x1[r, :])
            dmod_ref[1, frame, :] = jnp.sum(g, axis=0, keepdims=True)
            dmod_ref[2, frame, :] = jnp.sum(g * y, axis=0, keepdims=True)
            d_x1 = dx2[r, :] + norm_rows_back(g * (1.0 + mod_row(2, c, k)), y, inv)
            dx1_ref[r, :] = d_x1
            dmod_ref[0, frame, :] = jnp.sum(d_x1 * att[r, :], axis=0, keepdims=True)
            datt[r, :] = (mod_row(0, c, k) * d_x1).astype(
                bf16
            )
        mine = datt[at(c * rows, rows), :]
        send_f[at(c * rows, rows), :] = dotf(mine, wox_ref[...]).astype(bf16)
        copy_f(c).start()
        return 0

    lax.fori_loop(0, chunks, phase_f, 0)

    def weight_grads(left, right, start):
        def put(slot, i):
            return pltpu.make_async_copy(
                stage.at[slot], rest_hbm.at[at(i * dt, dt), pl.ds(start, ff)], gsem.at[slot]
            )

        def tile(i, _):
            slot = lax.rem(i, 2)

            @pl.when(i >= 2)
            def _():
                put(slot, i - 2).wait()

            def cols_of(j, _):
                cols = at(j * ft, ft)
                stage[slot, :, cols] = dotf(left[at(i * dt, dt), :], right[:, cols]).astype(bf16)
                return 0

            lax.fori_loop(0, ff // ft, cols_of, 0)
            put(slot, i).start()
            return 0

        lax.fori_loop(0, width // dt, tile, 0)
        for i in (width // dt - 2, width // dt - 1):
            put(i % 2, i).wait()

    weight_grads(n2t, dgl, 0)
    weight_grads(doutt, act, ff)

    def own_mix(c, _):
        first = h * half + c * rows
        r = at(c * rows, rows)
        datt_t[:, r] = datt[r, :].T
        dmix_ref[at(first, rows), :] = dotf(datt[r, :], wo_ref[...]).astype(bf16)
        mix_keep(first, c).start()
        mix_give(first, c, core).start()
        return 0

    lax.fori_loop(0, chunks, own_mix, 0)

    def phase_g(c, _):
        first = (1 - h) * half + c * rows
        arrived = dmix_ref.at[at(first, rows)]
        copy(send_f.at[at(c * rows, rows)], arrived, 5, c, x_peer).wait_recv()
        mix_keep(first, chunks + c).start()
        mix_give(first, chunks + c, core).start()
        return 0

    lax.fori_loop(0, chunks, phase_g, 0)

    def grad_out(i, _):
        d = at(i * dt, dt)
        go_ref[d, :e] = dotf(datt_t[d, :], o_ref[at(h * half, half), :]).astype(bf16)
        go_ref[d, e:] = dotf(datt_t[d, :], recv_o[...]).astype(bf16)
        return 0

    lax.fori_loop(0, width // dt, grad_out, 0)
    gh_t[...] = ghead_ref[...].T.astype(bf16)
    ends = [
        pltpu.make_async_copy(go_ref, rest_hbm.at[:, pl.ds(2 * ff, 2 * e)], gsem.at[2]),
        pltpu.make_async_copy(gh_t, rest_hbm.at[:, pl.ds(2 * ff + 2 * e, 128)], gsem.at[3]),
    ]
    for one in ends:
        one.start()
    for one in ends:
        one.wait()
    def sent(c, _):
        for one in (copy_a, copy_b, copy_c, copy_d, copy_e, copy_f):
            one(c).wait_send()
        for side in range(2):
            first = (h if side == 0 else 1 - h) * half + c * rows
            i = side * chunks + c
            mix_keep(first, i).wait()
            mix_give(first, i, core).wait_send()
            mix_give(first, i, 1 - core).wait_recv()
        return 0

    lax.fori_loop(0, chunks, sent, 0)
    give_o(core).wait_send()


def mid_block(o, hid, mod, noise, tw, head, gs, wu, wd, wa, wox, tp, cid):
    tok, e = o.shape[0] // 2, 2 * o.shape[1]
    half, width = hid.shape
    ff = wu.shape[1]
    own_frames = half // TPF
    f32, bf16 = jnp.float32, jnp.bfloat16
    vm = pl.BlockSpec(memory_space=pltpu.VMEM)
    anym = pl.BlockSpec(memory_space=pl.ANY)
    V = pltpu.VMEM
    return pl.pallas_call(
        functools.partial(mid_kernel, tp=tp),
        in_specs=[anym] + [vm] * 5 + [pl.BlockSpec(memory_space=pltpu.SMEM)] + [anym] * 4,
        out_specs=[anym] + [vm] * 3 + [anym],
        out_shape=[
            jax.ShapeDtypeStruct((2 * tok, e // 2), bf16),
            jax.ShapeDtypeStruct((half, width), f32),
            jax.ShapeDtypeStruct((4, own_frames, width), f32),
            jax.ShapeDtypeStruct((TPF, 128), f32),
            jax.ShapeDtypeStruct((width, 2 * ff + 2 * e + 128), bf16),
        ],
        scratch_shapes=[
            V((tok, e), bf16), V((tok, e), bf16),
            V((width, e), bf16), V((width, e), bf16), V((width, ff), bf16), V((width, ff), bf16),
            V((half, width), f32), V((half, width), f32), V((half, width), f32),
            V((half, width), f32),
            V((2 * half, width), bf16), V((width, 2 * half), bf16),
            V((2 * half, ff), bf16), V((2 * half, ff), bf16),
            V((2 * half, width), bf16), V((width, 2 * half), bf16),
            V((half, width), bf16), V((width, half), bf16),
            V((half, e), bf16), V((half, e), bf16),
            V((half, width), bf16), V((half, width), bf16),
            V((half, width), bf16), V((half, width), bf16),
            V((2, 256, ff), bf16), V((128, width), f32), V((width, 2 * e), bf16),
            V((width, 128), bf16),
            pltpu.SemaphoreType.DMA((4,)), pltpu.SemaphoreType.DMA((4,)),
            pltpu.SemaphoreType.DMA((6, half // 128)), pltpu.SemaphoreType.DMA((6, half // 128)),
            pltpu.SemaphoreType.DMA((3,)), pltpu.SemaphoreType.DMA((2 * half // 128,)),
            pltpu.SemaphoreType.DMA((2 * half // 128,)), pltpu.SemaphoreType.DMA((2 * half // 128,)),
        ],
        compiler_params=pltpu.CompilerParams(
            vmem_limit_bytes=62 << 20, collective_id=cid, has_side_effects=True
        ),
        cost_estimate=pl.CostEstimate(
            flops=4 * 10**10, bytes_accessed=3 * 10**7, transcendentals=2 * 10**6
        ),
        name="feed_forward",
    )(o, hid, mod, noise, tw, head, gs, wu, wd, wa, wox)


def split_three(v):
    high = v.astype(jnp.bfloat16)
    left = v - high.astype(jnp.float32)
    middle = left.astype(jnp.bfloat16)
    return high, middle, (left - middle.astype(jnp.float32)).astype(jnp.bfloat16)


def turn_back(g, cosine, sine, rot):
    parts = split_three(g * sine)
    return (g * cosine + sum(dotf(p, rot, NT) for p in parts)).astype(jnp.bfloat16)


def tail_kernel(
    dq_ref, n1_ref, w_ref, fcos_ref, fsin_ref, pcos_ref, psin_ref, rot_ref, hid_ref, scale_ref, dx1_ref, inp_ref,
    dk_hbm, dv_hbm,
    gq_ref, gin_ref, dss_ref,
    relayed, own, yrecv, zrecv, give, n1t, dproj, send_x, recv_x, part,
    lsem, s_d, r_d, s_y, r_y, s_z, r_z, s_x, r_x,
):
    f = lax.axis_index("frames")
    h = lax.axis_index("mp")
    n = lax.axis_size("frames")
    core = lax.rem(f, 2)
    odd = lax.rem(lax.div(f, 2), 2)
    core_peer = {"frames": f + 1 - 2 * core}
    y_peer = {"frames": f + 2 - 4 * odd}
    before = {"frames": lax.rem(f - 4 + n, n)}
    after = {"frames": lax.rem(f + 4, n)}
    x_peer = {"mp": 1 - h}
    tok, width = n1_ref.shape
    eh = dq_ref.shape[1]
    half = tok // 2
    rows = 256
    f32, bf16 = jnp.float32, jnp.bfloat16
    MESH = pl.DeviceIdType.MESH
    sides = (dk_hbm, dv_hbm)
    share = width // n

    def at(start, size):
        return pl.ds(pl.multiple_of(start, size), size)

    loads = [
        pltpu.make_async_copy(
            sides[s].at[pl.ds(b * 2 * tok, 2 * tok)], (own, relayed)[j].at[s], lsem.at[s, j]
        )
        for s in range(2)
        for j, b in enumerate((2, 0))
    ]
    for one in loads:
        one.start()

    barrier = pltpu.get_barrier_semaphore()
    for peer in (core_peer, y_peer, x_peer):
        pl.semaphore_signal(barrier, inc=1, device_id=peer, device_id_type=MESH)

    @pl.when(f >= 4)
    def _():
        pl.semaphore_signal(barrier, inc=1, device_id=before, device_id_type=MESH)

    @pl.when(f + 4 < n)
    def _():
        pl.semaphore_signal(barrier, inc=1, device_id=after, device_id_type=MESH)

    pl.semaphore_wait(barrier, 3 + jnp.where(f >= 4, 1, 0) + jnp.where(f + 4 < n, 1, 0))

    def half_at(i2):
        return lax.rem(i2 + 1 - h, 2) * half

    def rows_of(i2, tc):
        return tc * tok + half_at(i2)

    def remote(src, dst, send, recv, peer):
        return pltpu.make_async_remote_copy(
            src_ref=src, dst_ref=dst, send_sem=send, recv_sem=recv, device_id=peer,
            device_id_type=MESH,
        )

    def y_copy(i2, tc, s):
        first = rows_of(i2, tc)
        i = 2 * i2 + tc
        return remote(
            sides[s].at[at(2 * tok + first, half)], yrecv.at[s, at(first, half)],
            s_y.at[s, i], r_y.at[s, i], y_peer,
        )

    def z_copy(i2, tc, s):
        r = at(rows_of(i2, tc), half)
        i = 2 * i2 + tc
        return remote(relayed.at[s, r], zrecv.at[s, r], s_z.at[s, i], r_z.at[s, i], before)

    def d_copy(k, i2, tc):
        r = at(half_at(i2), half)
        return remote(
            give.at[k, r], dproj.at[k, r, pl.ds(tc * eh, eh)], s_d.at[k, i2], r_d.at[k, i2],
            core_peer,
        )

    def x_copy(i):
        r = at(i * rows, rows)
        return remote(send_x.at[r], recv_x.at[r], s_x.at[i], r_x.at[i], x_peer)

    for one in loads:
        one.wait()

    def start_far(i2, _):
        for tc in range(2):
            for s in range(2):
                y_copy(i2, tc, s).start()

                @pl.when((odd == 0) & (f >= 4))
                def _():
                    z_copy(i2, tc, s).start()

        return 0

    lax.fori_loop(0, 2, start_far, 0)

    @pl.when(f + 4 >= n)
    def _():
        zrecv[...] = jnp.zeros_like(zrecv)

    def settle(k, i2, tc, value):
        r = at(half_at(i2), half)

        @pl.when(core == tc)
        def _():
            dproj[k, r, tc * eh : (tc + 1) * eh] = value

        @pl.when(core != tc)
        def _():
            give[k, r, :] = value
            d_copy(k, i2, 1 - tc).start()

    def arrived(k, i2):
        for tc in range(2):

            @pl.when(core == tc)
            def _():
                d_copy(k, i2, 1 - tc).wait_recv()

    def turned(g, i2, tc):
        first = tc * (tok // TPF) + lax.div(half_at(i2), TPF)
        cosine = turn_table(fcos_ref, pcos_ref, first, half // TPF)
        sine = turn_table(fsin_ref, psin_ref, first, half // TPF)
        return turn_back(g, cosine, sine, rot_ref[...])

    def relay(i2, _):
        for tc in range(2):
            r = at(rows_of(i2, tc), half)
            settle(0, i2, tc, turned(dq_ref[r, :], i2, tc))

            @pl.when(odd == 1)
            def _():
                for s in range(2):
                    y_copy(i2, tc, s).wait_recv()

                    @pl.when(f >= 4)
                    def _():
                        relayed[s, r, :] = (
                            relayed[s, r, :].astype(f32) + yrecv[s, r, :].astype(f32)
                        ).astype(bf16)
                        z_copy(i2, tc, s).start()

        for b in range(2):
            r = at(half_at(i2) + b * rows, rows)
            n1t[:, r] = n1_ref[r, :].T
        return 0

    lax.fori_loop(0, 2, relay, 0)
    for i2 in range(2):
        arrived(0, i2)

    def grads(k):
        def tile(i, _):
            res = dotf(n1t[at(i * 256, 256), :], dproj[k]).astype(bf16)
            for q in range(256 // share):
                j = i * (256 // share // 4) + q // 4
                gq_ref[q % 2, (q // 2) % 2, k, at(j * share, share), :] = res[
                    q * share : (q + 1) * share
                ]
            return 0

        lax.fori_loop(0, width // 256, tile, 0)

    grads(0)

    def finish(i2, _):
        for tc in range(2):
            r = at(rows_of(i2, tc), half)
            for s in range(2):

                @pl.when(odd == 0)
                def _():
                    y_copy(i2, tc, s).wait_recv()

                @pl.when(f + 4 < n)
                def _():
                    z_copy(i2, tc, s).wait_recv()

                total = (
                    own[s, r, :].astype(f32)
                    + jnp.where(odd == 0, yrecv[s, r, :].astype(f32), 0.0)
                    + zrecv[s, r, :].astype(f32)
                )
                if s == 0:
                    settle(1, i2, tc, turned(total, i2, tc))
                else:
                    settle(2, i2, tc, total.astype(bf16))

        arrived(1, i2)
        arrived(2, i2)

        def block_of(q, _):
            b = lax.div(q, width // 256)
            cols = at(lax.rem(q, width // 256) * 256, 256)
            r = at(half_at(i2) + b * rows, rows)
            res = sum(dotf(dproj[k, r, :], w_ref[k, cols, :], NT) for k in range(3))

            @pl.when(i2 == 0)
            def _():
                send_x[at(b * rows, rows), cols] = res.astype(bf16)

            @pl.when((i2 == 0) & (lax.rem(q, width // 256) == width // 256 - 1))
            def _():
                x_copy(b).start()

            @pl.when(i2 == 1)
            def _():
                part[at(b * rows, rows), cols] = res

            return 0

        lax.fori_loop(0, half // rows * (width // 256), block_of, 0)
        return 0

    lax.fori_loop(0, 2, finish, 0)
    grads(1)
    grads(2)
    gin_ref[...] = jnp.zeros_like(gin_ref)

    def norm_back(i, _):
        x_copy(i).wait_recv()
        for k in range(rows // TPF):
            r = at(i * rows + k * TPF, TPF)
            frame = pl.ds(i * (rows // TPF) + k, 1)
            first = h * (half // TPF) + i * (rows // TPF) + k
            g = part[r, :] + recv_x[r, :].astype(f32)
            y, inv = norm_rows(hid_ref[r, :])
            dss_ref[0, frame, :] = jnp.sum(g, axis=0, keepdims=True)
            dss_ref[1, frame, :] = jnp.sum(g * y, axis=0, keepdims=True)
            d_hid = dx1_ref[r, :] + norm_rows_back(g * (1.0 + scale_ref[pl.ds(first, 1), width : 2 * width]), y, inv)
            gin_ref[...] += dotf(inp_ref[at(first * TPF, TPF), :], d_hid.astype(bf16), TN)
        return 0

    lax.fori_loop(0, half // rows, norm_back, 0)

    def sent(i2, _):
        for tc in range(2):
            for s in range(2):
                y_copy(i2, tc, s).wait_send()

                @pl.when(f >= 4)
                def _():
                    z_copy(i2, tc, s).wait_send()

            @pl.when(core != tc)
            def _():
                for k in range(3):
                    d_copy(k, i2, 1 - tc).wait_send()

        x_copy(i2).wait_send()
        return 0

    lax.fori_loop(0, half // rows, sent, 0)


def tail_block(dq, n1, w, tables, rot, hid, scale, dx1, inp, dk, dv, cid):
    tok, width = n1.shape
    e = 2 * dq.shape[1]
    half = tok // 2
    f32, bf16 = jnp.float32, jnp.bfloat16
    vm = pl.BlockSpec(memory_space=pltpu.VMEM)
    anym = pl.BlockSpec(memory_space=pl.ANY)
    V = pltpu.VMEM
    D_ = pltpu.SemaphoreType.DMA
    return pl.pallas_call(
        tail_kernel,
        in_specs=[vm] * 12 + [anym] * 2,
        out_specs=[vm] * 3,
        out_shape=[
            jax.ShapeDtypeStruct((2, 2, 3, width // 4, e), bf16),
            jax.ShapeDtypeStruct((128, width), f32),
            jax.ShapeDtypeStruct((2, half // TPF, width), f32),
        ],
        scratch_shapes=[
            V((2, tok * 2, e // 2), bf16), V((2, tok * 2, e // 2), bf16),
            V((2, tok * 2, e // 2), bf16), V((2, tok * 2, e // 2), bf16),
            V((3, tok, e // 2), bf16), V((width, tok), bf16), V((3, tok, e), bf16),
            V((half, width), bf16), V((half, width), bf16), V((half, width), f32),
            D_((2, 2)), D_((3, 2)), D_((3, 2)), D_((2, 4)), D_((2, 4)),
            D_((2, 4)), D_((2, 4)), D_((half // 256,)), D_((half // 256,)),
        ],
        compiler_params=pltpu.CompilerParams(
            vmem_limit_bytes=56 << 20, collective_id=cid, has_side_effects=True
        ),
        cost_estimate=pl.CostEstimate(
            flops=10**9, bytes_accessed=10**6, transcendentals=0
        ),
        name="projection_backward",
    )(dq, n1, w, *tables, rot, hid, scale, dx1, inp, dk, dv)


def proj_kernel(
    inp_ref, win_ref, mod_ref, w_ref, fcos_ref, fsin_ref, pcos_ref, psin_ref, rot_ref,
    n1_ref, hid_ref, q_hbm, k_hbm, v_hbm, wox_hbm,
    kv, give, q_keep, wr,
    wsem, lsem, qsem, s_core, r_core, s_y, r_y, s_z, r_z,
):
    f = lax.axis_index("frames")
    h = lax.axis_index("mp")
    n = lax.axis_size("frames")
    core = lax.rem(f, 2)
    odd = lax.rem(lax.div(f, 2), 2)
    core_peer = {"frames": f + 1 - 2 * core}
    y_peer = {"frames": f + 2 - 4 * odd}
    before = {"frames": lax.rem(f - 4 + n, n)}
    after = {"frames": lax.rem(f + 4, n)}
    tok, width = n1_ref.shape
    e = w_ref.shape[2]
    eh = e // 2
    low_core = core == 0
    half = tok // 2
    rows = 256
    chunks = tok // rows
    bf16 = jnp.bfloat16
    MESH = pl.DeviceIdType.MESH
    sides = (k_hbm, v_hbm)
    has_z = f >= 4
    has_next = f + 4 < n
    has_y = has_z | (odd == 1)

    def at(start, size):
        return pl.ds(pl.multiple_of(start, size), size)

    barrier = pltpu.get_barrier_semaphore()
    x_peer = {"mp": 1 - h}
    for peer in (core_peer, y_peer, x_peer):
        pl.semaphore_signal(barrier, inc=1, device_id=peer, device_id_type=MESH)

    @pl.when(has_z)
    def _():
        pl.semaphore_signal(barrier, inc=1, device_id=before, device_id_type=MESH)

    @pl.when(has_next)
    def _():
        pl.semaphore_signal(barrier, inc=1, device_id=after, device_id_type=MESH)

    def embed(i, _):
        for k in range(2):
            r = at(i * 2 * TPF + k * TPF, TPF)
            frame = pl.ds(i * 2 + k, 1)
            v = dotf(inp_ref[r, :], win_ref[...])
            y, _inv = norm_rows(v)
            scale = 1.0 + mod_ref[frame, width : 2 * width]
            n1_ref[r, :] = (y * scale + mod_ref[frame, :width]).astype(bf16)

            @pl.when(lax.div(i * 2 * TPF, half) == h)
            def _():
                hid_ref[at(lax.rem(i * 2 * TPF, half) + k * TPF, TPF), :] = v

        return 0

    lax.fori_loop(0, tok // (2 * TPF), embed, 0)

    def turn_weights(i, _):
        d = at(i * 256, 256)
        for k in range(2):
            for b in range(e // 256):
                cols = slice(b * 256, (b + 1) * 256)
                wr[k, d, cols] = dotf(w_ref[k, d, cols], rot_ref[...]).astype(bf16)
        return 0

    lax.fori_loop(0, width // 256, turn_weights, 0)
    pl.semaphore_wait(barrier, 3 + jnp.where(has_z, 1, 0) + jnp.where(has_next, 1, 0))

    def remote(src, dst, send, recv, peer):
        return pltpu.make_async_remote_copy(
            src_ref=src, dst_ref=dst, send_sem=send, recv_sem=recv, device_id=peer,
            device_id_type=MESH,
        )

    out_copy = remote(w_ref.at[3], wox_hbm, wsem.at[0], wsem.at[1], x_peer)
    out_copy.start()

    def block(s, b, i):
        return sides[s].at[at(b * tok + i * rows, rows)]

    def mine(s, tc, i):
        return kv.at[s, tc, at(i * rows, rows)]

    def keep(s, tc, i):
        return pltpu.make_async_copy(mine(s, tc, i), block(s, 4 + tc, i), lsem.at[s, tc, i])

    def z_copy(s, tc, i):
        return remote(
            mine(s, tc, i), block(s, tc, i), s_z.at[s, tc, i], r_z.at[s, tc, i], after
        )

    def y_copy(s, tc, i, src):
        return remote(src, block(s, 2 + tc, i), s_y.at[s, tc, i], r_y.at[s, tc, i], y_peer)

    def core_copy(s, i, tc):
        return remote(
            give.at[s, at(i * rows, rows)], mine(s, tc, i), s_core.at[s, i], r_core.at[s, i],
            core_peer,
        )

    def q_rows(tc, i):
        return q_hbm.at[at(tc * tok + i * rows, rows)]

    def q_own(i):
        return pltpu.make_async_copy(
            q_keep.at[at(i * rows, rows)], q_rows(core, i), qsem.at[i]
        )

    def q_copy(i, tc):
        return remote(
            give.at[2, at(i * rows, rows)], q_rows(tc, i), s_core.at[2, i], r_core.at[2, i],
            core_peer,
        )

    def onward(s, tc, i):
        keep(s, tc, i).start()

        @pl.when(has_next)
        def _():
            z_copy(s, tc, i).start()

        @pl.when(odd == 0)
        def _():
            y_copy(s, tc, i, mine(s, tc, i)).start()

    def rotated(r, i, k):
        frames = rows // TPF
        first = core * (tok // TPF) + i * frames
        cosine = turn_table(fcos_ref, pcos_ref, first, frames)
        sine = turn_table(fsin_ref, psin_ref, first, frames)
        parts = []
        for b in range(e // 256):
            cols = slice(b * 256, (b + 1) * 256)
            plain = dotf(n1_ref[r, :], w_ref[k, :, cols])
            turned = dotf(n1_ref[r, :], wr[k, :, cols])
            parts.append((plain * cosine + turned * sine).astype(bf16))
        return parts

    def own_chunk(i, _):
        r = at(i * rows, rows)
        keys = rotated(r, i, 1)
        values = dotf(n1_ref[r, :], w_ref[2]).astype(bf16)
        for s, pair in enumerate((keys, (values[:, :eh], values[:, eh:]))):
            kv[s, core, r, :] = jnp.where(low_core, pair[0], pair[1])
            give[s, r, :] = jnp.where(low_core, pair[1], pair[0])
            core_copy(s, i, core).start()
            onward(s, core, i)
        return 0

    lax.fori_loop(0, chunks, own_chunk, 0)

    def from_core(i, _):
        for s in range(2):
            core_copy(s, i, 1 - core).wait_recv()
            onward(s, 1 - core, i)
        return 0

    lax.fori_loop(0, chunks, from_core, 0)

    def queries(i, _):
        r = at(i * rows, rows)
        pair = rotated(r, i, 0)
        q_keep[r, :] = jnp.where(low_core, pair[0], pair[1])
        give[2, r, :] = jnp.where(low_core, pair[1], pair[0])
        q_own(i).start()
        q_copy(i, core).start()
        return 0

    lax.fori_loop(0, chunks, queries, 0)

    def from_z(g, _):
        tc = lax.rem(core + lax.div(g, chunks), 2)
        i = lax.rem(g, chunks)

        @pl.when(has_z)
        def _():
            for s in range(2):
                z_copy(s, tc, i).wait_recv()

                @pl.when(odd == 1)
                def _():
                    y_copy(s, tc, i, block(s, tc, i)).start()

        return 0

    lax.fori_loop(0, 2 * chunks, from_z, 0)

    def ended(i, _):
        q_own(i).wait()
        q_copy(i, 1 - core).wait_recv()
        q_copy(i, core).wait_send()
        for s in range(2):
            core_copy(s, i, core).wait_send()
            for tc in range(2):
                keep(s, tc, i).wait()

                @pl.when(has_y)
                def _():
                    y_copy(s, tc, i, mine(s, tc, i)).wait_recv()

                @pl.when(has_next)
                def _():
                    z_copy(s, tc, i).wait_send()

                @pl.when((odd == 0) | has_z)
                def _():
                    y_copy(s, tc, i, mine(s, tc, i)).wait_send()

        return 0

    lax.fori_loop(0, chunks, ended, 0)
    out_copy.wait_send()
    out_copy.wait_recv()


def proj_block(inp, win, mod, w, tables, rot, reach, cid):
    tok = inp.shape[0]
    width, e = w.shape[1:]
    f32, bf16 = jnp.float32, jnp.bfloat16
    vm = pl.BlockSpec(memory_space=pltpu.VMEM)
    anym = pl.BlockSpec(memory_space=pl.ANY)
    V = pltpu.VMEM
    D_ = pltpu.SemaphoreType.DMA
    chunks = tok // 256
    return pl.pallas_call(
        proj_kernel,
        in_specs=[vm] * 9,
        out_specs=[vm] * 2 + [anym] * 4,
        out_shape=[
            jax.ShapeDtypeStruct((tok, width), bf16),
            jax.ShapeDtypeStruct((tok // 2, width), f32),
            jax.ShapeDtypeStruct((2 * tok, e // 2), bf16),
            jax.ShapeDtypeStruct(((reach + 2) * tok, e // 2), bf16),
            jax.ShapeDtypeStruct(((reach + 2) * tok, e // 2), bf16),
            jax.ShapeDtypeStruct((width, e), bf16),
        ],
        scratch_shapes=[
            V((2, 2, tok, e // 2), bf16), V((3, tok, e // 2), bf16), V((tok, e // 2), bf16),
            V((2, width, e), bf16),
            D_((2,)), D_((2, 2, chunks)), D_((chunks,)), D_((3, chunks)), D_((3, chunks)),
            D_((2, 2, chunks)), D_((2, 2, chunks)), D_((2, 2, chunks)), D_((2, 2, chunks)),
        ],
        compiler_params=pltpu.CompilerParams(
            vmem_limit_bytes=48 << 20, collective_id=cid, has_side_effects=True
        ),
        cost_estimate=pl.CostEstimate(
            flops=6 * 10**10, bytes_accessed=3 * 10**7, transcendentals=0
        ),
        name="projection_forward",
    )(inp, win, mod, w, *tables, rot)


def last_kernel(
    g_hbm, gin_ref, dm_ref, cond_ref, wm_ref, loss_ref,
    sq_ref, sin_ref, smod_ref, dct_ref,
    g_own, g_in, near, near_in, side, side_in, far, far_in, ends, ends_peer, dm_peer, dm,
    dc_send, dc_peer,
    lsem, s_x, r_x, s_g, r_g, s_f, r_f, s_d, r_d, s_dz, r_dz,
):
    f = lax.axis_index("frames")
    h = lax.axis_index("mp")
    n = lax.axis_size("frames")
    nj = n // 4
    core = lax.rem(f, 2)
    y = lax.rem(lax.div(f, 2), 2)
    j = lax.div(f, 4)
    core_peer = {"frames": f + 1 - 2 * core}
    y_peer = {"frames": f + 2 - 4 * y}
    x_peer = {"mp": 1 - h}
    f32, bf16 = jnp.float32, jnp.bfloat16
    MESH = pl.DeviceIdType.MESH
    rows = g_hbm.shape[3] // nj

    def z_peer(t):
        return {"frames": lax.rem(f + 4 * t, n)}

    def from_j(t):
        return lax.rem(j - t + nj, nj)

    def at(start, size):
        return pl.ds(pl.multiple_of(start, size), size)

    load = pltpu.make_async_copy(g_hbm.at[core], g_own, lsem.at[0])
    load.start()
    barrier = pltpu.get_barrier_semaphore()
    for peer in [core_peer, y_peer, x_peer] + [z_peer(t) for t in range(1, nj)]:
        pl.semaphore_signal(barrier, inc=1, device_id=peer, device_id_type=MESH)
    pl.semaphore_wait(barrier, 2 + nj)

    def remote(src, dst, send, recv, peer):
        return pltpu.make_async_remote_copy(
            src_ref=src, dst_ref=dst, send_sem=send, recv_sem=recv, device_id=peer,
            device_id_type=MESH,
        )

    dm_x = remote(dm_ref.at[1 - h], dm_peer, s_x.at[0], r_x.at[0], x_peer)
    dm_x.start()
    core_g = remote(g_hbm.at[1 - core], near, s_g.at[0], r_g.at[0], core_peer)
    core_in = remote(gin_ref.at[1 - core], near_in, s_g.at[1], r_g.at[1], core_peer)
    core_g.start()
    core_in.start()

    dm_x.wait_recv()
    mine = dm_ref[h]
    theirs = dm_peer[...]
    low = h == 0
    dm[core, y, j] = jnp.concatenate(
        [jnp.where(low, mine, theirs), jnp.where(low, theirs, mine)], axis=0
    ).astype(bf16)

    def dm_z(t, src):
        block = dm.at[core, y, src]
        return remote(block, block, s_dz.at[0, t], r_dz.at[0, t], z_peer(t))

    for t in range(1, nj):
        dm_z(t, j).start()
    load.wait()
    core_g.wait_recv()
    core_in.wait_recv()

    def add_near(i, _):
        for s in range(2):
            for k in range(g_own.shape[1]):
                r = at(i * rows, rows)
                g_own[s, k, r, :] = (
                    g_own[s, k, r, :].astype(f32) + near[s, k, r, :].astype(f32)
                ).astype(bf16)
        return 0

    lax.fori_loop(0, nj, add_near, 0)
    g_in[...] = (gin_ref[core].astype(f32) + near_in[...].astype(f32)).astype(bf16)
    for t in range(1, nj):
        dm_z(t, from_j(t)).wait_recv()

    def dm_y(side_index):
        block = dm.at[core, side_index]
        return remote(block, block, s_d.at[0], r_d.at[0], y_peer)

    dm_y(y).start()
    y_g = remote(g_own.at[1 - y], side, s_g.at[2], r_g.at[2], y_peer)
    y_in = remote(g_in.at[1 - y], side_in, s_g.at[3], r_g.at[3], y_peer)
    y_g.start()
    y_in.start()
    dm_y(1 - y).wait_recv()

    def dm_core(core_index):
        block = dm.at[core_index]
        return remote(block, block, s_d.at[1], r_d.at[1], core_peer)

    dm_core(core).start()
    y_g.wait_recv()
    y_in.wait_recv()

    def add_side(i, _):
        for k in range(g_own.shape[1]):
            r = at(i * rows, rows)
            side[k, r, :] = (
                g_own[y, k, r, :].astype(f32) + side[k, r, :].astype(f32)
            ).astype(bf16)
        return 0

    lax.fori_loop(0, nj, add_side, 0)
    side_in[...] = (g_in[y].astype(f32) + side_in[...].astype(f32)).astype(bf16)

    def far_g(t):
        there = at(lax.rem(j + t, nj) * rows, rows)
        return remote(
            side.at[:, there], far.at[t - 1], s_f.at[0, t], r_f.at[0, t], z_peer(t)
        )

    def far_i(t):
        there = at(lax.rem(j + t, nj) * rows, rows)
        return remote(
            side_in.at[there], far_in.at[t - 1], s_f.at[1, t], r_f.at[1, t], z_peer(t)
        )

    for t in range(1, nj):
        far_g(t).start()
        far_i(t).start()

    dm_core(1 - core).wait_recv()
    frames = dm.shape[0] * dm.shape[1] * dm.shape[2] * dm.shape[3]
    wide = dm.shape[4]
    every = dm[...].reshape(frames, wide)
    part = dotf(wm_ref[...], every, NT)
    dc_send[:rows, :] = part
    dc_send[rows:, :] = jnp.broadcast_to(jnp.sum(loss_ref[...]), (8, frames))
    dc_x = remote(dc_send, dc_peer, s_x.at[1], r_x.at[1], x_peer)
    dc_x.start()

    def mod_cols(i, _):
        cols = at(i * 512, 512)
        block = dm[:, :, :, :, cols].reshape(frames, 512)
        res = dotf(cond_ref[...], block)
        smod_ref[:, cols] = res[:rows] + res[rows : 2 * rows] + res[2 * rows :]
        return 0

    lax.fori_loop(0, wide // 512, mod_cols, 0)
    dc_x.wait_recv()
    total = dc_send[...] + dc_peer[...]
    dct_ref[core, y, j, :rows, :] = total[:rows].astype(bf16)
    pieces = [p[:1].astype(f32) for p in split_three(total[rows:])]
    dct_ref[core, y, j, rows:, :] = jnp.concatenate(
        pieces + [jnp.zeros((13, frames), f32)], axis=0
    ).astype(bf16)

    def dc_z(t, src):
        block = dct_ref.at[core, y, src]
        return remote(block, block, s_dz.at[1, t], r_dz.at[1, t], z_peer(t))

    for t in range(1, nj):
        dc_z(t, j).start()
    for t in range(1, nj):
        dc_z(t, from_j(t)).wait_recv()

    def dc_y(side_index):
        block = dct_ref.at[core, side_index]
        return remote(block, block, s_d.at[2], r_d.at[2], y_peer)

    dc_y(y).start()

    here = at(j * rows, rows)
    for t in range(1, nj):
        far_g(t).wait_recv()
        far_i(t).wait_recv()
    for k in range(sq_ref.shape[0]):
        sq_ref[k] = side[k, here, :].astype(f32) + sum(
            far[t, k].astype(f32) for t in range(nj - 1)
        )
    ends[...] = side_in[here, :].astype(f32) + sum(
        far_in[t].astype(f32) for t in range(nj - 1)
    )
    ends_x = remote(ends, ends_peer, s_x.at[2], r_x.at[2], x_peer)
    ends_x.start()
    dc_y(1 - y).wait_recv()

    def dc_core(core_index):
        block = dct_ref.at[core_index]
        return remote(block, block, s_d.at[3], r_d.at[3], core_peer)

    dc_core(core).start()
    ends_x.wait_recv()
    sin_ref[...] = ends[...] + ends_peer[...]
    dc_core(1 - core).wait_recv()

    for one in (dm_x, core_g, core_in, y_g, y_in, dc_x, ends_x):
        one.wait_send()
    for one in (dm_y(y), dm_core(core), dc_y(y), dc_core(core)):
        one.wait_send()
    for t in range(1, nj):
        for one in (dm_z(t, j), dc_z(t, j), far_g(t), far_i(t)):
            one.wait_send()


def last_block(g, gin, dm, cond, wm, loss, cid):
    _, _, kinds, block_rows, e = g.shape
    n = lax.axis_size("frames")
    nj = n // 4
    rows = block_rows // nj
    own_frames, wide = dm.shape[1:]
    frames = n * 2 * own_frames
    f32, bf16 = jnp.float32, jnp.bfloat16
    vm = pl.BlockSpec(memory_space=pltpu.VMEM)
    anym = pl.BlockSpec(memory_space=pl.ANY)
    V = pltpu.VMEM
    D_ = pltpu.SemaphoreType.DMA
    return pl.pallas_call(
        last_kernel,
        in_specs=[anym] + [vm] * 5,
        out_specs=[vm] * 4,
        out_shape=[
            jax.ShapeDtypeStruct((kinds, rows, e), f32),
            jax.ShapeDtypeStruct((rows, 128), f32),
            jax.ShapeDtypeStruct((rows, wide), f32),
            jax.ShapeDtypeStruct((2, 2, nj, rows + 16, frames), bf16),
        ],
        scratch_shapes=[
            V((2, kinds, block_rows, e), bf16), V((2, block_rows, 128), bf16),
            V((2, kinds, block_rows, e), bf16), V((2, block_rows, 128), bf16),
            V((kinds, block_rows, e), bf16), V((block_rows, 128), bf16),
            V((nj - 1, kinds, rows, e), bf16), V((nj - 1, rows, 128), bf16),
            V((rows, 128), f32), V((rows, 128), f32),
            V((own_frames, wide), f32), V((2, 2, nj, 2 * own_frames, wide), bf16),
            V((rows + 8, frames), f32), V((rows + 8, frames), f32),
            D_((1,)), D_((3,)), D_((3,)), D_((4,)), D_((4,)), D_((2, nj)), D_((2, nj)),
            D_((4,)), D_((4,)), D_((2, nj)), D_((2, nj)),
        ],
        compiler_params=pltpu.CompilerParams(
            vmem_limit_bytes=48 << 20, collective_id=cid, has_side_effects=True
        ),
        cost_estimate=pl.CostEstimate(
            flops=2 * 10**10, bytes_accessed=2 * 10**7, transcendentals=0
        ),
        name="weight_sums",
    )(g, gin, dm, cond, wm, loss)


def front_kernel(
    small_ref, feat_ref, wm_ref, w_ref,
    st_ref, feats_ref, pre1_ref, pre2_ref, wout_ref, ends_ref, mod_ref,
    wcol, mods,
    s_x, r_x, s_z, r_z, s_y, r_y, s_c, r_c, s_a, r_a, s_m, r_m,
):
    f = lax.axis_index("frames")
    h = lax.axis_index("mp")
    n = lax.axis_size("frames")
    nj = n // 4
    c = lax.rem(f, 2)
    y = lax.rem(lax.div(f, 2), 2)
    j = lax.div(f, 4)
    f32, bf16 = jnp.float32, jnp.bfloat16
    MESH = pl.DeviceIdType.MESH
    x_peer = {"mp": 1 - h}
    core_peer = {"frames": f + 1 - 2 * c}
    y_peer = {"frames": f + 2 - 4 * y}
    offsets = [
        (tj, ty, tc) for tj in range(nj) for ty in range(2) for tc in range(2)
    ][1:]

    def place(tj, ty, tc):
        return (
            lax.rem(j + tj, nj),
            y + ty - 2 * y * ty,
            c + tc - 2 * c * tc,
        )

    def peer_of(spot):
        return {"frames": 4 * spot[0] + 2 * spot[1] + spot[2]}

    def from_j(t):
        return lax.rem(j - t + nj, nj)

    def remote(src, dst, send, recv, peer):
        return pltpu.make_async_remote_copy(
            src_ref=src, dst_ref=dst, send_sem=send, recv_sem=recv, device_id=peer,
            device_id_type=MESH,
        )

    barrier = pltpu.get_barrier_semaphore()
    for o in offsets:
        pl.semaphore_signal(barrier, inc=1, device_id=peer_of(place(*o)), device_id_type=MESH)
    pl.semaphore_signal(barrier, inc=1, device_id=x_peer, device_id_type=MESH)
    pl.semaphore_wait(barrier, n)

    class Gather:
        def __init__(self, block, k):
            self.block, self.k = block, k

        def over_z(self, t, jj):
            b = self.block(jj, y, c)
            return remote(
                b, b, s_z.at[self.k, t], r_z.at[self.k, t], {"frames": lax.rem(f + 4 * t, n)}
            )

        def over_y(self, t, yy):
            b = self.block(from_j(t), yy, c)
            return remote(b, b, s_y.at[self.k, t], r_y.at[self.k, t], y_peer)

        def over_core(self, t, same, yy, cc):
            b = self.block(from_j(t), yy, cc)
            return remote(
                b, b, s_c.at[self.k, same, t], r_c.at[self.k, same, t], core_peer
            )

        def start(self):
            for t in range(1, nj):
                self.over_z(t, j).start()
            self.over_y(0, y).start()
            self.over_core(0, 0, y, c).start()

        def pass_z(self):
            for t in range(1, nj):
                self.over_z(t, from_j(t)).wait_recv()
                self.over_y(t, y).start()
                self.over_core(t, 0, y, c).start()

        def pass_y(self):
            for t in range(nj):
                self.over_y(t, 1 - y).wait_recv()
                self.over_core(t, 1, 1 - y, c).start()

        def finish(self):
            for t in range(nj):
                self.over_core(t, 0, y, 1 - c).wait_recv()
                self.over_core(t, 1, 1 - y, 1 - c).wait_recv()

        def sent(self):
            for t in range(1, nj):
                self.over_z(t, j).wait_send()
            for t in range(nj):
                self.over_y(t, y).wait_send()
                self.over_core(t, 0, y, c).wait_send()
                self.over_core(t, 1, 1 - y, c).wait_send()

    small = Gather(lambda a, b, d: st_ref.at[a, b, d], 0)
    feats = Gather(lambda a, b, d: feats_ref.at[d, b, a], 1)
    weights = Gather(lambda a, b, d: wout_ref.at[:, a, b, d], 2)

    small_x = remote(small_ref, st_ref.at[j, y, c, h], s_x.at[0], r_x.at[0], x_peer)
    small_x.start()
    feats_ref[c, y, j] = feat_ref[...]
    feats.start()

    def column_copy(i, spot, slot):
        return remote(
            wm_ref.at[spot[2], spot[1], spot[0]], wcol.at[slot[0], slot[1], slot[2]],
            s_a.at[i], r_a.at[i], peer_of(spot),
        )

    def source(o):
        return place((nj - o[0]) % nj, o[1], o[2])

    for i, o in enumerate(offsets):
        column_copy(i, place(*o), (j, y, c)).start()
    st_ref[j, y, c, h] = small_ref[...]
    wout_ref[:, j, y, c] = w_ref[...]
    wcol[j, y, c] = wm_ref[c, y, j]
    remote(
        small_ref, st_ref.at[j, y, c, 1 - h], s_x.at[0], r_x.at[0], x_peer
    ).wait_recv()
    small.start()
    feats.pass_z()
    small.pass_z()
    weights.start()
    feats.pass_y()
    small.pass_y()
    feats.finish()
    small.finish()

    total = st_ref.shape[0] * 4
    width = total * 2 * st_ref.shape[4]
    frames = feats_ref.shape[2] * 4 * feats_ref.shape[3]
    inner = feats_ref.shape[4]

    def exact(left, right, dims):
        m = left.shape[0]
        res = dotf(jnp.concatenate(split_three(left), axis=0), right, dims)
        return res[:m] + res[m : 2 * m] + res[2 * m :]

    def silu(v):
        return v * jax.nn.sigmoid(v)

    table = st_ref[...].reshape(width, st_ref.shape[5])
    fv = feats_ref[...].reshape(frames, inner)
    pre1 = exact(fv, table[:, :inner], NT)
    pre1_ref[...] = pre1
    pre2 = exact(silu(pre1), table[:, inner : inner + width], NT)
    pre2_ref[...] = pre2
    ends_ref[...] = table[:, inner + width : inner + width + 128].T
    for i, o in enumerate(offsets):
        column_copy(i, place(*o), source(o)).wait_recv()
    cols = wcol[...].reshape(width, wcol.shape[4])
    mods[...] = exact(silu(pre2), cols, NN).reshape(mods.shape)

    def mods_copy(i, spot, slot):
        return remote(
            mods.at[spot[2], spot[1], spot[0]], mod_ref.at[h, slot[2], slot[1], slot[0]],
            s_m.at[i], r_m.at[i], peer_of(spot),
        )

    for i, o in enumerate(offsets):
        mods_copy(i, place(*o), (j, y, c)).start()
    mod_ref[h, c, y, j] = mods[c, y, j]
    weights.pass_z()
    for i, o in enumerate(offsets):
        mods_copy(i, place(*o), source(o)).wait_recv()
    mods_x = remote(mod_ref.at[h], mod_ref.at[h], s_x.at[1], r_x.at[1], x_peer)
    mods_x.start()
    weights.pass_y()
    weights.finish()
    theirs = mod_ref.at[1 - h]
    remote(theirs, theirs, s_x.at[1], r_x.at[1], x_peer).wait_recv()

    small_x.wait_send()
    mods_x.wait_send()
    for g in (small, feats, weights):
        g.sent()
    for i, o in enumerate(offsets):
        column_copy(i, place(*o), (j, y, c)).wait_send()
        mods_copy(i, place(*o), (j, y, c)).wait_send()


def front_block(small, feat, wm, w, cid):
    n = lax.axis_size("frames")
    nj = n // 4
    cols, lanes = small.shape
    own_frames, inner = feat.shape
    frames = n * own_frames
    kinds, rows, e = w.shape
    wide = wm.shape[-1]
    width = rows * n
    f32, bf16 = jnp.float32, jnp.bfloat16
    vm = pl.BlockSpec(memory_space=pltpu.VMEM)
    V = pltpu.VMEM
    D_ = pltpu.SemaphoreType.DMA
    return pl.pallas_call(
        front_kernel,
        in_specs=[vm] * 4,
        out_specs=[vm] * 7,
        out_shape=[
            jax.ShapeDtypeStruct((nj, 2, 2, 2, cols, lanes), bf16),
            jax.ShapeDtypeStruct((2, 2, nj, own_frames, inner), f32),
            jax.ShapeDtypeStruct((frames, width), f32),
            jax.ShapeDtypeStruct((frames, width), f32),
            jax.ShapeDtypeStruct((kinds, nj, 2, 2, rows, e), bf16),
            jax.ShapeDtypeStruct((128, width), bf16),
            jax.ShapeDtypeStruct((2, 2, 2, nj, own_frames, wide), f32),
        ],
        scratch_shapes=[
            V((nj, 2, 2, rows, wide), bf16), V((2, 2, nj, own_frames, wide), f32),
            D_((2,)), D_((2,)), D_((3, nj)), D_((3, nj)), D_((3, nj)), D_((3, nj)),
            D_((3, 2, nj)), D_((3, 2, nj)), D_((n - 1,)), D_((n - 1,)), D_((n - 1,)),
            D_((n - 1,)),
        ],
        compiler_params=pltpu.CompilerParams(
            vmem_limit_bytes=48 << 20, collective_id=cid, has_side_effects=True
        ),
        cost_estimate=pl.CostEstimate(
            flops=4 * 10**10, bytes_accessed=2 * 10**7, transcendentals=0
        ),
        name="conditioning",
    )(small, feat, wm, w)


def per_device(
    latents,
    noise,
    levels,
    clip_ids,
    clean_flags,
    attn_weights,
    mlp_weights,
    mod_weight,
    small_weights,
    attn_moment,
    mlp_moment,
    mod_moment,
    small_moment,
    attn_average,
    mlp_average,
    mod_average,
    small_average,
):
    frame_count = latents.shape[0]
    tok_count = frame_count * TPF
    patch_side = GRID // 2
    frames_total = clip_ids.shape[0]
    tokens_total = frames_total * TPF
    width_local = attn_weights.shape[2]
    heads_local = width_local // HD
    key_span = (REACH + 1) * tok_count
    device = lax.axis_index("frames")
    mp_index = lax.axis_index("mp")
    first_frame = device * frame_count
    scale_qk = HD ** (-0.5)
    attn_low = attn_weights.astype(jnp.bfloat16)
    mlp_low = mlp_weights.astype(jnp.bfloat16)
    low_mod = mod_weight.astype(jnp.bfloat16)
    noised_all = (1 - clean_flags).astype(jnp.float32)
    noised_count = jnp.sum(noised_all)
    noised = lax.dynamic_slice_in_dim(noised_all, first_frame, frame_count)
    level_eff = levels * noised
    signal_scale = jnp.cos(0.5 * math.pi * level_eff)
    noise_scale = jnp.sin(0.5 * math.pi * level_eff)
    noise_patches = patchify(noise)
    inputs = patchify(signal_scale[:, None] * latents + noise_scale[:, None] * noise)
    in_clip_all = clip_positions(clip_ids)
    chip_frames = 2 * frame_count
    chip_first = (device // 2) * chip_frames
    in_clip = lax.dynamic_slice_in_dim(in_clip_all, chip_first, chip_frames).astype(jnp.float32)
    within = np.arange(TPF)
    patch_zero = np.zeros((TPF, HD // 4), np.float32)
    patch_angles = np.concatenate(
        [patch_zero]
        + turn_phases((within // patch_side).astype(np.float32), 3 * HD // 8)
        + turn_phases((within % patch_side).astype(np.float32), 3 * HD // 8),
        axis=1,
    )
    patch_angles = np.tile(patch_angles, (1, 4))
    frame_angles = jnp.tile(
        jnp.concatenate(
            turn_phases(in_clip, HD // 4) + [jnp.zeros((chip_frames, 3 * HD // 4))], axis=1
        ),
        (1, 4),
    )
    tables = (
        jnp.cos(frame_angles),
        jnp.sin(frame_angles),
        jnp.asarray(np.cos(patch_angles), jnp.float32),
        jnp.asarray(np.sin(patch_angles), jnp.float32),
    )
    turn_four = jnp.asarray(np.kron(np.eye(4, dtype=np.float32), rotation_matrix(HD)), jnp.bfloat16)
    clip_start = (
        lax.dynamic_slice_in_dim(
            jnp.arange(frames_total, dtype=jnp.int32) - in_clip_all, chip_first, chip_frames
        )
        - chip_first
        + REACH * frame_count
    )
    peers = lax.axis_size("frames")
    frame_groups = peers // 4
    small_rows, small_cols = small_weights.shape
    mod_rows, mod_cols = mod_weight.shape
    mod_share = mod_cols // peers
    mod_wide = -(-mod_share // 128) * 128
    small_lanes = FREQ + D + 128
    small_t = jnp.pad(
        small_weights.astype(jnp.bfloat16).T, ((0, 0), (0, small_lanes - small_rows))
    )
    mod_blocks = jnp.pad(
        low_mod.reshape(mod_rows, frame_groups, 2, 2, mod_share).transpose(3, 2, 1, 0, 4),
        ((0, 0),) * 4 + ((0, mod_wide - mod_share),),
    )
    small_full, features_placed, pre_one, pre_two, w_qkv, end_rows, mod_parts = front_block(
        small_t, time_features(level_eff), mod_blocks, attn_low, 4
    )
    w_qkv, up_low = lax.optimization_barrier((w_qkv, mlp_low[0]))
    w_up = lax.all_gather(up_low, "frames", axis=0, tiled=True)
    w_qkv = w_qkv.reshape(4, D, width_local)
    features_placed = features_placed.reshape(frames_total, FREQ)
    first_placed = jax.nn.silu(pre_one)
    pre_two_t = pre_two.T
    first_col = (device * lax.axis_size("mp") + mp_index) * small_cols
    pre_one_own = lax.dynamic_slice_in_dim(pre_one, first_col, small_cols, 1).T
    cond_rows = jax.nn.silu(
        lax.dynamic_slice_in_dim(pre_two, device * mod_rows, mod_rows, 1)
    )
    cond_parts = jnp.concatenate([part.T for part in split_three(cond_rows)], axis=0)
    modulation = (
        mod_parts[..., :mod_share].transpose(4, 0, 3, 2, 1, 5).reshape(frame_count, 6 * D)
    )
    inputs_low = inputs.astype(jnp.bfloat16)
    padding = ((0, 0), (0, 128 - P_SIZE))
    inputs_low = jnp.pad(inputs_low, padding)
    normed_one, hidden_half, queries, keys_wide, values_wide, w_out_far = proj_block(
        inputs_low,
        end_rows,
        modulation,
        w_qkv,
        tables,
        turn_four,
        REACH,
        2,
    )
    down_low = mlp_low[1]
    queries, down_low, w_up = lax.optimization_barrier((queries, down_low, w_up))
    w_down = lax.all_gather(down_low, "frames", axis=0, tiled=True)
    heads_wide, heads_low, log_totals = attn_fwd(queries, keys_wide, values_wide, clip_start)
    half = tok_count // 2
    own_frames = frame_count // 2

    def half_of(array, dim=0):
        size = array.shape[dim] // 2
        return lax.dynamic_slice_in_dim(array, mp_index * size, size, dim)

    grad_scale = 1.0 / jnp.maximum(noised_count, 1.0)
    head_lanes = ((0, 0), (P_SIZE, 128 - 2 * P_SIZE))
    frame_weight = jnp.broadcast_to(noised[:, None] / (TPF * P_SIZE), (frame_count, P_SIZE))
    d_mixed, d_shaped_one, d_mod_mid, loss_parts, grad_rest = mid_block(
        heads_low,
        hidden_half,
        modulation,
        jnp.pad(noise_patches, head_lanes),
        jnp.pad(frame_weight, head_lanes),
        end_rows,
        grad_scale.reshape(1),
        w_up,
        w_down,
        w_qkv,
        w_out_far,
        TP_AXIS,
        0,
    )
    sum_rest = lax.psum_scatter(grad_rest, "frames", scatter_dimension=0, tiled=True)
    d_queries, keys_grad_wide, values_grad_wide = attn_bwd(
        queries, keys_wide, values_wide, d_mixed, heads_wide, log_totals, clip_start
    )
    grad_qkv, grad_in, d_first_mods = tail_block(
        d_queries,
        normed_one,
        w_qkv,
        tables,
        turn_four,
        hidden_half,
        modulation,
        d_shaped_one,
        inputs_low,
        keys_grad_wide,
        values_grad_wide,
        1,
    )
    d_first_mods, sum_rest = lax.optimization_barrier((d_first_mods, sum_rest))
    def by_place(array, dim):
        shape = array.shape
        size = shape[dim] // (4 * frame_groups)
        split = array.reshape(shape[:dim] + (frame_groups, 2, 2, size) + shape[dim + 1 :])
        order = list(range(split.ndim))
        order[dim], order[dim + 2] = dim + 2, dim
        return split.transpose(order)

    in_columns = by_place(grad_in.T, 0).reshape(2, 2, D // 4, 128).astype(jnp.bfloat16)
    d_mods = jnp.stack(
        [
            jnp.concatenate([d_first_mods[0], d_first_mods[1], d_mod_mid[0]], axis=1),
            jnp.concatenate([d_mod_mid[1], d_mod_mid[2], d_mod_mid[3]], axis=1),
        ]
    )
    sum_qkv, sum_in, sum_mod, d_cond_rows = last_block(
        grad_qkv, in_columns, d_mods, cond_parts, low_mod, loss_parts, 3
    )
    loss_sum = jnp.sum(d_cond_rows[:, :, :, mod_rows : mod_rows + 3, 0].astype(jnp.float32))
    d_cond_t = (
        d_cond_rows[:, :, :, :mod_rows, :].transpose(2, 1, 0, 3, 4).reshape(D, frames_total)
    ).astype(jnp.float32)
    d_pre_two = jax.vjp(jax.nn.silu, pre_two_t)[1](d_cond_t)[0]
    d_pre_own = lax.dynamic_slice_in_dim(d_pre_two, first_col, small_cols, 0)
    grad_second = jnp.einsum("fi,jf->ij", first_placed, d_pre_own, precision=HIGH)
    second_cols = lax.dynamic_slice_in_dim(
        small_full.reshape(D, small_lanes), FREQ + first_col, small_cols, 1
    ).astype(jnp.float32)
    d_first = jnp.einsum("kf,kj->jf", d_pre_two, second_cols, precision=HIGH)
    d_pre_one = jax.vjp(jax.nn.silu, pre_one_own)[1](d_first)[0]
    grad_first = jnp.einsum("fi,jf->ij", features_placed, d_pre_one, precision=HIGH)
    ff_cols = mlp_weights.shape[2]
    sum_rest = sum_rest.astype(jnp.float32)
    sum_mlp = jnp.stack([sum_rest[:, :ff_cols], sum_rest[:, ff_cols : 2 * ff_cols]])
    far_first = 2 * ff_cols + width_local
    far = lax.ppermute(sum_rest[:, far_first:], "mp", [(0, 1), (1, 0)])
    sum_out = sum_rest[:, 2 * ff_cols : far_first] + far[:, :width_local]
    sum_attn = jnp.stack([sum_qkv[0], sum_qkv[1], sum_qkv[2], sum_out])
    head_first = width_local + P_SIZE
    sum_head = (sum_rest[:, far_first:] + far)[:, head_first : head_first + P_SIZE]
    sum_ends = half_of(jnp.concatenate([sum_in[:, :P_SIZE], sum_head], axis=1).T, 1)
    sum_small = jnp.concatenate([grad_first, grad_second, sum_ends], axis=0)
    learning_rate = 0.5 * math.sqrt(tokens_total * P_SIZE / D)
    attn_new, attn_moment_new, attn_average_new, attn_copy = update(
        attn_weights, sum_attn, attn_moment, attn_average, learning_rate
    )
    mlp_new, mlp_moment_new, mlp_average_new, mlp_copy = update(
        mlp_weights, sum_mlp, mlp_moment, mlp_average, learning_rate
    )
    mod_new, mod_moment_new, mod_average_new, mod_copy = update(
        mod_weight, sum_mod, mod_moment, mod_average, learning_rate
    )
    small_new, small_moment_new, small_average_new, small_copy = update(
        small_weights, sum_small, small_moment, small_average, learning_rate
    )
    return (
        loss_sum,
        noised_count,
        attn_new,
        attn_moment_new,
        attn_average_new,
        attn_copy,
        mlp_new,
        mlp_moment_new,
        mlp_average_new,
        mlp_copy,
        mod_new,
        mod_moment_new,
        mod_average_new,
        mod_copy,
        small_new,
        small_moment_new,
        small_average_new,
        small_copy,
    )


def solution(mesh):
    return jax.shard_map(
        per_device,
        mesh=mesh,
        in_specs=(
            P("frames", None),
            P("frames", None),
            P("frames"),
            P(),
            P(),
            P(None, "frames", "mp"),
            P(None, "frames", "mp"),
            P("frames", "mp"),
            P(None, ("frames", "mp")),
            P(None, "frames", "mp"),
            P(None, "frames", "mp"),
            P("frames", "mp"),
            P(None, ("frames", "mp")),
            P(None, "frames", "mp"),
            P(None, "frames", "mp"),
            P("frames", "mp"),
            P(None, ("frames", "mp")),
        ),
        out_specs=(
            P(),
            P(),
            P(None, "frames", "mp"),
            P(None, "frames", "mp"),
            P(None, "frames", "mp"),
            P(None, "frames", "mp"),
            P(None, "frames", "mp"),
            P(None, "frames", "mp"),
            P(None, "frames", "mp"),
            P(None, "frames", "mp"),
            P("frames", "mp"),
            P("frames", "mp"),
            P("frames", "mp"),
            P("frames", "mp"),
            P(None, ("frames", "mp")),
            P(None, ("frames", "mp")),
            P(None, ("frames", "mp")),
            P(None, ("frames", "mp")),
        ),
        check_vma=False,
    )
```

```python
import functools
import math

import jax
import jax.numpy as jnp
import numpy as np
from jax import lax
from jax.experimental import pallas as pl
from jax.experimental.pallas import tpu as pltpu
from jax.sharding import PartitionSpec as P

D = 1024
HD = 64
CH = 4
FREQ = 256
GRID = 16
P_SIZE = 16
TPF = 64
REACH = 4


HIGH = lax.Precision.HIGHEST
EPSILON = 1e-06
MOMENTUM = 0.5
EMA_DECAY = 0.5
TP_AXIS = "mp"


def rotation_matrix(head_width):
    groups = [head_width // 4, 3 * head_width // 8, 3 * head_width // 8]
    rotation = np.zeros((head_width, head_width), np.float32)
    offset = 0
    for group_size in groups:
        half_size = group_size // 2
        for pair_index in range(half_size):
            rotation[offset + half_size + pair_index, offset + pair_index] = -1.0
            rotation[offset + pair_index, offset + half_size + pair_index] = 1.0
        offset += group_size
    return rotation


def turn_phases(positions, group_size):
    half_size = group_size // 2
    frequency = 10000.0 ** (-np.arange(half_size, dtype=np.float32) / half_size)
    phases = positions[:, None] * frequency.astype(np.float32)[None, :]
    return [phases, phases]


def turn_table(frame_ref, patch_ref, first, count):
    lanes = lax.broadcasted_iota(jnp.int32, (1, patch_ref.shape[1]), 1)
    by_frame = lax.rem(lanes, HD) < HD // 4
    rows = [
        jnp.where(by_frame, frame_ref[pl.ds(first + k, 1), :], patch_ref[...])
        for k in range(count)
    ]
    return jnp.concatenate(rows, axis=0)


def clip_positions(clip_ids):
    frame_index = jnp.arange(clip_ids.shape[0], dtype=jnp.int32)
    starts_here = jnp.concatenate([jnp.ones((1,), bool), clip_ids[1:] != clip_ids[:-1]])
    clip_start = lax.cummax(jnp.where(starts_here, frame_index, 0), axis=0)
    return frame_index - clip_start


def patchify(frame_data):
    frame_total = frame_data.shape[0]
    patch_side = GRID // 2
    shaped = frame_data.reshape(frame_total, CH, patch_side, 2, patch_side, 2)
    return shaped.transpose(0, 2, 4, 1, 3, 5).reshape(frame_total * patch_side * patch_side, CH * 4)


def layer_norm(vector):
    row_mean = jnp.mean(vector, axis=-1, keepdims=True)
    centred = vector - row_mean
    variance = jnp.mean(centred * centred, axis=-1, keepdims=True)
    return centred * lax.rsqrt(variance + EPSILON)


def modulate_local(shaped, shift_rows, scale_rows):
    return layer_norm(shaped) * (1.0 + scale_rows) + shift_rows


def time_features(level_eff):
    half_size = FREQ // 2
    frequency = jnp.exp(-math.log(10000.0) * jnp.arange(half_size, dtype=jnp.float32) / half_size)
    phases = (level_eff * 1000.0)[:, None] * frequency[None, :]
    return jnp.concatenate([jnp.cos(phases), jnp.sin(phases)], axis=1)


NT=(((1,),(1,)),((),()))
NN=(((1,),(0,)),((),()))

def dotf(a,b,dims=NN):
    return lax.dot_general(a,b,dims,preferred_element_type=jnp.float32)

def split_pair(xT):
    r=lax.broadcasted_iota(jnp.int32,xT.shape,0)
    z=jnp.zeros_like(xT)
    return jnp.where(r<HD,xT,z), jnp.where(r<HD,z,xT)

def keep_of(t,TK,TQ,cs,qf):
    kf=lax.broadcasted_iota(jnp.int32,(TK,TQ),0)//TPF+t*(TK//TPF)
    return (kf>=cs)&(kf<=qf)

def fwd_kernel(lo_ref,mid_ref,hi_ref,q_ref,k_ref,v_ref,cs_ref,o_ref,ol_ref,lse_ref,vT,*,TQ,TK,W0,NQ):
    KS=k_ref.shape[0]
    def tr(i,_):
        s=pl.multiple_of(i*TK,TK)
        vT[:,pl.ds(s,TK)]=v_ref[pl.ds(s,TK),:].T
        return 0
    lax.fori_loop(lo_ref[0],KS//TK,tr,0)
    def qtile(j,_):
        qs=pl.multiple_of(j*TQ,TQ)
        qT=(q_ref[pl.ds(qs,TQ),:].T)*jnp.bfloat16(0.125)
        qA,qB=split_pair(qT)
        cs=cs_ref[0:1,pl.ds(qs,TQ)]
        qf=lax.broadcasted_iota(jnp.int32,(1,TQ),1)//TPF+(W0+j*(TQ//TPF))
        def step(t,carry,masked):
            ks=pl.multiple_of(t*TK,TK)
            kt=k_ref[pl.ds(ks,TK),:]
            out=[]
            if masked: keep=keep_of(t,TK,TQ,cs,qf)
            ones=jnp.ones((16,TK),jnp.bfloat16)
            both=[dotf(kt,qh) for qh in (qA,qB)]
            for h,(s,(m,l,o)) in enumerate(zip(both,carry)):
                if masked: s=jnp.where(keep,s,-1e30)
                mn=jnp.maximum(m,jnp.max(s,axis=0,keepdims=True))
                a=jnp.exp(m-mn)
                p=jnp.exp(s-mn)
                vh=jnp.concatenate([vT[h*HD:(h+1)*HD,pl.ds(ks,TK)],ones],axis=0)
                ov=dotf(vh,p.astype(jnp.bfloat16))
                l=l*a+ov[HD:HD+1]
                o=o*a+ov[:HD]
                out.append((mn,l,o))
            return tuple(out)
        init=tuple((jnp.full((1,TQ),-1e29,jnp.float32),jnp.zeros((1,TQ),jnp.float32),jnp.zeros((HD,TQ),jnp.float32)) for _ in range(2))
        c=lax.fori_loop(lo_ref[j],mid_ref[j],lambda t,c:step(t,c,True),init)
        c=lax.fori_loop(mid_ref[j],hi_ref[j],lambda t,c:step(t,c,False),c)
        c=lax.fori_loop(hi_ref[j],(W0*TPF+(j+1)*TQ+TK-1)//TK,lambda t,c:step(t,c,True),c)
        oT=jnp.concatenate([c[0][2]/c[0][1],c[1][2]/c[1][1]],axis=0)
        o_nat=oT.T
        o_ref[pl.ds(qs,TQ),:]=o_nat
        ol_ref[pl.ds(qs,TQ),:]=o_nat.astype(jnp.bfloat16)
        lse_ref[0,0:1,pl.ds(qs,TQ)]=c[0][0]+jnp.log(c[0][1])
        lse_ref[0,1:2,pl.ds(qs,TQ)]=c[1][0]+jnp.log(c[1][1])
        return 0
    lax.fori_loop(0,NQ,qtile,0)

def tile_bounds(cs_rel,TQ,TK,W0,NQ):
    fq=TQ//TPF; fk=TK//TPF
    j=jnp.arange(NQ)
    first=cs_rel[::fq]; last=cs_rel[fq-1::fq]
    lo=first//fk
    dg=(W0+j*fq+1)//fk
    mid=jnp.minimum((last+fk-1)//fk,dg)
    mid=jnp.maximum(mid,lo)
    hi=jnp.maximum(dg,mid)
    return lo.astype(jnp.int32),mid.astype(jnp.int32),hi.astype(jnp.int32)

def attn_fwd(q,k,v,cs_rel,TQ=512,TK=512):
    T,Wd=q.shape; KS=k.shape[0]; P=Wd//128
    W0=(KS-T)//TPF; NQ=T//TQ
    lo,mid,hi=tile_bounds(cs_rel,TQ,TK,W0,NQ)
    cs_tok=jnp.broadcast_to(jnp.repeat(cs_rel,TPF)[None,:],(8,T)).astype(jnp.int32)
    return pl.pallas_call(
        functools.partial(fwd_kernel,TQ=TQ,TK=TK,W0=W0,NQ=NQ),
        grid_spec=pltpu.PrefetchScalarGridSpec(num_scalar_prefetch=3,grid=(P,),
            in_specs=[pl.BlockSpec((T,128),lambda p,*_:(0,p)),pl.BlockSpec((KS,128),lambda p,*_:(0,p)),pl.BlockSpec((KS,128),lambda p,*_:(0,p)),pl.BlockSpec((8,T),lambda p,*_:(0,0))],
            out_specs=[pl.BlockSpec((T,128),lambda p,*_:(0,p)),pl.BlockSpec((T,128),lambda p,*_:(0,p)),pl.BlockSpec((1,8,T),lambda p,*_:(p,0,0))],
            scratch_shapes=[pltpu.VMEM((128,KS),jnp.bfloat16)]),
        out_shape=[jax.ShapeDtypeStruct((T,Wd),jnp.float32),jax.ShapeDtypeStruct((T,Wd),jnp.bfloat16),jax.ShapeDtypeStruct((P,8,T),jnp.float32)],
        compiler_params=pltpu.CompilerParams(vmem_limit_bytes=48<<20),
        cost_estimate=pl.CostEstimate(flops=10**11,bytes_accessed=2*10**7,transcendentals=3*10**7),
        name="attn_forward",
    )(lo,mid,hi,q,k,v,cs_tok)

def bwd_kernel(lo_ref,mid_ref,hi_ref,q_ref,k_ref,v_ref,do_ref,o_ref,lse_ref,cs_ref,dq_ref,dk_ref,dv_ref,kT,dkT,dvT,*,TQ,TK,W0,NQ):
    KS=k_ref.shape[0]
    def tr(i,_):
        s=pl.multiple_of(i*TK,TK)
        kT[:,pl.ds(s,TK)]=k_ref[pl.ds(s,TK),:].T
        return 0
    lax.fori_loop(lo_ref[0],KS//TK,tr,0)
    dkT[...]=jnp.zeros_like(dkT); dvT[...]=jnp.zeros_like(dvT)
    def qtile(j,_):
        qs=pl.multiple_of(j*TQ,TQ)
        qT=(q_ref[pl.ds(qs,TQ),:].T)*jnp.bfloat16(0.125)
        qh=split_pair(qT)
        doT=do_ref[pl.ds(qs,TQ),:].T
        doh=split_pair(doT)
        oT=o_ref[pl.ds(qs,TQ),:].T
        prod=oT*doT.astype(jnp.float32)
        delta=(jnp.sum(prod[:HD],axis=0,keepdims=True),jnp.sum(prod[HD:],axis=0,keepdims=True))
        lse=(lse_ref[0,0:1,pl.ds(qs,TQ)],lse_ref[0,1:2,pl.ds(qs,TQ)])
        cs=cs_ref[0:1,pl.ds(qs,TQ)]
        qf=lax.broadcasted_iota(jnp.int32,(1,TQ),1)//TPF+(W0+j*(TQ//TPF))
        def step(t,carry,masked):
            ks=pl.multiple_of(t*TK,TK)
            kt=k_ref[pl.ds(ks,TK),:]; vt=v_ref[pl.ds(ks,TK),:]
            out=[]
            if masked: keep=keep_of(t,TK,TQ,cs,qf)
            for h in range(2):
                r=slice(h*HD,(h+1)*HD)
                s=dotf(kt,qh[h])
                p=jnp.exp(s-lse[h])
                if masked: p=jnp.where(keep,p,0.0)
                dp=dotf(vt,doh[h])
                ds=(p*(dp-delta[h])).astype(jnp.bfloat16)
                pb=p.astype(jnp.bfloat16)
                dvT[r,pl.ds(ks,TK)]+=dotf(doT[r],pb,NT)
                dkT[r,pl.ds(ks,TK)]+=dotf(qT[r],ds,NT)
                out.append(carry[h]+dotf(kT[r,pl.ds(ks,TK)],ds))
            return tuple(out)
        init=(jnp.zeros((HD,TQ),jnp.float32),)*2
        c=lax.fori_loop(lo_ref[j],mid_ref[j],lambda t,c:step(t,c,True),init)
        c=lax.fori_loop(mid_ref[j],hi_ref[j],lambda t,c:step(t,c,False),c)
        c=lax.fori_loop(hi_ref[j],(W0*TPF+(j+1)*TQ+TK-1)//TK,lambda t,c:step(t,c,True),c)
        dq_ref[pl.ds(qs,TQ),:]=(jnp.concatenate(c,axis=0)*0.125).T
        return 0
    lax.fori_loop(0,NQ,qtile,0)
    def back(i,_):
        s=pl.multiple_of(i*TK,TK)
        dk_ref[pl.ds(s,TK),:]=dkT[:,pl.ds(s,TK)].T.astype(dk_ref.dtype)
        dv_ref[pl.ds(s,TK),:]=dvT[:,pl.ds(s,TK)].T.astype(dv_ref.dtype)
        return 0
    lax.fori_loop(0,KS//TK,back,0)

def attn_bwd(q,k,v,do,o,lse,cs_rel,TQ=512,TK=512,out_dt=jnp.bfloat16):
    T,Wd=q.shape; KS=k.shape[0]; P=Wd//128
    W0=(KS-T)//TPF; NQ=T//TQ
    lo,mid,hi=tile_bounds(cs_rel,TQ,TK,W0,NQ)
    cs_tok=jnp.broadcast_to(jnp.repeat(cs_rel,TPF)[None,:],(8,T)).astype(jnp.int32)
    tb=pl.BlockSpec((T,128),lambda p,*_:(0,p)); kb=pl.BlockSpec((KS,128),lambda p,*_:(0,p))
    return pl.pallas_call(
        functools.partial(bwd_kernel,TQ=TQ,TK=TK,W0=W0,NQ=NQ),
        grid_spec=pltpu.PrefetchScalarGridSpec(num_scalar_prefetch=3,grid=(P,),
            in_specs=[tb,kb,kb,tb,tb,pl.BlockSpec((1,8,T),lambda p,*_:(p,0,0)),pl.BlockSpec((8,T),lambda p,*_:(0,0))],
            out_specs=[tb,kb,kb],
            scratch_shapes=[pltpu.VMEM((128,KS),jnp.bfloat16),pltpu.VMEM((128,KS),jnp.float32),pltpu.VMEM((128,KS),jnp.float32)]),
        out_shape=[jax.ShapeDtypeStruct((T,Wd),jnp.float32),jax.ShapeDtypeStruct((KS,Wd),out_dt),jax.ShapeDtypeStruct((KS,Wd),out_dt)],
        compiler_params=pltpu.CompilerParams(vmem_limit_bytes=56<<20),
        cost_estimate=pl.CostEstimate(flops=2*10**11,bytes_accessed=5*10**7,transcendentals=3*10**7),
        name="attn_backward",
    )(lo,mid,hi,q,k,v,do,o,lse,cs_tok)


def update(weight, gradient, moment, average, learning_rate):
    moment_new = MOMENTUM * moment + gradient
    weight_new = weight - learning_rate * (gradient + MOMENTUM * moment_new)
    average_new = EMA_DECAY * average + (1.0 - EMA_DECAY) * weight_new
    return (weight_new, moment_new, average_new, weight_new.astype(jnp.bfloat16))


TN = (((0,), (0,)), ((), ()))


def norm_rows(v):
    centred = v - jnp.mean(v, axis=-1, keepdims=True)
    inverse = lax.rsqrt(jnp.mean(centred * centred, axis=-1, keepdims=True) + EPSILON)
    return centred * inverse, inverse


def norm_rows_back(grad, normed, inverse):
    return inverse * (
        grad
        - jnp.mean(grad, axis=-1, keepdims=True)
        - normed * jnp.mean(grad * normed, axis=-1, keepdims=True)
    )


def gelu_pair(x):
    c = math.sqrt(2.0 / math.pi)
    sq = x * x
    t = jnp.tanh(c * (x + 0.044715 * (x * sq)))
    half = 0.5 * (1.0 + t)
    return x * half, half + (0.5 * c) * x * (1.0 - t * t) * (1.0 + 0.134145 * sq)


def mid_kernel(
    o_hbm, hid_ref, mod_ref, noise_ref, tw_ref, head_ref, gs_ref, wu_hbm, wd_hbm, wa_hbm, wox_hbm,
    dmix_hbm, dx1_ref, dmod_ref, loss_ref, rest_hbm,
    o_ref, dmix_ref, wo_ref, wox_ref, wu_ref, wd_ref, att, x1, out, dx2, n2, n2t, act, dgl, dout, doutt, datt, datt_t,
    recv_o, send_f, send_c, recv_c, send_e, recv_e, stage, ghead_ref, go_ref, gh_t,
    wsem, gsem, ssem, rsem, o_sem, m_sem, s_m, r_m, *, tp,
):
    f = lax.axis_index("frames")
    h = lax.axis_index("mp")
    bf16 = jnp.bfloat16
    x_peer = {"mp": 1 - h}
    tp_peer = x_peer
    core = lax.rem(f, 2)
    core_peer = {"frames": f + 1 - 2 * core}
    half = hid_ref.shape[0]
    rows = 128
    chunks = half // rows
    width = hid_ref.shape[1]
    ff = wu_hbm.shape[1]
    e = o_ref.shape[1]
    ft = 512
    dt = 256

    weights = [
        pltpu.make_async_copy(wu_hbm, wu_ref, wsem.at[0]),
        pltpu.make_async_copy(wd_hbm, wd_ref, wsem.at[1]),
    ]
    load_out = pltpu.make_async_copy(wa_hbm.at[3], wo_ref, wsem.at[2])
    load_far = pltpu.make_async_copy(wox_hbm, wox_ref, wsem.at[3])
    load_out.start()
    load_far.start()
    for w in weights:
        w.start()

    barrier = pltpu.get_barrier_semaphore()
    for peer in (x_peer, core_peer):
        pl.semaphore_signal(barrier, inc=1, device_id=peer, device_id_type=pl.DeviceIdType.MESH)
    pl.semaphore_wait(barrier, 2)
    tok_all = o_ref.shape[0]
    eh = e // 2

    def at(start, size):
        return pl.ds(pl.multiple_of(start, size), size)

    def frame_at(c, k):
        return pl.ds(h * (half // TPF) + c * (rows // TPF) + k, 1)

    def mod_row(i, c, k):
        return mod_ref[frame_at(c, k), (2 + i) * width : (3 + i) * width]

    def copy(src, dst, phase, c, peer):
        return pltpu.make_async_remote_copy(
            src_ref=src, dst_ref=dst, send_sem=ssem.at[phase, c], recv_sem=rsem.at[phase, c],
            device_id=peer, device_id_type=pl.DeviceIdType.MESH,
        )

    def copy_a(c):
        theirs = o_ref.at[at((1 - h) * half + c * rows, rows)]
        return copy(theirs, recv_o.at[at(c * rows, rows)], 0, c, x_peer)

    def copy_b(c):
        return copy(
            n2.at[at(c * 2 * rows, rows)], n2.at[at(c * 2 * rows + rows, rows)], 1, c, tp_peer
        )

    def copy_c(c):
        return copy(send_c.at[at(c * rows, rows)], recv_c.at[at(c * rows, rows)], 2, c, tp_peer)

    def copy_d(c):
        return copy(
            dout.at[at(c * 2 * rows, rows)], dout.at[at(c * 2 * rows + rows, rows)], 3, c, tp_peer
        )

    def copy_e(c):
        return copy(send_e.at[at(c * rows, rows)], recv_e.at[at(c * rows, rows)], 4, c, tp_peer)

    def copy_f(c):
        there = dmix_ref.at[at(h * half + c * rows, rows)]
        return copy(send_f.at[at(c * rows, rows)], there, 5, c, x_peer)

    def lanes(k):
        return pl.ds(pl.multiple_of(k * eh, eh), eh)

    mine_o = pltpu.make_async_copy(
        o_hbm.at[at(core * tok_all, tok_all)], o_ref.at[:, lanes(core)], o_sem.at[0]
    )

    def give_o(k):
        return pltpu.make_async_remote_copy(
            src_ref=o_hbm.at[at((1 - core) * tok_all, tok_all)], dst_ref=o_ref.at[:, lanes(k)],
            send_sem=o_sem.at[1], recv_sem=o_sem.at[2], device_id=core_peer,
            device_id_type=pl.DeviceIdType.MESH,
        )

    give_o(core).start()
    mine_o.start()
    load_out.wait()
    mine_o.wait()
    give_o(1 - core).wait_recv()

    def mix_keep(rows_at, i):
        return pltpu.make_async_copy(
            dmix_ref.at[at(rows_at, rows), lanes(core)],
            dmix_hbm.at[at(core * tok_all + rows_at, rows)],
            m_sem.at[i],
        )

    def mix_give(rows_at, i, k):
        return pltpu.make_async_remote_copy(
            src_ref=dmix_ref.at[at(rows_at, rows), lanes(1 - core)],
            dst_ref=dmix_hbm.at[at(k * tok_all + rows_at, rows)],
            send_sem=s_m.at[i], recv_sem=r_m.at[i], device_id=core_peer,
            device_id_type=pl.DeviceIdType.MESH,
        )

    def phase_a(c, _):
        copy_a(c).start()
        return 0

    lax.fori_loop(0, chunks, phase_a, 0)
    load_far.wait()

    def phase_b(c, _):
        part = o_ref[at(h * half + c * rows, rows), :]
        copy_a(c).wait_recv()
        att[at(c * rows, rows), :] = dotf(part, wo_ref[...], NT) + dotf(
            recv_o[at(c * rows, rows), :], wox_ref[...], NT
        )
        for k in range(rows // TPF):
            r = at(c * rows + k * TPF, TPF)
            frame = pl.ds(c * (rows // TPF) + k, 1)
            a = att[r, :]
            v = hid_ref[r, :] + mod_row(0, c, k) * a
            x1[r, :] = v
            y, _inv = norm_rows(v)
            n2[at(c * 2 * rows + k * TPF, TPF), :] = (
                y * (1.0 + mod_row(2, c, k)) + mod_row(1, c, k)
            ).astype(bf16)
        copy_b(c).start()
        return 0

    lax.fori_loop(0, chunks, phase_b, 0)
    for w in weights:
        w.wait()

    def phase_c(c, _):
        copy_b(c).wait_recv()
        tok = at(c * 2 * rows, 2 * rows)
        n2t[:, tok] = n2[tok, :].T

        def up(i, _):
            cols = at(i * ft, ft)
            a, g = gelu_pair(dotf(n2[tok, :], wu_ref[:, cols]))
            act[tok, cols] = a.astype(bf16)
            dgl[tok, cols] = g.astype(bf16)
            return 0

        lax.fori_loop(0, ff // ft, up, 0)

        def down(i, _):
            cols = at(i * dt, dt)
            res = dotf(act[tok, :], wd_ref[cols, :], NT)
            out[at(c * rows, rows), cols] = res[:rows]
            send_c[at(c * rows, rows), cols] = res[rows:].astype(bf16)
            return 0

        lax.fori_loop(0, width // dt, down, 0)
        copy_c(c).start()
        return 0

    lax.fori_loop(0, chunks, phase_c, 0)

    ghead_ref[...] = jnp.zeros_like(ghead_ref)
    loss_ref[...] = jnp.zeros_like(loss_ref)

    def phase_d(c, _):
        copy_c(c).wait_recv()
        for k in range(rows // TPF):
            r = at(c * rows + k * TPF, TPF)
            frame = pl.ds(c * (rows // TPF) + k, 1)
            o = out[r, :] + recv_c[r, :].astype(jnp.float32)
            gate = mod_row(3, c, k)
            y, inv = norm_rows(x1[r, :] + gate * o)
            fn = y.astype(bf16)
            misfit = dotf(fn, head_ref[...], NT) - noise_ref[at(h * half + c * rows + k * TPF, TPF), :]
            weighted = tw_ref[frame_at(c, k), :] * misfit
            loss_ref[...] += weighted * misfit
            d_pred = (2.0 * gs_ref[0] * weighted).astype(bf16)
            ghead_ref[...] += dotf(d_pred, fn, TN)
            d_x2 = norm_rows_back(dotf(d_pred, head_ref[...]), y, inv)
            dx2[r, :] = d_x2
            dmod_ref[3, frame, :] = jnp.sum(d_x2 * o, axis=0, keepdims=True)
            dout[at(c * 2 * rows + k * TPF, TPF), :] = (gate * d_x2).astype(bf16)
        copy_d(c).start()
        return 0

    lax.fori_loop(0, chunks, phase_d, 0)

    def phase_e(c, _):
        copy_d(c).wait_recv()
        tok = at(c * 2 * rows, 2 * rows)
        doutt[:, tok] = dout[tok, :].T

        def down(i, _):
            cols = at(i * ft, ft)
            g = dotf(dout[tok, :], wd_ref[:, cols]) * dgl[tok, cols].astype(jnp.float32)
            dgl[tok, cols] = g.astype(bf16)
            return 0

        lax.fori_loop(0, ff // ft, down, 0)

        def up(i, _):
            cols = at(i * dt, dt)
            res = dotf(dgl[tok, :], wu_ref[cols, :], NT)
            out[at(c * rows, rows), cols] = res[:rows]
            send_e[at(c * rows, rows), cols] = res[rows:].astype(bf16)
            return 0

        lax.fori_loop(0, width // dt, up, 0)
        copy_e(c).start()
        return 0

    lax.fori_loop(0, chunks, phase_e, 0)

    def phase_f(c, _):
        copy_e(c).wait_recv()
        for k in range(rows // TPF):
            r = at(c * rows + k * TPF, TPF)
            frame = pl.ds(c * (rows // TPF) + k, 1)
            g = out[r, :] + recv_e[r, :].astype(jnp.float32)
            y, inv = norm_rows(x1[r, :])
            dmod_ref[1, frame, :] = jnp.sum(g, axis=0, keepdims=True)
            dmod_ref[2, frame, :] = jnp.sum(g * y, axis=0, keepdims=True)
            d_x1 = dx2[r, :] + norm_rows_back(g * (1.0 + mod_row(2, c, k)), y, inv)
            dx1_ref[r, :] = d_x1
            dmod_ref[0, frame, :] = jnp.sum(d_x1 * att[r, :], axis=0, keepdims=True)
            datt[r, :] = (mod_row(0, c, k) * d_x1).astype(
                bf16
            )
        mine = datt[at(c * rows, rows), :]
        send_f[at(c * rows, rows), :] = dotf(mine, wox_ref[...]).astype(bf16)
        copy_f(c).start()
        return 0

    lax.fori_loop(0, chunks, phase_f, 0)

    def weight_grads(left, right, start):
        def put(slot, i):
            return pltpu.make_async_copy(
                stage.at[slot], rest_hbm.at[at(i * dt, dt), pl.ds(start, ff)], gsem.at[slot]
            )

        def tile(i, _):
            slot = lax.rem(i, 2)

            @pl.when(i >= 2)
            def _():
                put(slot, i - 2).wait()

            def cols_of(j, _):
                cols = at(j * ft, ft)
                stage[slot, :, cols] = dotf(left[at(i * dt, dt), :], right[:, cols]).astype(bf16)
                return 0

            lax.fori_loop(0, ff // ft, cols_of, 0)
            put(slot, i).start()
            return 0

        lax.fori_loop(0, width // dt, tile, 0)
        for i in (width // dt - 2, width // dt - 1):
            put(i % 2, i).wait()

    weight_grads(n2t, dgl, 0)
    weight_grads(doutt, act, ff)

    def own_mix(c, _):
        first = h * half + c * rows
        r = at(c * rows, rows)
        datt_t[:, r] = datt[r, :].T
        dmix_ref[at(first, rows), :] = dotf(datt[r, :], wo_ref[...]).astype(bf16)
        mix_keep(first, c).start()
        mix_give(first, c, core).start()
        return 0

    lax.fori_loop(0, chunks, own_mix, 0)

    def phase_g(c, _):
        first = (1 - h) * half + c * rows
        arrived = dmix_ref.at[at(first, rows)]
        copy(send_f.at[at(c * rows, rows)], arrived, 5, c, x_peer).wait_recv()
        mix_keep(first, chunks + c).start()
        mix_give(first, chunks + c, core).start()
        return 0

    lax.fori_loop(0, chunks, phase_g, 0)

    def grad_out(i, _):
        d = at(i * dt, dt)
        go_ref[d, :e] = dotf(datt_t[d, :], o_ref[at(h * half, half), :]).astype(bf16)
        go_ref[d, e:] = dotf(datt_t[d, :], recv_o[...]).astype(bf16)
        return 0

    lax.fori_loop(0, width // dt, grad_out, 0)
    gh_t[...] = ghead_ref[...].T.astype(bf16)
    ends = [
        pltpu.make_async_copy(go_ref, rest_hbm.at[:, pl.ds(2 * ff, 2 * e)], gsem.at[2]),
        pltpu.make_async_copy(gh_t, rest_hbm.at[:, pl.ds(2 * ff + 2 * e, 128)], gsem.at[3]),
    ]
    for one in ends:
        one.start()
    for one in ends:
        one.wait()
    def sent(c, _):
        for one in (copy_a, copy_b, copy_c, copy_d, copy_e, copy_f):
            one(c).wait_send()
        for side in range(2):
            first = (h if side == 0 else 1 - h) * half + c * rows
            i = side * chunks + c
            mix_keep(first, i).wait()
            mix_give(first, i, core).wait_send()
            mix_give(first, i, 1 - core).wait_recv()
        return 0

    lax.fori_loop(0, chunks, sent, 0)
    give_o(core).wait_send()


def mid_block(o, hid, mod, noise, tw, head, gs, wu, wd, wa, wox, tp, cid):
    tok, e = o.shape[0] // 2, 2 * o.shape[1]
    half, width = hid.shape
    ff = wu.shape[1]
    own_frames = half // TPF
    f32, bf16 = jnp.float32, jnp.bfloat16
    vm = pl.BlockSpec(memory_space=pltpu.VMEM)
    anym = pl.BlockSpec(memory_space=pl.ANY)
    V = pltpu.VMEM
    return pl.pallas_call(
        functools.partial(mid_kernel, tp=tp),
        in_specs=[anym] + [vm] * 5 + [pl.BlockSpec(memory_space=pltpu.SMEM)] + [anym] * 4,
        out_specs=[anym] + [vm] * 3 + [anym],
        out_shape=[
            jax.ShapeDtypeStruct((2 * tok, e // 2), bf16),
            jax.ShapeDtypeStruct((half, width), f32),
            jax.ShapeDtypeStruct((4, own_frames, width), f32),
            jax.ShapeDtypeStruct((TPF, 128), f32),
            jax.ShapeDtypeStruct((width, 2 * ff + 2 * e + 128), bf16),
        ],
        scratch_shapes=[
            V((tok, e), bf16), V((tok, e), bf16),
            V((width, e), bf16), V((width, e), bf16), V((width, ff), bf16), V((width, ff), bf16),
            V((half, width), f32), V((half, width), f32), V((half, width), f32),
            V((half, width), f32),
            V((2 * half, width), bf16), V((width, 2 * half), bf16),
            V((2 * half, ff), bf16), V((2 * half, ff), bf16),
            V((2 * half, width), bf16), V((width, 2 * half), bf16),
            V((half, width), bf16), V((width, half), bf16),
            V((half, e), bf16), V((half, e), bf16),
            V((half, width), bf16), V((half, width), bf16),
            V((half, width), bf16), V((half, width), bf16),
            V((2, 256, ff), bf16), V((128, width), f32), V((width, 2 * e), bf16),
            V((width, 128), bf16),
            pltpu.SemaphoreType.DMA((4,)), pltpu.SemaphoreType.DMA((4,)),
            pltpu.SemaphoreType.DMA((6, half // 128)), pltpu.SemaphoreType.DMA((6, half // 128)),
            pltpu.SemaphoreType.DMA((3,)), pltpu.SemaphoreType.DMA((2 * half // 128,)),
            pltpu.SemaphoreType.DMA((2 * half // 128,)), pltpu.SemaphoreType.DMA((2 * half // 128,)),
        ],
        compiler_params=pltpu.CompilerParams(
            vmem_limit_bytes=62 << 20, collective_id=cid, has_side_effects=True
        ),
        cost_estimate=pl.CostEstimate(
            flops=4 * 10**10, bytes_accessed=3 * 10**7, transcendentals=2 * 10**6
        ),
        name="feed_forward",
    )(o, hid, mod, noise, tw, head, gs, wu, wd, wa, wox)


def split_three(v):
    high = v.astype(jnp.bfloat16)
    left = v - high.astype(jnp.float32)
    middle = left.astype(jnp.bfloat16)
    return high, middle, (left - middle.astype(jnp.float32)).astype(jnp.bfloat16)


def turn_back(g, cosine, sine, rot):
    parts = split_three(g * sine)
    return (g * cosine + sum(dotf(p, rot, NT) for p in parts)).astype(jnp.bfloat16)


def tail_kernel(
    dq_ref, n1_ref, w_ref, fcos_ref, fsin_ref, pcos_ref, psin_ref, rot_ref, hid_ref, scale_ref, dx1_ref, inp_ref,
    dk_hbm, dv_hbm,
    gq_ref, gin_ref, dss_ref,
    relayed, own, yrecv, zrecv, give, n1t, dproj, send_x, recv_x, part,
    lsem, s_d, r_d, s_y, r_y, s_z, r_z, s_x, r_x,
):
    f = lax.axis_index("frames")
    h = lax.axis_index("mp")
    n = lax.axis_size("frames")
    core = lax.rem(f, 2)
    odd = lax.rem(lax.div(f, 2), 2)
    core_peer = {"frames": f + 1 - 2 * core}
    y_peer = {"frames": f + 2 - 4 * odd}
    before = {"frames": lax.rem(f - 4 + n, n)}
    after = {"frames": lax.rem(f + 4, n)}
    x_peer = {"mp": 1 - h}
    tok, width = n1_ref.shape
    eh = dq_ref.shape[1]
    half = tok // 2
    rows = 256
    f32, bf16 = jnp.float32, jnp.bfloat16
    MESH = pl.DeviceIdType.MESH
    sides = (dk_hbm, dv_hbm)
    share = width // n

    def at(start, size):
        return pl.ds(pl.multiple_of(start, size), size)

    loads = [
        pltpu.make_async_copy(
            sides[s].at[pl.ds(b * 2 * tok, 2 * tok)], (own, relayed)[j].at[s], lsem.at[s, j]
        )
        for s in range(2)
        for j, b in enumerate((2, 0))
    ]
    for one in loads:
        one.start()

    barrier = pltpu.get_barrier_semaphore()
    for peer in (core_peer, y_peer, x_peer):
        pl.semaphore_signal(barrier, inc=1, device_id=peer, device_id_type=MESH)

    @pl.when(f >= 4)
    def _():
        pl.semaphore_signal(barrier, inc=1, device_id=before, device_id_type=MESH)

    @pl.when(f + 4 < n)
    def _():
        pl.semaphore_signal(barrier, inc=1, device_id=after, device_id_type=MESH)

    pl.semaphore_wait(barrier, 3 + jnp.where(f >= 4, 1, 0) + jnp.where(f + 4 < n, 1, 0))

    def half_at(i2):
        return lax.rem(i2 + 1 - h, 2) * half

    def rows_of(i2, tc):
        return tc * tok + half_at(i2)

    def remote(src, dst, send, recv, peer):
        return pltpu.make_async_remote_copy(
            src_ref=src, dst_ref=dst, send_sem=send, recv_sem=recv, device_id=peer,
            device_id_type=MESH,
        )

    def y_copy(i2, tc, s):
        first = rows_of(i2, tc)
        i = 2 * i2 + tc
        return remote(
            sides[s].at[at(2 * tok + first, half)], yrecv.at[s, at(first, half)],
            s_y.at[s, i], r_y.at[s, i], y_peer,
        )

    def z_copy(i2, tc, s):
        r = at(rows_of(i2, tc), half)
        i = 2 * i2 + tc
        return remote(relayed.at[s, r], zrecv.at[s, r], s_z.at[s, i], r_z.at[s, i], before)

    def d_copy(k, i2, tc):
        r = at(half_at(i2), half)
        return remote(
            give.at[k, r], dproj.at[k, r, pl.ds(tc * eh, eh)], s_d.at[k, i2], r_d.at[k, i2],
            core_peer,
        )

    def x_copy(i):
        r = at(i * rows, rows)
        return remote(send_x.at[r], recv_x.at[r], s_x.at[i], r_x.at[i], x_peer)

    for one in loads:
        one.wait()

    def start_far(i2, _):
        for tc in range(2):
            for s in range(2):
                y_copy(i2, tc, s).start()

                @pl.when((odd == 0) & (f >= 4))
                def _():
                    z_copy(i2, tc, s).start()

        return 0

    lax.fori_loop(0, 2, start_far, 0)

    @pl.when(f + 4 >= n)
    def _():
        zrecv[...] = jnp.zeros_like(zrecv)

    def settle(k, i2, tc, value):
        r = at(half_at(i2), half)

        @pl.when(core == tc)
        def _():
            dproj[k, r, tc * eh : (tc + 1) * eh] = value

        @pl.when(core != tc)
        def _():
            give[k, r, :] = value
            d_copy(k, i2, 1 - tc).start()

    def arrived(k, i2):
        for tc in range(2):

            @pl.when(core == tc)
            def _():
                d_copy(k, i2, 1 - tc).wait_recv()

    def turned(g, i2, tc):
        first = tc * (tok // TPF) + lax.div(half_at(i2), TPF)
        cosine = turn_table(fcos_ref, pcos_ref, first, half // TPF)
        sine = turn_table(fsin_ref, psin_ref, first, half // TPF)
        return turn_back(g, cosine, sine, rot_ref[...])

    def relay(i2, _):
        for tc in range(2):
            r = at(rows_of(i2, tc), half)
            settle(0, i2, tc, turned(dq_ref[r, :], i2, tc))

            @pl.when(odd == 1)
            def _():
                for s in range(2):
                    y_copy(i2, tc, s).wait_recv()

                    @pl.when(f >= 4)
                    def _():
                        relayed[s, r, :] = (
                            relayed[s, r, :].astype(f32) + yrecv[s, r, :].astype(f32)
                        ).astype(bf16)
                        z_copy(i2, tc, s).start()

        for b in range(2):
            r = at(half_at(i2) + b * rows, rows)
            n1t[:, r] = n1_ref[r, :].T
        return 0

    lax.fori_loop(0, 2, relay, 0)
    for i2 in range(2):
        arrived(0, i2)

    def grads(k):
        def tile(i, _):
            res = dotf(n1t[at(i * 256, 256), :], dproj[k]).astype(bf16)
            for q in range(256 // share):
                j = i * (256 // share // 4) + q // 4
                gq_ref[q % 2, (q // 2) % 2, k, at(j * share, share), :] = res[
                    q * share : (q + 1) * share
                ]
            return 0

        lax.fori_loop(0, width // 256, tile, 0)

    grads(0)

    def finish(i2, _):
        for tc in range(2):
            r = at(rows_of(i2, tc), half)
            for s in range(2):

                @pl.when(odd == 0)
                def _():
                    y_copy(i2, tc, s).wait_recv()

                @pl.when(f + 4 < n)
                def _():
                    z_copy(i2, tc, s).wait_recv()

                total = (
                    own[s, r, :].astype(f32)
                    + jnp.where(odd == 0, yrecv[s, r, :].astype(f32), 0.0)
                    + zrecv[s, r, :].astype(f32)
                )
                if s == 0:
                    settle(1, i2, tc, turned(total, i2, tc))
                else:
                    settle(2, i2, tc, total.astype(bf16))

        arrived(1, i2)
        arrived(2, i2)

        def block_of(q, _):
            b = lax.div(q, width // 256)
            cols = at(lax.rem(q, width // 256) * 256, 256)
            r = at(half_at(i2) + b * rows, rows)
            res = sum(dotf(dproj[k, r, :], w_ref[k, cols, :], NT) for k in range(3))

            @pl.when(i2 == 0)
            def _():
                send_x[at(b * rows, rows), cols] = res.astype(bf16)

            @pl.when((i2 == 0) & (lax.rem(q, width // 256) == width // 256 - 1))
            def _():
                x_copy(b).start()

            @pl.when(i2 == 1)
            def _():
                part[at(b * rows, rows), cols] = res

            return 0

        lax.fori_loop(0, half // rows * (width // 256), block_of, 0)
        return 0

    lax.fori_loop(0, 2, finish, 0)
    grads(1)
    grads(2)
    gin_ref[...] = jnp.zeros_like(gin_ref)

    def norm_back(i, _):
        x_copy(i).wait_recv()
        for k in range(rows // TPF):
            r = at(i * rows + k * TPF, TPF)
            frame = pl.ds(i * (rows // TPF) + k, 1)
            first = h * (half // TPF) + i * (rows // TPF) + k
            g = part[r, :] + recv_x[r, :].astype(f32)
            y, inv = norm_rows(hid_ref[r, :])
            dss_ref[0, frame, :] = jnp.sum(g, axis=0, keepdims=True)
            dss_ref[1, frame, :] = jnp.sum(g * y, axis=0, keepdims=True)
            d_hid = dx1_ref[r, :] + norm_rows_back(g * (1.0 + scale_ref[pl.ds(first, 1), width : 2 * width]), y, inv)
            gin_ref[...] += dotf(inp_ref[at(first * TPF, TPF), :], d_hid.astype(bf16), TN)
        return 0

    lax.fori_loop(0, half // rows, norm_back, 0)

    def sent(i2, _):
        for tc in range(2):
            for s in range(2):
                y_copy(i2, tc, s).wait_send()

                @pl.when(f >= 4)
                def _():
                    z_copy(i2, tc, s).wait_send()

            @pl.when(core != tc)
            def _():
                for k in range(3):
                    d_copy(k, i2, 1 - tc).wait_send()

        x_copy(i2).wait_send()
        return 0

    lax.fori_loop(0, half // rows, sent, 0)


def tail_block(dq, n1, w, tables, rot, hid, scale, dx1, inp, dk, dv, cid):
    tok, width = n1.shape
    e = 2 * dq.shape[1]
    half = tok // 2
    f32, bf16 = jnp.float32, jnp.bfloat16
    vm = pl.BlockSpec(memory_space=pltpu.VMEM)
    anym = pl.BlockSpec(memory_space=pl.ANY)
    V = pltpu.VMEM
    D_ = pltpu.SemaphoreType.DMA
    return pl.pallas_call(
        tail_kernel,
        in_specs=[vm] * 12 + [anym] * 2,
        out_specs=[vm] * 3,
        out_shape=[
            jax.ShapeDtypeStruct((2, 2, 3, width // 4, e), bf16),
            jax.ShapeDtypeStruct((128, width), f32),
            jax.ShapeDtypeStruct((2, half // TPF, width), f32),
        ],
        scratch_shapes=[
            V((2, tok * 2, e // 2), bf16), V((2, tok * 2, e // 2), bf16),
            V((2, tok * 2, e // 2), bf16), V((2, tok * 2, e // 2), bf16),
            V((3, tok, e // 2), bf16), V((width, tok), bf16), V((3, tok, e), bf16),
            V((half, width), bf16), V((half, width), bf16), V((half, width), f32),
            D_((2, 2)), D_((3, 2)), D_((3, 2)), D_((2, 4)), D_((2, 4)),
            D_((2, 4)), D_((2, 4)), D_((half // 256,)), D_((half // 256,)),
        ],
        compiler_params=pltpu.CompilerParams(
            vmem_limit_bytes=56 << 20, collective_id=cid, has_side_effects=True
        ),
        cost_estimate=pl.CostEstimate(
            flops=10**9, bytes_accessed=10**6, transcendentals=0
        ),
        name="projection_backward",
    )(dq, n1, w, *tables, rot, hid, scale, dx1, inp, dk, dv)


def proj_kernel(
    inp_ref, win_ref, mod_ref, w_ref, fcos_ref, fsin_ref, pcos_ref, psin_ref, rot_ref,
    n1_ref, hid_ref, q_hbm, k_hbm, v_hbm, wox_hbm,
    kv, give, q_keep, wr,
    wsem, lsem, qsem, s_core, r_core, s_y, r_y, s_z, r_z,
):
    f = lax.axis_index("frames")
    h = lax.axis_index("mp")
    n = lax.axis_size("frames")
    core = lax.rem(f, 2)
    odd = lax.rem(lax.div(f, 2), 2)
    core_peer = {"frames": f + 1 - 2 * core}
    y_peer = {"frames": f + 2 - 4 * odd}
    before = {"frames": lax.rem(f - 4 + n, n)}
    after = {"frames": lax.rem(f + 4, n)}
    tok, width = n1_ref.shape
    e = w_ref.shape[2]
    eh = e // 2
    low_core = core == 0
    half = tok // 2
    rows = 256
    chunks = tok // rows
    bf16 = jnp.bfloat16
    MESH = pl.DeviceIdType.MESH
    sides = (k_hbm, v_hbm)
    has_z = f >= 4
    has_next = f + 4 < n
    has_y = has_z | (odd == 1)

    def at(start, size):
        return pl.ds(pl.multiple_of(start, size), size)

    barrier = pltpu.get_barrier_semaphore()
    x_peer = {"mp": 1 - h}
    for peer in (core_peer, y_peer, x_peer):
        pl.semaphore_signal(barrier, inc=1, device_id=peer, device_id_type=MESH)

    @pl.when(has_z)
    def _():
        pl.semaphore_signal(barrier, inc=1, device_id=before, device_id_type=MESH)

    @pl.when(has_next)
    def _():
        pl.semaphore_signal(barrier, inc=1, device_id=after, device_id_type=MESH)

    def embed(i, _):
        for k in range(2):
            r = at(i * 2 * TPF + k * TPF, TPF)
            frame = pl.ds(i * 2 + k, 1)
            v = dotf(inp_ref[r, :], win_ref[...])
            y, _inv = norm_rows(v)
            scale = 1.0 + mod_ref[frame, width : 2 * width]
            n1_ref[r, :] = (y * scale + mod_ref[frame, :width]).astype(bf16)

            @pl.when(lax.div(i * 2 * TPF, half) == h)
            def _():
                hid_ref[at(lax.rem(i * 2 * TPF, half) + k * TPF, TPF), :] = v

        return 0

    lax.fori_loop(0, tok // (2 * TPF), embed, 0)

    def turn_weights(i, _):
        d = at(i * 256, 256)
        for k in range(2):
            for b in range(e // 256):
                cols = slice(b * 256, (b + 1) * 256)
                wr[k, d, cols] = dotf(w_ref[k, d, cols], rot_ref[...]).astype(bf16)
        return 0

    lax.fori_loop(0, width // 256, turn_weights, 0)
    pl.semaphore_wait(barrier, 3 + jnp.where(has_z, 1, 0) + jnp.where(has_next, 1, 0))

    def remote(src, dst, send, recv, peer):
        return pltpu.make_async_remote_copy(
            src_ref=src, dst_ref=dst, send_sem=send, recv_sem=recv, device_id=peer,
            device_id_type=MESH,
        )

    out_copy = remote(w_ref.at[3], wox_hbm, wsem.at[0], wsem.at[1], x_peer)
    out_copy.start()

    def block(s, b, i):
        return sides[s].at[at(b * tok + i * rows, rows)]

    def mine(s, tc, i):
        return kv.at[s, tc, at(i * rows, rows)]

    def keep(s, tc, i):
        return pltpu.make_async_copy(mine(s, tc, i), block(s, 4 + tc, i), lsem.at[s, tc, i])

    def z_copy(s, tc, i):
        return remote(
            mine(s, tc, i), block(s, tc, i), s_z.at[s, tc, i], r_z.at[s, tc, i], after
        )

    def y_copy(s, tc, i, src):
        return remote(src, block(s, 2 + tc, i), s_y.at[s, tc, i], r_y.at[s, tc, i], y_peer)

    def core_copy(s, i, tc):
        return remote(
            give.at[s, at(i * rows, rows)], mine(s, tc, i), s_core.at[s, i], r_core.at[s, i],
            core_peer,
        )

    def q_rows(tc, i):
        return q_hbm.at[at(tc * tok + i * rows, rows)]

    def q_own(i):
        return pltpu.make_async_copy(
            q_keep.at[at(i * rows, rows)], q_rows(core, i), qsem.at[i]
        )

    def q_copy(i, tc):
        return remote(
            give.at[2, at(i * rows, rows)], q_rows(tc, i), s_core.at[2, i], r_core.at[2, i],
            core_peer,
        )

    def onward(s, tc, i):
        keep(s, tc, i).start()

        @pl.when(has_next)
        def _():
            z_copy(s, tc, i).start()

        @pl.when(odd == 0)
        def _():
            y_copy(s, tc, i, mine(s, tc, i)).start()

    def rotated(r, i, k):
        frames = rows // TPF
        first = core * (tok // TPF) + i * frames
        cosine = turn_table(fcos_ref, pcos_ref, first, frames)
        sine = turn_table(fsin_ref, psin_ref, first, frames)
        parts = []
        for b in range(e // 256):
            cols = slice(b * 256, (b + 1) * 256)
            plain = dotf(n1_ref[r, :], w_ref[k, :, cols])
            turned = dotf(n1_ref[r, :], wr[k, :, cols])
            parts.append((plain * cosine + turned * sine).astype(bf16))
        return parts

    def own_chunk(i, _):
        r = at(i * rows, rows)
        keys = rotated(r, i, 1)
        values = dotf(n1_ref[r, :], w_ref[2]).astype(bf16)
        for s, pair in enumerate((keys, (values[:, :eh], values[:, eh:]))):
            kv[s, core, r, :] = jnp.where(low_core, pair[0], pair[1])
            give[s, r, :] = jnp.where(low_core, pair[1], pair[0])
            core_copy(s, i, core).start()
            onward(s, core, i)
        return 0

    lax.fori_loop(0, chunks, own_chunk, 0)

    def from_core(i, _):
        for s in range(2):
            core_copy(s, i, 1 - core).wait_recv()
            onward(s, 1 - core, i)
        return 0

    lax.fori_loop(0, chunks, from_core, 0)

    def queries(i, _):
        r = at(i * rows, rows)
        pair = rotated(r, i, 0)
        q_keep[r, :] = jnp.where(low_core, pair[0], pair[1])
        give[2, r, :] = jnp.where(low_core, pair[1], pair[0])
        q_own(i).start()
        q_copy(i, core).start()
        return 0

    lax.fori_loop(0, chunks, queries, 0)

    def from_z(g, _):
        tc = lax.rem(core + lax.div(g, chunks), 2)
        i = lax.rem(g, chunks)

        @pl.when(has_z)
        def _():
            for s in range(2):
                z_copy(s, tc, i).wait_recv()

                @pl.when(odd == 1)
                def _():
                    y_copy(s, tc, i, block(s, tc, i)).start()

        return 0

    lax.fori_loop(0, 2 * chunks, from_z, 0)

    def ended(i, _):
        q_own(i).wait()
        q_copy(i, 1 - core).wait_recv()
        q_copy(i, core).wait_send()
        for s in range(2):
            core_copy(s, i, core).wait_send()
            for tc in range(2):
                keep(s, tc, i).wait()

                @pl.when(has_y)
                def _():
                    y_copy(s, tc, i, mine(s, tc, i)).wait_recv()

                @pl.when(has_next)
                def _():
                    z_copy(s, tc, i).wait_send()

                @pl.when((odd == 0) | has_z)
                def _():
                    y_copy(s, tc, i, mine(s, tc, i)).wait_send()

        return 0

    lax.fori_loop(0, chunks, ended, 0)
    out_copy.wait_send()
    out_copy.wait_recv()


def proj_block(inp, win, mod, w, tables, rot, reach, cid):
    tok = inp.shape[0]
    width, e = w.shape[1:]
    f32, bf16 = jnp.float32, jnp.bfloat16
    vm = pl.BlockSpec(memory_space=pltpu.VMEM)
    anym = pl.BlockSpec(memory_space=pl.ANY)
    V = pltpu.VMEM
    D_ = pltpu.SemaphoreType.DMA
    chunks = tok // 256
    return pl.pallas_call(
        proj_kernel,
        in_specs=[vm] * 9,
        out_specs=[vm] * 2 + [anym] * 4,
        out_shape=[
            jax.ShapeDtypeStruct((tok, width), bf16),
            jax.ShapeDtypeStruct((tok // 2, width), f32),
            jax.ShapeDtypeStruct((2 * tok, e // 2), bf16),
            jax.ShapeDtypeStruct(((reach + 2) * tok, e // 2), bf16),
            jax.ShapeDtypeStruct(((reach + 2) * tok, e // 2), bf16),
            jax.ShapeDtypeStruct((width, e), bf16),
        ],
        scratch_shapes=[
            V((2, 2, tok, e // 2), bf16), V((3, tok, e // 2), bf16), V((tok, e // 2), bf16),
            V((2, width, e), bf16),
            D_((2,)), D_((2, 2, chunks)), D_((chunks,)), D_((3, chunks)), D_((3, chunks)),
            D_((2, 2, chunks)), D_((2, 2, chunks)), D_((2, 2, chunks)), D_((2, 2, chunks)),
        ],
        compiler_params=pltpu.CompilerParams(
            vmem_limit_bytes=48 << 20, collective_id=cid, has_side_effects=True
        ),
        cost_estimate=pl.CostEstimate(
            flops=6 * 10**10, bytes_accessed=3 * 10**7, transcendentals=0
        ),
        name="projection_forward",
    )(inp, win, mod, w, *tables, rot)


def last_kernel(
    g_hbm, gin_ref, dm_ref, cond_ref, wm_ref, loss_ref,
    sq_ref, sin_ref, smod_ref, dct_ref,
    g_own, g_in, near, near_in, side, side_in, far, far_in, ends, ends_peer, dm_peer, dm,
    dc_send, dc_peer,
    lsem, s_x, r_x, s_g, r_g, s_f, r_f, s_d, r_d, s_dz, r_dz,
):
    f = lax.axis_index("frames")
    h = lax.axis_index("mp")
    n = lax.axis_size("frames")
    nj = n // 4
    core = lax.rem(f, 2)
    y = lax.rem(lax.div(f, 2), 2)
    j = lax.div(f, 4)
    core_peer = {"frames": f + 1 - 2 * core}
    y_peer = {"frames": f + 2 - 4 * y}
    x_peer = {"mp": 1 - h}
    f32, bf16 = jnp.float32, jnp.bfloat16
    MESH = pl.DeviceIdType.MESH
    rows = g_hbm.shape[3] // nj

    def z_peer(t):
        return {"frames": lax.rem(f + 4 * t, n)}

    def from_j(t):
        return lax.rem(j - t + nj, nj)

    def at(start, size):
        return pl.ds(pl.multiple_of(start, size), size)

    load = pltpu.make_async_copy(g_hbm.at[core], g_own, lsem.at[0])
    load.start()
    barrier = pltpu.get_barrier_semaphore()
    for peer in [core_peer, y_peer, x_peer] + [z_peer(t) for t in range(1, nj)]:
        pl.semaphore_signal(barrier, inc=1, device_id=peer, device_id_type=MESH)
    pl.semaphore_wait(barrier, 2 + nj)

    def remote(src, dst, send, recv, peer):
        return pltpu.make_async_remote_copy(
            src_ref=src, dst_ref=dst, send_sem=send, recv_sem=recv, device_id=peer,
            device_id_type=MESH,
        )

    dm_x = remote(dm_ref.at[1 - h], dm_peer, s_x.at[0], r_x.at[0], x_peer)
    dm_x.start()
    core_g = remote(g_hbm.at[1 - core], near, s_g.at[0], r_g.at[0], core_peer)
    core_in = remote(gin_ref.at[1 - core], near_in, s_g.at[1], r_g.at[1], core_peer)
    core_g.start()
    core_in.start()

    dm_x.wait_recv()
    mine = dm_ref[h]
    theirs = dm_peer[...]
    low = h == 0
    dm[core, y, j] = jnp.concatenate(
        [jnp.where(low, mine, theirs), jnp.where(low, theirs, mine)], axis=0
    ).astype(bf16)

    def dm_z(t, src):
        block = dm.at[core, y, src]
        return remote(block, block, s_dz.at[0, t], r_dz.at[0, t], z_peer(t))

    for t in range(1, nj):
        dm_z(t, j).start()
    load.wait()
    core_g.wait_recv()
    core_in.wait_recv()

    def add_near(i, _):
        for s in range(2):
            for k in range(g_own.shape[1]):
                r = at(i * rows, rows)
                g_own[s, k, r, :] = (
                    g_own[s, k, r, :].astype(f32) + near[s, k, r, :].astype(f32)
                ).astype(bf16)
        return 0

    lax.fori_loop(0, nj, add_near, 0)
    g_in[...] = (gin_ref[core].astype(f32) + near_in[...].astype(f32)).astype(bf16)
    for t in range(1, nj):
        dm_z(t, from_j(t)).wait_recv()

    def dm_y(side_index):
        block = dm.at[core, side_index]
        return remote(block, block, s_d.at[0], r_d.at[0], y_peer)

    dm_y(y).start()
    y_g = remote(g_own.at[1 - y], side, s_g.at[2], r_g.at[2], y_peer)
    y_in = remote(g_in.at[1 - y], side_in, s_g.at[3], r_g.at[3], y_peer)
    y_g.start()
    y_in.start()
    dm_y(1 - y).wait_recv()

    def dm_core(core_index):
        block = dm.at[core_index]
        return remote(block, block, s_d.at[1], r_d.at[1], core_peer)

    dm_core(core).start()
    y_g.wait_recv()
    y_in.wait_recv()

    def add_side(i, _):
        for k in range(g_own.shape[1]):
            r = at(i * rows, rows)
            side[k, r, :] = (
                g_own[y, k, r, :].astype(f32) + side[k, r, :].astype(f32)
            ).astype(bf16)
        return 0

    lax.fori_loop(0, nj, add_side, 0)
    side_in[...] = (g_in[y].astype(f32) + side_in[...].astype(f32)).astype(bf16)

    def far_g(t):
        there = at(lax.rem(j + t, nj) * rows, rows)
        return remote(
            side.at[:, there], far.at[t - 1], s_f.at[0, t], r_f.at[0, t], z_peer(t)
        )

    def far_i(t):
        there = at(lax.rem(j + t, nj) * rows, rows)
        return remote(
            side_in.at[there], far_in.at[t - 1], s_f.at[1, t], r_f.at[1, t], z_peer(t)
        )

    for t in range(1, nj):
        far_g(t).start()
        far_i(t).start()

    dm_core(1 - core).wait_recv()
    frames = dm.shape[0] * dm.shape[1] * dm.shape[2] * dm.shape[3]
    wide = dm.shape[4]
    every = dm[...].reshape(frames, wide)
    part = dotf(wm_ref[...], every, NT)
    dc_send[:rows, :] = part
    dc_send[rows:, :] = jnp.broadcast_to(jnp.sum(loss_ref[...]), (8, frames))
    dc_x = remote(dc_send, dc_peer, s_x.at[1], r_x.at[1], x_peer)
    dc_x.start()

    def mod_cols(i, _):
        cols = at(i * 512, 512)
        block = dm[:, :, :, :, cols].reshape(frames, 512)
        res = dotf(cond_ref[...], block)
        smod_ref[:, cols] = res[:rows] + res[rows : 2 * rows] + res[2 * rows :]
        return 0

    lax.fori_loop(0, wide // 512, mod_cols, 0)
    dc_x.wait_recv()
    total = dc_send[...] + dc_peer[...]
    dct_ref[j, y, core, :rows, :] = total[:rows].astype(bf16)
    pieces = [p[:1].astype(f32) for p in split_three(total[rows:])]
    dct_ref[j, y, core, rows:, :] = jnp.concatenate(
        pieces + [jnp.zeros((13, frames), f32)], axis=0
    ).astype(bf16)

    def dc_z(t, src):
        block = dct_ref.at[src, y, core]
        return remote(block, block, s_dz.at[1, t], r_dz.at[1, t], z_peer(t))

    for t in range(1, nj):
        dc_z(t, j).start()
    for t in range(1, nj):
        dc_z(t, from_j(t)).wait_recv()

    def dc_y(side_index):
        block = dct_ref.at[:, side_index, core]
        return remote(block, block, s_d.at[2], r_d.at[2], y_peer)

    dc_y(y).start()

    here = at(j * rows, rows)
    for t in range(1, nj):
        far_g(t).wait_recv()
        far_i(t).wait_recv()
    for k in range(sq_ref.shape[0]):
        sq_ref[k] = side[k, here, :].astype(f32) + sum(
            far[t, k].astype(f32) for t in range(nj - 1)
        )
    ends[...] = side_in[here, :].astype(f32) + sum(
        far_in[t].astype(f32) for t in range(nj - 1)
    )
    ends_x = remote(ends, ends_peer, s_x.at[2], r_x.at[2], x_peer)
    ends_x.start()
    dc_y(1 - y).wait_recv()

    def dc_core(core_index):
        block = dct_ref.at[:, :, core_index]
        return remote(block, block, s_d.at[3], r_d.at[3], core_peer)

    dc_core(core).start()
    ends_x.wait_recv()
    sin_ref[...] = ends[...] + ends_peer[...]
    dc_core(1 - core).wait_recv()

    for one in (dm_x, core_g, core_in, y_g, y_in, dc_x, ends_x):
        one.wait_send()
    for one in (dm_y(y), dm_core(core), dc_y(y), dc_core(core)):
        one.wait_send()
    for t in range(1, nj):
        for one in (dm_z(t, j), dc_z(t, j), far_g(t), far_i(t)):
            one.wait_send()


def last_block(g, gin, dm, cond, wm, loss, cid):
    _, _, kinds, block_rows, e = g.shape
    n = lax.axis_size("frames")
    nj = n // 4
    rows = block_rows // nj
    own_frames, wide = dm.shape[1:]
    frames = n * 2 * own_frames
    f32, bf16 = jnp.float32, jnp.bfloat16
    vm = pl.BlockSpec(memory_space=pltpu.VMEM)
    anym = pl.BlockSpec(memory_space=pl.ANY)
    V = pltpu.VMEM
    D_ = pltpu.SemaphoreType.DMA
    return pl.pallas_call(
        last_kernel,
        in_specs=[anym] + [vm] * 5,
        out_specs=[vm] * 4,
        out_shape=[
            jax.ShapeDtypeStruct((kinds, rows, e), f32),
            jax.ShapeDtypeStruct((rows, 128), f32),
            jax.ShapeDtypeStruct((rows, wide), f32),
            jax.ShapeDtypeStruct((nj, 2, 2, rows + 16, frames), bf16),
        ],
        scratch_shapes=[
            V((2, kinds, block_rows, e), bf16), V((2, block_rows, 128), bf16),
            V((2, kinds, block_rows, e), bf16), V((2, block_rows, 128), bf16),
            V((kinds, block_rows, e), bf16), V((block_rows, 128), bf16),
            V((nj - 1, kinds, rows, e), bf16), V((nj - 1, rows, 128), bf16),
            V((rows, 128), f32), V((rows, 128), f32),
            V((own_frames, wide), f32), V((2, 2, nj, 2 * own_frames, wide), bf16),
            V((rows + 8, frames), f32), V((rows + 8, frames), f32),
            D_((1,)), D_((3,)), D_((3,)), D_((4,)), D_((4,)), D_((2, nj)), D_((2, nj)),
            D_((4,)), D_((4,)), D_((2, nj)), D_((2, nj)),
        ],
        compiler_params=pltpu.CompilerParams(
            vmem_limit_bytes=48 << 20, collective_id=cid, has_side_effects=True
        ),
        cost_estimate=pl.CostEstimate(
            flops=2 * 10**10, bytes_accessed=2 * 10**7, transcendentals=0
        ),
        name="weight_sums",
    )(g, gin, dm, cond, wm, loss)


def front_kernel(
    small_ref, feat_ref, wm_ref, w_ref,
    st_ref, feats_ref, pre1_ref, pre2_ref, wout_ref, ends_ref, mod_ref,
    wcol, mods,
    s_x, r_x, s_z, r_z, s_y, r_y, s_c, r_c, s_a, r_a, s_m, r_m,
):
    f = lax.axis_index("frames")
    h = lax.axis_index("mp")
    n = lax.axis_size("frames")
    nj = n // 4
    c = lax.rem(f, 2)
    y = lax.rem(lax.div(f, 2), 2)
    j = lax.div(f, 4)
    f32, bf16 = jnp.float32, jnp.bfloat16
    MESH = pl.DeviceIdType.MESH
    x_peer = {"mp": 1 - h}
    core_peer = {"frames": f + 1 - 2 * c}
    y_peer = {"frames": f + 2 - 4 * y}
    offsets = [
        (tj, ty, tc) for tj in range(nj) for ty in range(2) for tc in range(2)
    ][1:]

    def place(tj, ty, tc):
        return (
            lax.rem(j + tj, nj),
            y + ty - 2 * y * ty,
            c + tc - 2 * c * tc,
        )

    def peer_of(spot):
        return {"frames": 4 * spot[0] + 2 * spot[1] + spot[2]}

    def from_j(t):
        return lax.rem(j - t + nj, nj)

    def remote(src, dst, send, recv, peer):
        return pltpu.make_async_remote_copy(
            src_ref=src, dst_ref=dst, send_sem=send, recv_sem=recv, device_id=peer,
            device_id_type=MESH,
        )

    barrier = pltpu.get_barrier_semaphore()
    for o in offsets:
        pl.semaphore_signal(barrier, inc=1, device_id=peer_of(place(*o)), device_id_type=MESH)
    pl.semaphore_signal(barrier, inc=1, device_id=x_peer, device_id_type=MESH)
    pl.semaphore_wait(barrier, n)

    class Gather:
        def __init__(self, block, k):
            self.block, self.k = block, k

        def over_z(self, t, jj):
            b = self.block(jj, y, c)
            return remote(
                b, b, s_z.at[self.k, t], r_z.at[self.k, t], {"frames": lax.rem(f + 4 * t, n)}
            )

        def over_y(self, t, yy):
            b = self.block(from_j(t), yy, c)
            return remote(b, b, s_y.at[self.k, t], r_y.at[self.k, t], y_peer)

        def over_core(self, t, same, yy, cc):
            b = self.block(from_j(t), yy, cc)
            return remote(
                b, b, s_c.at[self.k, same, t], r_c.at[self.k, same, t], core_peer
            )

        def start(self):
            for t in range(1, nj):
                self.over_z(t, j).start()
            self.over_y(0, y).start()
            self.over_core(0, 0, y, c).start()

        def pass_z(self):
            for t in range(1, nj):
                self.over_z(t, from_j(t)).wait_recv()
                self.over_y(t, y).start()
                self.over_core(t, 0, y, c).start()

        def pass_y(self):
            for t in range(nj):
                self.over_y(t, 1 - y).wait_recv()
                self.over_core(t, 1, 1 - y, c).start()

        def finish(self):
            for t in range(nj):
                self.over_core(t, 0, y, 1 - c).wait_recv()
                self.over_core(t, 1, 1 - y, 1 - c).wait_recv()

        def sent(self):
            for t in range(1, nj):
                self.over_z(t, j).wait_send()
            for t in range(nj):
                self.over_y(t, y).wait_send()
                self.over_core(t, 0, y, c).wait_send()
                self.over_core(t, 1, 1 - y, c).wait_send()

    small = Gather(lambda a, b, d: st_ref.at[a, b, d], 0)
    feats = Gather(lambda a, b, d: feats_ref.at[d, b, a], 1)
    weights = Gather(lambda a, b, d: wout_ref.at[:, a, b, d], 2)

    small_x = remote(small_ref, st_ref.at[j, y, c, h], s_x.at[0], r_x.at[0], x_peer)
    small_x.start()
    feats_ref[c, y, j] = feat_ref[...]
    feats.start()

    def column_copy(i, spot, slot):
        return remote(
            wm_ref.at[spot[2], spot[1], spot[0]], wcol.at[slot[0], slot[1], slot[2]],
            s_a.at[i], r_a.at[i], peer_of(spot),
        )

    def source(o):
        return place((nj - o[0]) % nj, o[1], o[2])

    for i, o in enumerate(offsets):
        column_copy(i, place(*o), (j, y, c)).start()
    st_ref[j, y, c, h] = small_ref[...]
    wout_ref[:, j, y, c] = w_ref[...]
    wcol[j, y, c] = wm_ref[c, y, j]
    remote(
        small_ref, st_ref.at[j, y, c, 1 - h], s_x.at[0], r_x.at[0], x_peer
    ).wait_recv()
    small.start()
    feats.pass_z()
    small.pass_z()
    weights.start()
    feats.pass_y()
    small.pass_y()
    feats.finish()
    small.finish()

    total = st_ref.shape[0] * 4
    width = total * 2 * st_ref.shape[4]
    frames = feats_ref.shape[2] * 4 * feats_ref.shape[3]
    inner = feats_ref.shape[4]

    def exact(left, right, dims):
        m = left.shape[0]
        res = dotf(jnp.concatenate(split_three(left), axis=0), right, dims)
        return res[:m] + res[m : 2 * m] + res[2 * m :]

    def silu(v):
        return v * jax.nn.sigmoid(v)

    table = st_ref[...].reshape(width, st_ref.shape[5])
    fv = feats_ref[...].reshape(frames, inner)
    pre1 = exact(fv, table[:, :inner], NT)
    pre1_ref[...] = pre1
    pre2 = exact(silu(pre1), table[:, inner : inner + width], NT)
    pre2_ref[...] = pre2
    ends_ref[...] = table[:, inner + width : inner + width + 128].T
    for i, o in enumerate(offsets):
        column_copy(i, place(*o), source(o)).wait_recv()
    cols = wcol[...].reshape(width, wcol.shape[4])
    mods[...] = exact(silu(pre2), cols, NN).reshape(mods.shape)

    def mods_copy(i, spot, slot):
        return remote(
            mods.at[spot[2], spot[1], spot[0]], mod_ref.at[h, slot[2], slot[1], slot[0]],
            s_m.at[i], r_m.at[i], peer_of(spot),
        )

    for i, o in enumerate(offsets):
        mods_copy(i, place(*o), (j, y, c)).start()
    mod_ref[h, c, y, j] = mods[c, y, j]
    weights.pass_z()
    for i, o in enumerate(offsets):
        mods_copy(i, place(*o), source(o)).wait_recv()
    mods_x = remote(mod_ref.at[h], mod_ref.at[h], s_x.at[1], r_x.at[1], x_peer)
    mods_x.start()
    weights.pass_y()
    weights.finish()
    theirs = mod_ref.at[1 - h]
    remote(theirs, theirs, s_x.at[1], r_x.at[1], x_peer).wait_recv()

    small_x.wait_send()
    mods_x.wait_send()
    for g in (small, feats, weights):
        g.sent()
    for i, o in enumerate(offsets):
        column_copy(i, place(*o), (j, y, c)).wait_send()
        mods_copy(i, place(*o), (j, y, c)).wait_send()


def front_block(small, feat, wm, w, cid):
    n = lax.axis_size("frames")
    nj = n // 4
    cols, lanes = small.shape
    own_frames, inner = feat.shape
    frames = n * own_frames
    kinds, rows, e = w.shape
    wide = wm.shape[-1]
    width = rows * n
    f32, bf16 = jnp.float32, jnp.bfloat16
    vm = pl.BlockSpec(memory_space=pltpu.VMEM)
    V = pltpu.VMEM
    D_ = pltpu.SemaphoreType.DMA
    return pl.pallas_call(
        front_kernel,
        in_specs=[vm] * 4,
        out_specs=[vm] * 7,
        out_shape=[
            jax.ShapeDtypeStruct((nj, 2, 2, 2, cols, lanes), bf16),
            jax.ShapeDtypeStruct((2, 2, nj, own_frames, inner), f32),
            jax.ShapeDtypeStruct((frames, width), f32),
            jax.ShapeDtypeStruct((frames, width), f32),
            jax.ShapeDtypeStruct((kinds, nj, 2, 2, rows, e), bf16),
            jax.ShapeDtypeStruct((128, width), bf16),
            jax.ShapeDtypeStruct((2, 2, 2, nj, own_frames, wide), f32),
        ],
        scratch_shapes=[
            V((nj, 2, 2, rows, wide), bf16), V((2, 2, nj, own_frames, wide), f32),
            D_((2,)), D_((2,)), D_((3, nj)), D_((3, nj)), D_((3, nj)), D_((3, nj)),
            D_((3, 2, nj)), D_((3, 2, nj)), D_((n - 1,)), D_((n - 1,)), D_((n - 1,)),
            D_((n - 1,)),
        ],
        compiler_params=pltpu.CompilerParams(
            vmem_limit_bytes=48 << 20, collective_id=cid, has_side_effects=True
        ),
        cost_estimate=pl.CostEstimate(
            flops=4 * 10**10, bytes_accessed=2 * 10**7, transcendentals=0
        ),
        name="conditioning",
    )(small, feat, wm, w)


def per_device(
    latents,
    noise,
    levels,
    clip_ids,
    clean_flags,
    attn_weights,
    mlp_weights,
    mod_weight,
    small_weights,
    attn_moment,
    mlp_moment,
    mod_moment,
    small_moment,
    attn_average,
    mlp_average,
    mod_average,
    small_average,
):
    frame_count = latents.shape[0]
    tok_count = frame_count * TPF
    patch_side = GRID // 2
    frames_total = clip_ids.shape[0]
    tokens_total = frames_total * TPF
    width_local = attn_weights.shape[2]
    heads_local = width_local // HD
    key_span = (REACH + 1) * tok_count
    device = lax.axis_index("frames")
    mp_index = lax.axis_index("mp")
    first_frame = device * frame_count
    scale_qk = HD ** (-0.5)
    attn_low = attn_weights.astype(jnp.bfloat16)
    mlp_low = mlp_weights.astype(jnp.bfloat16)
    low_mod = mod_weight.astype(jnp.bfloat16)
    noised_all = (1 - clean_flags).astype(jnp.float32)
    noised_count = jnp.sum(noised_all)
    noised = lax.dynamic_slice_in_dim(noised_all, first_frame, frame_count)
    level_eff = levels * noised
    signal_scale = jnp.cos(0.5 * math.pi * level_eff)
    noise_scale = jnp.sin(0.5 * math.pi * level_eff)
    noise_patches = patchify(noise)
    inputs = patchify(signal_scale[:, None] * latents + noise_scale[:, None] * noise)
    in_clip_all = clip_positions(clip_ids)
    chip_frames = 2 * frame_count
    chip_first = (device // 2) * chip_frames
    in_clip = lax.dynamic_slice_in_dim(in_clip_all, chip_first, chip_frames).astype(jnp.float32)
    within = np.arange(TPF)
    patch_zero = np.zeros((TPF, HD // 4), np.float32)
    patch_angles = np.concatenate(
        [patch_zero]
        + turn_phases((within // patch_side).astype(np.float32), 3 * HD // 8)
        + turn_phases((within % patch_side).astype(np.float32), 3 * HD // 8),
        axis=1,
    )
    patch_angles = np.tile(patch_angles, (1, 4))
    frame_angles = jnp.tile(
        jnp.concatenate(
            turn_phases(in_clip, HD // 4) + [jnp.zeros((chip_frames, 3 * HD // 4))], axis=1
        ),
        (1, 4),
    )
    tables = (
        jnp.cos(frame_angles),
        jnp.sin(frame_angles),
        jnp.asarray(np.cos(patch_angles), jnp.float32),
        jnp.asarray(np.sin(patch_angles), jnp.float32),
    )
    turn_four = jnp.asarray(np.kron(np.eye(4, dtype=np.float32), rotation_matrix(HD)), jnp.bfloat16)
    clip_start = (
        lax.dynamic_slice_in_dim(
            jnp.arange(frames_total, dtype=jnp.int32) - in_clip_all, chip_first, chip_frames
        )
        - chip_first
        + REACH * frame_count
    )
    peers = lax.axis_size("frames")
    frame_groups = peers // 4
    small_rows, small_cols = small_weights.shape
    mod_rows, mod_cols = mod_weight.shape
    mod_share = mod_cols // peers
    mod_wide = -(-mod_share // 128) * 128
    small_lanes = FREQ + D + 128
    small_t = jnp.pad(
        small_weights.astype(jnp.bfloat16).T, ((0, 0), (0, small_lanes - small_rows))
    )
    mod_blocks = jnp.pad(
        low_mod.reshape(mod_rows, frame_groups, 2, 2, mod_share).transpose(3, 2, 1, 0, 4),
        ((0, 0),) * 4 + ((0, mod_wide - mod_share),),
    )
    small_full, features_placed, pre_one, pre_two, w_qkv, end_rows, mod_parts = front_block(
        small_t, time_features(level_eff), mod_blocks, attn_low, 4
    )
    w_qkv, up_low = lax.optimization_barrier((w_qkv, mlp_low[0]))
    w_up = lax.all_gather(up_low, "frames", axis=0, tiled=True)
    w_qkv = w_qkv.reshape(4, D, width_local)
    features_placed = features_placed.reshape(frames_total, FREQ)
    first_placed = jax.nn.silu(pre_one)
    pre_two_t = pre_two.T
    first_col = (device * lax.axis_size("mp") + mp_index) * small_cols
    pre_one_own = lax.dynamic_slice_in_dim(pre_one, first_col, small_cols, 1).T
    cond_rows = jax.nn.silu(
        lax.dynamic_slice_in_dim(pre_two, device * mod_rows, mod_rows, 1)
    )
    cond_parts = jnp.concatenate([part.T for part in split_three(cond_rows)], axis=0)
    modulation = (
        mod_parts[..., :mod_share].transpose(4, 0, 3, 2, 1, 5).reshape(frame_count, 6 * D)
    )
    inputs_low = inputs.astype(jnp.bfloat16)
    padding = ((0, 0), (0, 128 - P_SIZE))
    inputs_low = jnp.pad(inputs_low, padding)
    normed_one, hidden_half, queries, keys_wide, values_wide, w_out_far = proj_block(
        inputs_low,
        end_rows,
        modulation,
        w_qkv,
        tables,
        turn_four,
        REACH,
        2,
    )
    down_low = mlp_low[1]
    queries, down_low, w_up = lax.optimization_barrier((queries, down_low, w_up))
    w_down = lax.all_gather(down_low, "frames", axis=0, tiled=True)
    heads_wide, heads_low, log_totals = attn_fwd(queries, keys_wide, values_wide, clip_start)
    half = tok_count // 2
    own_frames = frame_count // 2

    def half_of(array, dim=0):
        size = array.shape[dim] // 2
        return lax.dynamic_slice_in_dim(array, mp_index * size, size, dim)

    grad_scale = 1.0 / jnp.maximum(noised_count, 1.0)
    head_lanes = ((0, 0), (P_SIZE, 128 - 2 * P_SIZE))
    frame_weight = jnp.broadcast_to(noised[:, None] / (TPF * P_SIZE), (frame_count, P_SIZE))
    d_mixed, d_shaped_one, d_mod_mid, loss_parts, grad_rest = mid_block(
        heads_low,
        hidden_half,
        modulation,
        jnp.pad(noise_patches, head_lanes),
        jnp.pad(frame_weight, head_lanes),
        end_rows,
        grad_scale.reshape(1),
        w_up,
        w_down,
        w_qkv,
        w_out_far,
        TP_AXIS,
        0,
    )
    sum_rest = lax.psum_scatter(grad_rest, "frames", scatter_dimension=0, tiled=True)
    d_queries, keys_grad_wide, values_grad_wide = attn_bwd(
        queries, keys_wide, values_wide, d_mixed, heads_wide, log_totals, clip_start
    )
    grad_qkv, grad_in, d_first_mods = tail_block(
        d_queries,
        normed_one,
        w_qkv,
        tables,
        turn_four,
        hidden_half,
        modulation,
        d_shaped_one,
        inputs_low,
        keys_grad_wide,
        values_grad_wide,
        1,
    )
    d_first_mods, sum_rest = lax.optimization_barrier((d_first_mods, sum_rest))
    def by_place(array, dim):
        shape = array.shape
        size = shape[dim] // (4 * frame_groups)
        split = array.reshape(shape[:dim] + (frame_groups, 2, 2, size) + shape[dim + 1 :])
        order = list(range(split.ndim))
        order[dim], order[dim + 2] = dim + 2, dim
        return split.transpose(order)

    in_columns = by_place(grad_in.T, 0).reshape(2, 2, D // 4, 128).astype(jnp.bfloat16)
    d_mods = jnp.stack(
        [
            jnp.concatenate([d_first_mods[0], d_first_mods[1], d_mod_mid[0]], axis=1),
            jnp.concatenate([d_mod_mid[1], d_mod_mid[2], d_mod_mid[3]], axis=1),
        ]
    )
    sum_qkv, sum_in, sum_mod, d_cond_rows = last_block(
        grad_qkv, in_columns, d_mods, cond_parts, low_mod, loss_parts, 3
    )
    loss_sum = jnp.sum(d_cond_rows[:, :, :, mod_rows : mod_rows + 3, 0].astype(jnp.float32))
    d_cond_t = (
        d_cond_rows[:, :, :, :mod_rows, :].reshape(D, frames_total)
    ).astype(jnp.float32)
    d_pre_two = jax.vjp(jax.nn.silu, pre_two_t)[1](d_cond_t)[0]
    d_pre_own = lax.dynamic_slice_in_dim(d_pre_two, first_col, small_cols, 0)
    grad_second = jnp.einsum("fi,jf->ij", first_placed, d_pre_own, precision=HIGH)
    second_cols = lax.dynamic_slice_in_dim(
        small_full.reshape(D, small_lanes), FREQ + first_col, small_cols, 1
    ).astype(jnp.float32)
    d_first = jnp.einsum("kf,kj->jf", d_pre_two, second_cols, precision=HIGH)
    d_pre_one = jax.vjp(jax.nn.silu, pre_one_own)[1](d_first)[0]
    grad_first = jnp.einsum("fi,jf->ij", features_placed, d_pre_one, precision=HIGH)
    ff_cols = mlp_weights.shape[2]
    sum_mlp = jnp.stack([sum_rest[:, :ff_cols], sum_rest[:, ff_cols : 2 * ff_cols]]).astype(
        jnp.float32
    )
    far_first = 2 * ff_cols + width_local
    near = sum_rest[:, far_first:]
    far = lax.ppermute(near, "mp", [(0, 1), (1, 0)]).astype(jnp.float32)
    sum_out = sum_rest[:, 2 * ff_cols : far_first].astype(jnp.float32) + far[:, :width_local]
    sum_attn = jnp.stack([sum_qkv[0], sum_qkv[1], sum_qkv[2], sum_out])
    head_first = width_local + P_SIZE
    sum_head = (near.astype(jnp.float32) + far)[:, head_first : head_first + P_SIZE]
    sum_ends = half_of(jnp.concatenate([sum_in[:, :P_SIZE], sum_head], axis=1).T, 1)
    sum_small = jnp.concatenate([grad_first, grad_second, sum_ends], axis=0)
    learning_rate = 0.5 * math.sqrt(tokens_total * P_SIZE / D)
    attn_new, attn_moment_new, attn_average_new, attn_copy = update(
        attn_weights, sum_attn, attn_moment, attn_average, learning_rate
    )
    mlp_new, mlp_moment_new, mlp_average_new, mlp_copy = update(
        mlp_weights, sum_mlp, mlp_moment, mlp_average, learning_rate
    )
    mod_new, mod_moment_new, mod_average_new, mod_copy = update(
        mod_weight, sum_mod, mod_moment, mod_average, learning_rate
    )
    small_new, small_moment_new, small_average_new, small_copy = update(
        small_weights, sum_small, small_moment, small_average, learning_rate
    )
    return (
        loss_sum,
        noised_count,
        attn_new,
        attn_moment_new,
        attn_average_new,
        attn_copy,
        mlp_new,
        mlp_moment_new,
        mlp_average_new,
        mlp_copy,
        mod_new,
        mod_moment_new,
        mod_average_new,
        mod_copy,
        small_new,
        small_moment_new,
        small_average_new,
        small_copy,
    )


def solution(mesh):
    return jax.shard_map(
        per_device,
        mesh=mesh,
        in_specs=(
            P("frames", None),
            P("frames", None),
            P("frames"),
            P(),
            P(),
            P(None, "frames", "mp"),
            P(None, "frames", "mp"),
            P("frames", "mp"),
            P(None, ("frames", "mp")),
            P(None, "frames", "mp"),
            P(None, "frames", "mp"),
            P("frames", "mp"),
            P(None, ("frames", "mp")),
            P(None, "frames", "mp"),
            P(None, "frames", "mp"),
            P("frames", "mp"),
            P(None, ("frames", "mp")),
        ),
        out_specs=(
            P(),
            P(),
            P(None, "frames", "mp"),
            P(None, "frames", "mp"),
            P(None, "frames", "mp"),
            P(None, "frames", "mp"),
            P(None, "frames", "mp"),
            P(None, "frames", "mp"),
            P(None, "frames", "mp"),
            P(None, "frames", "mp"),
            P("frames", "mp"),
            P("frames", "mp"),
            P("frames", "mp"),
            P("frames", "mp"),
            P(None, ("frames", "mp")),
            P(None, ("frames", "mp")),
            P(None, ("frames", "mp")),
            P(None, ("frames", "mp")),
        ),
        check_vma=False,
    )
```
